32 devices in a mesh: dp: 8 (over y, x, core), tensor: 4 (over z).
Axes of the slice: x: 2, y: 2, z: 4, core: 2. Of those that a mesh axis runs over, the one named last changes fastest.
Arguments:
- hidden_in: bfloat16 [4096, 1024], P(('dp', 'tensor')), may hold values from -6 to 6
- norm_in_gain: float32 [1024], replicated, may hold values from 0.5 to 1.5
- query_weight: bfloat16 [1024, 512], P('dp', 'tensor'), may hold values from -0.1875 to 0.1875
- key_weight: bfloat16 [1024, 128], P('dp'), may hold values from -0.1875 to 0.1875
- value_weight: bfloat16 [1024, 128], P('dp'), may hold values from -0.1875 to 0.1875
- output_weight: bfloat16 [512, 1024], P('tensor', 'dp'), may hold values from -2 to 2
- gate_weight: bfloat16 [1024, 1536], P('dp', 'tensor'), may hold values from -0.1875 to 0.1875
- inner_weight: bfloat16 [1024, 1536], P('dp', 'tensor'), may hold values from -0.1875 to 0.1875
- write_weight: bfloat16 [1024, 128], P('dp'), may hold values from -0.1875 to 0.1875
- read_weight: bfloat16 [1024, 128], P('dp'), may hold values from -0.1875 to 0.1875
- step_weight: bfloat16 [1024, 24], P('dp', 'tensor'), may hold values from -0.1875 to 0.1875
- conv_weight: float32 [4, 1536], P(None, 'tensor'), may hold values from -0.5 to 0.5
- conv_bias: float32 [1536], P('tensor'), may hold values from -0.5 to 0.5
- pair_conv_weight: float32 [4, 256], replicated, may hold values from -0.5 to 0.5
- pair_conv_bias: float32 [256], replicated, may hold values from -0.5 to 0.5
- step_bias: float32 [24], P('tensor'), may hold values from -4.5 to -1.5
- decay_log: float32 [24], P('tensor'), may hold values from 0 to 2.77
- skip_gain: float32 [24], P('tensor'), may hold values from 0.5 to 1.5
- state_gain: float32 [1536], P('tensor'), may hold values from 0.5 to 1.5
- state_out_weight: bfloat16 [1536, 1024], P('tensor', 'dp'), may hold values from -0.15625 to 0.15625
- norm_ffn_gain: float32 [1024], replicated, may hold values from 0.5 to 1.5
- feed_gate_weight: bfloat16 [1024, 2048], P('dp', 'tensor'), may hold values from -0.1875 to 0.1875
- feed_up_weight: bfloat16 [1024, 2048], P('dp', 'tensor'), may hold values from -0.1875 to 0.1875
- feed_down_weight: bfloat16 [2048, 1024], P('tensor', 'dp'), may hold values from -0.125 to 0.125
- out_cotangent: bfloat16 [4096, 1024], P(('dp', 'tensor')), may hold values from -6 to 6
Outputs:
- hidden_out: bfloat16 [4096, 1024], P(('dp', 'tensor'))
- gradient_hidden: float32 [4096, 1024], P(('dp', 'tensor'))
- gradient_norm_in_gain: float32 [1024], replicated
- gradient_query_weight: float32 [1024, 512], P('dp', 'tensor')
- gradient_key_weight: float32 [1024, 128], replicated
- gradient_value_weight: float32 [1024, 128], replicated
- gradient_output_weight: float32 [512, 1024], P('tensor', 'dp')
- gradient_gate_weight: float32 [1024, 1536], P('dp', 'tensor')
- gradient_inner_weight: float32 [1024, 1536], P('dp', 'tensor')
- gradient_write_weight: float32 [1024, 128], replicated
- gradient_read_weight: float32 [1024, 128], replicated
- gradient_step_weight: float32 [1024, 24], P('dp', 'tensor')
- gradient_conv_weight: float32 [4, 1536], P(None, 'tensor')
- gradient_conv_bias: float32 [1536], P('tensor')
- gradient_pair_conv_weight: float32 [4, 256], replicated
- gradient_pair_conv_bias: float32 [256], replicated
- gradient_step_bias: float32 [24], P('tensor')
- gradient_decay_log: float32 [24], P('tensor')
- gradient_skip_gain: float32 [24], P('tensor')
- gradient_state_gain: float32 [1536], P('tensor')
- gradient_state_out_weight: float32 [1536, 1024], P('tensor', 'dp')
- gradient_norm_ffn_gain: float32 [1024], replicated
- gradient_feed_gate_weight: float32 [1024, 2048], P('dp', 'tensor')
- gradient_feed_up_weight: float32 [1024, 2048], P('dp', 'tensor')
- gradient_feed_down_weight: float32 [2048, 1024], P('tensor', 'dp')
The draws below stay inside these ranges and needn't reach their ends.
All inputs are finite; a program needn't handle non-finite values.
Results may differ from the reference program's by a relative error of at most 0.014.
Values may be sent and summed in bfloat16 or wider, within the bound.
No kernel may reach another device: no remote copies, remote signals or barrier semaphores. Data moves between devices by JAX's collectives and lax.ppermute only.
A program may use at most 128 MiB of HBM per device.

```python
import jax
import jax.numpy as jnp
from jax import lax

D = 1024
QH = 8
KVH = 2
HD = 64
SH = 24
NSTATE = 128
FF = 2048
CONV = 4
LEN = 512
BLOCK = 128
SD = 1536
TOKENS = 4096
N_DP = 8
N_TENSOR = 4


def level_of(key, dims, split, low, top_value):
    def one(position, blocks):
        heights = jax.random.uniform(jax.random.fold_in(jax.random.fold_in(key, 6), position), (blocks,), jnp.float32, low / len(split), top_value / len(split))
        return jnp.repeat(jnp.exp(heights), dims[position] // blocks).reshape((-1,) + (1,) * (len(dims) - position - 1))

    factor_of = one(*split[0])
    for cut in split[1:]:
        factor_of = factor_of * one(*cut)
    return factor_of


def centred(stream_key, extent, scale, bound, cuts=(), held_as=jnp.bfloat16):
    loudness = level_of(stream_key, extent, cuts, -0.22, 0.18) if cuts else 1.0
    values = jax.random.normal(stream_key, extent, jnp.float32) * scale * loudness
    return jnp.minimum(jnp.maximum(values, -bound), bound).astype(held_as)


def setup_inputs(seed: int = 0) -> dict:
    key_list = jax.random.split(jax.random.key(seed), 26)
    return {
        "hidden_in": centred(key_list[0], (TOKENS, D), 1.0, 6.0, ((0, 32),)),
        "norm_in_gain": jnp.clip(1.0 + 0.1 * jax.random.normal(key_list[1], (D,), jnp.float32), 0.5, 1.5),
        "query_weight": centred(key_list[2], (D, QH * HD), D ** -0.5, 0.1875, ((0, 8), (1, 4))),
        "key_weight": centred(key_list[3], (D, KVH * HD), D ** -0.5, 0.1875, ((0, 8),)),
        "value_weight": centred(key_list[4], (D, KVH * HD), D ** -0.5, 0.1875, ((0, 8),)),
        "output_weight": centred(key_list[5], (QH * HD, D), (max(QH * HD // 64, 1)) ** -0.5, 2.0, ((0, 4), (1, 8))),
        "gate_weight": centred(key_list[6], (D, SD), D ** -0.5, 0.1875, ((0, 8), (1, 4))),
        "inner_weight": centred(key_list[7], (D, SD), D ** -0.5, 0.1875, ((0, 8), (1, 4))),
        "write_weight": centred(key_list[8], (D, NSTATE), D ** -0.5, 0.1875, ((0, 8),)),
        "read_weight": centred(key_list[9], (D, NSTATE), D ** -0.5, 0.1875, ((0, 8),)),
        "step_weight": centred(key_list[10], (D, SH), D ** -0.5, 0.1875, ((0, 8), (1, 4))),
        "conv_weight": jnp.clip(jax.random.uniform(key_list[11], (CONV, SD), jnp.float32, -0.5, 0.5) * level_of(key_list[11], (CONV, SD), ((1, 4),), -0.4, 0.0), -0.5, 0.5),
        "conv_bias": jnp.clip(jax.random.uniform(key_list[12], (SD,), jnp.float32, -0.5, 0.5) * level_of(key_list[12], (SD,), ((0, 4),), -0.4, 0.0), -0.5, 0.5),
        "pair_conv_weight": jnp.clip(jax.random.uniform(key_list[13], (CONV, 2 * NSTATE), jnp.float32, -0.5, 0.5), -0.5, 0.5),
        "pair_conv_bias": jnp.clip(jax.random.uniform(key_list[14], (2 * NSTATE,), jnp.float32, -0.5, 0.5), -0.5, 0.5),
        "step_bias": jnp.clip(-4.5 + 3.0 * jax.random.uniform(key_list[15], (SH,), jnp.float32) ** level_of(key_list[15], (SH,), ((0, 4),), -0.2, 0.2), -4.5, -1.5),
        "decay_log": jnp.clip(2.77 * jax.random.uniform(key_list[16], (SH,), jnp.float32) ** level_of(key_list[16], (SH,), ((0, 4),), -0.2, 0.2), 0.0, 2.77),
        "skip_gain": jnp.clip(0.5 + 1.0 * jax.random.uniform(key_list[17], (SH,), jnp.float32) ** level_of(key_list[17], (SH,), ((0, 4),), -0.2, 0.2), 0.5, 1.5),
        "state_gain": jnp.clip(1.0 + 0.1 * jax.random.normal(key_list[18], (SD,), jnp.float32), 0.5, 1.5),
        "state_out_weight": centred(key_list[19], (SD, D), SD ** -0.5, 0.15625, ((0, 4), (1, 8))),
        "norm_ffn_gain": jnp.clip(1.0 + 0.1 * jax.random.normal(key_list[20], (D,), jnp.float32), 0.5, 1.5),
        "feed_gate_weight": centred(key_list[21], (D, FF), D ** -0.5, 0.1875, ((0, 8), (1, 4))),
        "feed_up_weight": centred(key_list[22], (D, FF), D ** -0.5, 0.1875, ((0, 8), (1, 4))),
        "feed_down_weight": centred(key_list[23], (FF, D), FF ** -0.5, 0.125, ((0, 4), (1, 8))),
        "out_cotangent": centred(key_list[24], (TOKENS, D), 1.0, 6.0, ((0, 32),)),
    }


EPS = 1e-05
THETA = 10000.0
HIGHEST = lax.Precision.HIGHEST

@jax.custom_vjp
def low(v):
    return lax.optimization_barrier(v.astype(jnp.bfloat16)).astype(jnp.float32)

@jax.custom_vjp
def low_back(v):
    return v

def low_keep(v):
    return (low(v), None)

def low_pass(kept, grad):
    return (grad,)

def back_keep(v):
    return (v, None)

def back_low(kept, grad):
    return (low(grad),)
low.defvjp(low_keep, low_pass)
low_back.defvjp(back_keep, back_low)

def product(left, right):
    return jnp.dot(left, right, precision=HIGHEST, preferred_element_type=jnp.float32)

def root_norm(rows, gain):
    return rows * lax.rsqrt(lax.optimization_barrier(jnp.mean(rows * rows, axis=-1, keepdims=True)) + EPS) * gain

def rotate(values, heads, sign):
    length = values.shape[0]
    shaped = values.reshape(length, heads, -1)
    half = shaped.shape[2] // 2
    freq = THETA ** (-jnp.arange(half, dtype=jnp.float32) / half)
    angle = jnp.arange(length, dtype=jnp.float32)[:, None] * freq[None, :]
    cosine = jnp.cos(angle)[:, None, :]
    sine = sign * jnp.sin(angle)[:, None, :]
    first = shaped[:, :, :half]
    second = shaped[:, :, half:]
    turned = jnp.concatenate([first * cosine - second * sine, second * cosine + first * sine], axis=2)
    return turned.reshape(length, -1)

def causal_conv(values, weight, bias):
    taps = weight.shape[0]
    length = values.shape[0]
    padded = jnp.pad(values, ((taps - 1, 0), (0, 0)))
    total = bias[None, :] + jnp.zeros_like(values)
    for tap in range(taps):
        total = total + weight[tap][None, :] * padded[tap:tap + length]
    return total

def state_block(state, block):
    scaled, decay, write_rows, read_rows = block
    size = decay.shape[0]
    running = jnp.cumsum(decay, axis=0)
    lower = jnp.arange(size)[:, None] >= jnp.arange(size)[None, :]
    spread = running[:, None, :] - running[None, :, :]
    weights = jnp.exp(jnp.where(lower[:, :, None], spread, -1e+30))
    intersection = jnp.einsum('tn,sn->ts', read_rows, write_rows, precision=HIGHEST)
    inside = jnp.einsum('tsh,shp->thp', intersection[:, :, None] * weights, scaled, precision=HIGHEST)
    earlier = jnp.exp(running)[:, :, None] * jnp.einsum('tn,hpn->thp', read_rows, state, precision=HIGHEST)
    last = running[-1]
    carry = jnp.exp(last[None, :] - running)
    fresh = jnp.einsum('sh,shp,sn->hpn', carry, scaled, write_rows, precision=HIGHEST)
    return (jnp.exp(last)[:, None, None] * state + fresh, inside + earlier)

def mixer_state(inputs, writes, reads, steps_raw, gate_z, conv_weight, conv_bias, pair_weight, pair_bias, step_bias, decay_log, skip_gain):
    length = inputs.shape[0]
    heads = steps_raw.shape[1]
    width = writes.shape[1]
    mixed_inputs = jax.nn.silu(causal_conv(inputs, conv_weight, conv_bias))
    paired = jax.nn.silu(causal_conv(jnp.concatenate([writes, reads], axis=1), pair_weight, pair_bias))
    write_rows = paired[:, :width]
    read_rows = paired[:, width:]
    step = jax.nn.softplus(steps_raw + step_bias[None, :])
    decay = step * (-jnp.exp(decay_log))[None, :]
    shaped = mixed_inputs.reshape(length, heads, -1)
    scaled = shaped * step[:, :, None]
    count = length // BLOCK
    blocks = (scaled.reshape(count, BLOCK, heads, -1), decay.reshape(count, BLOCK, heads), write_rows.reshape(count, BLOCK, width), read_rows.reshape(count, BLOCK, width))
    start = jnp.zeros((heads, shaped.shape[2], width), jnp.float32)
    final, outputs = lax.scan(jax.checkpoint(state_block), start, blocks)
    result = outputs.reshape(length, heads, -1) + skip_gain[None, :, None] * shaped
    return result.reshape(length, -1) * jax.nn.silu(gate_z)

def layer(rows, norm_in_gain, query_weight, key_weight, value_weight, output_weight, gate_weight, inner_weight, write_weight, read_weight, step_weight, conv_weight, conv_bias, pair_conv_weight, pair_conv_bias, step_bias, decay_log, skip_gain, state_gain, state_out_weight, norm_ffn_gain, feed_gate_weight, feed_up_weight, feed_down_weight):
    length = rows.shape[0]
    group = QH // KVH
    normed = low(root_norm(rows, norm_in_gain))
    queries = low(rotate(low_back(product(normed, query_weight)), QH, 1.0)).reshape(length, QH, HD)
    key_heads = jnp.repeat(product(normed, key_weight).reshape(length, KVH, HD), group, axis=1)
    keys = low(rotate(low_back(key_heads.reshape(length, QH * HD)), QH, 1.0)).reshape(length, QH, HD)
    value_heads = jnp.repeat(product(normed, value_weight).reshape(length, KVH, HD), group, axis=1)
    values = low(low_back(value_heads))
    scores = low_back(jnp.einsum('qhd,khd->hqk', queries, keys, precision=HIGHEST) * HD ** (-0.5))
    causal = jnp.arange(length)[:, None] >= jnp.arange(length)[None, :]
    scores = jnp.where(causal[None], scores, -1e+30)
    top = lax.optimization_barrier(jnp.max(scores, axis=-1, keepdims=True))
    exponent = jnp.exp(scores - top)
    probs = exponent / lax.optimization_barrier(jnp.sum(exponent, axis=-1, keepdims=True))
    mixed = jnp.einsum('hqk,khd->qhd', low(probs), values, precision=HIGHEST)
    mixed = low(low_back(mixed.reshape(length, QH * HD)))
    gate_z = low_back(product(normed, gate_weight))
    inputs = low_back(product(normed, inner_weight))
    writes = product(normed, write_weight)
    reads = product(normed, read_weight)
    steps_raw = low_back(product(normed, step_weight))
    heads_group = SH // N_TENSOR
    width_group = heads_group * HD
    pieces = []
    for member in range(N_TENSOR):
        col_start = member * width_group
        col_end = col_start + width_group
        head_start = member * heads_group
        head_end = head_start + heads_group
        pieces.append(mixer_state(inputs[:, col_start:col_end], low_back(writes), low_back(reads), steps_raw[:, head_start:head_end], gate_z[:, col_start:col_end], conv_weight[:, col_start:col_end], conv_bias[col_start:col_end], pair_conv_weight, pair_conv_bias, step_bias[head_start:head_end], decay_log[head_start:head_end], skip_gain[head_start:head_end]))
    gated = jnp.concatenate(pieces, axis=1)
    state_scale = lax.rsqrt(lax.optimization_barrier(jnp.mean(gated * gated, axis=-1, keepdims=True)) + EPS)
    state_normed = low(low_back(gated * state_scale * state_gain))
    mixer = low_back(product(mixed, output_weight) + product(state_normed, state_out_weight))
    middle = rows + mixer
    second = low(root_norm(middle, norm_ffn_gain))
    gate_value = low_back(product(second, feed_gate_weight))
    up_value = low_back(product(second, feed_up_weight))
    active = low(jax.nn.silu(gate_value) * up_value)
    return middle + product(active, feed_down_weight)

def reference(hidden_in, norm_in_gain, query_weight, key_weight, value_weight, output_weight, gate_weight, inner_weight, write_weight, read_weight, step_weight, conv_weight, conv_bias, pair_conv_weight, pair_conv_bias, step_bias, decay_log, skip_gain, state_gain, state_out_weight, norm_ffn_gain, feed_gate_weight, feed_up_weight, feed_down_weight, out_cotangent):
    params = (norm_in_gain, query_weight, key_weight, value_weight, output_weight, gate_weight, inner_weight, write_weight, read_weight, step_weight, conv_weight, conv_bias, pair_conv_weight, pair_conv_bias, step_bias, decay_log, skip_gain, state_gain, state_out_weight, norm_ffn_gain, feed_gate_weight, feed_up_weight, feed_down_weight)
    params = tuple((item.astype(jnp.float32) for item in params))
    hidden = hidden_in.astype(jnp.float32).reshape(N_DP, LEN, D)
    cotangent = out_cotangent.astype(jnp.float32).reshape(N_DP, LEN, D)
    zeros = tuple((jnp.zeros(item.shape, jnp.float32) for item in params))

    def one_sequence(totals, pair):
        rows, grad = pair
        result, pullback = jax.vjp(layer, rows, *params)
        grads = pullback(grad)
        totals = tuple((left + right for left, right in zip(totals, grads[1:])))
        return (totals, (result.astype(jnp.bfloat16), grads[0]))
    totals, (outputs, input_grads) = lax.scan(one_sequence, zeros, (hidden, cotangent))
    return (outputs.reshape(TOKENS, D), input_grads.reshape(TOKENS, D)) + totals
```

```python
import jax
import jax.numpy as jnp
from jax import lax
from jax.sharding import PartitionSpec as P

QH = 8
KVH = 2
HD = 64
BLOCK = 128


EPS = 1e-05
THETA = 10000.0
HIGHEST = lax.Precision.HIGHEST


def product(left, right):
    return jnp.dot(left, right, preferred_element_type=jnp.float32)


def product_left(left, right):
    return lax.dot_general(
        left, right, (((0,), (0,)), ((), ())), preferred_element_type=jnp.float32
    )


def product_right(left, right):
    return lax.dot_general(
        left, right, (((1,), (1,)), ((), ())), preferred_element_type=jnp.float32
    )


def rounded(values):
    return lax.optimization_barrier(values.astype(jnp.bfloat16)).astype(jnp.float32)


def root_norm(rows, gain):
    scale = lax.rsqrt(jnp.mean(rows * rows, axis=-1, keepdims=True) + EPS)
    return (rows * scale * gain, scale)


def root_norm_back(rows, scale, gain, upstream):
    weighted = upstream * gain
    inner = jnp.sum(weighted * rows, axis=-1, keepdims=True)
    grad_rows = scale * weighted - rows * scale**3 * inner / rows.shape[-1]
    grad_gain = jnp.sum(upstream * rows * scale, axis=0)
    return (grad_rows, grad_gain)


def rotate(values, heads, sign):
    length = values.shape[0]
    shaped = values.reshape(length, heads, -1)
    half = shaped.shape[2] // 2
    freq = THETA ** (-jnp.arange(half, dtype=jnp.float32) / half)
    angle = jnp.arange(length, dtype=jnp.float32)[:, None] * freq[None, :]
    cosine = jnp.cos(angle)[:, None, :]
    sine = sign * jnp.sin(angle)[:, None, :]
    first = shaped[:, :, :half]
    second = shaped[:, :, half:]
    turned = jnp.concatenate(
        [first * cosine - second * sine, second * cosine + first * sine], axis=2
    )
    return turned.reshape(length, -1)


def causal_conv(values, weight, bias):
    taps = weight.shape[0]
    length = values.shape[0]
    padded = jnp.pad(values, ((taps - 1, 0), (0, 0)))
    total = bias[None, :] + jnp.zeros_like(values)
    for tap in range(taps):
        total = total + weight[tap][None, :] * padded[tap : tap + length]
    return total


def state_block(state, block):
    scaled, decay, write_rows, read_rows = block
    size = decay.shape[0]
    running = jnp.cumsum(decay, axis=0)
    lower = jnp.arange(size)[:, None] >= jnp.arange(size)[None, :]
    spread = running[:, None, :] - running[None, :, :]
    weights = jnp.exp(jnp.where(lower[:, :, None], spread, -1e30))
    intersection = jnp.einsum("tn,sn->ts", read_rows, write_rows, precision=HIGHEST)
    inside = jnp.einsum(
        "tsh,shp->thp", intersection[:, :, None] * weights, scaled, precision=HIGHEST
    )
    earlier = jnp.exp(running)[:, :, None] * jnp.einsum(
        "tn,hpn->thp", read_rows, state, precision=HIGHEST
    )
    last = running[-1]
    carry = jnp.exp(last[None, :] - running)
    fresh = jnp.einsum("sh,shp,sn->hpn", carry, scaled, write_rows, precision=HIGHEST)
    return (jnp.exp(last)[:, None, None] * state + fresh, inside + earlier)


def mixer_state(
    inputs,
    writes,
    reads,
    steps_raw,
    gate_z,
    conv_weight,
    conv_bias,
    pair_weight,
    pair_bias,
    step_bias,
    decay_log,
    skip_gain,
):
    length = inputs.shape[0]
    heads = steps_raw.shape[1]
    width = writes.shape[1]
    mixed_inputs = jax.nn.silu(causal_conv(inputs, conv_weight, conv_bias))
    paired = jax.nn.silu(
        causal_conv(jnp.concatenate([writes, reads], axis=1), pair_weight, pair_bias)
    )
    write_rows = paired[:, :width]
    read_rows = paired[:, width:]
    step = jax.nn.softplus(steps_raw + step_bias[None, :])
    decay = step * (-jnp.exp(decay_log))[None, :]
    shaped = mixed_inputs.reshape(length, heads, -1)
    scaled = shaped * step[:, :, None]
    count = length // BLOCK
    blocks = (
        scaled.reshape(count, BLOCK, heads, -1),
        decay.reshape(count, BLOCK, heads),
        write_rows.reshape(count, BLOCK, width),
        read_rows.reshape(count, BLOCK, width),
    )
    start = jnp.zeros((heads, shaped.shape[2], width), jnp.float32)
    final, outputs = lax.scan(jax.checkpoint(state_block), start, blocks)
    result = outputs.reshape(length, heads, -1) + skip_gain[None, :, None] * shaped
    return result.reshape(length, -1) * jax.nn.silu(gate_z)


def swap(values, axis, mask):
    size = lax.axis_size(axis)
    return lax.ppermute(values, axis, [(index, index ^ mask) for index in range(size)])


def tensor_gather(block):
    return [block] + [swap(block, "tensor", mask) for mask in range(1, lax.axis_size("tensor"))]


def paired_sum(terms):
    while len(terms) > 1:
        terms = [terms[at] + terms[at + 1] for at in range(0, len(terms), 2)]
    return terms[0]


def tensor_scatter(blocks):
    got = [
        swap(block.astype(jnp.bfloat16), "tensor", mask).astype(jnp.float32)
        for mask, block in enumerate(blocks)
        if mask
    ]
    return paired_sum([blocks[0]] + got)


def tensor_sum(values):
    return paired_sum(tensor_gather(values))


def in_order(slots, place):
    stacked = jnp.stack(slots)
    parts = len(slots)
    return jnp.concatenate(
        [lax.dynamic_index_in_dim(stacked, place ^ at, 0, keepdims=False) for at in range(parts)]
    )


def dp_gather(block):
    size = lax.axis_size("dp")
    if size != 8:
        return lax.all_gather(block, "dp", axis=0, tiled=True)
    me = lax.axis_index("dp")
    rows = block.shape[0]
    mine = [block] + [swap(block, "dp", 2 * chip) for chip in range(1, size // 2)]
    near = swap(block, "dp", 1)
    far = swap(jnp.stack(mine[1:]), "dp", 1)
    pieces = [(0, block), (1, near)]
    for chip in range(1, size // 2):
        pieces += [(2 * chip, mine[chip]), (2 * chip + 1, far[chip - 1])]
    whole = jnp.zeros((size * rows,) + block.shape[1:], block.dtype)
    for mask, piece in pieces:
        whole = lax.dynamic_update_slice_in_dim(whole, piece, (me ^ mask) * rows, 0)
    return whole


def dp_scatter(whole):
    size = lax.axis_size("dp")
    if size != 8:
        return lax.psum_scatter(whole, "dp", scatter_dimension=0, tiled=True)
    me = lax.axis_index("dp")
    chips = size // 2
    rows = whole.shape[0] // size
    shaped = whole.reshape(chips, 2, rows, whole.shape[1])
    core = me % 2
    chip = me // 2
    keep = lax.dynamic_index_in_dim(shaped, core, 1, keepdims=False)
    give = lax.dynamic_index_in_dim(shaped, 1 - core, 1, keepdims=False)
    low = jnp.bfloat16
    both = keep.astype(jnp.float32) + swap(give.astype(low), "dp", 1).astype(jnp.float32)
    terms = [lax.dynamic_index_in_dim(both, chip, 0, keepdims=False)]
    for mask in range(1, chips):
        part = lax.dynamic_index_in_dim(both, chip ^ mask, 0, keepdims=False).astype(low)
        terms.append(swap(part, "dp", 2 * mask).astype(jnp.float32))
    return paired_sum(terms)


def dp_sum(values):
    size = lax.axis_size("dp")
    if size != 8:
        return lax.psum(values, "dp")
    both = values + swap(values, "dp", 1)
    return paired_sum([both] + [swap(both, "dp", 2 * chip) for chip in range(1, size // 2)])


def body(
    hidden_in,
    norm_in_gain,
    query_weight,
    key_weight,
    value_weight,
    output_weight,
    gate_weight,
    inner_weight,
    write_weight,
    read_weight,
    step_weight,
    conv_weight,
    conv_bias,
    pair_conv_weight,
    pair_conv_bias,
    step_bias,
    decay_log,
    skip_gain,
    state_gain,
    state_out_weight,
    norm_ffn_gain,
    feed_gate_weight,
    feed_up_weight,
    feed_down_weight,
    out_cotangent,
):
    low = jnp.bfloat16
    parts = lax.axis_size("tensor")
    place = lax.axis_index("tensor")
    heads_here = query_weight.shape[1] // HD
    key_head = place * heads_here // (QH // KVH)
    heads_state = step_weight.shape[1]
    width = gate_weight.shape[1]
    units = feed_gate_weight.shape[1]
    scale = HD ** (-0.5)

    mixer_local = jnp.concatenate(
        [
            query_weight,
            lax.dynamic_slice_in_dim(key_weight, key_head * HD, HD, 1),
            lax.dynamic_slice_in_dim(value_weight, key_head * HD, HD, 1),
            write_weight,
            read_weight,
            gate_weight,
            inner_weight,
            jnp.pad(step_weight, ((0, 0), (0, 128 - heads_state))),
        ],
        axis=1,
    )
    late_local = jnp.concatenate(
        [output_weight.T, state_out_weight.T, feed_gate_weight, feed_up_weight, feed_down_weight.T],
        axis=1,
    )
    rows_in = hidden_in.astype(jnp.float32)
    normed, first_scale = root_norm(rows_in, norm_in_gain)
    normed_slots = tensor_gather(normed.astype(low))
    mixer_full = dp_gather(mixer_local)
    late_full = lax.all_gather(late_local, "dp", axis=0, tiled=True)
    out_full = late_full[:, : 128 + width]
    feed_full = late_full[:, 128 + width : 128 + width + 2 * units]
    down_full = late_full[:, 128 + width + 2 * units :]
    mixer_rows = in_order(normed_slots, place)
    length = mixer_rows.shape[0]

    raw = product(mixer_rows, mixer_full)
    raw, cot_block = lax.optimization_barrier((raw, out_cotangent))
    cot_slots = tensor_gather(cot_block)
    query_low = rotate(raw[:, :128], heads_here, 1.0).astype(low).reshape(length, heads_here, HD)
    key_low = rotate(raw[:, 128:192], 1, 1.0).astype(low)
    value_low = raw[:, 192:256].astype(low)
    write_raw = raw[:, 256:384]
    read_raw = raw[:, 384:512]
    gate_raw = raw[:, 512 : 512 + width]
    inner_raw = raw[:, 512 + width : 512 + 2 * width]
    step_raw = raw[:, 512 + 2 * width : 512 + 2 * width + heads_state]

    gated, state_pull = jax.vjp(
        mixer_state,
        inner_raw,
        write_raw,
        read_raw,
        step_raw,
        gate_raw,
        conv_weight,
        conv_bias,
        pair_conv_weight,
        pair_conv_bias,
        step_bias,
        decay_log,
        skip_gain,
    )
    width_all = width * parts
    power = tensor_sum(jnp.sum(gated * gated, axis=1))

    causal = jnp.arange(length)[:, None] >= jnp.arange(length)[None, :]

    def score_rows():
        raw_scores = (
            jnp.einsum("qhd,kd->hqk", query_low, key_low, preferred_element_type=jnp.float32)
            * scale
        )
        return jnp.where(causal[None], raw_scores, -1e30)

    scores = score_rows()
    top = jnp.max(scores, axis=2, keepdims=True)
    exponent = jnp.exp(scores - top)
    total = jnp.sum(exponent, axis=2, keepdims=True)
    probs = exponent / total
    probs_low = probs.astype(low)
    mixed = jnp.einsum("hqk,kd->qhd", probs_low, value_low, preferred_element_type=jnp.float32)
    mixed_low = mixed.reshape(length, -1).astype(low)

    state_scale = lax.rsqrt(power / width_all + EPS)[:, None]
    state_low = (gated * state_scale * state_gain).astype(low)
    both_low = jnp.concatenate([mixed_low, state_low], axis=1)

    def to_slots(values):
        block = values.shape[0] // parts
        return [
            lax.dynamic_slice_in_dim(values, (place ^ mask) * block, block, 0)
            for mask in range(parts)
        ]

    mixer_shard = tensor_scatter(to_slots(product_right(both_low, out_full)))
    middle = rows_in + mixer_shard
    second, second_scale = root_norm(middle, norm_ffn_gain)
    feed_rows = jnp.concatenate(tensor_gather(second.astype(low)))
    cotangent = jnp.concatenate(cot_slots)
    grad_active = product(cotangent, down_full)
    gate_up = product(feed_rows, feed_full)
    gate_value = gate_up[:, :units]
    up_value = gate_up[:, units:]
    sigma = jax.nn.sigmoid(gate_value)
    swish = gate_value * sigma
    active = (swish * up_value).astype(low)
    grad_gate = grad_active * up_value * sigma * (1.0 + gate_value * (1.0 - sigma))
    grad_up = grad_active * swish
    grad_pair = jnp.concatenate([grad_gate, grad_up], axis=1).astype(low)
    block = length // parts

    def cut(values):
        return [values[mask * block : (mask + 1) * block] for mask in range(parts)]

    grad_second = tensor_scatter(cut(product_right(grad_pair, feed_full)))
    feed_terms = product_right(active, down_full)
    grad_second, feed_terms = lax.optimization_barrier((grad_second, feed_terms))
    feed_shard = tensor_scatter(cut(feed_terms))
    hidden_out = (middle + feed_shard).astype(low)
    grad_feed = jnp.concatenate(
        [product_left(feed_rows, grad_pair), product_left(cotangent, active)], axis=1
    ).astype(low)
    feed_sums = lax.psum_scatter(grad_feed, "dp", scatter_dimension=0, tiled=True)
    feed_sums = feed_sums.astype(jnp.float32)

    weighted_second = grad_second * norm_ffn_gain
    inner_second = jnp.sum(weighted_second * middle, axis=-1, keepdims=True)
    grad_middle = (
        out_cotangent.astype(jnp.float32)
        + second_scale * weighted_second
        - middle * second_scale**3 * inner_second / middle.shape[-1]
    )
    mixer_cot = in_order(tensor_gather(grad_middle.astype(low)), place)
    grad_both = product(mixer_cot, out_full)
    grad_out = product_left(mixer_cot, both_low).astype(low)
    grad_state = grad_both[:, 128:]
    weighted = grad_state * state_gain
    inner_sum = tensor_sum(jnp.sum(weighted * gated, axis=1))
    grad_mixed = grad_both[:, :128].astype(low).reshape(length, heads_here, HD)
    grad_probs = jnp.einsum(
        "qhd,kd->hqk", grad_mixed, value_low, preferred_element_type=jnp.float32
    )
    inner_probs = jnp.sum(probs * grad_probs, axis=2, keepdims=True)
    grad_scores = (probs * (grad_probs - inner_probs)).astype(low)
    grad_query_rot = (
        jnp.einsum("hqk,kd->qhd", grad_scores, key_low, preferred_element_type=jnp.float32) * scale
    )
    grad_query = rotate(grad_query_rot.reshape(length, -1), heads_here, -1.0)
    grad_key = rotate(
        jnp.einsum("hqk,qhd->kd", grad_scores, query_low, preferred_element_type=jnp.float32)
        * scale,
        1,
        -1.0,
    )
    grad_value = jnp.einsum(
        "hqk,qhd->kd", probs_low, grad_mixed, preferred_element_type=jnp.float32
    )
    grad_gated = state_scale * weighted - gated * state_scale**3 * inner_sum[:, None] / width_all
    grad_state_gain = jnp.sum(grad_state * gated * state_scale, axis=0)
    (
        grad_inner_raw,
        grad_write_raw,
        grad_read_raw,
        grad_step_raw,
        grad_gate_raw,
        grad_conv_weight,
        grad_conv_bias,
        grad_pair_weight,
        grad_pair_bias,
        grad_step_bias,
        grad_decay,
        grad_skip,
    ) = state_pull(grad_gated)
    grad_raw = jnp.concatenate(
        [
            grad_query,
            grad_key,
            grad_value,
            grad_write_raw,
            grad_read_raw,
            grad_gate_raw,
            grad_inner_raw,
            jnp.pad(grad_step_raw, ((0, 0), (0, 128 - heads_state))),
        ],
        axis=1,
    ).astype(low)
    grad_first = tensor_scatter(to_slots(product_right(grad_raw, mixer_full)))
    grad_mixer = product_left(mixer_rows, grad_raw).astype(low)
    out_sums = dp_scatter(grad_out)
    mixer_sums = dp_scatter(grad_mixer).astype(jnp.float32)

    grad_rows_norm, _ = root_norm_back(rows_in, first_scale, norm_in_gain, grad_first)
    gradient_hidden = grad_middle + grad_rows_norm

    rows_here = mixer_local.shape[0]
    at_rows = lax.axis_index("dp") * rows_here
    in_gain = jnp.sum(mixer_sums * mixer_local.astype(jnp.float32), axis=1, keepdims=True)
    in_gain = in_gain / lax.dynamic_slice_in_dim(norm_in_gain, at_rows, rows_here)[:, None]
    feed_local = late_local[:, 128 + width : 128 + width + 2 * units].astype(jnp.float32)
    ffn_gain = jnp.sum(feed_sums[:, : 2 * units] * feed_local, axis=1, keepdims=True)
    ffn_gain = ffn_gain / lax.dynamic_slice_in_dim(norm_ffn_gain, at_rows, rows_here)[:, None]
    shared = jnp.concatenate(
        [mixer_sums[:, 128:512], jnp.pad(jnp.concatenate([in_gain, ffn_gain], 1), ((0, 0), (0, 126)))],
        axis=1,
    ).astype(low)
    few = rows_here // parts
    terms = [
        swap(lax.dynamic_slice_in_dim(shared, (place ^ mask) * few, few, 0), "tensor", mask)
        if mask
        else lax.dynamic_slice_in_dim(shared, place * few, few, 0)
        for mask in range(parts)
    ]
    terms = [term.astype(jnp.float32) for term in terms]
    near = paired_sum(terms[: parts // 2])
    far = paired_sum(terms[parts // 2 :])
    rest = (near + far)[:, 128:]
    first_half = place < parts // 2
    heads_low = jnp.where(first_half, near[:, :128], far[:, :128])
    heads_high = jnp.where(first_half, far[:, :128], near[:, :128])
    shared = jnp.concatenate([heads_low, heads_high, rest], axis=1).astype(low)
    shared = in_order(tensor_gather(shared), place)
    shared = dp_gather(shared).astype(jnp.float32)
    gradient_key = jnp.concatenate([shared[:, :64], shared[:, 128:192]], axis=1)
    gradient_value = jnp.concatenate([shared[:, 64:128], shared[:, 192:256]], axis=1)

    small = [
        grad_pair_weight.reshape(-1),
        grad_pair_bias,
        grad_conv_weight.reshape(-1),
        grad_conv_bias,
        grad_state_gain,
        grad_step_bias,
        grad_decay,
        grad_skip,
    ]
    sizes = [item.shape[0] for item in small]
    flat = jnp.concatenate(small)
    filled = -(-flat.shape[0] // 1024) * 1024
    flat = jnp.pad(flat, (0, filled - flat.shape[0])).reshape(-1, 128)
    flat = dp_sum(flat)
    pair_rows = (sizes[0] + sizes[1]) // 128
    pair_sum = tensor_sum(flat[:pair_rows]).reshape(-1)
    flat = flat.reshape(-1)
    cuts = []
    start = 0
    for size in sizes:
        cuts.append(flat[start : start + size])
        start += size
    return (
        hidden_out,
        gradient_hidden,
        shared[:, 512],
        mixer_sums[:, :128],
        gradient_key,
        gradient_value,
        out_sums[:, :128].T.astype(jnp.float32),
        mixer_sums[:, 512 : 512 + width],
        mixer_sums[:, 512 + width : 512 + 2 * width],
        shared[:, 256:384],
        shared[:, 384:512],
        mixer_sums[:, 512 + 2 * width : 512 + 2 * width + heads_state],
        cuts[2].reshape(grad_conv_weight.shape),
        cuts[3],
        pair_sum[: sizes[0]].reshape(grad_pair_weight.shape),
        pair_sum[sizes[0] :],
        cuts[5],
        cuts[6],
        cuts[7],
        cuts[4],
        out_sums[:, 128:].T.astype(jnp.float32),
        shared[:, 513],
        feed_sums[:, :units],
        feed_sums[:, units : 2 * units],
        feed_sums[:, 2 * units :].T,
    )


def solution(mesh):
    placed = (
        P(("dp", "tensor"), None),
        P(),
        P("dp", "tensor"),
        P("dp", None),
        P("dp", None),
        P("tensor", "dp"),
        P("dp", "tensor"),
        P("dp", "tensor"),
        P("dp", None),
        P("dp", None),
        P("dp", "tensor"),
        P(None, "tensor"),
        P("tensor"),
        P(),
        P(),
        P("tensor"),
        P("tensor"),
        P("tensor"),
        P("tensor"),
        P("tensor", "dp"),
        P(),
        P("dp", "tensor"),
        P("dp", "tensor"),
        P("tensor", "dp"),
        P(("dp", "tensor"), None),
    )
    return jax.shard_map(
        body,
        mesh=mesh,
        in_specs=placed,
        out_specs=(
            P(("dp", "tensor"), None),
            P(("dp", "tensor"), None),
            P(),
            P("dp", "tensor"),
            P(),
            P(),
            P("tensor", "dp"),
            P("dp", "tensor"),
            P("dp", "tensor"),
            P(),
            P(),
            P("dp", "tensor"),
            P(None, "tensor"),
            P("tensor"),
            P(),
            P(),
            P("tensor"),
            P("tensor"),
            P("tensor"),
            P("tensor"),
            P("tensor", "dp"),
            P(),
            P("dp", "tensor"),
            P("dp", "tensor"),
            P("tensor", "dp"),
        ),
        check_vma=False,
    )
```

```python
import jax
import jax.numpy as jnp
import numpy as np
from jax import lax
from jax.experimental import pallas as pl
from jax.experimental.pallas import tpu as pltpu
from jax.sharding import PartitionSpec as P

QH = 8
KVH = 2
HD = 64
BLOCK = 128


EPS = 1e-05
THETA = 10000.0
HIGHEST = lax.Precision.HIGHEST


def product(left, right):
    return jnp.dot(left, right, preferred_element_type=jnp.float32)


def product_left(left, right):
    return lax.dot_general(
        left, right, (((0,), (0,)), ((), ())), preferred_element_type=jnp.float32
    )


def product_right(left, right):
    return lax.dot_general(
        left, right, (((1,), (1,)), ((), ())), preferred_element_type=jnp.float32
    )


def root_norm(rows, gain):
    scale = lax.rsqrt(jnp.mean(rows * rows, axis=-1, keepdims=True) + EPS)
    return (rows * scale * gain, scale)


def dot(left, right, dims=((1,), (0,)), precision=None):
    return lax.dot_general(
        left, right, (dims, ((), ())), precision=precision, preferred_element_type=jnp.float32
    )


NN = ((1,), (0,))
NT = ((1,), (1,))
TN = ((0,), (0,))


def sigmoid(values):
    return 1.0 / (1.0 + jnp.exp(-values))


def softplus(values):
    return jnp.maximum(values, 0.0) + jnp.log1p(jnp.exp(-jnp.abs(values)))


def lane_index(rows):
    return lax.broadcasted_iota(jnp.int32, (rows, 128), 1)


def spread_heads(values, width):
    first = lane_index(values.shape[0]) < HD
    return jnp.concatenate(
        [
            jnp.where(first, values[:, at : at + 1], values[:, at + 1 : at + 2])
            for at in range(0, width // HD, 2)
        ],
        axis=1,
    )


def slot_rows(place_ref, at):
    return pl.ds(pl.multiple_of((place_ref[0] ^ at) * BLOCK, BLOCK), BLOCK)


def lower_mask():
    rows = lax.broadcasted_iota(jnp.int32, (BLOCK, BLOCK), 0)
    columns = lax.broadcasted_iota(jnp.int32, (BLOCK, BLOCK), 1)
    return rows >= columns


def block_decay(raw_steps, step_bias, rate, lower):
    step = softplus(raw_steps + step_bias)
    running = dot(lower.astype(jnp.float32), step * rate, NN, HIGHEST)
    return step, running, running.T


def block_weights(running, running_t, lower, head):
    spread = running[:, head : head + 1] - running_t[head : head + 1, :]
    return jnp.exp(jnp.where(lower, spread, -1e30))


def fill_history(place_ref, raw_ref, history_ref, blocks, width):
    history_ref[0:8, :] = jnp.zeros((8, history_ref.shape[1]), jnp.float32)
    for at in range(blocks):
        rows = slot_rows(place_ref, at)
        here = slice(8 + at * BLOCK, 8 + (at + 1) * BLOCK)
        history_ref[here, 0:width] = raw_ref[rows, 512 + width : 512 + 2 * width]
        history_ref[here, width : width + 256] = raw_ref[rows, 256:512]


def state_forward_kernel(
    place_ref,
    raw_ref,
    taps_ref,
    heads_ref,
    skip_ref,
    gated_ref,
    power_ref,
    conv_ref,
    y_ref,
    states_ref,
    history_ref,
):
    low = jnp.bfloat16
    width = gated_ref.shape[1]
    blocks = gated_ref.shape[0] // BLOCK
    fill_history(place_ref, raw_ref, history_ref, blocks, width)
    lower = lower_mask()
    first = lane_index(BLOCK) < HD
    state = jnp.zeros((states_ref.shape[1], width), jnp.float32)
    for at in range(blocks):
        rows = slot_rows(place_ref, at)
        conv = taps_ref[4:5, :]
        for tap in range(4):
            conv = conv + taps_ref[tap : tap + 1, :] * history_ref[pl.ds(5 + tap + at * BLOCK, BLOCK), :]
        conv_ref[rows, :] = conv
        acted = conv * sigmoid(conv)
        inner = acted[:, :width]
        write = acted[:, width : width + 128].astype(low)
        read = acted[:, width + 128 :].astype(low)
        step, running, running_t = block_decay(
            raw_ref[rows, 512 + 2 * width :], heads_ref[0:1, :], heads_ref[1:2, :], lower
        )
        scaled = inner * spread_heads(step, width)
        scaled_low = scaled.astype(low)
        zero = jnp.zeros((BLOCK, 128), low)
        meet = dot(read, write, NT)
        inside = []
        for pair in range(width // 128):
            both = jnp.concatenate(
                [
                    (meet * block_weights(running, running_t, lower, 2 * pair)).astype(low),
                    (meet * block_weights(running, running_t, lower, 2 * pair + 1)).astype(low),
                ],
                axis=1,
            )
            piece = scaled_low[:, pair * 128 : (pair + 1) * 128]
            split = jnp.concatenate([jnp.where(first, piece, zero), jnp.where(first, zero, piece)])
            inside.append(dot(both, split))
        earlier = dot(read, state.astype(low))
        y = jnp.concatenate(inside, axis=1) + spread_heads(jnp.exp(running), width) * earlier
        y_ref[rows, :] = y
        states_ref[at] = state
        last = running[BLOCK - 1 : BLOCK, :]
        carried = (spread_heads(jnp.exp(last - running), width) * scaled).astype(low)
        state = spread_heads(jnp.exp(last), width) * state + dot(write, carried, TN)
        gate = raw_ref[rows, 512 : 512 + width]
        gated = (y + skip_ref[0:1, :] * inner) * gate * sigmoid(gate)
        gated_ref[rows, :] = gated
        power_ref[:, rows] = dot(jnp.ones((8, width), jnp.float32), gated * gated, NT, HIGHEST)


def state_backward_kernel(
    place_ref,
    raw_ref,
    conv_ref,
    y_ref,
    states_ref,
    up_ref,
    taps_ref,
    heads_ref,
    skip_ref,
    grad_ref,
    grad_taps_ref,
    grad_heads_ref,
    history_ref,
    later_ref,
):
    low = jnp.bfloat16
    width = up_ref.shape[1]
    blocks = up_ref.shape[0] // BLOCK
    length = up_ref.shape[0]
    every = width + 256
    fill_history(place_ref, raw_ref, history_ref, blocks, width)
    later_ref[length : length + 8, :] = jnp.zeros((8, every), jnp.float32)
    lower = lower_mask()
    first = lane_index(BLOCK) < HD
    zero = jnp.zeros((BLOCK, 128), low)
    picks = (
        lax.broadcasted_iota(jnp.int32, (width, 128), 0) // HD
        == lax.broadcasted_iota(jnp.int32, (width, 128), 1)
    ).astype(jnp.float32)
    skip = skip_ref[0:1, :]
    rate = heads_ref[1:2, :]
    grad_state = jnp.zeros((states_ref.shape[1], width), jnp.float32)
    grad_taps = [jnp.zeros((1, every), jnp.float32) for _ in range(5)]
    grad_bias = jnp.zeros((1, 128), jnp.float32)
    grad_decay = jnp.zeros((1, 128), jnp.float32)
    grad_skip = jnp.zeros((1, width), jnp.float32)
    for at in reversed(range(blocks)):
        rows = slot_rows(place_ref, at)
        gate = raw_ref[rows, 512 : 512 + width]
        gate_sigma = sigmoid(gate)
        conv = conv_ref[rows, :]
        conv_sigma = sigmoid(conv)
        acted = conv * conv_sigma
        inner = acted[:, :width]
        write = acted[:, width : width + 128].astype(low)
        read = acted[:, width + 128 :].astype(low)
        y = y_ref[rows, :]
        up = up_ref[rows, :]
        grad_gate = up * (y + skip * inner) * gate_sigma * (1.0 + gate * (1.0 - gate_sigma))
        grad_ref[rows, 256 : 256 + width] = grad_gate.astype(low)
        grad_y = up * gate * gate_sigma
        raw_steps = raw_ref[rows, 512 + 2 * width :]
        step, running, running_t = block_decay(raw_steps, heads_ref[0:1, :], rate, lower)
        step_wide = spread_heads(step, width)
        grow = spread_heads(jnp.exp(running), width)
        last = running[BLOCK - 1 : BLOCK, :]
        carry = spread_heads(jnp.exp(last - running), width)
        last_wide = spread_heads(jnp.exp(last), width)
        scaled = inner * step_wide
        scaled_low = scaled.astype(low)
        grad_low = grad_y.astype(low)
        grown_low = (grad_y * grow).astype(low)
        state = states_ref[at]
        state_low = state.astype(low)
        grad_state_low = grad_state.astype(low)
        meet = dot(read, write, NT)
        grad_meet = jnp.zeros((BLOCK, BLOCK), jnp.float32)
        inside = []
        for pair in range(width // 128):
            weights = [
                block_weights(running, running_t, lower, head) for head in (2 * pair, 2 * pair + 1)
            ]
            both = jnp.concatenate([(meet * item).astype(low) for item in weights], axis=0)
            piece = grad_low[:, pair * 128 : (pair + 1) * 128]
            split = jnp.concatenate([jnp.where(first, piece, zero), jnp.where(first, zero, piece)])
            grad_both = dot(split, scaled_low[:, pair * 128 : (pair + 1) * 128], NT)
            grad_meet = (
                grad_meet + grad_both[:BLOCK] * weights[0] + grad_both[BLOCK:] * weights[1]
            )
            inside.append(dot(both, split, TN))
        grad_inside = jnp.concatenate(inside, axis=1)
        from_state = carry * dot(write, grad_state_low)
        carried = carry * scaled
        grad_scaled = grad_inside + from_state
        moved = scaled * from_state
        turn = grad_low.astype(jnp.float32) * y - scaled_low.astype(jnp.float32) * grad_inside - moved
        direct = grad_y * inner
        ends = jnp.sum(moved, axis=0, keepdims=True) + last_wide * jnp.sum(
            state * grad_state, axis=0, keepdims=True
        )
        summed = dot(
            jnp.concatenate([turn, grad_scaled * inner, jnp.broadcast_to(ends, (8, width))]),
            picks,
            NN,
            HIGHEST,
        )
        grad_running = (
            dot(lower.astype(jnp.float32), summed[:BLOCK], TN, HIGHEST)
            + summed[2 * BLOCK : 2 * BLOCK + 1]
        )
        grad_step = grad_running * rate + summed[BLOCK : 2 * BLOCK]
        grad_decay = grad_decay + jnp.sum(grad_running * step * rate, axis=0, keepdims=True)
        grad_steps = grad_step * sigmoid(raw_steps + heads_ref[0:1, :])
        grad_bias = grad_bias + jnp.sum(grad_steps, axis=0, keepdims=True)
        grad_skip = grad_skip + jnp.sum(direct, axis=0, keepdims=True)
        grad_ref[rows, 256 + 2 * width :] = grad_steps.astype(low)
        grad_inner = grad_scaled * step_wide + skip * grad_y
        grad_meet_low = grad_meet.astype(low)
        grad_read = dot(grad_meet_low, write) + dot(grown_low, state_low, NT)
        grad_write = dot(grad_meet_low, read, TN) + dot(carried.astype(low), grad_state_low, NT)
        grad_state = last_wide * grad_state + dot(read, grown_low, TN)
        grad_conv = jnp.concatenate([grad_inner, grad_write, grad_read], axis=1) * (
            conv_sigma * (1.0 + conv * (1.0 - conv_sigma))
        )
        later_ref[at * BLOCK : (at + 1) * BLOCK, :] = grad_conv
        back = jnp.zeros((BLOCK, every), jnp.float32)
        for tap in range(4):
            back = back + taps_ref[tap : tap + 1, :] * later_ref[pl.ds(at * BLOCK + 3 - tap, BLOCK), :]
            seen = history_ref[pl.ds(5 + tap + at * BLOCK, BLOCK), :]
            grad_taps[tap] = grad_taps[tap] + jnp.sum(grad_conv * seen, axis=0, keepdims=True)
        grad_taps[4] = grad_taps[4] + jnp.sum(grad_conv, axis=0, keepdims=True)
        grad_ref[rows, 256 + width : 256 + 2 * width] = back[:, :width].astype(low)
        grad_ref[rows, 0:256] = back[:, width:].astype(low)
    for tap in range(5):
        grad_taps_ref[tap : tap + 1, :] = grad_taps[tap]
    grad_taps_ref[5:8, :] = jnp.zeros((3, every), jnp.float32)
    skip_heads = dot(jnp.broadcast_to(grad_skip, (8, width)), picks, NN, HIGHEST)
    grad_heads_ref[...] = jnp.zeros(grad_heads_ref.shape, jnp.float32)
    grad_heads_ref[0:1, :] = grad_bias
    grad_heads_ref[1:2, :] = grad_decay
    grad_heads_ref[2:3, :] = skip_heads[0:1]


def turned(values, cosine, sine):
    early = lane_index(values.shape[0]) % HD < HD // 2
    other = jnp.where(early, pltpu.roll(values, 128 - HD // 2, 1), pltpu.roll(values, HD // 2, 1))
    return values * cosine + other * sine


def both_heads(values, first):
    zero = jnp.zeros(values.shape, values.dtype)
    return jnp.concatenate([jnp.where(first, values, zero), jnp.where(first, zero, values)])


def attention_forward_kernel(
    place_ref, raw_ref, angle_ref, mixed_ref, kept_ref, probs_ref
):
    low = jnp.bfloat16
    blocks = mixed_ref.shape[0] // BLOCK
    first = lane_index(BLOCK) < HD
    for at in range(blocks):
        rows = slot_rows(place_ref, at)
        here = slice(at * BLOCK, (at + 1) * BLOCK)
        cosine = angle_ref[here, 0:128]
        sine = angle_ref[here, 128:256]
        pair = raw_ref[rows, 128:256]
        key = turned(pair, cosine, sine)
        kept_ref[here, 0:128] = turned(raw_ref[rows, 0:128], cosine, sine).astype(low)
        kept_ref[here, 128:256] = jnp.where(first, key, pltpu.roll(key, HD, 1)).astype(low)
        kept_ref[here, 256:384] = jnp.where(first, pltpu.roll(pair, HD, 1), pair).astype(low)
    for at in range(blocks):
        rows = slot_rows(place_ref, at)
        here = slice(at * BLOCK, (at + 1) * BLOCK)
        reach = (at + 1) * BLOCK
        query = both_heads(kept_ref[here, 0:128], first)
        scores = dot(query, kept_ref[0:reach, 128:256], NT) * (HD ** (-0.5))
        row = lax.broadcasted_iota(jnp.int32, (2 * BLOCK, reach), 0) % BLOCK + at * BLOCK
        column = lax.broadcasted_iota(jnp.int32, (2 * BLOCK, reach), 1)
        scores = jnp.where(row >= column, scores, -1e30)
        exponent = jnp.exp(scores - jnp.max(scores, axis=1, keepdims=True))
        probs = (exponent / jnp.sum(exponent, axis=1, keepdims=True)).astype(low)
        probs_ref[at, :, 0:reach] = probs
        out = dot(probs, kept_ref[0:reach, 256:384])
        mixed_ref[rows, :] = jnp.where(first, out[:BLOCK], out[BLOCK:]).astype(low)


def attention_backward_kernel(
    place_ref, up_ref, angle_ref, kept_ref, probs_ref, grad_ref, key_ref, value_ref
):
    low = jnp.bfloat16
    blocks = up_ref.shape[0] // BLOCK
    first = lane_index(BLOCK) < HD
    scale = HD ** (-0.5)
    key_ref[...] = jnp.zeros(key_ref.shape, jnp.float32)
    value_ref[...] = jnp.zeros(value_ref.shape, jnp.float32)
    for at in range(blocks):
        rows = slot_rows(place_ref, at)
        here = slice(at * BLOCK, (at + 1) * BLOCK)
        reach = (at + 1) * BLOCK
        query = both_heads(kept_ref[here, 0:128], first)
        up = both_heads(up_ref[rows, :], first)
        probs_low = probs_ref[at, :, 0:reach]
        probs = probs_low.astype(jnp.float32)
        grad_probs = dot(up, kept_ref[0:reach, 256:384], NT)
        inner = jnp.sum(probs * grad_probs, axis=1, keepdims=True)
        grad_scores = (probs * (grad_probs - inner)).astype(low)
        both = dot(grad_scores, kept_ref[0:reach, 128:256]) * scale
        grad_query = jnp.where(first, both[:BLOCK], both[BLOCK:])
        grad_ref[rows, 0:128] = turned(
            grad_query, angle_ref[here, 0:128], -angle_ref[here, 128:256]
        ).astype(low)
        key_ref[0:reach, :] += dot(grad_scores, query, TN)
        value_ref[0:reach, :] += dot(probs_low, up, TN)
    for at in range(blocks):
        rows = slot_rows(place_ref, at)
        here = slice(at * BLOCK, (at + 1) * BLOCK)
        key = key_ref[here, :]
        value = value_ref[here, :]
        key = (key + pltpu.roll(key, HD, 1)) * scale
        key = turned(key, angle_ref[here, 0:128], -angle_ref[here, 128:256])
        value = value + pltpu.roll(value, HD, 1)
        grad_ref[rows, 128:256] = jnp.where(first, key, value).astype(low)


def angle_table(length):
    half = HD // 2
    freq = THETA ** (-np.arange(half, dtype=np.float32) / half)
    angle = np.arange(length, dtype=np.float32)[:, None] * freq[None, :]
    cosine = np.tile(np.cos(angle), (1, 4))
    sine = np.tile(np.concatenate([-np.sin(angle), np.sin(angle)], axis=1), (1, 2))
    return np.concatenate([cosine, sine], axis=1).astype(np.float32)


def run_kernel(kernel, place, operands, outs, scratch, name, flops=8e9):
    whole = pl.BlockSpec(memory_space=pltpu.VMEM)
    return pl.pallas_call(
        kernel,
        out_shape=[jax.ShapeDtypeStruct(shape, dtype) for shape, dtype in outs],
        in_specs=[pl.BlockSpec(memory_space=pltpu.SMEM)] + [whole] * len(operands),
        out_specs=[whole] * len(outs),
        scratch_shapes=scratch,
        compiler_params=pltpu.CompilerParams(vmem_limit_bytes=48 * 1024 * 1024),
        cost_estimate=pl.CostEstimate(flops=int(flops), bytes_accessed=1 << 20, transcendentals=0),
        name=name,
    )(place, *operands)


def state_forward(place, raw, taps, heads, skip, states):
    length = raw.shape[0]
    width = skip.shape[1]
    wide = jnp.float32
    return run_kernel(
        state_forward_kernel,
        place,
        (raw, taps, heads, skip),
        [
            ((length, width), wide),
            ((8, length), wide),
            ((length, width + 256), wide),
            ((length, width), wide),
            ((length // BLOCK, states, width), wide),
        ],
        [pltpu.VMEM((length + 8, width + 256), wide)],
        "state_forward",
    )


def state_backward(place, raw, conv, y, states, up, taps, heads, skip):
    length = raw.shape[0]
    width = skip.shape[1]
    wide = jnp.float32
    return run_kernel(
        state_backward_kernel,
        place,
        (raw, conv, y, states, up, taps, heads, skip),
        [
            ((length, 256 + 2 * width + 128), jnp.bfloat16),
            ((8, width + 256), wide),
            ((8, 128), wide),
        ],
        [pltpu.VMEM((length + 8, width + 256), wide), pltpu.VMEM((length + 8, width + 256), wide)],
        "state_backward",
    )


def attention_forward(place, raw, angles):
    length = raw.shape[0]
    low = jnp.bfloat16
    return run_kernel(
        attention_forward_kernel,
        place,
        (raw, angles),
        [
            ((length, 128), low),
            ((length, 384), low),
            ((length // BLOCK, 2 * BLOCK, length), low),
        ],
        [],
        "attention_forward",
    )


def attention_backward(place, up, angles, kept, probs):
    length = up.shape[0]
    return run_kernel(
        attention_backward_kernel,
        place,
        (up, angles, kept, probs),
        [((length, 256), jnp.bfloat16)],
        [pltpu.VMEM((length, 128), jnp.float32), pltpu.VMEM((length, 128), jnp.float32)],
        "attention_backward",
    )[0]


def swap(values, axis, mask):
    size = lax.axis_size(axis)
    return lax.ppermute(values, axis, [(index, index ^ mask) for index in range(size)])


def tensor_gather(block):
    return [block] + [swap(block, "tensor", mask) for mask in range(1, lax.axis_size("tensor"))]


def paired_sum(terms):
    while len(terms) > 1:
        terms = [terms[at] + terms[at + 1] for at in range(0, len(terms), 2)]
    return terms[0]


def tensor_scatter(blocks):
    got = [
        swap(block.astype(jnp.bfloat16), "tensor", mask).astype(jnp.float32)
        for mask, block in enumerate(blocks)
        if mask
    ]
    return paired_sum([blocks[0]] + got)


def slot_sum(values):
    parts = lax.axis_size("tensor")
    shaped = values.reshape(parts, -1)
    terms = [shaped]
    for mask in range(1, parts):
        got = swap(shaped, "tensor", mask)
        terms.append(jnp.stack([got[at ^ mask] for at in range(parts)]))
    return paired_sum(terms).reshape(-1)


def dp_gather(block):
    size = lax.axis_size("dp")
    if size != 8:
        return lax.all_gather(block, "dp", axis=0, tiled=True)
    me = lax.axis_index("dp")
    rows = block.shape[0]
    mine = [block] + [swap(block, "dp", 2 * chip) for chip in range(1, size // 2)]
    other = swap(jnp.stack(mine), "dp", 1)
    whole = jnp.zeros((size * rows,) + block.shape[1:], block.dtype)
    for chip in range(size // 2):
        whole = lax.dynamic_update_slice_in_dim(whole, mine[chip], (me ^ 2 * chip) * rows, 0)
        whole = lax.dynamic_update_slice_in_dim(whole, other[chip], (me ^ 2 * chip ^ 1) * rows, 0)
    return whole


def dp_scatter(whole, small=None):
    size = lax.axis_size("dp")
    low = jnp.bfloat16
    if size != 8:
        summed = lax.psum_scatter(whole, "dp", scatter_dimension=0, tiled=True)
        return summed.astype(jnp.float32), None if small is None else lax.psum(small, "dp")
    me = lax.axis_index("dp")
    chips = size // 2
    rows = whole.shape[0] // size
    columns = whole.shape[1]
    shaped = whole.reshape(chips, 2, rows, columns)
    core = me % 2
    chip = me // 2
    keep = lax.dynamic_index_in_dim(shaped, core, 1, keepdims=False).reshape(chips * rows, columns)
    give = lax.dynamic_index_in_dim(shaped, 1 - core, 1, keepdims=False).reshape(chips * rows, columns)
    if small is not None:
        small = small.astype(low)
        keep = jnp.concatenate([keep, small])
        give = jnp.concatenate([give, small])
    both = (keep.astype(jnp.float32) + swap(give, "dp", 1).astype(jnp.float32)).astype(low)
    terms = []
    for mask in range(chips):
        part = lax.dynamic_slice_in_dim(both, (chip ^ mask) * rows, rows, 0)
        if small is not None:
            part = jnp.concatenate([part, both[chips * rows :]])
        terms.append((swap(part, "dp", 2 * mask) if mask else part).astype(jnp.float32))
    summed = paired_sum(terms)
    return summed[:rows], None if small is None else summed[rows:]


def body(
    hidden_in,
    norm_in_gain,
    query_weight,
    key_weight,
    value_weight,
    output_weight,
    gate_weight,
    inner_weight,
    write_weight,
    read_weight,
    step_weight,
    conv_weight,
    conv_bias,
    pair_conv_weight,
    pair_conv_bias,
    step_bias,
    decay_log,
    skip_gain,
    state_gain,
    state_out_weight,
    norm_ffn_gain,
    feed_gate_weight,
    feed_up_weight,
    feed_down_weight,
    out_cotangent,
):
    low = jnp.bfloat16
    wide = jnp.float32
    parts = lax.axis_size("tensor")
    place = lax.axis_index("tensor")
    place_ref = place.astype(jnp.int32).reshape(1)
    heads_here = query_weight.shape[1] // HD
    key_head = place * heads_here // (QH // KVH)
    heads_state = step_weight.shape[1]
    width = gate_weight.shape[1]
    units = feed_gate_weight.shape[1]
    states = write_weight.shape[1]

    mixer_local = jnp.concatenate(
        [
            query_weight,
            lax.dynamic_slice_in_dim(key_weight, key_head * HD, HD, 1),
            lax.dynamic_slice_in_dim(value_weight, key_head * HD, HD, 1),
            write_weight,
            read_weight,
            gate_weight,
            inner_weight,
            jnp.pad(step_weight, ((0, 0), (0, 128 - heads_state))),
        ],
        axis=1,
    )
    late_local = jnp.concatenate(
        [output_weight.T, state_out_weight.T, feed_gate_weight, feed_up_weight, feed_down_weight.T],
        axis=1,
    )
    rows_in = hidden_in.astype(wide)
    normed, first_scale = root_norm(rows_in, norm_in_gain)
    mixer_rows = jnp.concatenate(tensor_gather(normed.astype(low)))
    mixer_full = dp_gather(mixer_local)
    late_full = lax.all_gather(late_local, "dp", axis=0, tiled=True)
    out_full = late_full[:, : 128 + width]
    feed_full = late_full[:, 128 + width : 128 + width + 2 * units]
    down_full = late_full[:, 128 + width + 2 * units :]
    length = mixer_rows.shape[0]
    block = length // parts

    def cut(values):
        return [values[mask * block : (mask + 1) * block] for mask in range(parts)]

    raw = product(mixer_rows, mixer_full)
    raw, cot_block = lax.optimization_barrier((raw, out_cotangent))
    cotangent = jnp.concatenate(tensor_gather(cot_block))

    taps = jnp.concatenate(
        [
            jnp.concatenate([conv_weight, conv_bias[None]]),
            jnp.concatenate([pair_conv_weight, pair_conv_bias[None]]),
        ],
        axis=1,
    )
    taps = jnp.pad(taps, ((0, 3), (0, 0)))
    heads = jnp.pad(
        jnp.stack([step_bias, -jnp.exp(decay_log)]), ((0, 6), (0, 128 - heads_state))
    )
    skip = jnp.repeat(skip_gain, HD)[None]
    angles = jnp.asarray(angle_table(length))

    gated, power, conv, y, kept_states = state_forward(place_ref, raw, taps, heads, skip, states)
    mixed_low, kept, probs = attention_forward(place_ref, raw, angles)
    width_all = width * parts
    power = slot_sum(power[0])
    state_scale = lax.rsqrt(power / width_all + EPS)[:, None]
    state_low = (gated * state_scale * state_gain).astype(low)
    both_low = jnp.concatenate([mixed_low, state_low], axis=1)

    mixer_shard = tensor_scatter(cut(product_right(both_low, out_full)))
    middle = rows_in + mixer_shard
    second, second_scale = root_norm(middle, norm_ffn_gain)
    feed_rows = jnp.concatenate(tensor_gather(second.astype(low)))
    grad_active = product(cotangent, down_full)
    gate_up = product(feed_rows, feed_full)
    gate_value = gate_up[:, :units]
    up_value = gate_up[:, units:]
    sigma = jax.nn.sigmoid(gate_value)
    swish = gate_value * sigma
    active = (swish * up_value).astype(low)
    grad_gate = grad_active * up_value * sigma * (1.0 + gate_value * (1.0 - sigma))
    grad_up = grad_active * swish
    grad_pair = jnp.concatenate([grad_gate, grad_up], axis=1).astype(low)

    grad_second = tensor_scatter(cut(product_right(grad_pair, feed_full)))
    feed_terms = product_right(active, down_full)
    grad_second, feed_terms = lax.optimization_barrier((grad_second, feed_terms))
    feed_shard = tensor_scatter(cut(feed_terms))
    hidden_out = (middle + feed_shard).astype(low)
    grad_feed = jnp.concatenate(
        [product_left(feed_rows, grad_pair), product_left(cotangent, active)], axis=1
    ).astype(low)
    feed_sums = lax.psum_scatter(grad_feed, "dp", scatter_dimension=0, tiled=True)
    feed_sums = feed_sums.astype(wide)

    weighted_second = grad_second * norm_ffn_gain
    inner_second = jnp.sum(weighted_second * middle, axis=-1, keepdims=True)
    grad_middle = (
        out_cotangent.astype(wide)
        + second_scale * weighted_second
        - middle * second_scale**3 * inner_second / middle.shape[-1]
    )
    ffn_gain = jnp.sum(grad_second * middle * second_scale, axis=0)
    mixer_cot = jnp.concatenate(tensor_gather(grad_middle.astype(low)))
    grad_both = product(mixer_cot, out_full)
    grad_state = grad_both[:, 128:]
    weighted = grad_state * state_gain
    inner_sum = slot_sum(jnp.sum(weighted * gated, axis=1))
    grad_attention = attention_backward(
        place_ref, grad_both[:, :128].astype(low), angles, kept, probs
    )
    early_terms = jnp.concatenate(
        [product_left(mixer_cot, both_low), product_left(mixer_rows, grad_attention)], axis=1
    ).astype(low)
    early_sums, _ = dp_scatter(early_terms)
    grad_gated = (
        state_scale * weighted - gated * state_scale**3 * (inner_sum / width_all)[:, None]
    )
    grad_state_gain = jnp.sum(grad_state * gated * state_scale, axis=0)
    grad_mixer, grad_taps, grad_heads = state_backward(
        place_ref, raw, conv, y, kept_states, grad_gated, taps, heads, skip
    )
    total_rows = product_right(grad_mixer, mixer_full[:, 256:]) + product_right(
        grad_attention, mixer_full[:, :256]
    )
    grad_first = tensor_scatter(cut(total_rows))
    in_gain = jnp.sum(total_rows * mixer_rows.astype(wide), axis=0) / norm_in_gain

    late_terms = product_left(mixer_rows, grad_mixer).astype(low)
    columns = late_terms.shape[1]
    small = [
        in_gain,
        ffn_gain,
        grad_taps[:4, width:].reshape(-1),
        grad_taps[4, width:],
        grad_taps[:4, :width].reshape(-1),
        grad_taps[4, :width],
        grad_state_gain,
        grad_heads[0, :heads_state],
        grad_heads[1, :heads_state],
        grad_heads[2, :heads_state],
    ]
    sizes = [item.shape[0] for item in small]
    flat = jnp.concatenate(small)
    small_rows = -(-flat.shape[0] // (16 * columns)) * 16
    flat = jnp.pad(flat, (0, small_rows * columns - flat.shape[0])).reshape(small_rows, columns)
    late_sums, flat = dp_scatter(late_terms, flat)
    flat = flat.reshape(-1)

    common = sum(sizes[:4])
    common_rows = -(-common // (16 * 384)) * 16
    rows_here = mixer_local.shape[0]
    shared = jnp.concatenate(
        [
            jnp.concatenate([early_sums[:, 128 + width + 128 :], late_sums[:, :256]], axis=1),
            jnp.pad(flat[:common], (0, common_rows * 384 - common)).reshape(common_rows, 384),
        ]
    ).astype(low)
    near = shared.astype(wide) + swap(shared, "tensor", 1).astype(wide)
    near = near.astype(low)
    far = swap(near, "tensor", 2).astype(wide)
    near = near.astype(wide)
    both = near + far
    first_half = place < parts // 2
    head_low = jnp.where(first_half, near[:rows_here, :128], far[:rows_here, :128])
    head_high = jnp.where(first_half, far[:rows_here, :128], near[:rows_here, :128])
    common_sums = both[rows_here:].reshape(-1)
    shared = jnp.concatenate([head_low, head_high, both[:rows_here, 128:]], axis=1).astype(low)
    shared = dp_gather(shared).astype(wide)
    gradient_key = jnp.concatenate([shared[:, :64], shared[:, 128:192]], axis=1)
    gradient_value = jnp.concatenate([shared[:, 64:128], shared[:, 192:256]], axis=1)

    weighted_first = grad_first * norm_in_gain
    inner_first = jnp.sum(weighted_first * rows_in, axis=-1, keepdims=True)
    gradient_hidden = (
        grad_middle
        + first_scale * weighted_first
        - rows_in * first_scale**3 * inner_first / rows_in.shape[-1]
    )

    cuts = []
    at = 0
    for index, size in enumerate(sizes):
        cuts.append((common_sums if index < 4 else flat)[at : at + size])
        at += size
    return (
        hidden_out,
        gradient_hidden,
        cuts[0],
        early_sums[:, 128 + width : 128 + width + 128],
        gradient_key,
        gradient_value,
        early_sums[:, :128].T,
        late_sums[:, 256 : 256 + width],
        late_sums[:, 256 + width : 256 + 2 * width],
        shared[:, 256:384],
        shared[:, 384:512],
        late_sums[:, 256 + 2 * width : 256 + 2 * width + heads_state],
        cuts[4].reshape(conv_weight.shape),
        cuts[5],
        cuts[2].reshape(pair_conv_weight.shape),
        cuts[3],
        cuts[7],
        cuts[8],
        cuts[9],
        cuts[6],
        early_sums[:, 128 : 128 + width].T,
        cuts[1],
        feed_sums[:, :units],
        feed_sums[:, units : 2 * units],
        feed_sums[:, 2 * units :].T,
    )


def solution(mesh):
    placed = (
        P(("dp", "tensor"), None),
        P(),
        P("dp", "tensor"),
        P("dp", None),
        P("dp", None),
        P("tensor", "dp"),
        P("dp", "tensor"),
        P("dp", "tensor"),
        P("dp", None),
        P("dp", None),
        P("dp", "tensor"),
        P(None, "tensor"),
        P("tensor"),
        P(),
        P(),
        P("tensor"),
        P("tensor"),
        P("tensor"),
        P("tensor"),
        P("tensor", "dp"),
        P(),
        P("dp", "tensor"),
        P("dp", "tensor"),
        P("tensor", "dp"),
        P(("dp", "tensor"), None),
    )
    return jax.shard_map(
        body,
        mesh=mesh,
        in_specs=placed,
        out_specs=(
            P(("dp", "tensor"), None),
            P(("dp", "tensor"), None),
            P(),
            P("dp", "tensor"),
            P(),
            P(),
            P("tensor", "dp"),
            P("dp", "tensor"),
            P("dp", "tensor"),
            P(),
            P(),
            P("dp", "tensor"),
            P(None, "tensor"),
            P("tensor"),
            P(),
            P(),
            P("tensor"),
            P("tensor"),
            P("tensor"),
            P("tensor"),
            P("tensor", "dp"),
            P(),
            P("dp", "tensor"),
            P("dp", "tensor"),
            P("tensor", "dp"),
        ),
        check_vma=False,
    )
```

```python
import jax
import jax.numpy as jnp
import numpy as np
from jax import lax
from jax.experimental import pallas as pl
from jax.experimental.pallas import tpu as pltpu
from jax.sharding import PartitionSpec as P

QH = 8
KVH = 2
HD = 64
BLOCK = 128


EPS = 1e-05
THETA = 10000.0
HIGHEST = lax.Precision.HIGHEST


def product(left, right):
    return jnp.dot(left, right, preferred_element_type=jnp.float32)


def product_left(left, right):
    return lax.dot_general(
        left, right, (((0,), (0,)), ((), ())), preferred_element_type=jnp.float32
    )


def product_right(left, right):
    return lax.dot_general(
        left, right, (((1,), (1,)), ((), ())), preferred_element_type=jnp.float32
    )


def root_norm(rows, gain):
    scale = lax.rsqrt(jnp.mean(rows * rows, axis=-1, keepdims=True) + EPS)
    return (rows * scale * gain, scale)


def dot(left, right, dims=((1,), (0,)), precision=None):
    return lax.dot_general(
        left, right, (dims, ((), ())), precision=precision, preferred_element_type=jnp.float32
    )


NN = ((1,), (0,))
NT = ((1,), (1,))
TN = ((0,), (0,))


def sigmoid(values):
    return 1.0 / (1.0 + jnp.exp(-values))


def softplus(values):
    return jnp.maximum(values, 0.0) + jnp.log1p(jnp.exp(-jnp.abs(values)))


def lane_index(rows):
    return lax.broadcasted_iota(jnp.int32, (rows, 128), 1)


def spread_heads(values, width):
    first = lane_index(values.shape[0]) < HD
    return jnp.concatenate(
        [
            jnp.where(first, values[:, at : at + 1], values[:, at + 1 : at + 2])
            for at in range(0, width // HD, 2)
        ],
        axis=1,
    )


def slot_rows(place_ref, at):
    return pl.ds(pl.multiple_of((place_ref[0] ^ at) * BLOCK, BLOCK), BLOCK)


def lower_mask():
    rows = lax.broadcasted_iota(jnp.int32, (BLOCK, BLOCK), 0)
    columns = lax.broadcasted_iota(jnp.int32, (BLOCK, BLOCK), 1)
    return rows >= columns


def block_decay(raw_steps, step_bias, rate, lower):
    step = softplus(raw_steps + step_bias)
    running = dot(lower.astype(jnp.float32), step * rate, NN, HIGHEST)
    return step, running, running.T


def block_weights(running, running_t, lower, head):
    spread = running[:, head : head + 1] - running_t[head : head + 1, :]
    return jnp.exp(jnp.where(lower, spread, -1e30))


def fill_history(place_ref, raw_ref, history_ref, blocks, width):
    history_ref[0:8, :] = jnp.zeros((8, history_ref.shape[1]), jnp.float32)
    for at in range(blocks):
        rows = slot_rows(place_ref, at)
        here = slice(8 + at * BLOCK, 8 + (at + 1) * BLOCK)
        history_ref[here, 0:width] = raw_ref[rows, 512 + width : 512 + 2 * width]
        history_ref[here, width : width + 256] = raw_ref[rows, 256:512]


def state_forward_kernel(
    place_ref,
    raw_ref,
    taps_ref,
    heads_ref,
    skip_ref,
    gated_ref,
    power_ref,
    conv_ref,
    y_ref,
    states_ref,
    history_ref,
):
    low = jnp.bfloat16
    width = gated_ref.shape[1]
    blocks = gated_ref.shape[0] // BLOCK
    fill_history(place_ref, raw_ref, history_ref, blocks, width)
    lower = lower_mask()
    first = lane_index(BLOCK) < HD
    state = jnp.zeros((states_ref.shape[1], width), jnp.float32)
    for at in range(blocks):
        rows = slot_rows(place_ref, at)
        conv = taps_ref[4:5, :]
        for tap in range(4):
            conv = conv + taps_ref[tap : tap + 1, :] * history_ref[pl.ds(5 + tap + at * BLOCK, BLOCK), :]
        conv_ref[rows, :] = conv
        acted = conv * sigmoid(conv)
        inner = acted[:, :width]
        write = acted[:, width : width + 128].astype(low)
        read = acted[:, width + 128 :].astype(low)
        step, running, running_t = block_decay(
            raw_ref[rows, 512 + 2 * width :], heads_ref[0:1, :], heads_ref[1:2, :], lower
        )
        scaled = inner * spread_heads(step, width)
        scaled_low = scaled.astype(low)
        zero = jnp.zeros((BLOCK, 128), low)
        meet = dot(read, write, NT)
        inside = []
        for pair in range(width // 128):
            both = jnp.concatenate(
                [
                    (meet * block_weights(running, running_t, lower, 2 * pair)).astype(low),
                    (meet * block_weights(running, running_t, lower, 2 * pair + 1)).astype(low),
                ],
                axis=1,
            )
            piece = scaled_low[:, pair * 128 : (pair + 1) * 128]
            split = jnp.concatenate([jnp.where(first, piece, zero), jnp.where(first, zero, piece)])
            inside.append(dot(both, split))
        earlier = dot(read, state.astype(low))
        y = jnp.concatenate(inside, axis=1) + spread_heads(jnp.exp(running), width) * earlier
        y_ref[rows, :] = y
        states_ref[at] = state
        last = running[BLOCK - 1 : BLOCK, :]
        carried = (spread_heads(jnp.exp(last - running), width) * scaled).astype(low)
        state = spread_heads(jnp.exp(last), width) * state + dot(write, carried, TN)
        gate = raw_ref[rows, 512 : 512 + width]
        gated = (y + skip_ref[0:1, :] * inner) * gate * sigmoid(gate)
        gated_ref[rows, :] = gated
        power_ref[:, rows] = dot(jnp.ones((8, width), jnp.float32), gated * gated, NT, HIGHEST)


def state_backward_kernel(
    place_ref,
    raw_ref,
    conv_ref,
    y_ref,
    states_ref,
    up_ref,
    taps_ref,
    heads_ref,
    skip_ref,
    grad_ref,
    grad_taps_ref,
    grad_heads_ref,
    history_ref,
    later_ref,
):
    low = jnp.bfloat16
    width = up_ref.shape[1]
    blocks = up_ref.shape[0] // BLOCK
    length = up_ref.shape[0]
    every = width + 256
    fill_history(place_ref, raw_ref, history_ref, blocks, width)
    later_ref[length : length + 8, :] = jnp.zeros((8, every), jnp.float32)
    lower = lower_mask()
    first = lane_index(BLOCK) < HD
    zero = jnp.zeros((BLOCK, 128), low)
    picks = (
        lax.broadcasted_iota(jnp.int32, (width, 128), 0) // HD
        == lax.broadcasted_iota(jnp.int32, (width, 128), 1)
    ).astype(jnp.float32)
    skip = skip_ref[0:1, :]
    rate = heads_ref[1:2, :]
    grad_state = jnp.zeros((states_ref.shape[1], width), jnp.float32)
    grad_taps = [jnp.zeros((1, every), jnp.float32) for _ in range(5)]
    grad_bias = jnp.zeros((1, 128), jnp.float32)
    grad_decay = jnp.zeros((1, 128), jnp.float32)
    grad_skip = jnp.zeros((1, width), jnp.float32)
    for at in reversed(range(blocks)):
        rows = slot_rows(place_ref, at)
        gate = raw_ref[rows, 512 : 512 + width]
        gate_sigma = sigmoid(gate)
        conv = conv_ref[rows, :]
        conv_sigma = sigmoid(conv)
        acted = conv * conv_sigma
        inner = acted[:, :width]
        write = acted[:, width : width + 128].astype(low)
        read = acted[:, width + 128 :].astype(low)
        y = y_ref[rows, :]
        up = up_ref[rows, :]
        grad_gate = up * (y + skip * inner) * gate_sigma * (1.0 + gate * (1.0 - gate_sigma))
        grad_ref[rows, 256 : 256 + width] = grad_gate.astype(low)
        grad_y = up * gate * gate_sigma
        raw_steps = raw_ref[rows, 512 + 2 * width :]
        step, running, running_t = block_decay(raw_steps, heads_ref[0:1, :], rate, lower)
        step_wide = spread_heads(step, width)
        grow = spread_heads(jnp.exp(running), width)
        last = running[BLOCK - 1 : BLOCK, :]
        carry = spread_heads(jnp.exp(last - running), width)
        last_wide = spread_heads(jnp.exp(last), width)
        scaled = inner * step_wide
        scaled_low = scaled.astype(low)
        grad_low = grad_y.astype(low)
        grown_low = (grad_y * grow).astype(low)
        state = states_ref[at]
        state_low = state.astype(low)
        grad_state_low = grad_state.astype(low)
        meet = dot(read, write, NT)
        grad_meet = jnp.zeros((BLOCK, BLOCK), jnp.float32)
        inside = []
        for pair in range(width // 128):
            weights = [
                block_weights(running, running_t, lower, head) for head in (2 * pair, 2 * pair + 1)
            ]
            both = jnp.concatenate([(meet * item).astype(low) for item in weights], axis=0)
            piece = grad_low[:, pair * 128 : (pair + 1) * 128]
            split = jnp.concatenate([jnp.where(first, piece, zero), jnp.where(first, zero, piece)])
            grad_both = dot(split, scaled_low[:, pair * 128 : (pair + 1) * 128], NT)
            grad_meet = (
                grad_meet + grad_both[:BLOCK] * weights[0] + grad_both[BLOCK:] * weights[1]
            )
            inside.append(dot(both, split, TN))
        grad_inside = jnp.concatenate(inside, axis=1)
        from_state = carry * dot(write, grad_state_low)
        carried = carry * scaled
        grad_scaled = grad_inside + from_state
        moved = scaled * from_state
        turn = grad_low.astype(jnp.float32) * y - scaled_low.astype(jnp.float32) * grad_inside - moved
        direct = grad_y * inner
        ends = jnp.sum(moved, axis=0, keepdims=True) + last_wide * jnp.sum(
            state * grad_state, axis=0, keepdims=True
        )
        summed = dot(
            jnp.concatenate([turn, grad_scaled * inner, jnp.broadcast_to(ends, (8, width))]),
            picks,
            NN,
            HIGHEST,
        )
        grad_running = (
            dot(lower.astype(jnp.float32), summed[:BLOCK], TN, HIGHEST)
            + summed[2 * BLOCK : 2 * BLOCK + 1]
        )
        grad_step = grad_running * rate + summed[BLOCK : 2 * BLOCK]
        grad_decay = grad_decay + jnp.sum(grad_running * step * rate, axis=0, keepdims=True)
        grad_steps = grad_step * sigmoid(raw_steps + heads_ref[0:1, :])
        grad_bias = grad_bias + jnp.sum(grad_steps, axis=0, keepdims=True)
        grad_skip = grad_skip + jnp.sum(direct, axis=0, keepdims=True)
        grad_ref[rows, 256 + 2 * width :] = grad_steps.astype(low)
        grad_inner = grad_scaled * step_wide + skip * grad_y
        grad_meet_low = grad_meet.astype(low)
        grad_read = dot(grad_meet_low, write) + dot(grown_low, state_low, NT)
        grad_write = dot(grad_meet_low, read, TN) + dot(carried.astype(low), grad_state_low, NT)
        grad_state = last_wide * grad_state + dot(read, grown_low, TN)
        grad_conv = jnp.concatenate([grad_inner, grad_write, grad_read], axis=1) * (
            conv_sigma * (1.0 + conv * (1.0 - conv_sigma))
        )
        later_ref[at * BLOCK : (at + 1) * BLOCK, :] = grad_conv
        back = jnp.zeros((BLOCK, every), jnp.float32)
        for tap in range(4):
            back = back + taps_ref[tap : tap + 1, :] * later_ref[pl.ds(at * BLOCK + 3 - tap, BLOCK), :]
            seen = history_ref[pl.ds(5 + tap + at * BLOCK, BLOCK), :]
            grad_taps[tap] = grad_taps[tap] + jnp.sum(grad_conv * seen, axis=0, keepdims=True)
        grad_taps[4] = grad_taps[4] + jnp.sum(grad_conv, axis=0, keepdims=True)
        grad_ref[rows, 256 + width : 256 + 2 * width] = back[:, :width].astype(low)
        grad_ref[rows, 0:256] = back[:, width:].astype(low)
    for tap in range(5):
        grad_taps_ref[tap : tap + 1, :] = grad_taps[tap]
    grad_taps_ref[5:8, :] = jnp.zeros((3, every), jnp.float32)
    skip_heads = dot(jnp.broadcast_to(grad_skip, (8, width)), picks, NN, HIGHEST)
    grad_heads_ref[...] = jnp.zeros(grad_heads_ref.shape, jnp.float32)
    grad_heads_ref[0:1, :] = grad_bias
    grad_heads_ref[1:2, :] = grad_decay
    grad_heads_ref[2:3, :] = skip_heads[0:1]


def turned(values, cosine, sine):
    early = lane_index(values.shape[0]) % HD < HD // 2
    other = jnp.where(early, pltpu.roll(values, 128 - HD // 2, 1), pltpu.roll(values, HD // 2, 1))
    return values * cosine + other * sine


def both_heads(values, first):
    zero = jnp.zeros(values.shape, values.dtype)
    return jnp.concatenate([jnp.where(first, values, zero), jnp.where(first, zero, values)])


def attention_forward_kernel(
    place_ref, raw_ref, angle_ref, mixed_ref, kept_ref, probs_ref
):
    low = jnp.bfloat16
    blocks = mixed_ref.shape[0] // BLOCK
    first = lane_index(BLOCK) < HD
    for at in range(blocks):
        rows = slot_rows(place_ref, at)
        here = slice(at * BLOCK, (at + 1) * BLOCK)
        cosine = angle_ref[here, 0:128]
        sine = angle_ref[here, 128:256]
        pair = raw_ref[rows, 128:256]
        key = turned(pair, cosine, sine)
        kept_ref[here, 0:128] = turned(raw_ref[rows, 0:128], cosine, sine).astype(low)
        kept_ref[here, 128:256] = jnp.where(first, key, pltpu.roll(key, HD, 1)).astype(low)
        kept_ref[here, 256:384] = jnp.where(first, pltpu.roll(pair, HD, 1), pair).astype(low)
    for at in range(blocks):
        rows = slot_rows(place_ref, at)
        here = slice(at * BLOCK, (at + 1) * BLOCK)
        reach = (at + 1) * BLOCK
        query = both_heads(kept_ref[here, 0:128], first)
        scores = dot(query, kept_ref[0:reach, 128:256], NT) * (HD ** (-0.5))
        row = lax.broadcasted_iota(jnp.int32, (2 * BLOCK, reach), 0) % BLOCK + at * BLOCK
        column = lax.broadcasted_iota(jnp.int32, (2 * BLOCK, reach), 1)
        scores = jnp.where(row >= column, scores, -1e30)
        exponent = jnp.exp(scores - jnp.max(scores, axis=1, keepdims=True))
        probs = (exponent / jnp.sum(exponent, axis=1, keepdims=True)).astype(low)
        probs_ref[at, :, 0:reach] = probs
        out = dot(probs, kept_ref[0:reach, 256:384])
        mixed_ref[rows, :] = jnp.where(first, out[:BLOCK], out[BLOCK:]).astype(low)


def attention_backward_kernel(
    place_ref, up_ref, angle_ref, kept_ref, probs_ref, grad_ref, key_ref, value_ref
):
    low = jnp.bfloat16
    blocks = up_ref.shape[0] // BLOCK
    first = lane_index(BLOCK) < HD
    scale = HD ** (-0.5)
    key_ref[...] = jnp.zeros(key_ref.shape, jnp.float32)
    value_ref[...] = jnp.zeros(value_ref.shape, jnp.float32)
    for at in range(blocks):
        rows = slot_rows(place_ref, at)
        here = slice(at * BLOCK, (at + 1) * BLOCK)
        reach = (at + 1) * BLOCK
        query = both_heads(kept_ref[here, 0:128], first)
        up = both_heads(up_ref[rows, :], first)
        probs_low = probs_ref[at, :, 0:reach]
        probs = probs_low.astype(jnp.float32)
        grad_probs = dot(up, kept_ref[0:reach, 256:384], NT)
        inner = jnp.sum(probs * grad_probs, axis=1, keepdims=True)
        grad_scores = (probs * (grad_probs - inner)).astype(low)
        both = dot(grad_scores, kept_ref[0:reach, 128:256]) * scale
        grad_query = jnp.where(first, both[:BLOCK], both[BLOCK:])
        grad_ref[rows, 0:128] = turned(
            grad_query, angle_ref[here, 0:128], -angle_ref[here, 128:256]
        ).astype(low)
        key_ref[0:reach, :] += dot(grad_scores, query, TN)
        value_ref[0:reach, :] += dot(probs_low, up, TN)
    for at in range(blocks):
        rows = slot_rows(place_ref, at)
        here = slice(at * BLOCK, (at + 1) * BLOCK)
        key = key_ref[here, :]
        value = value_ref[here, :]
        key = (key + pltpu.roll(key, HD, 1)) * scale
        key = turned(key, angle_ref[here, 0:128], -angle_ref[here, 128:256])
        value = value + pltpu.roll(value, HD, 1)
        grad_ref[rows, 128:256] = jnp.where(first, key, value).astype(low)


def angle_table(length):
    half = HD // 2
    freq = THETA ** (-np.arange(half, dtype=np.float32) / half)
    angle = np.arange(length, dtype=np.float32)[:, None] * freq[None, :]
    cosine = np.tile(np.cos(angle), (1, 4))
    sine = np.tile(np.concatenate([-np.sin(angle), np.sin(angle)], axis=1), (1, 2))
    return np.concatenate([cosine, sine], axis=1).astype(np.float32)


def run_kernel(kernel, place, operands, outs, scratch, name, flops=8e9):
    whole = pl.BlockSpec(memory_space=pltpu.VMEM)
    return pl.pallas_call(
        kernel,
        out_shape=[jax.ShapeDtypeStruct(shape, dtype) for shape, dtype in outs],
        in_specs=[pl.BlockSpec(memory_space=pltpu.SMEM)] + [whole] * len(operands),
        out_specs=[whole] * len(outs),
        scratch_shapes=scratch,
        compiler_params=pltpu.CompilerParams(vmem_limit_bytes=48 * 1024 * 1024),
        cost_estimate=pl.CostEstimate(flops=int(flops), bytes_accessed=1 << 20, transcendentals=0),
        name=name,
    )(place, *operands)


def state_forward(place, raw, taps, heads, skip, states):
    length = raw.shape[0]
    width = skip.shape[1]
    wide = jnp.float32
    return run_kernel(
        state_forward_kernel,
        place,
        (raw, taps, heads, skip),
        [
            ((length, width), wide),
            ((8, length), wide),
            ((length, width + 256), wide),
            ((length, width), wide),
            ((length // BLOCK, states, width), wide),
        ],
        [pltpu.VMEM((length + 8, width + 256), wide)],
        "state_forward",
    )


def state_backward(place, raw, conv, y, states, up, taps, heads, skip):
    length = raw.shape[0]
    width = skip.shape[1]
    wide = jnp.float32
    return run_kernel(
        state_backward_kernel,
        place,
        (raw, conv, y, states, up, taps, heads, skip),
        [
            ((length, 256 + 2 * width + 128), jnp.bfloat16),
            ((8, width + 256), wide),
            ((8, 128), wide),
        ],
        [pltpu.VMEM((length + 8, width + 256), wide), pltpu.VMEM((length + 8, width + 256), wide)],
        "state_backward",
    )


def attention_forward(place, raw, angles):
    length = raw.shape[0]
    low = jnp.bfloat16
    return run_kernel(
        attention_forward_kernel,
        place,
        (raw, angles),
        [
            ((length, 128), low),
            ((length, 384), low),
            ((length // BLOCK, 2 * BLOCK, length), low),
        ],
        [],
        "attention_forward",
    )


def attention_backward(place, up, angles, kept, probs):
    length = up.shape[0]
    return run_kernel(
        attention_backward_kernel,
        place,
        (up, angles, kept, probs),
        [((length, 256), jnp.bfloat16)],
        [pltpu.VMEM((length, 128), jnp.float32), pltpu.VMEM((length, 128), jnp.float32)],
        "attention_backward",
    )[0]


def swap(values, axis, mask):
    size = lax.axis_size(axis)
    return lax.ppermute(values, axis, [(index, index ^ mask) for index in range(size)])


def tensor_gather(block):
    return [block] + [swap(block, "tensor", mask) for mask in range(1, lax.axis_size("tensor"))]


def paired_sum(terms):
    while len(terms) > 1:
        terms = [terms[at] + terms[at + 1] for at in range(0, len(terms), 2)]
    return terms[0]


def tensor_send(blocks):
    return [
        swap(block.astype(jnp.bfloat16), "tensor", mask)
        for mask, block in enumerate(blocks)
        if mask
    ]


def tensor_scatter(blocks):
    got = tensor_send(blocks)
    return paired_sum([blocks[0]] + [item.astype(jnp.float32) for item in got])


def slot_sum(values):
    parts = lax.axis_size("tensor")
    shaped = values.reshape(parts, -1)
    terms = [shaped]
    for mask in range(1, parts):
        got = swap(shaped, "tensor", mask)
        terms.append(jnp.stack([got[at ^ mask] for at in range(parts)]))
    return paired_sum(terms).reshape(-1)


def tie(*values):
    return lax.optimization_barrier(values)


def dp_gather(block, beside=None):
    size = lax.axis_size("dp")
    if size != 8:
        whole = lax.all_gather(block, "dp", axis=0, tiled=True)
        return whole if beside is None else (whole, beside)
    me = lax.axis_index("dp")
    rows = block.shape[0]
    mine = [block] + [swap(block, "dp", 2 * chip) for chip in range(1, size // 2)]
    mine = jnp.stack(mine)
    if beside is not None:
        mine, beside = tie(mine, beside)
    other = swap(mine, "dp", 1)
    whole = jnp.zeros((size * rows,) + block.shape[1:], block.dtype)
    for chip in range(size // 2):
        whole = lax.dynamic_update_slice_in_dim(whole, mine[chip], (me ^ 2 * chip) * rows, 0)
        whole = lax.dynamic_update_slice_in_dim(whole, other[chip], (me ^ 2 * chip ^ 1) * rows, 0)
    return whole if beside is None else (whole, beside)


def core_sum(whole):
    size = lax.axis_size("dp")
    if size != 8:
        return whole
    chips = size // 2
    rows = whole.shape[0] // size
    shaped = whole.reshape(chips, 2, rows, whole.shape[1])
    core = lax.axis_index("dp") % 2
    give = lax.dynamic_index_in_dim(shaped, 1 - core, 1, keepdims=False)
    give = swap(give, "dp", 1)
    keep = lax.dynamic_index_in_dim(shaped, core, 1, keepdims=False)
    return (keep.astype(jnp.float32) + give.astype(jnp.float32)).astype(jnp.bfloat16)


def chip_sum(both, small=None):
    size = lax.axis_size("dp")
    if size != 8:
        summed = lax.psum_scatter(both, "dp", scatter_dimension=0, tiled=True)
        return summed.astype(jnp.float32), None if small is None else lax.psum(small, "dp")
    chip = lax.axis_index("dp") // 2
    rows = both.shape[1]
    if small is not None:
        small = small.astype(jnp.bfloat16)
        near = swap(small, "dp", 1)
        small = (small.astype(jnp.float32) + near.astype(jnp.float32)).astype(jnp.bfloat16)
    terms = []
    for mask in range(size // 2):
        part = lax.dynamic_index_in_dim(both, chip ^ mask, 0, keepdims=False)
        if small is not None:
            part = jnp.concatenate([part, small])
        terms.append((swap(part, "dp", 2 * mask) if mask else part).astype(jnp.float32))
    summed = paired_sum(terms)
    return summed[:rows], None if small is None else summed[rows:]


def body(
    hidden_in,
    norm_in_gain,
    query_weight,
    key_weight,
    value_weight,
    output_weight,
    gate_weight,
    inner_weight,
    write_weight,
    read_weight,
    step_weight,
    conv_weight,
    conv_bias,
    pair_conv_weight,
    pair_conv_bias,
    step_bias,
    decay_log,
    skip_gain,
    state_gain,
    state_out_weight,
    norm_ffn_gain,
    feed_gate_weight,
    feed_up_weight,
    feed_down_weight,
    out_cotangent,
):
    low = jnp.bfloat16
    wide = jnp.float32
    parts = lax.axis_size("tensor")
    place = lax.axis_index("tensor")
    place_ref = place.astype(jnp.int32).reshape(1)
    heads_here = query_weight.shape[1] // HD
    key_head = place * heads_here // (QH // KVH)
    heads_state = step_weight.shape[1]
    width = gate_weight.shape[1]
    units = feed_gate_weight.shape[1]
    states = write_weight.shape[1]

    mixer_local = jnp.concatenate(
        [
            query_weight,
            lax.dynamic_slice_in_dim(key_weight, key_head * HD, HD, 1),
            lax.dynamic_slice_in_dim(value_weight, key_head * HD, HD, 1),
            write_weight,
            read_weight,
            gate_weight,
            inner_weight,
            jnp.pad(step_weight, ((0, 0), (0, 128 - heads_state))),
        ],
        axis=1,
    )
    out_local = jnp.concatenate([output_weight.T, state_out_weight.T], axis=1)
    feed_local = jnp.concatenate([feed_gate_weight, feed_up_weight, feed_down_weight.T], axis=1)
    rows_in = hidden_in.astype(wide)
    normed, first_scale = root_norm(rows_in, norm_in_gain)
    mixer_rows = jnp.concatenate(tensor_gather(normed.astype(low)))
    mixer_full, mixer_rows = dp_gather(mixer_local, mixer_rows)
    mixer_rows, out_local, feed_local, cot_block = tie(
        mixer_rows, out_local, feed_local, out_cotangent
    )
    out_full = lax.all_gather(out_local, "dp", axis=0, tiled=True)
    late_full = lax.all_gather(feed_local, "dp", axis=0, tiled=True)
    feed_full = late_full[:, : 2 * units]
    down_full = late_full[:, 2 * units :]
    length = mixer_rows.shape[0]
    block = length // parts

    def cut(values):
        return [values[mask * block : (mask + 1) * block] for mask in range(parts)]

    raw = product(mixer_rows, mixer_full)
    cot_slots = tensor_gather(cot_block)

    taps = jnp.concatenate(
        [
            jnp.concatenate([conv_weight, conv_bias[None]]),
            jnp.concatenate([pair_conv_weight, pair_conv_bias[None]]),
        ],
        axis=1,
    )
    taps = jnp.pad(taps, ((0, 3), (0, 0)))
    heads = jnp.pad(
        jnp.stack([step_bias, -jnp.exp(decay_log)]), ((0, 6), (0, 128 - heads_state))
    )
    skip = jnp.repeat(skip_gain, HD)[None]
    angles = jnp.asarray(angle_table(length))

    gated, power, conv, y, kept_states = state_forward(place_ref, raw, taps, heads, skip, states)
    mixed_low, kept, probs = attention_forward(place_ref, raw, angles)
    width_all = width * parts
    power = slot_sum(power[0])
    state_scale = lax.rsqrt(power / width_all + EPS)[:, None]
    state_low = (gated * state_scale * state_gain).astype(low)
    both_low = jnp.concatenate([mixed_low, state_low], axis=1)
    both_low, cot_slots = tie(both_low, cot_slots)
    cotangent = jnp.concatenate(cot_slots)

    mixer_shard = tensor_scatter(cut(product_right(both_low, out_full)))
    middle = rows_in + mixer_shard
    second, second_scale = root_norm(middle, norm_ffn_gain)
    feed_rows = jnp.concatenate(tensor_gather(second.astype(low)))
    grad_active = product(cotangent, down_full)
    gate_up = product(feed_rows, feed_full)
    gate_value = gate_up[:, :units]
    up_value = gate_up[:, units:]
    sigma = jax.nn.sigmoid(gate_value)
    swish = gate_value * sigma
    active = (swish * up_value).astype(low)
    grad_gate = grad_active * up_value * sigma * (1.0 + gate_value * (1.0 - sigma))
    grad_up = grad_active * swish
    grad_pair = jnp.concatenate([grad_gate, grad_up], axis=1).astype(low)

    grad_second = tensor_scatter(cut(product_right(grad_pair, feed_full)))
    grad_feed = jnp.concatenate(
        [product_left(feed_rows, grad_pair), product_left(cotangent, active)], axis=1
    ).astype(low)
    grad_second, grad_feed = tie(grad_second, grad_feed)
    feed_sums = lax.psum_scatter(grad_feed, "dp", scatter_dimension=0, tiled=True)

    weighted_second = grad_second * norm_ffn_gain
    inner_second = jnp.sum(weighted_second * middle, axis=-1, keepdims=True)
    grad_middle = (
        out_cotangent.astype(wide)
        + second_scale * weighted_second
        - middle * second_scale**3 * inner_second / middle.shape[-1]
    )
    ffn_gain = jnp.sum(grad_second * middle * second_scale, axis=0)
    mixer_cot = jnp.concatenate(tensor_gather(grad_middle.astype(low)))
    mixer_cot, active = tie(mixer_cot, active)
    feed_terms = cut(product_right(active, down_full))
    feed_got = tensor_send(feed_terms)
    grad_both = product(mixer_cot, out_full)
    grad_state = grad_both[:, 128:]
    weighted = grad_state * state_gain
    inner_sum = slot_sum(jnp.sum(weighted * gated, axis=1))
    grad_attention = attention_backward(
        place_ref, grad_both[:, :128].astype(low), angles, kept, probs
    )
    early_terms = jnp.concatenate(
        [product_left(mixer_cot, both_low), product_left(mixer_rows, grad_attention)], axis=1
    ).astype(low)
    early_terms = core_sum(early_terms)
    early_terms, inner_sum = tie(early_terms, inner_sum)
    early_sums, _ = chip_sum(early_terms)
    grad_gated = (
        state_scale * weighted - gated * state_scale**3 * (inner_sum / width_all)[:, None]
    )
    grad_state_gain = jnp.sum(grad_state * gated * state_scale, axis=0)
    grad_mixer, grad_taps, grad_heads = state_backward(
        place_ref, raw, conv, y, kept_states, grad_gated, taps, heads, skip
    )
    grad_mixer, early_sums, feed_sums, *feed_got = tie(grad_mixer, early_sums, feed_sums, *feed_got)
    feed_shard = paired_sum([feed_terms[0]] + [item.astype(wide) for item in feed_got])
    hidden_out = (middle + feed_shard).astype(low)
    feed_sums = feed_sums.astype(wide)
    late_terms = core_sum(product_left(mixer_rows, grad_mixer).astype(low))
    total_rows = product_right(grad_mixer, mixer_full[:, 256:]) + product_right(
        grad_attention, mixer_full[:, :256]
    )
    first_got = tensor_send(cut(total_rows))
    in_gain = jnp.sum(total_rows * mixer_rows.astype(wide), axis=0) / norm_in_gain

    columns = late_terms.shape[-1]
    small = [
        in_gain,
        ffn_gain,
        grad_taps[:4, width:].reshape(-1),
        grad_taps[4, width:],
        grad_taps[:4, :width].reshape(-1),
        grad_taps[4, :width],
        grad_state_gain,
        grad_heads[0, :heads_state],
        grad_heads[1, :heads_state],
        grad_heads[2, :heads_state],
    ]
    sizes = [item.shape[0] for item in small]
    flat = jnp.concatenate(small)
    small_rows = -(-flat.shape[0] // (16 * columns)) * 16
    flat = jnp.pad(flat, (0, small_rows * columns - flat.shape[0])).reshape(small_rows, columns)
    late_sums, flat = chip_sum(late_terms, flat)
    done = (
        hidden_out,
        early_sums[:, 128 + width : 128 + width + 128],
        early_sums[:, :128].T,
        early_sums[:, 128 : 128 + width].T,
        feed_sums[:, :units],
        feed_sums[:, units : 2 * units],
        feed_sums[:, 2 * units :].T,
    )
    late_sums, done = tie(late_sums, done)
    flat = flat.reshape(-1)

    common = sum(sizes[:4])
    common_rows = -(-common // (16 * 384)) * 16
    rows_here = mixer_local.shape[0]
    shared = jnp.concatenate(
        [
            jnp.concatenate([early_sums[:, 128 + width + 128 :], late_sums[:, :256]], axis=1),
            jnp.pad(flat[:common], (0, common_rows * 384 - common)).reshape(common_rows, 384),
        ]
    ).astype(low)
    near = shared.astype(wide) + swap(shared, "tensor", 1).astype(wide)
    near = near.astype(low)
    far = swap(near, "tensor", 2).astype(wide)
    near = near.astype(wide)
    both = near + far
    first_half = place < parts // 2
    head_low = jnp.where(first_half, near[:rows_here, :128], far[:rows_here, :128])
    head_high = jnp.where(first_half, far[:rows_here, :128], near[:rows_here, :128])
    common_sums = both[rows_here:].reshape(-1)
    shared = jnp.concatenate([head_low, head_high, both[:rows_here, 128:]], axis=1).astype(low)
    shared, first_got = tie(shared, first_got)
    grad_first = paired_sum([total_rows[:block]] + [item.astype(wide) for item in first_got])
    shared = dp_gather(shared).astype(wide)
    gradient_key = jnp.concatenate([shared[:, :64], shared[:, 128:192]], axis=1)
    gradient_value = jnp.concatenate([shared[:, 64:128], shared[:, 192:256]], axis=1)

    weighted_first = grad_first * norm_in_gain
    inner_first = jnp.sum(weighted_first * rows_in, axis=-1, keepdims=True)
    gradient_hidden = (
        grad_middle
        + first_scale * weighted_first
        - rows_in * first_scale**3 * inner_first / rows_in.shape[-1]
    )

    cuts = []
    at = 0
    for index, size in enumerate(sizes):
        cuts.append((common_sums if index < 4 else flat)[at : at + size])
        at += size
    return (
        done[0],
        gradient_hidden,
        cuts[0],
        done[1],
        gradient_key,
        gradient_value,
        done[2],
        late_sums[:, 256 : 256 + width],
        late_sums[:, 256 + width : 256 + 2 * width],
        shared[:, 256:384],
        shared[:, 384:512],
        late_sums[:, 256 + 2 * width : 256 + 2 * width + heads_state],
        cuts[4].reshape(conv_weight.shape),
        cuts[5],
        cuts[2].reshape(pair_conv_weight.shape),
        cuts[3],
        cuts[7],
        cuts[8],
        cuts[9],
        cuts[6],
        done[3],
        cuts[1],
        done[4],
        done[5],
        done[6],
    )


def solution(mesh):
    placed = (
        P(("dp", "tensor"), None),
        P(),
        P("dp", "tensor"),
        P("dp", None),
        P("dp", None),
        P("tensor", "dp"),
        P("dp", "tensor"),
        P("dp", "tensor"),
        P("dp", None),
        P("dp", None),
        P("dp", "tensor"),
        P(None, "tensor"),
        P("tensor"),
        P(),
        P(),
        P("tensor"),
        P("tensor"),
        P("tensor"),
        P("tensor"),
        P("tensor", "dp"),
        P(),
        P("dp", "tensor"),
        P("dp", "tensor"),
        P("tensor", "dp"),
        P(("dp", "tensor"), None),
    )
    return jax.shard_map(
        body,
        mesh=mesh,
        in_specs=placed,
        out_specs=(
            P(("dp", "tensor"), None),
            P(("dp", "tensor"), None),
            P(),
            P("dp", "tensor"),
            P(),
            P(),
            P("tensor", "dp"),
            P("dp", "tensor"),
            P("dp", "tensor"),
            P(),
            P(),
            P("dp", "tensor"),
            P(None, "tensor"),
            P("tensor"),
            P(),
            P(),
            P("tensor"),
            P("tensor"),
            P("tensor"),
            P("tensor"),
            P("tensor", "dp"),
            P(),
            P("dp", "tensor"),
            P("dp", "tensor"),
            P("tensor", "dp"),
        ),
        check_vma=False,
    )
```

```python
import functools

import jax
import jax.numpy as jnp
import numpy as np
from jax import lax
from jax.experimental import pallas as pl
from jax.experimental.pallas import tpu as pltpu
from jax.sharding import PartitionSpec as P

QH = 8
KVH = 2
HD = 64
BLOCK = 128


EPS = 1e-05
THETA = 10000.0
HIGHEST = lax.Precision.HIGHEST


def product(left, right):
    return jnp.dot(left, right, preferred_element_type=jnp.float32)


def product_left(left, right):
    return lax.dot_general(
        left, right, (((0,), (0,)), ((), ())), preferred_element_type=jnp.float32
    )


def product_right(left, right):
    return lax.dot_general(
        left, right, (((1,), (1,)), ((), ())), preferred_element_type=jnp.float32
    )


def root_norm(rows, gain):
    scale = lax.rsqrt(jnp.mean(rows * rows, axis=-1, keepdims=True) + EPS)
    return (rows * scale * gain, scale)


def dot(left, right, dims=((1,), (0,)), precision=None):
    return lax.dot_general(
        left, right, (dims, ((), ())), precision=precision, preferred_element_type=jnp.float32
    )


NN = ((1,), (0,))
NT = ((1,), (1,))
TN = ((0,), (0,))


def sigmoid(values):
    return 1.0 / (1.0 + jnp.exp(-values))


def softplus(values):
    return jnp.maximum(values, 0.0) + jnp.log1p(jnp.exp(-jnp.abs(values)))


def lane_index(rows):
    return lax.broadcasted_iota(jnp.int32, (rows, 128), 1)


def spread_heads(values, width):
    first = lane_index(values.shape[0]) < HD
    return jnp.concatenate(
        [
            jnp.where(first, values[:, at : at + 1], values[:, at + 1 : at + 2])
            for at in range(0, width // HD, 2)
        ],
        axis=1,
    )


def slot_rows(place_ref, at):
    return pl.ds(pl.multiple_of((place_ref[0] ^ at) * BLOCK, BLOCK), BLOCK)


def lower_mask():
    rows = lax.broadcasted_iota(jnp.int32, (BLOCK, BLOCK), 0)
    columns = lax.broadcasted_iota(jnp.int32, (BLOCK, BLOCK), 1)
    return rows >= columns


def block_decay(raw_steps, step_bias, rate, lower):
    step = softplus(raw_steps + step_bias)
    running = dot(lower.astype(jnp.float32), step * rate, NN, HIGHEST)
    return step, running, running.T


def block_weights(running, running_t, lower, head):
    spread = running[:, head : head + 1] - running_t[head : head + 1, :]
    return jnp.exp(jnp.where(lower, spread, -1e30))


def fill_history(place_ref, raw_ref, history_ref, blocks, width):
    history_ref[0:8, :] = jnp.zeros((8, history_ref.shape[1]), jnp.float32)
    for at in range(blocks):
        rows = slot_rows(place_ref, at)
        here = slice(8 + at * BLOCK, 8 + (at + 1) * BLOCK)
        history_ref[here, 0:width] = raw_ref[rows, 512 + width : 512 + 2 * width]
        history_ref[here, width : width + 256] = raw_ref[rows, 256:512]


def state_forward_kernel(
    place_ref,
    raw_ref,
    taps_ref,
    heads_ref,
    skip_ref,
    gated_ref,
    power_ref,
    conv_ref,
    y_ref,
    states_ref,
    history_ref,
):
    low = jnp.bfloat16
    width = gated_ref.shape[1]
    blocks = gated_ref.shape[0] // BLOCK
    fill_history(place_ref, raw_ref, history_ref, blocks, width)
    lower = lower_mask()
    first = lane_index(BLOCK) < HD
    state = jnp.zeros((states_ref.shape[1], width), jnp.float32)
    for at in range(blocks):
        rows = slot_rows(place_ref, at)
        conv = taps_ref[4:5, :]
        for tap in range(4):
            conv = conv + taps_ref[tap : tap + 1, :] * history_ref[pl.ds(5 + tap + at * BLOCK, BLOCK), :]
        conv_ref[rows, :] = conv
        acted = conv * sigmoid(conv)
        inner = acted[:, :width]
        write = acted[:, width : width + 128].astype(low)
        read = acted[:, width + 128 :].astype(low)
        step, running, running_t = block_decay(
            raw_ref[rows, 512 + 2 * width :], heads_ref[0:1, :], heads_ref[1:2, :], lower
        )
        scaled = inner * spread_heads(step, width)
        scaled_low = scaled.astype(low)
        zero = jnp.zeros((BLOCK, 128), low)
        meet = dot(read, write, NT)
        inside = []
        for pair in range(width // 128):
            both = jnp.concatenate(
                [
                    (meet * block_weights(running, running_t, lower, 2 * pair)).astype(low),
                    (meet * block_weights(running, running_t, lower, 2 * pair + 1)).astype(low),
                ],
                axis=1,
            )
            piece = scaled_low[:, pair * 128 : (pair + 1) * 128]
            split = jnp.concatenate([jnp.where(first, piece, zero), jnp.where(first, zero, piece)])
            inside.append(dot(both, split))
        earlier = dot(read, state.astype(low))
        y = jnp.concatenate(inside, axis=1) + spread_heads(jnp.exp(running), width) * earlier
        y_ref[rows, :] = y
        states_ref[at] = state
        last = running[BLOCK - 1 : BLOCK, :]
        carried = (spread_heads(jnp.exp(last - running), width) * scaled).astype(low)
        state = spread_heads(jnp.exp(last), width) * state + dot(write, carried, TN)
        gate = raw_ref[rows, 512 : 512 + width]
        gated = (y + skip_ref[0:1, :] * inner) * gate * sigmoid(gate)
        gated_ref[rows, :] = gated
        power_ref[:, rows] = dot(jnp.ones((8, width), jnp.float32), gated * gated, NT, HIGHEST)


def state_backward_kernel(
    place_ref,
    raw_ref,
    conv_ref,
    y_ref,
    states_ref,
    up_ref,
    taps_ref,
    heads_ref,
    skip_ref,
    grad_ref,
    grad_taps_ref,
    grad_heads_ref,
    history_ref,
    later_ref,
):
    low = jnp.bfloat16
    width = up_ref.shape[1]
    blocks = up_ref.shape[0] // BLOCK
    length = up_ref.shape[0]
    every = width + 256
    fill_history(place_ref, raw_ref, history_ref, blocks, width)
    later_ref[length : length + 8, :] = jnp.zeros((8, every), jnp.float32)
    lower = lower_mask()
    first = lane_index(BLOCK) < HD
    zero = jnp.zeros((BLOCK, 128), low)
    picks = (
        lax.broadcasted_iota(jnp.int32, (width, 128), 0) // HD
        == lax.broadcasted_iota(jnp.int32, (width, 128), 1)
    ).astype(jnp.float32)
    skip = skip_ref[0:1, :]
    rate = heads_ref[1:2, :]
    grad_state = jnp.zeros((states_ref.shape[1], width), jnp.float32)
    grad_taps = [jnp.zeros((1, every), jnp.float32) for _ in range(5)]
    grad_bias = jnp.zeros((1, 128), jnp.float32)
    grad_decay = jnp.zeros((1, 128), jnp.float32)
    grad_skip = jnp.zeros((1, width), jnp.float32)
    for at in reversed(range(blocks)):
        rows = slot_rows(place_ref, at)
        gate = raw_ref[rows, 512 : 512 + width]
        gate_sigma = sigmoid(gate)
        conv = conv_ref[rows, :]
        conv_sigma = sigmoid(conv)
        acted = conv * conv_sigma
        inner = acted[:, :width]
        write = acted[:, width : width + 128].astype(low)
        read = acted[:, width + 128 :].astype(low)
        y = y_ref[rows, :]
        up = up_ref[rows, :]
        grad_gate = up * (y + skip * inner) * gate_sigma * (1.0 + gate * (1.0 - gate_sigma))
        grad_ref[rows, 256 : 256 + width] = grad_gate.astype(low)
        grad_y = up * gate * gate_sigma
        raw_steps = raw_ref[rows, 512 + 2 * width :]
        step, running, running_t = block_decay(raw_steps, heads_ref[0:1, :], rate, lower)
        step_wide = spread_heads(step, width)
        grow = spread_heads(jnp.exp(running), width)
        last = running[BLOCK - 1 : BLOCK, :]
        carry = spread_heads(jnp.exp(last - running), width)
        last_wide = spread_heads(jnp.exp(last), width)
        scaled = inner * step_wide
        scaled_low = scaled.astype(low)
        grad_low = grad_y.astype(low)
        grown_low = (grad_y * grow).astype(low)
        state = states_ref[at]
        state_low = state.astype(low)
        grad_state_low = grad_state.astype(low)
        meet = dot(read, write, NT)
        grad_meet = jnp.zeros((BLOCK, BLOCK), jnp.float32)
        inside = []
        for pair in range(width // 128):
            weights = [
                block_weights(running, running_t, lower, head) for head in (2 * pair, 2 * pair + 1)
            ]
            both = jnp.concatenate([(meet * item).astype(low) for item in weights], axis=0)
            piece = grad_low[:, pair * 128 : (pair + 1) * 128]
            split = jnp.concatenate([jnp.where(first, piece, zero), jnp.where(first, zero, piece)])
            grad_both = dot(split, scaled_low[:, pair * 128 : (pair + 1) * 128], NT)
            grad_meet = (
                grad_meet + grad_both[:BLOCK] * weights[0] + grad_both[BLOCK:] * weights[1]
            )
            inside.append(dot(both, split, TN))
        grad_inside = jnp.concatenate(inside, axis=1)
        from_state = carry * dot(write, grad_state_low)
        carried = carry * scaled
        grad_scaled = grad_inside + from_state
        moved = scaled * from_state
        turn = grad_low.astype(jnp.float32) * y - scaled_low.astype(jnp.float32) * grad_inside - moved
        direct = grad_y * inner
        ends = jnp.sum(moved, axis=0, keepdims=True) + last_wide * jnp.sum(
            state * grad_state, axis=0, keepdims=True
        )
        summed = dot(
            jnp.concatenate([turn, grad_scaled * inner, jnp.broadcast_to(ends, (8, width))]),
            picks,
            NN,
            HIGHEST,
        )
        grad_running = (
            dot(lower.astype(jnp.float32), summed[:BLOCK], TN, HIGHEST)
            + summed[2 * BLOCK : 2 * BLOCK + 1]
        )
        grad_step = grad_running * rate + summed[BLOCK : 2 * BLOCK]
        grad_decay = grad_decay + jnp.sum(grad_running * step * rate, axis=0, keepdims=True)
        grad_steps = grad_step * sigmoid(raw_steps + heads_ref[0:1, :])
        grad_bias = grad_bias + jnp.sum(grad_steps, axis=0, keepdims=True)
        grad_skip = grad_skip + jnp.sum(direct, axis=0, keepdims=True)
        grad_ref[rows, 256 + 2 * width :] = grad_steps.astype(low)
        grad_inner = grad_scaled * step_wide + skip * grad_y
        grad_meet_low = grad_meet.astype(low)
        grad_read = dot(grad_meet_low, write) + dot(grown_low, state_low, NT)
        grad_write = dot(grad_meet_low, read, TN) + dot(carried.astype(low), grad_state_low, NT)
        grad_state = last_wide * grad_state + dot(read, grown_low, TN)
        grad_conv = jnp.concatenate([grad_inner, grad_write, grad_read], axis=1) * (
            conv_sigma * (1.0 + conv * (1.0 - conv_sigma))
        )
        later_ref[at * BLOCK : (at + 1) * BLOCK, :] = grad_conv
        back = jnp.zeros((BLOCK, every), jnp.float32)
        for tap in range(4):
            back = back + taps_ref[tap : tap + 1, :] * later_ref[pl.ds(at * BLOCK + 3 - tap, BLOCK), :]
            seen = history_ref[pl.ds(5 + tap + at * BLOCK, BLOCK), :]
            grad_taps[tap] = grad_taps[tap] + jnp.sum(grad_conv * seen, axis=0, keepdims=True)
        grad_taps[4] = grad_taps[4] + jnp.sum(grad_conv, axis=0, keepdims=True)
        grad_ref[rows, 256 + width : 256 + 2 * width] = back[:, :width].astype(low)
        grad_ref[rows, 0:256] = back[:, width:].astype(low)
    for tap in range(5):
        grad_taps_ref[tap : tap + 1, :] = grad_taps[tap]
    grad_taps_ref[5:8, :] = jnp.zeros((3, every), jnp.float32)
    skip_heads = dot(jnp.broadcast_to(grad_skip, (8, width)), picks, NN, HIGHEST)
    grad_heads_ref[...] = jnp.zeros(grad_heads_ref.shape, jnp.float32)
    grad_heads_ref[0:1, :] = grad_bias
    grad_heads_ref[1:2, :] = grad_decay
    grad_heads_ref[2:3, :] = skip_heads[0:1]


def turned(values, cosine, sine):
    early = lane_index(values.shape[0]) % HD < HD // 2
    other = jnp.where(early, pltpu.roll(values, 128 - HD // 2, 1), pltpu.roll(values, HD // 2, 1))
    return values * cosine + other * sine


def both_heads(values, first):
    zero = jnp.zeros(values.shape, values.dtype)
    return jnp.concatenate([jnp.where(first, values, zero), jnp.where(first, zero, values)])


def attention_forward_kernel(
    place_ref, raw_ref, angle_ref, mixed_ref, kept_ref, probs_ref
):
    low = jnp.bfloat16
    blocks = mixed_ref.shape[0] // BLOCK
    first = lane_index(BLOCK) < HD
    for at in range(blocks):
        rows = slot_rows(place_ref, at)
        here = slice(at * BLOCK, (at + 1) * BLOCK)
        cosine = angle_ref[here, 0:128]
        sine = angle_ref[here, 128:256]
        pair = raw_ref[rows, 128:256]
        key = turned(pair, cosine, sine)
        kept_ref[here, 0:128] = turned(raw_ref[rows, 0:128], cosine, sine).astype(low)
        kept_ref[here, 128:256] = jnp.where(first, key, pltpu.roll(key, HD, 1)).astype(low)
        kept_ref[here, 256:384] = jnp.where(first, pltpu.roll(pair, HD, 1), pair).astype(low)
    for at in range(blocks):
        rows = slot_rows(place_ref, at)
        here = slice(at * BLOCK, (at + 1) * BLOCK)
        reach = (at + 1) * BLOCK
        query = both_heads(kept_ref[here, 0:128], first)
        scores = dot(query, kept_ref[0:reach, 128:256], NT) * (HD ** (-0.5))
        row = lax.broadcasted_iota(jnp.int32, (2 * BLOCK, reach), 0) % BLOCK + at * BLOCK
        column = lax.broadcasted_iota(jnp.int32, (2 * BLOCK, reach), 1)
        scores = jnp.where(row >= column, scores, -1e30)
        exponent = jnp.exp(scores - jnp.max(scores, axis=1, keepdims=True))
        probs = (exponent / jnp.sum(exponent, axis=1, keepdims=True)).astype(low)
        probs_ref[at, :, 0:reach] = probs
        out = dot(probs, kept_ref[0:reach, 256:384])
        mixed_ref[rows, :] = jnp.where(first, out[:BLOCK], out[BLOCK:]).astype(low)


def attention_backward_kernel(
    place_ref, up_ref, angle_ref, kept_ref, probs_ref, grad_ref, key_ref, value_ref
):
    low = jnp.bfloat16
    blocks = up_ref.shape[0] // BLOCK
    first = lane_index(BLOCK) < HD
    scale = HD ** (-0.5)
    key_ref[...] = jnp.zeros(key_ref.shape, jnp.float32)
    value_ref[...] = jnp.zeros(value_ref.shape, jnp.float32)
    for at in range(blocks):
        rows = slot_rows(place_ref, at)
        here = slice(at * BLOCK, (at + 1) * BLOCK)
        reach = (at + 1) * BLOCK
        query = both_heads(kept_ref[here, 0:128], first)
        up = both_heads(up_ref[rows, :], first)
        probs_low = probs_ref[at, :, 0:reach]
        probs = probs_low.astype(jnp.float32)
        grad_probs = dot(up, kept_ref[0:reach, 256:384], NT)
        inner = jnp.sum(probs * grad_probs, axis=1, keepdims=True)
        grad_scores = (probs * (grad_probs - inner)).astype(low)
        both = dot(grad_scores, kept_ref[0:reach, 128:256]) * scale
        grad_query = jnp.where(first, both[:BLOCK], both[BLOCK:])
        grad_ref[rows, 0:128] = turned(
            grad_query, angle_ref[here, 0:128], -angle_ref[here, 128:256]
        ).astype(low)
        key_ref[0:reach, :] += dot(grad_scores, query, TN)
        value_ref[0:reach, :] += dot(probs_low, up, TN)
    for at in range(blocks):
        rows = slot_rows(place_ref, at)
        here = slice(at * BLOCK, (at + 1) * BLOCK)
        key = key_ref[here, :]
        value = value_ref[here, :]
        key = (key + pltpu.roll(key, HD, 1)) * scale
        key = turned(key, angle_ref[here, 0:128], -angle_ref[here, 128:256])
        value = value + pltpu.roll(value, HD, 1)
        grad_ref[rows, 128:256] = jnp.where(first, key, value).astype(low)


def angle_table(length):
    half = HD // 2
    freq = THETA ** (-np.arange(half, dtype=np.float32) / half)
    angle = np.arange(length, dtype=np.float32)[:, None] * freq[None, :]
    cosine = np.tile(np.cos(angle), (1, 4))
    sine = np.tile(np.concatenate([-np.sin(angle), np.sin(angle)], axis=1), (1, 2))
    return np.concatenate([cosine, sine], axis=1).astype(np.float32)


def run_kernel(kernel, place, operands, outs, scratch, name, flops=8e9):
    whole = pl.BlockSpec(memory_space=pltpu.VMEM)
    return pl.pallas_call(
        kernel,
        out_shape=[jax.ShapeDtypeStruct(shape, dtype) for shape, dtype in outs],
        in_specs=[pl.BlockSpec(memory_space=pltpu.SMEM)] + [whole] * len(operands),
        out_specs=[whole] * len(outs),
        scratch_shapes=scratch,
        compiler_params=pltpu.CompilerParams(vmem_limit_bytes=48 * 1024 * 1024),
        cost_estimate=pl.CostEstimate(flops=int(flops), bytes_accessed=1 << 20, transcendentals=0),
        name=name,
    )(place, *operands)


def state_forward(place, raw, taps, heads, skip, states):
    length = raw.shape[0]
    width = skip.shape[1]
    wide = jnp.float32
    return run_kernel(
        state_forward_kernel,
        place,
        (raw, taps, heads, skip),
        [
            ((length, width), wide),
            ((8, length), wide),
            ((length, width + 256), wide),
            ((length, width), wide),
            ((length // BLOCK, states, width), wide),
        ],
        [pltpu.VMEM((length + 8, width + 256), wide)],
        "state_forward",
    )


def state_backward(place, raw, conv, y, states, up, taps, heads, skip):
    length = raw.shape[0]
    width = skip.shape[1]
    wide = jnp.float32
    return run_kernel(
        state_backward_kernel,
        place,
        (raw, conv, y, states, up, taps, heads, skip),
        [
            ((length, 256 + 2 * width + 128), jnp.bfloat16),
            ((8, width + 256), wide),
            ((8, 128), wide),
        ],
        [pltpu.VMEM((length + 8, width + 256), wide), pltpu.VMEM((length + 8, width + 256), wide)],
        "state_backward",
    )


def attention_forward(place, raw, angles):
    length = raw.shape[0]
    low = jnp.bfloat16
    return run_kernel(
        attention_forward_kernel,
        place,
        (raw, angles),
        [
            ((length, 128), low),
            ((length, 384), low),
            ((length // BLOCK, 2 * BLOCK, length), low),
        ],
        [],
        "attention_forward",
    )


def attention_backward(place, up, angles, kept, probs):
    length = up.shape[0]
    return run_kernel(
        attention_backward_kernel,
        place,
        (up, angles, kept, probs),
        [((length, 256), jnp.bfloat16)],
        [pltpu.VMEM((length, 128), jnp.float32), pltpu.VMEM((length, 128), jnp.float32)],
        "attention_backward",
    )[0]


def block_columns(me_ref, mask):
    return pl.ds(pl.multiple_of((me_ref[0] ^ mask) * 128, 128), 128)


def join_rows(slots, whole_ref):
    rows = slots[0].shape[0]
    for at, slot in enumerate(slots):
        whole_ref[at * rows : (at + 1) * rows, :] = slot[...]


def project_kernel(me_ref, *refs):
    slots, (near_ref, far_ref, rows_ref, raw_ref) = refs[:-4], refs[-4:]
    join_rows(slots, rows_ref)
    chips = near_ref.shape[0] // 128
    near = jnp.concatenate([rows_ref[:, block_columns(me_ref, 2 * at)] for at in range(chips)], axis=1)
    far = jnp.concatenate(
        [rows_ref[:, block_columns(me_ref, 2 * at + 1)] for at in range(chips)], axis=1
    )
    raw_ref[...] = dot(near, near_ref[...]) + dot(far, far_ref[...])


def write_spread(total, own_ref, sends):
    rows = own_ref.shape[0]
    own_ref[...] = total[:rows]
    for at, send in enumerate(sends):
        send[...] = total[(at + 1) * rows : (at + 2) * rows].astype(jnp.bfloat16)


def spread_kernel(start, count, place_ref, *refs):
    lefts, weight_ref, own_ref, sends = refs[:count], refs[count], refs[count + 1], refs[count + 2 :]
    left = jnp.concatenate([item[...] for item in lefts], axis=1)
    total = dot(left, weight_ref[:, start : start + left.shape[1]], NT)
    write_spread(total, own_ref, sends)


def total_kernel(
    me_ref, attention_ref, mixer_ref, near_ref, far_ref, rows_ref, gain_ref, own_ref, *rest
):
    sends, total_ref = rest[:-1], rest[-1]
    left = jnp.concatenate([attention_ref[...], mixer_ref[...]], axis=1)
    chips = near_ref.shape[0] // 128
    for side, weight_ref in enumerate((near_ref, far_ref)):
        piece = dot(left, weight_ref[...], NT)
        for at in range(chips):
            total_ref[:, block_columns(me_ref, 2 * at + side)] = piece[:, at * 128 : (at + 1) * 128]
    total = total_ref[...]
    gain_ref[...] = jnp.broadcast_to(
        jnp.sum(total * rows_ref[...].astype(jnp.float32), axis=0, keepdims=True), gain_ref.shape
    )
    write_spread(total, own_ref, sends)


def feed_kernel(place_ref, *refs):
    low = jnp.bfloat16
    slots, cots = refs[:4], refs[4:8]
    feed_ref, pair_ref, active_ref, own_ref = refs[8:12]
    sends = refs[12:15]
    units = active_ref.shape[1]
    rows = slots[0].shape[0]
    for half in range(2):
        here = slice(2 * half * rows, 2 * (half + 1) * rows)
        left = jnp.concatenate([slots[2 * half][...], slots[2 * half + 1][...]])
        cot = jnp.concatenate([cots[2 * half][...], cots[2 * half + 1][...]])
        gate_up = dot(left, feed_ref[:, : 2 * units])
        grad_active = dot(cot, feed_ref[:, 2 * units :])
        gate = gate_up[:, :units]
        up = gate_up[:, units:]
        sigma = sigmoid(gate)
        swish = gate * sigma
        active_ref[here, :] = (swish * up).astype(low)
        grad_gate = grad_active * up * sigma * (1.0 + gate * (1.0 - sigma))
        pair = jnp.concatenate([grad_gate, grad_active * swish], axis=1).astype(low)
        pair_ref[here, :] = pair
        total = dot(pair, feed_ref[:, : 2 * units], NT)
        if half == 0:
            own_ref[...] = total[:rows]
            sends[0][...] = total[rows:].astype(low)
        else:
            sends[1][...] = total[:rows].astype(low)
            sends[2][...] = total[rows:].astype(low)


def feed_grad_kernel(place_ref, *refs):
    slots, cots = refs[:4], refs[4:8]
    pair_ref, active_ref, out_ref, rows_ref, cot_ref = refs[8:]
    join_rows(slots, rows_ref)
    join_rows(cots, cot_ref)
    both = pair_ref.shape[1]
    for at in range(0, rows_ref.shape[1], 256):
        here = slice(at, at + 256)
        out_ref[here, :both] = dot(rows_ref[:, here], pair_ref[...], TN).astype(out_ref.dtype)
        out_ref[here, both:] = dot(cot_ref[:, here], active_ref[...], TN).astype(out_ref.dtype)


def weight_grad_kernel(groups, me_ref, *refs):
    keep_ref, give_ref = refs[-2:]
    even = me_ref[0] % 2 == 0
    for chip in range(keep_ref.shape[0]):
        here = slice(chip * 256, (chip + 1) * 256)
        pieces = []
        at = 0
        for count in groups:
            left = refs[at][:, here]
            right = jnp.concatenate([item[...] for item in refs[at + 1 : at + 1 + count]], axis=1)
            pieces.append(dot(left, right, TN))
            at += 1 + count
        piece = jnp.concatenate(pieces, axis=1).astype(keep_ref.dtype)
        keep_ref[chip] = jnp.where(even, piece[:128], piece[128:])
        give_ref[chip] = jnp.where(even, piece[128:], piece[:128])


def mixer_back_kernel(place_ref, *refs):
    slots = refs[:4]
    weight_ref, gated_ref, gain_ref, cot_ref, mixed_ref, state_ref, inner_ref = refs[4:]
    join_rows(slots, cot_ref)
    both = dot(cot_ref[...], weight_ref[...])
    mixed_ref[...] = both[:, :128].astype(jnp.bfloat16)
    state = both[:, 128:]
    state_ref[...] = state
    product_rows = state * gain_ref[0:1, :] * gated_ref[...]
    inner_ref[...] = dot(
        jnp.ones((8, product_rows.shape[1]), jnp.float32), product_rows, NT, HIGHEST
    )


def project(me, slots, near, far):
    length = len(slots) * slots[0].shape[0]
    return run_kernel(
        project_kernel,
        me,
        (*slots, near, far),
        [((length, slots[0].shape[1]), jnp.bfloat16), ((length, near.shape[1]), jnp.float32)],
        [],
        "project",
    )


def spread_outs(rows, columns, parts):
    return [((rows, columns), jnp.float32)] + [((rows, columns), jnp.bfloat16)] * (parts - 1)


def spread_product(place, lefts, weight, start, parts):
    rows = lefts[0].shape[0] // parts
    return run_kernel(
        functools.partial(spread_kernel, start, len(lefts)),
        place,
        (*lefts, weight),
        spread_outs(rows, weight.shape[0], parts),
        [],
        "spread_product",
    )


def total_product(me, attention, mixer, near, far, rows, parts):
    length, columns = rows.shape
    return run_kernel(
        total_kernel,
        me,
        (attention, mixer, near, far, rows),
        [((8, columns), jnp.float32)] + spread_outs(length // parts, columns, parts),
        [pltpu.VMEM((length, columns), jnp.float32)],
        "total_product",
    )


def feed_forward(place, slots, cots, feed):
    rows, columns = slots[0].shape
    units = feed.shape[1] // 3
    parts = len(slots)
    return run_kernel(
        feed_kernel,
        place,
        (*slots, *cots, feed),
        [((parts * rows, 2 * units), jnp.bfloat16), ((parts * rows, units), jnp.bfloat16)]
        + spread_outs(rows, columns, parts),
        [],
        "feed_forward",
    )


def feed_grad(place, slots, cots, pair, active):
    length, columns = pair.shape[0], slots[0].shape[1]
    scratch = pltpu.VMEM((length, columns), jnp.bfloat16)
    return run_kernel(
        feed_grad_kernel,
        place,
        (*slots, *cots, pair, active),
        [((columns, pair.shape[1] + active.shape[1]), jnp.bfloat16)],
        [scratch, scratch],
        "feed_grad",
    )[0]


def weight_grad(me, groups):
    counts = tuple(len(rights) for _, rights in groups)
    columns = sum(item.shape[1] for _, rights in groups for item in rights)
    operands = [item for left, rights in groups for item in (left, *rights)]
    blocks = groups[0][0].shape[1] // 256
    return run_kernel(
        functools.partial(weight_grad_kernel, counts),
        me,
        operands,
        [((blocks, 128, columns), jnp.bfloat16)] * 2,
        [],
        "weight_grad",
    )


def mixer_back(place, slots, weight, gated, gain):
    rows, columns = slots[0].shape
    length = len(slots) * rows
    width = gated.shape[1]
    return run_kernel(
        mixer_back_kernel,
        place,
        (*slots, weight, gated, gain),
        [
            ((length, columns), jnp.bfloat16),
            ((length, 128), jnp.bfloat16),
            ((length, width), jnp.float32),
            ((8, length), jnp.float32),
        ],
        [],
        "mixer_back",
    )


def swap(values, axis, mask):
    size = lax.axis_size(axis)
    return lax.ppermute(values, axis, [(index, index ^ mask) for index in range(size)])


def tensor_gather(block):
    return [block] + [swap(block, "tensor", mask) for mask in range(1, lax.axis_size("tensor"))]


def paired_sum(terms):
    while len(terms) > 1:
        terms = [terms[at] + terms[at + 1] for at in range(0, len(terms), 2)]
    return terms[0]


def tensor_send(sends):
    return [swap(item, "tensor", at + 1) for at, item in enumerate(sends)]


def finish_scatter(own, got):
    return paired_sum([own] + [item.astype(jnp.float32) for item in got])


def slot_sum(values):
    parts = lax.axis_size("tensor")
    shaped = values.reshape(parts, -1)
    terms = [shaped]
    for mask in range(1, parts):
        got = swap(shaped, "tensor", mask)
        terms.append(jnp.stack([got[at ^ mask] for at in range(parts)]))
    return paired_sum(terms).reshape(-1)


def tie(*values):
    return lax.optimization_barrier(values)


def dp_pieces(block):
    mine = jnp.stack([block] + [swap(block, "dp", 2 * chip) for chip in range(1, 4)])
    return mine.reshape(-1, block.shape[1])


def dp_gather(block):
    size = lax.axis_size("dp")
    if size != 8:
        return lax.all_gather(block, "dp", axis=0, tiled=True)
    me = lax.axis_index("dp")
    rows = block.shape[0]
    mine = dp_pieces(block)
    other = swap(mine, "dp", 1)
    whole = jnp.zeros((size * rows,) + block.shape[1:], block.dtype)
    for chip in range(size // 2):
        here = slice(chip * rows, (chip + 1) * rows)
        whole = lax.dynamic_update_slice_in_dim(whole, mine[here], (me ^ 2 * chip) * rows, 0)
        whole = lax.dynamic_update_slice_in_dim(whole, other[here], (me ^ 2 * chip ^ 1) * rows, 0)
    return whole


def weight_sum(me_ref, groups):
    if lax.axis_size("dp") != 8:
        return jnp.concatenate(
            [product_left(left, jnp.concatenate(rights, axis=1)) for left, rights in groups], axis=1
        ).astype(jnp.bfloat16)
    keep, give = weight_grad(me_ref, groups)
    give = swap(give, "dp", 1)
    return (keep.astype(jnp.float32) + give.astype(jnp.float32)).astype(jnp.bfloat16)


def chip_sum(both, small=None):
    size = lax.axis_size("dp")
    if size != 8:
        summed = lax.psum_scatter(both, "dp", scatter_dimension=0, tiled=True)
        return summed.astype(jnp.float32), None if small is None else lax.psum(small, "dp")
    chip = lax.axis_index("dp") // 2
    rows = both.shape[1]
    if small is not None:
        small = small.astype(jnp.bfloat16)
        near = swap(small, "dp", 1)
        small = (small.astype(jnp.float32) + near.astype(jnp.float32)).astype(jnp.bfloat16)
    terms = []
    for mask in range(size // 2):
        part = lax.dynamic_index_in_dim(both, chip ^ mask, 0, keepdims=False)
        if small is not None:
            part = jnp.concatenate([part, small])
        terms.append((swap(part, "dp", 2 * mask) if mask else part).astype(jnp.float32))
    summed = paired_sum(terms)
    return summed[:rows], None if small is None else summed[rows:]


def body(
    hidden_in,
    norm_in_gain,
    query_weight,
    key_weight,
    value_weight,
    output_weight,
    gate_weight,
    inner_weight,
    write_weight,
    read_weight,
    step_weight,
    conv_weight,
    conv_bias,
    pair_conv_weight,
    pair_conv_bias,
    step_bias,
    decay_log,
    skip_gain,
    state_gain,
    state_out_weight,
    norm_ffn_gain,
    feed_gate_weight,
    feed_up_weight,
    feed_down_weight,
    out_cotangent,
):
    low = jnp.bfloat16
    wide = jnp.float32
    parts = lax.axis_size("tensor")
    place = lax.axis_index("tensor")
    place_ref = place.astype(jnp.int32).reshape(1)
    heads_here = query_weight.shape[1] // HD
    key_head = place * heads_here // (QH // KVH)
    heads_state = step_weight.shape[1]
    width = gate_weight.shape[1]
    units = feed_gate_weight.shape[1]
    states = write_weight.shape[1]

    mixer_local = jnp.concatenate(
        [
            query_weight,
            lax.dynamic_slice_in_dim(key_weight, key_head * HD, HD, 1),
            lax.dynamic_slice_in_dim(value_weight, key_head * HD, HD, 1),
            write_weight,
            read_weight,
            gate_weight,
            inner_weight,
            jnp.pad(step_weight, ((0, 0), (0, 128 - heads_state))),
        ],
        axis=1,
    )
    out_local = jnp.concatenate([output_weight.T, state_out_weight.T], axis=1)
    feed_local = jnp.concatenate([feed_gate_weight, feed_up_weight, feed_down_weight.T], axis=1)
    rows_in = hidden_in.astype(wide)
    normed, first_scale = root_norm(rows_in, norm_in_gain)
    row_slots = tensor_gather(normed.astype(low))
    me_ref = lax.axis_index("dp").astype(jnp.int32).reshape(1)
    whole_dp = lax.axis_size("dp") != 8
    if whole_dp:
        mixer_full = lax.all_gather(mixer_local, "dp", axis=0, tiled=True)
        mixer_rows = jnp.concatenate(row_slots)
        raw = product(mixer_rows, mixer_full)
    else:
        near_full = dp_pieces(mixer_local)
        near_full, row_slots = tie(near_full, row_slots)
        far_full = swap(near_full, "dp", 1)
    row_slots, out_local, feed_local, cot_block = tie(
        row_slots, out_local, feed_local, out_cotangent
    )
    out_full = lax.all_gather(out_local, "dp", axis=0, tiled=True)
    feed_full = lax.all_gather(feed_local, "dp", axis=0, tiled=True)
    cot_slots = tensor_gather(cot_block)
    if not whole_dp:
        mixer_rows, raw = project(me_ref, row_slots, near_full, far_full)
    length = mixer_rows.shape[0]
    block = length // parts

    taps = jnp.concatenate(
        [
            jnp.concatenate([conv_weight, conv_bias[None]]),
            jnp.concatenate([pair_conv_weight, pair_conv_bias[None]]),
        ],
        axis=1,
    )
    taps = jnp.pad(taps, ((0, 3), (0, 0)))
    heads = jnp.pad(
        jnp.stack([step_bias, -jnp.exp(decay_log)]), ((0, 6), (0, 128 - heads_state))
    )
    skip = jnp.repeat(skip_gain, HD)[None]
    angles = jnp.asarray(angle_table(length))

    gated, power, conv, y, kept_states = state_forward(place_ref, raw, taps, heads, skip, states)
    mixed_low, kept, probs = attention_forward(place_ref, raw, angles)
    width_all = width * parts
    power = slot_sum(power[0])
    state_scale = lax.rsqrt(power / width_all + EPS)[:, None]
    state_low = (gated * state_scale * state_gain).astype(low)
    state_low, cot_slots = tie(state_low, cot_slots)
    own, *sends = spread_product(place_ref, (mixed_low, state_low), out_full, 0, parts)
    mixer_shard = finish_scatter(own, tensor_send(sends))
    middle = rows_in + mixer_shard
    second, second_scale = root_norm(middle, norm_ffn_gain)
    feed_slots = tensor_gather(second.astype(low))
    grad_pair, active, own, *sends = feed_forward(place_ref, feed_slots, cot_slots, feed_full)
    grad_second = finish_scatter(own, tensor_send(sends))
    grad_feed = feed_grad(place_ref, feed_slots, cot_slots, grad_pair, active)
    grad_second, grad_feed = tie(grad_second, grad_feed)
    feed_sums = lax.psum_scatter(grad_feed, "dp", scatter_dimension=0, tiled=True)

    weighted_second = grad_second * norm_ffn_gain
    inner_second = jnp.sum(weighted_second * middle, axis=-1, keepdims=True)
    grad_middle = (
        out_cotangent.astype(wide)
        + second_scale * weighted_second
        - middle * second_scale**3 * inner_second / middle.shape[-1]
    )
    ffn_gain = jnp.sum(grad_second * middle * second_scale, axis=0)
    cot_rows = tensor_gather(grad_middle.astype(low))
    mixer_cot, grad_mixed, grad_state, inner_sum = mixer_back(
        place_ref, cot_rows, out_full, gated, state_gain[None]
    )
    grad_mixed, active = tie(grad_mixed, active)
    weighted = grad_state * state_gain
    inner_sum = slot_sum(inner_sum[0])
    grad_attention = attention_backward(place_ref, grad_mixed, angles, kept, probs)
    early_terms = weight_sum(
        me_ref, [(mixer_cot, (mixed_low, state_low)), (mixer_rows, (grad_attention,))]
    )
    feed_own, *sends = spread_product(place_ref, (active,), feed_full, 2 * units, parts)
    feed_got = tensor_send(sends)
    early_terms, inner_sum = tie(early_terms, inner_sum)
    early_sums, _ = chip_sum(early_terms)
    grad_gated = (
        state_scale * weighted - gated * state_scale**3 * (inner_sum / width_all)[:, None]
    )
    grad_state_gain = jnp.sum(grad_state * gated * state_scale, axis=0)
    grad_mixer, grad_taps, grad_heads = state_backward(
        place_ref, raw, conv, y, kept_states, grad_gated, taps, heads, skip
    )
    grad_mixer, early_sums = tie(grad_mixer, early_sums)
    late_terms = weight_sum(me_ref, [(mixer_rows, (grad_mixer,))])
    if whole_dp:
        total_rows = product_right(grad_mixer, mixer_full[:, 256:]) + product_right(
            grad_attention, mixer_full[:, :256]
        )
        gain_rows = jnp.sum(total_rows * mixer_rows.astype(wide), axis=0, keepdims=True)
        own, *sends = [total_rows[at * block : (at + 1) * block] for at in range(parts)]
        sends = [item.astype(low) for item in sends]
    else:
        gain_rows, own, *sends = total_product(
            me_ref, grad_attention, grad_mixer, near_full, far_full, mixer_rows, parts
        )
    first_got = tensor_send(sends)
    in_gain = gain_rows[0] / norm_in_gain

    columns = late_terms.shape[-1]
    small = [
        in_gain,
        ffn_gain,
        grad_taps[:4, width:].reshape(-1),
        grad_taps[4, width:],
        grad_taps[:4, :width].reshape(-1),
        grad_taps[4, :width],
        grad_state_gain,
        grad_heads[0, :heads_state],
        grad_heads[1, :heads_state],
        grad_heads[2, :heads_state],
    ]
    sizes = [item.shape[0] for item in small]
    flat = jnp.concatenate(small)
    small_rows = -(-flat.shape[0] // (16 * columns)) * 16
    flat = jnp.pad(flat, (0, small_rows * columns - flat.shape[0])).reshape(small_rows, columns)
    late_sums, flat = chip_sum(late_terms, flat)
    feed_sums, feed_got = tie(feed_sums, feed_got)
    feed_sums = feed_sums.astype(wide)
    hidden_out = (middle + finish_scatter(feed_own, feed_got)).astype(low)
    done = (
        hidden_out,
        early_sums[:, 128 + width : 128 + width + 128],
        early_sums[:, :128].T,
        early_sums[:, 128 : 128 + width].T,
        feed_sums[:, :units],
        feed_sums[:, units : 2 * units],
        feed_sums[:, 2 * units :].T,
    )
    late_sums, done = tie(late_sums, done)
    flat = flat.reshape(-1)

    common = sum(sizes[:4])
    common_rows = -(-common // (16 * 384)) * 16
    rows_here = mixer_local.shape[0]
    shared = jnp.concatenate(
        [
            jnp.concatenate([early_sums[:, 128 + width + 128 :], late_sums[:, :256]], axis=1),
            jnp.pad(flat[:common], (0, common_rows * 384 - common)).reshape(common_rows, 384),
        ]
    ).astype(low)
    near = shared.astype(wide) + swap(shared, "tensor", 1).astype(wide)
    near = near.astype(low)
    far = swap(near, "tensor", 2).astype(wide)
    near = near.astype(wide)
    both = near + far
    first_half = place < parts // 2
    head_low = jnp.where(first_half, near[:rows_here, :128], far[:rows_here, :128])
    head_high = jnp.where(first_half, far[:rows_here, :128], near[:rows_here, :128])
    common_sums = both[rows_here:].reshape(-1)
    shared = jnp.concatenate([head_low, head_high, both[:rows_here, 128:]], axis=1).astype(low)
    shared, first_got = tie(shared, first_got)
    grad_first = finish_scatter(own, first_got)
    shared = dp_gather(shared).astype(wide)
    gradient_key = jnp.concatenate([shared[:, :64], shared[:, 128:192]], axis=1)
    gradient_value = jnp.concatenate([shared[:, 64:128], shared[:, 192:256]], axis=1)

    weighted_first = grad_first * norm_in_gain
    inner_first = jnp.sum(weighted_first * rows_in, axis=-1, keepdims=True)
    gradient_hidden = (
        grad_middle
        + first_scale * weighted_first
        - rows_in * first_scale**3 * inner_first / rows_in.shape[-1]
    )

    cuts = []
    at = 0
    for index, size in enumerate(sizes):
        cuts.append((common_sums if index < 4 else flat)[at : at + size])
        at += size
    return (
        done[0],
        gradient_hidden,
        cuts[0],
        done[1],
        gradient_key,
        gradient_value,
        done[2],
        late_sums[:, 256 : 256 + width],
        late_sums[:, 256 + width : 256 + 2 * width],
        shared[:, 256:384],
        shared[:, 384:512],
        late_sums[:, 256 + 2 * width : 256 + 2 * width + heads_state],
        cuts[4].reshape(conv_weight.shape),
        cuts[5],
        cuts[2].reshape(pair_conv_weight.shape),
        cuts[3],
        cuts[7],
        cuts[8],
        cuts[9],
        cuts[6],
        done[3],
        cuts[1],
        done[4],
        done[5],
        done[6],
    )


def solution(mesh):
    placed = (
        P(("dp", "tensor"), None),
        P(),
        P("dp", "tensor"),
        P("dp", None),
        P("dp", None),
        P("tensor", "dp"),
        P("dp", "tensor"),
        P("dp", "tensor"),
        P("dp", None),
        P("dp", None),
        P("dp", "tensor"),
        P(None, "tensor"),
        P("tensor"),
        P(),
        P(),
        P("tensor"),
        P("tensor"),
        P("tensor"),
        P("tensor"),
        P("tensor", "dp"),
        P(),
        P("dp", "tensor"),
        P("dp", "tensor"),
        P("tensor", "dp"),
        P(("dp", "tensor"), None),
    )
    return jax.shard_map(
        body,
        mesh=mesh,
        in_specs=placed,
        out_specs=(
            P(("dp", "tensor"), None),
            P(("dp", "tensor"), None),
            P(),
            P("dp", "tensor"),
            P(),
            P(),
            P("tensor", "dp"),
            P("dp", "tensor"),
            P("dp", "tensor"),
            P(),
            P(),
            P("dp", "tensor"),
            P(None, "tensor"),
            P("tensor"),
            P(),
            P(),
            P("tensor"),
            P("tensor"),
            P("tensor"),
            P("tensor"),
            P("tensor", "dp"),
            P(),
            P("dp", "tensor"),
            P("dp", "tensor"),
            P("tensor", "dp"),
        ),
        check_vma=False,
    )
```

```python
import functools
import math

import jax
import jax.numpy as jnp
import numpy as np
from jax import lax
from jax.experimental import pallas as pl
from jax.experimental.pallas import tpu as pltpu
from jax.sharding import PartitionSpec as P

QH = 8
KVH = 2
HD = 64
BLOCK = 128


EPS = 1e-05
THETA = 10000.0
HIGHEST = lax.Precision.HIGHEST


def product(left, right):
    return jnp.dot(left, right, preferred_element_type=jnp.float32)


def product_left(left, right):
    return lax.dot_general(
        left, right, (((0,), (0,)), ((), ())), preferred_element_type=jnp.float32
    )


def product_right(left, right):
    return lax.dot_general(
        left, right, (((1,), (1,)), ((), ())), preferred_element_type=jnp.float32
    )


def root_norm(rows, gain):
    scale = lax.rsqrt(jnp.mean(rows * rows, axis=-1, keepdims=True) + EPS)
    return (rows * scale * gain, scale)


def dot(left, right, dims=((1,), (0,)), precision=None):
    return lax.dot_general(
        left, right, (dims, ((), ())), precision=precision, preferred_element_type=jnp.float32
    )


NN = ((1,), (0,))
NT = ((1,), (1,))
TN = ((0,), (0,))


def sigmoid(values):
    return 1.0 / (1.0 + jnp.exp(-values))


def softplus(values):
    return jnp.maximum(values, 0.0) + jnp.log1p(jnp.exp(-jnp.abs(values)))


def lane_index(rows):
    return lax.broadcasted_iota(jnp.int32, (rows, 128), 1)


def spread_heads(values, width):
    first = lane_index(values.shape[0]) < HD
    return jnp.concatenate(
        [
            jnp.where(first, values[:, at : at + 1], values[:, at + 1 : at + 2])
            for at in range(0, width // HD, 2)
        ],
        axis=1,
    )


def slot_rows(place_ref, at):
    return pl.ds(pl.multiple_of((place_ref[0] ^ at) * BLOCK, BLOCK), BLOCK)


def lower_mask():
    rows = lax.broadcasted_iota(jnp.int32, (BLOCK, BLOCK), 0)
    columns = lax.broadcasted_iota(jnp.int32, (BLOCK, BLOCK), 1)
    return rows >= columns


def block_decay(raw_steps, step_bias, rate, lower):
    step = softplus(raw_steps + step_bias)
    running = dot(lower.astype(jnp.float32), step * rate, NN, HIGHEST)
    return step, running, running.T


def block_weights(running, running_t, lower, head):
    spread = running[:, head : head + 1] - running_t[head : head + 1, :]
    return jnp.exp(jnp.where(lower, spread, -1e30))


def fill_history(place_ref, raw_ref, history_ref, blocks, width):
    history_ref[0:8, :] = jnp.zeros((8, history_ref.shape[1]), jnp.float32)
    for at in range(blocks):
        rows = slot_rows(place_ref, at)
        here = slice(8 + at * BLOCK, 8 + (at + 1) * BLOCK)
        history_ref[here, 0:width] = raw_ref[rows, 512 + width : 512 + 2 * width]
        history_ref[here, width : width + 256] = raw_ref[rows, 256:512]


def state_forward_kernel(
    place_ref,
    raw_ref,
    taps_ref,
    heads_ref,
    skip_ref,
    gated_ref,
    power_ref,
    conv_ref,
    y_ref,
    states_ref,
    history_ref,
):
    low = jnp.bfloat16
    width = gated_ref.shape[1]
    blocks = gated_ref.shape[0] // BLOCK
    fill_history(place_ref, raw_ref, history_ref, blocks, width)
    lower = lower_mask()
    first = lane_index(BLOCK) < HD
    state = jnp.zeros((states_ref.shape[1], width), jnp.float32)
    for at in range(blocks):
        rows = slot_rows(place_ref, at)
        conv = taps_ref[4:5, :]
        for tap in range(4):
            conv = conv + taps_ref[tap : tap + 1, :] * history_ref[pl.ds(5 + tap + at * BLOCK, BLOCK), :]
        conv_ref[rows, :] = conv
        acted = conv * sigmoid(conv)
        inner = acted[:, :width]
        write = acted[:, width : width + 128].astype(low)
        read = acted[:, width + 128 :].astype(low)
        step, running, running_t = block_decay(
            raw_ref[rows, 512 + 2 * width :], heads_ref[0:1, :], heads_ref[1:2, :], lower
        )
        scaled = inner * spread_heads(step, width)
        scaled_low = scaled.astype(low)
        zero = jnp.zeros((BLOCK, 128), low)
        meet = dot(read, write, NT)
        inside = []
        for pair in range(width // 128):
            both = jnp.concatenate(
                [
                    (meet * block_weights(running, running_t, lower, 2 * pair)).astype(low),
                    (meet * block_weights(running, running_t, lower, 2 * pair + 1)).astype(low),
                ],
                axis=1,
            )
            piece = scaled_low[:, pair * 128 : (pair + 1) * 128]
            split = jnp.concatenate([jnp.where(first, piece, zero), jnp.where(first, zero, piece)])
            inside.append(dot(both, split))
        earlier = dot(read, state.astype(low))
        y = jnp.concatenate(inside, axis=1) + spread_heads(jnp.exp(running), width) * earlier
        y_ref[rows, :] = y
        states_ref[at] = state
        last = running[BLOCK - 1 : BLOCK, :]
        carried = (spread_heads(jnp.exp(last - running), width) * scaled).astype(low)
        state = spread_heads(jnp.exp(last), width) * state + dot(write, carried, TN)
        gate = raw_ref[rows, 512 : 512 + width]
        gated = (y + skip_ref[0:1, :] * inner) * gate * sigmoid(gate)
        gated_ref[rows, :] = gated
        power_ref[:, rows] = dot(jnp.ones((8, width), jnp.float32), gated * gated, NT, HIGHEST)


def state_backward_kernel(
    place_ref,
    raw_ref,
    conv_ref,
    y_ref,
    states_ref,
    up_ref,
    taps_ref,
    heads_ref,
    skip_ref,
    grad_ref,
    grad_taps_ref,
    grad_heads_ref,
    history_ref,
    later_ref,
):
    low = jnp.bfloat16
    width = up_ref.shape[1]
    blocks = up_ref.shape[0] // BLOCK
    length = up_ref.shape[0]
    every = width + 256
    fill_history(place_ref, raw_ref, history_ref, blocks, width)
    later_ref[length : length + 8, :] = jnp.zeros((8, every), jnp.float32)
    lower = lower_mask()
    first = lane_index(BLOCK) < HD
    zero = jnp.zeros((BLOCK, 128), low)
    picks = (
        lax.broadcasted_iota(jnp.int32, (width, 128), 0) // HD
        == lax.broadcasted_iota(jnp.int32, (width, 128), 1)
    ).astype(jnp.float32)
    skip = skip_ref[0:1, :]
    rate = heads_ref[1:2, :]
    grad_state = jnp.zeros((states_ref.shape[1], width), jnp.float32)
    grad_taps = [jnp.zeros((1, every), jnp.float32) for _ in range(5)]
    grad_bias = jnp.zeros((1, 128), jnp.float32)
    grad_decay = jnp.zeros((1, 128), jnp.float32)
    grad_skip = jnp.zeros((1, width), jnp.float32)
    for at in reversed(range(blocks)):
        rows = slot_rows(place_ref, at)
        gate = raw_ref[rows, 512 : 512 + width]
        gate_sigma = sigmoid(gate)
        conv = conv_ref[rows, :]
        conv_sigma = sigmoid(conv)
        acted = conv * conv_sigma
        inner = acted[:, :width]
        write = acted[:, width : width + 128].astype(low)
        read = acted[:, width + 128 :].astype(low)
        y = y_ref[rows, :]
        up = up_ref[rows, :]
        grad_gate = up * (y + skip * inner) * gate_sigma * (1.0 + gate * (1.0 - gate_sigma))
        grad_ref[rows, 256 : 256 + width] = grad_gate.astype(low)
        grad_y = up * gate * gate_sigma
        raw_steps = raw_ref[rows, 512 + 2 * width :]
        step, running, running_t = block_decay(raw_steps, heads_ref[0:1, :], rate, lower)
        step_wide = spread_heads(step, width)
        grow = spread_heads(jnp.exp(running), width)
        last = running[BLOCK - 1 : BLOCK, :]
        carry = spread_heads(jnp.exp(last - running), width)
        last_wide = spread_heads(jnp.exp(last), width)
        scaled = inner * step_wide
        scaled_low = scaled.astype(low)
        grad_low = grad_y.astype(low)
        grown_low = (grad_y * grow).astype(low)
        state = states_ref[at]
        state_low = state.astype(low)
        grad_state_low = grad_state.astype(low)
        meet = dot(read, write, NT)
        grad_meet = jnp.zeros((BLOCK, BLOCK), jnp.float32)
        inside = []
        for pair in range(width // 128):
            weights = [
                block_weights(running, running_t, lower, head) for head in (2 * pair, 2 * pair + 1)
            ]
            both = jnp.concatenate([(meet * item).astype(low) for item in weights], axis=0)
            piece = grad_low[:, pair * 128 : (pair + 1) * 128]
            split = jnp.concatenate([jnp.where(first, piece, zero), jnp.where(first, zero, piece)])
            grad_both = dot(split, scaled_low[:, pair * 128 : (pair + 1) * 128], NT)
            grad_meet = (
                grad_meet + grad_both[:BLOCK] * weights[0] + grad_both[BLOCK:] * weights[1]
            )
            inside.append(dot(both, split, TN))
        grad_inside = jnp.concatenate(inside, axis=1)
        from_state = carry * dot(write, grad_state_low)
        carried = carry * scaled
        grad_scaled = grad_inside + from_state
        moved = scaled * from_state
        turn = grad_low.astype(jnp.float32) * y - scaled_low.astype(jnp.float32) * grad_inside - moved
        direct = grad_y * inner
        ends = jnp.sum(moved, axis=0, keepdims=True) + last_wide * jnp.sum(
            state * grad_state, axis=0, keepdims=True
        )
        summed = dot(
            jnp.concatenate([turn, grad_scaled * inner, jnp.broadcast_to(ends, (8, width))]),
            picks,
            NN,
            HIGHEST,
        )
        grad_running = (
            dot(lower.astype(jnp.float32), summed[:BLOCK], TN, HIGHEST)
            + summed[2 * BLOCK : 2 * BLOCK + 1]
        )
        grad_step = grad_running * rate + summed[BLOCK : 2 * BLOCK]
        grad_decay = grad_decay + jnp.sum(grad_running * step * rate, axis=0, keepdims=True)
        grad_steps = grad_step * sigmoid(raw_steps + heads_ref[0:1, :])
        grad_bias = grad_bias + jnp.sum(grad_steps, axis=0, keepdims=True)
        grad_skip = grad_skip + jnp.sum(direct, axis=0, keepdims=True)
        grad_ref[rows, 256 + 2 * width :] = grad_steps.astype(low)
        grad_inner = grad_scaled * step_wide + skip * grad_y
        grad_meet_low = grad_meet.astype(low)
        grad_read = dot(grad_meet_low, write) + dot(grown_low, state_low, NT)
        grad_write = dot(grad_meet_low, read, TN) + dot(carried.astype(low), grad_state_low, NT)
        grad_state = last_wide * grad_state + dot(read, grown_low, TN)
        grad_conv = jnp.concatenate([grad_inner, grad_write, grad_read], axis=1) * (
            conv_sigma * (1.0 + conv * (1.0 - conv_sigma))
        )
        later_ref[at * BLOCK : (at + 1) * BLOCK, :] = grad_conv
        back = jnp.zeros((BLOCK, every), jnp.float32)
        for tap in range(4):
            back = back + taps_ref[tap : tap + 1, :] * later_ref[pl.ds(at * BLOCK + 3 - tap, BLOCK), :]
            seen = history_ref[pl.ds(5 + tap + at * BLOCK, BLOCK), :]
            grad_taps[tap] = grad_taps[tap] + jnp.sum(grad_conv * seen, axis=0, keepdims=True)
        grad_taps[4] = grad_taps[4] + jnp.sum(grad_conv, axis=0, keepdims=True)
        grad_ref[rows, 256 + width : 256 + 2 * width] = back[:, :width].astype(low)
        grad_ref[rows, 0:256] = back[:, width:].astype(low)
    for tap in range(5):
        grad_taps_ref[tap : tap + 1, :] = grad_taps[tap]
    grad_taps_ref[5:8, :] = jnp.zeros((3, every), jnp.float32)
    skip_heads = dot(jnp.broadcast_to(grad_skip, (8, width)), picks, NN, HIGHEST)
    grad_heads_ref[...] = jnp.zeros(grad_heads_ref.shape, jnp.float32)
    grad_heads_ref[0:1, :] = grad_bias
    grad_heads_ref[1:2, :] = grad_decay
    grad_heads_ref[2:3, :] = skip_heads[0:1]


def turned(values, cosine, sine):
    early = lane_index(values.shape[0]) % HD < HD // 2
    other = jnp.where(early, pltpu.roll(values, 128 - HD // 2, 1), pltpu.roll(values, HD // 2, 1))
    return values * cosine + other * sine


def both_heads(values, first):
    zero = jnp.zeros(values.shape, values.dtype)
    return jnp.concatenate([jnp.where(first, values, zero), jnp.where(first, zero, values)])


def attention_forward_kernel(
    place_ref, raw_ref, angle_ref, mixed_ref, kept_ref, probs_ref
):
    low = jnp.bfloat16
    blocks = mixed_ref.shape[0] // BLOCK
    first = lane_index(BLOCK) < HD
    for at in range(blocks):
        rows = slot_rows(place_ref, at)
        here = slice(at * BLOCK, (at + 1) * BLOCK)
        cosine = angle_ref[here, 0:128]
        sine = angle_ref[here, 128:256]
        pair = raw_ref[rows, 128:256]
        key = turned(pair, cosine, sine)
        kept_ref[here, 0:128] = turned(raw_ref[rows, 0:128], cosine, sine).astype(low)
        kept_ref[here, 128:256] = jnp.where(first, key, pltpu.roll(key, HD, 1)).astype(low)
        kept_ref[here, 256:384] = jnp.where(first, pltpu.roll(pair, HD, 1), pair).astype(low)
    for at in range(blocks):
        rows = slot_rows(place_ref, at)
        here = slice(at * BLOCK, (at + 1) * BLOCK)
        reach = (at + 1) * BLOCK
        query = both_heads(kept_ref[here, 0:128], first)
        scores = dot(query, kept_ref[0:reach, 128:256], NT) * (HD ** (-0.5))
        row = lax.broadcasted_iota(jnp.int32, (2 * BLOCK, reach), 0) % BLOCK + at * BLOCK
        column = lax.broadcasted_iota(jnp.int32, (2 * BLOCK, reach), 1)
        scores = jnp.where(row >= column, scores, -1e30)
        exponent = jnp.exp(scores - jnp.max(scores, axis=1, keepdims=True))
        probs = (exponent / jnp.sum(exponent, axis=1, keepdims=True)).astype(low)
        probs_ref[at, :, 0:reach] = probs
        out = dot(probs, kept_ref[0:reach, 256:384])
        mixed_ref[rows, :] = jnp.where(first, out[:BLOCK], out[BLOCK:]).astype(low)


def attention_backward_kernel(
    place_ref, up_ref, angle_ref, kept_ref, probs_ref, grad_ref, key_ref, value_ref
):
    low = jnp.bfloat16
    blocks = up_ref.shape[0] // BLOCK
    first = lane_index(BLOCK) < HD
    scale = HD ** (-0.5)
    key_ref[...] = jnp.zeros(key_ref.shape, jnp.float32)
    value_ref[...] = jnp.zeros(value_ref.shape, jnp.float32)
    for at in range(blocks):
        rows = slot_rows(place_ref, at)
        here = slice(at * BLOCK, (at + 1) * BLOCK)
        reach = (at + 1) * BLOCK
        query = both_heads(kept_ref[here, 0:128], first)
        up = both_heads(up_ref[rows, :], first)
        probs_low = probs_ref[at, :, 0:reach]
        probs = probs_low.astype(jnp.float32)
        grad_probs = dot(up, kept_ref[0:reach, 256:384], NT)
        inner = jnp.sum(probs * grad_probs, axis=1, keepdims=True)
        grad_scores = (probs * (grad_probs - inner)).astype(low)
        both = dot(grad_scores, kept_ref[0:reach, 128:256]) * scale
        grad_query = jnp.where(first, both[:BLOCK], both[BLOCK:])
        grad_ref[rows, 0:128] = turned(
            grad_query, angle_ref[here, 0:128], -angle_ref[here, 128:256]
        ).astype(low)
        key_ref[0:reach, :] += dot(grad_scores, query, TN)
        value_ref[0:reach, :] += dot(probs_low, up, TN)
    for at in range(blocks):
        rows = slot_rows(place_ref, at)
        here = slice(at * BLOCK, (at + 1) * BLOCK)
        key = key_ref[here, :]
        value = value_ref[here, :]
        key = (key + pltpu.roll(key, HD, 1)) * scale
        key = turned(key, angle_ref[here, 0:128], -angle_ref[here, 128:256])
        value = value + pltpu.roll(value, HD, 1)
        grad_ref[rows, 128:256] = jnp.where(first, key, value).astype(low)


def angle_table(length):
    half = HD // 2
    freq = THETA ** (-np.arange(half, dtype=np.float32) / half)
    angle = np.arange(length, dtype=np.float32)[:, None] * freq[None, :]
    cosine = np.tile(np.cos(angle), (1, 4))
    sine = np.tile(np.concatenate([-np.sin(angle), np.sin(angle)], axis=1), (1, 2))
    return np.concatenate([cosine, sine], axis=1).astype(np.float32)


def run_kernel(kernel, place, operands, outs, scratch, name, flops=2e8, margin=8):
    whole = pl.BlockSpec(memory_space=pltpu.VMEM)
    held = sum(item.size * item.dtype.itemsize for item in operands)
    held += sum(math.prod(shape) * jnp.dtype(dtype).itemsize for shape, dtype in outs)
    held += sum(math.prod(item.shape) * jnp.dtype(item.dtype).itemsize for item in scratch)
    return pl.pallas_call(
        kernel,
        out_shape=[jax.ShapeDtypeStruct(shape, dtype) for shape, dtype in outs],
        in_specs=[pl.BlockSpec(memory_space=pltpu.SMEM)] + [whole] * len(operands),
        out_specs=[whole] * len(outs),
        scratch_shapes=scratch,
        compiler_params=pltpu.CompilerParams(vmem_limit_bytes=held + margin * 2**20),
        cost_estimate=pl.CostEstimate(flops=int(flops), bytes_accessed=1 << 20, transcendentals=0),
        name=name,
    )(place, *operands)


def state_forward(place, raw, taps, heads, skip, states):
    length = raw.shape[0]
    width = skip.shape[1]
    wide = jnp.float32
    return run_kernel(
        state_forward_kernel,
        place,
        (raw, taps, heads, skip),
        [
            ((length, width), wide),
            ((8, length), wide),
            ((length, width + 256), wide),
            ((length, width), wide),
            ((length // BLOCK, states, width), wide),
        ],
        [pltpu.VMEM((length + 8, width + 256), wide)],
        "state_forward",
    )


def state_backward(place, raw, conv, y, states, up, taps, heads, skip):
    length = raw.shape[0]
    width = skip.shape[1]
    wide = jnp.float32
    return run_kernel(
        state_backward_kernel,
        place,
        (raw, conv, y, states, up, taps, heads, skip),
        [
            ((length, 256 + 2 * width + 128), jnp.bfloat16),
            ((8, width + 256), wide),
            ((8, 128), wide),
        ],
        [pltpu.VMEM((length + 8, width + 256), wide), pltpu.VMEM((length + 8, width + 256), wide)],
        "state_backward",
    )


def attention_forward(place, raw, angles):
    length = raw.shape[0]
    low = jnp.bfloat16
    return run_kernel(
        attention_forward_kernel,
        place,
        (raw, angles),
        [
            ((length, 128), low),
            ((length, 384), low),
            ((length // BLOCK, 2 * BLOCK, length), low),
        ],
        [],
        "attention_forward",
    )


def attention_backward(place, up, angles, kept, probs):
    length = up.shape[0]
    return run_kernel(
        attention_backward_kernel,
        place,
        (up, angles, kept, probs),
        [((length, 256), jnp.bfloat16)],
        [pltpu.VMEM((length, 128), jnp.float32), pltpu.VMEM((length, 128), jnp.float32)],
        "attention_backward",
    )[0]


def block_columns(me_ref, mask):
    return pl.ds(pl.multiple_of((me_ref[0] ^ mask) * 128, 128), 128)


def join_rows(slots, whole_ref):
    rows = slots[0].shape[0]
    for at, slot in enumerate(slots):
        whole_ref[at * rows : (at + 1) * rows, :] = slot[...]


def project_kernel(me_ref, *refs):
    slots, (near_ref, far_ref, rows_ref, raw_ref) = refs[:-4], refs[-4:]
    join_rows(slots, rows_ref)
    chips = near_ref.shape[0] // 128
    near = jnp.concatenate([rows_ref[:, block_columns(me_ref, 2 * at)] for at in range(chips)], axis=1)
    far = jnp.concatenate(
        [rows_ref[:, block_columns(me_ref, 2 * at + 1)] for at in range(chips)], axis=1
    )
    raw_ref[...] = dot(near, near_ref[...]) + dot(far, far_ref[...])


def write_spread(total, own_ref, sends):
    rows = own_ref.shape[0]
    own_ref[...] = total[:rows]
    for at, send in enumerate(sends):
        send[...] = total[(at + 1) * rows : (at + 2) * rows].astype(jnp.bfloat16)


def spread_kernel(start, count, place_ref, *refs):
    lefts, weight_ref, own_ref, sends = refs[:count], refs[count], refs[count + 1], refs[count + 2 :]
    left = jnp.concatenate([item[...] for item in lefts], axis=1)
    total = dot(left, weight_ref[:, start : start + left.shape[1]], NT)
    write_spread(total, own_ref, sends)


def ordered_kernel(start, place_ref, left_ref, weight_ref, out_ref):
    total = dot(left_ref[...], weight_ref[:, start : start + left_ref.shape[1]], NT)
    for at in range(total.shape[0] // BLOCK):
        out_ref[slot_rows(place_ref, at), :] = total[at * BLOCK : (at + 1) * BLOCK].astype(
            out_ref.dtype
        )


def total_kernel(
    me_ref, attention_ref, mixer_ref, near_ref, far_ref, rows_ref, gain_ref, own_ref, *rest
):
    sends, total_ref = rest[:-1], rest[-1]
    left = jnp.concatenate([attention_ref[...], mixer_ref[...]], axis=1)
    chips = near_ref.shape[0] // 128
    for side, weight_ref in enumerate((near_ref, far_ref)):
        piece = dot(left, weight_ref[...], NT)
        for at in range(chips):
            total_ref[:, block_columns(me_ref, 2 * at + side)] = piece[:, at * 128 : (at + 1) * 128]
    total = total_ref[...]
    gain_ref[...] = jnp.broadcast_to(
        jnp.sum(total * rows_ref[...].astype(jnp.float32), axis=0, keepdims=True), gain_ref.shape
    )
    write_spread(total, own_ref, sends)


def feed_kernel(place_ref, *refs):
    low = jnp.bfloat16
    slots, cots_ref = refs[:4], refs[4]
    feed_ref, pair_ref, active_ref, own_ref = refs[5:9]
    sends = refs[9:12]
    units = active_ref.shape[1]
    rows = slots[0].shape[0]
    for half in range(2):
        here = slice(2 * half * rows, 2 * (half + 1) * rows)
        left = jnp.concatenate([slots[2 * half][...], slots[2 * half + 1][...]])
        cot = jnp.concatenate([cots_ref[slot_rows(place_ref, 2 * half + at), :] for at in range(2)])
        gate_up = dot(left, feed_ref[:, : 2 * units])
        grad_active = dot(cot, feed_ref[:, 2 * units :])
        gate = gate_up[:, :units]
        up = gate_up[:, units:]
        sigma = sigmoid(gate)
        swish = gate * sigma
        active_ref[here, :] = (swish * up).astype(low)
        grad_gate = grad_active * up * sigma * (1.0 + gate * (1.0 - sigma))
        pair = jnp.concatenate([grad_gate, grad_active * swish], axis=1).astype(low)
        pair_ref[here, :] = pair
        total = dot(pair, feed_ref[:, : 2 * units], NT)
        if half == 0:
            own_ref[...] = total[:rows]
            sends[0][...] = total[rows:].astype(low)
        else:
            sends[1][...] = total[:rows].astype(low)
            sends[2][...] = total[rows:].astype(low)


def feed_grad_kernel(place_ref, *refs):
    slots, cots_ref = refs[:4], refs[4]
    pair_ref, active_ref, out_ref, rows_ref, cot_ref = refs[5:]
    join_rows(slots, rows_ref)
    for at in range(len(slots)):
        cot_ref[at * BLOCK : (at + 1) * BLOCK, :] = cots_ref[slot_rows(place_ref, at), :]
    both = pair_ref.shape[1]
    for at in range(0, rows_ref.shape[1], 256):
        here = slice(at, at + 256)
        out_ref[here, :both] = dot(rows_ref[:, here], pair_ref[...], TN).astype(out_ref.dtype)
        out_ref[here, both:] = dot(cot_ref[:, here], active_ref[...], TN).astype(out_ref.dtype)


def weight_grad_kernel(groups, me_ref, *refs):
    keep_ref, give_ref = refs[-2:]
    even = me_ref[0] % 2 == 0
    for chip in range(keep_ref.shape[0]):
        here = slice(chip * 256, (chip + 1) * 256)
        pieces = []
        at = 0
        for count in groups:
            left = refs[at][:, here]
            right = jnp.concatenate([item[...] for item in refs[at + 1 : at + 1 + count]], axis=1)
            pieces.append(dot(left, right, TN))
            at += 1 + count
        piece = jnp.concatenate(pieces, axis=1).astype(keep_ref.dtype)
        keep_ref[chip] = jnp.where(even, piece[:128], piece[128:])
        give_ref[chip] = jnp.where(even, piece[128:], piece[:128])


def mixer_back_kernel(place_ref, *refs):
    slots = refs[:4]
    weight_ref, gated_ref, gain_ref, cot_ref, mixed_ref, state_ref, inner_ref = refs[4:]
    join_rows(slots, cot_ref)
    both = dot(cot_ref[...], weight_ref[...])
    mixed_ref[...] = both[:, :128].astype(jnp.bfloat16)
    state = both[:, 128:]
    state_ref[...] = state
    product_rows = state * gain_ref[0:1, :] * gated_ref[...]
    inner_ref[...] = dot(
        jnp.ones((8, product_rows.shape[1]), jnp.float32), product_rows, NT, HIGHEST
    )


def project(me, slots, near, far):
    length = len(slots) * slots[0].shape[0]
    return run_kernel(
        project_kernel,
        me,
        (*slots, near, far),
        [((length, slots[0].shape[1]), jnp.bfloat16), ((length, near.shape[1]), jnp.float32)],
        [],
        "project",
    )


def spread_outs(rows, columns, parts):
    return [((rows, columns), jnp.float32)] + [((rows, columns), jnp.bfloat16)] * (parts - 1)


def spread_product(place, lefts, weight, start, parts):
    rows = lefts[0].shape[0] // parts
    return run_kernel(
        functools.partial(spread_kernel, start, len(lefts)),
        place,
        (*lefts, weight),
        spread_outs(rows, weight.shape[0], parts),
        [],
        "spread_product",
    )


def ordered_product(place, left, weight, start):
    return run_kernel(
        functools.partial(ordered_kernel, start),
        place,
        (left, weight),
        [((left.shape[0], weight.shape[0]), jnp.bfloat16)],
        [],
        "ordered_product",
    )[0]


def total_product(me, attention, mixer, near, far, rows, parts):
    length, columns = rows.shape
    return run_kernel(
        total_kernel,
        me,
        (attention, mixer, near, far, rows),
        [((8, columns), jnp.float32)] + spread_outs(length // parts, columns, parts),
        [pltpu.VMEM((length, columns), jnp.float32)],
        "total_product",
    )


def feed_forward(place, slots, cotangent, feed):
    rows, columns = slots[0].shape
    units = feed.shape[1] // 3
    parts = len(slots)
    return run_kernel(
        feed_kernel,
        place,
        (*slots, cotangent, feed),
        [((parts * rows, 2 * units), jnp.bfloat16), ((parts * rows, units), jnp.bfloat16)]
        + spread_outs(rows, columns, parts),
        [],
        "feed_forward",
    )


def feed_grad(place, slots, cotangent, pair, active):
    length, columns = pair.shape[0], slots[0].shape[1]
    scratch = pltpu.VMEM((length, columns), jnp.bfloat16)
    return run_kernel(
        feed_grad_kernel,
        place,
        (*slots, cotangent, pair, active),
        [((columns, pair.shape[1] + active.shape[1]), jnp.bfloat16)],
        [scratch, scratch],
        "feed_grad",
    )[0]


def weight_grad(me, groups):
    counts = tuple(len(rights) for _, rights in groups)
    columns = sum(item.shape[1] for _, rights in groups for item in rights)
    operands = [item for left, rights in groups for item in (left, *rights)]
    blocks = groups[0][0].shape[1] // 256
    return run_kernel(
        functools.partial(weight_grad_kernel, counts),
        me,
        operands,
        [((blocks, 128, columns), jnp.bfloat16)] * 2,
        [],
        "weight_grad",
    )


def mixer_back(place, slots, weight, gated, gain):
    rows, columns = slots[0].shape
    length = len(slots) * rows
    width = gated.shape[1]
    return run_kernel(
        mixer_back_kernel,
        place,
        (*slots, weight, gated, gain),
        [
            ((length, columns), jnp.bfloat16),
            ((length, 128), jnp.bfloat16),
            ((length, width), jnp.float32),
            ((8, length), jnp.float32),
        ],
        [],
        "mixer_back",
    )


def swap(values, axis, mask):
    size = lax.axis_size(axis)
    return lax.ppermute(values, axis, [(index, index ^ mask) for index in range(size)])


def tensor_gather(block):
    return [block] + [swap(block, "tensor", mask) for mask in range(1, lax.axis_size("tensor"))]


def paired_sum(terms):
    while len(terms) > 1:
        terms = [terms[at] + terms[at + 1] for at in range(0, len(terms), 2)]
    return terms[0]


def tensor_send(sends):
    return [swap(item, "tensor", at + 1) for at, item in enumerate(sends)]


def finish_scatter(own, got):
    return paired_sum([own] + [item.astype(jnp.float32) for item in got])


def slot_sum(values):
    parts = lax.axis_size("tensor")
    shaped = values.reshape(parts, -1)
    terms = [shaped]
    for mask in range(1, parts):
        got = swap(shaped, "tensor", mask)
        terms.append(jnp.stack([got[at ^ mask] for at in range(parts)]))
    return paired_sum(terms).reshape(-1)


def tie(*values):
    return lax.optimization_barrier(values)


def dp_pieces(block):
    mine = jnp.stack([block] + [swap(block, "dp", 2 * chip) for chip in range(1, 4)])
    return mine.reshape(-1, block.shape[1])


def dp_gather(block):
    size = lax.axis_size("dp")
    if size != 8:
        return lax.all_gather(block, "dp", axis=0, tiled=True)
    me = lax.axis_index("dp")
    rows = block.shape[0]
    mine = dp_pieces(block)
    other = swap(mine, "dp", 1)
    whole = jnp.zeros((size * rows,) + block.shape[1:], block.dtype)
    for chip in range(size // 2):
        here = slice(chip * rows, (chip + 1) * rows)
        whole = lax.dynamic_update_slice_in_dim(whole, mine[here], (me ^ 2 * chip) * rows, 0)
        whole = lax.dynamic_update_slice_in_dim(whole, other[here], (me ^ 2 * chip ^ 1) * rows, 0)
    return whole


def weight_sum(me_ref, groups):
    if lax.axis_size("dp") != 8:
        return jnp.concatenate(
            [product_left(left, jnp.concatenate(rights, axis=1)) for left, rights in groups], axis=1
        ).astype(jnp.bfloat16)
    keep, give = weight_grad(me_ref, groups)
    give = swap(give, "dp", 1)
    return (keep.astype(jnp.float32) + give.astype(jnp.float32)).astype(jnp.bfloat16)


def chip_sum(both, small=None):
    size = lax.axis_size("dp")
    if size != 8:
        summed = lax.psum_scatter(both, "dp", scatter_dimension=0, tiled=True)
        return summed.astype(jnp.float32), None if small is None else lax.psum(small, "dp")
    chip = lax.axis_index("dp") // 2
    rows = both.shape[1]
    if small is not None:
        small = small.astype(jnp.bfloat16)
        near = swap(small, "dp", 1)
        small = (small.astype(jnp.float32) + near.astype(jnp.float32)).astype(jnp.bfloat16)
    terms = []
    for mask in range(size // 2):
        part = lax.dynamic_index_in_dim(both, chip ^ mask, 0, keepdims=False)
        if small is not None:
            part = jnp.concatenate([part, small])
        terms.append((swap(part, "dp", 2 * mask) if mask else part).astype(jnp.float32))
    summed = paired_sum(terms)
    return summed[:rows], None if small is None else summed[rows:]


def body(
    hidden_in,
    norm_in_gain,
    query_weight,
    key_weight,
    value_weight,
    output_weight,
    gate_weight,
    inner_weight,
    write_weight,
    read_weight,
    step_weight,
    conv_weight,
    conv_bias,
    pair_conv_weight,
    pair_conv_bias,
    step_bias,
    decay_log,
    skip_gain,
    state_gain,
    state_out_weight,
    norm_ffn_gain,
    feed_gate_weight,
    feed_up_weight,
    feed_down_weight,
    out_cotangent,
):
    low = jnp.bfloat16
    wide = jnp.float32
    parts = lax.axis_size("tensor")
    place = lax.axis_index("tensor")
    place_ref = place.astype(jnp.int32).reshape(1)
    heads_here = query_weight.shape[1] // HD
    key_head = place * heads_here // (QH // KVH)
    heads_state = step_weight.shape[1]
    width = gate_weight.shape[1]
    units = feed_gate_weight.shape[1]
    states = write_weight.shape[1]

    mixer_local = jnp.concatenate(
        [
            query_weight,
            lax.dynamic_slice_in_dim(key_weight, key_head * HD, HD, 1),
            lax.dynamic_slice_in_dim(value_weight, key_head * HD, HD, 1),
            write_weight,
            read_weight,
            gate_weight,
            inner_weight,
            jnp.pad(step_weight, ((0, 0), (0, 128 - heads_state))),
        ],
        axis=1,
    )
    out_local = jnp.concatenate([output_weight.T, state_out_weight.T], axis=1)
    feed_local = jnp.concatenate([feed_gate_weight, feed_up_weight, feed_down_weight.T], axis=1)
    rows_in = hidden_in.astype(wide)
    normed, first_scale = root_norm(rows_in, norm_in_gain)
    row_slots = tensor_gather(normed.astype(low))
    me_ref = lax.axis_index("dp").astype(jnp.int32).reshape(1)
    whole_dp = lax.axis_size("dp") != 8
    if whole_dp:
        mixer_full = lax.all_gather(mixer_local, "dp", axis=0, tiled=True)
        mixer_rows = jnp.concatenate(row_slots)
        raw = product(mixer_rows, mixer_full)
    else:
        near_full = dp_pieces(mixer_local)
        near_full, row_slots = tie(near_full, row_slots)
        far_full = swap(near_full, "dp", 1)
    row_slots, out_local, feed_local, cot_block = tie(
        row_slots, out_local, feed_local, out_cotangent
    )
    out_full = lax.all_gather(out_local, "dp", axis=0, tiled=True)
    feed_full = lax.all_gather(feed_local, "dp", axis=0, tiled=True)
    cotangent = lax.all_gather(cot_block, "tensor", axis=0, tiled=True)
    if not whole_dp:
        mixer_rows, raw = project(me_ref, row_slots, near_full, far_full)
    length = mixer_rows.shape[0]
    block = length // parts

    taps = jnp.concatenate(
        [
            jnp.concatenate([conv_weight, conv_bias[None]]),
            jnp.concatenate([pair_conv_weight, pair_conv_bias[None]]),
        ],
        axis=1,
    )
    taps = jnp.pad(taps, ((0, 3), (0, 0)))
    heads = jnp.pad(
        jnp.stack([step_bias, -jnp.exp(decay_log)]), ((0, 6), (0, 128 - heads_state))
    )
    skip = jnp.repeat(skip_gain, HD)[None]
    angles = jnp.asarray(angle_table(length))

    gated, power, conv, y, kept_states = state_forward(place_ref, raw, taps, heads, skip, states)
    mixed_low, kept, probs = attention_forward(place_ref, raw, angles)
    width_all = width * parts
    power = slot_sum(power[0])
    state_scale = lax.rsqrt(power / width_all + EPS)[:, None]
    state_low = (gated * state_scale * state_gain).astype(low)
    state_low, cotangent = tie(state_low, cotangent)
    own, *sends = spread_product(place_ref, (mixed_low, state_low), out_full, 0, parts)
    mixer_shard = finish_scatter(own, tensor_send(sends))
    middle = rows_in + mixer_shard
    second, second_scale = root_norm(middle, norm_ffn_gain)
    feed_slots = tensor_gather(second.astype(low))
    grad_pair, active, own, *sends = feed_forward(place_ref, feed_slots, cotangent, feed_full)
    grad_second = finish_scatter(own, tensor_send(sends))
    grad_feed = feed_grad(place_ref, feed_slots, cotangent, grad_pair, active)
    grad_second, grad_feed = tie(grad_second, grad_feed)
    feed_sums = lax.psum_scatter(grad_feed, "dp", scatter_dimension=0, tiled=True)

    weighted_second = grad_second * norm_ffn_gain
    inner_second = jnp.sum(weighted_second * middle, axis=-1, keepdims=True)
    grad_middle = (
        out_cotangent.astype(wide)
        + second_scale * weighted_second
        - middle * second_scale**3 * inner_second / middle.shape[-1]
    )
    ffn_gain = jnp.sum(grad_second * middle * second_scale, axis=0)
    cot_rows = tensor_gather(grad_middle.astype(low))
    mixer_cot, grad_mixed, grad_state, inner_sum = mixer_back(
        place_ref, cot_rows, out_full, gated, state_gain[None]
    )
    grad_mixed, active = tie(grad_mixed, active)
    weighted = grad_state * state_gain
    inner_sum = slot_sum(inner_sum[0])
    grad_attention = attention_backward(place_ref, grad_mixed, angles, kept, probs)
    early_terms = weight_sum(
        me_ref, [(mixer_cot, (mixed_low, state_low)), (mixer_rows, (grad_attention,))]
    )
    feed_terms = ordered_product(place_ref, active, feed_full, 2 * units)
    feed_shard = lax.psum_scatter(feed_terms, "tensor", scatter_dimension=0, tiled=True)
    early_terms, inner_sum = tie(early_terms, inner_sum)
    early_sums, _ = chip_sum(early_terms)
    grad_gated = (
        state_scale * weighted - gated * state_scale**3 * (inner_sum / width_all)[:, None]
    )
    grad_state_gain = jnp.sum(grad_state * gated * state_scale, axis=0)
    grad_mixer, grad_taps, grad_heads = state_backward(
        place_ref, raw, conv, y, kept_states, grad_gated, taps, heads, skip
    )
    grad_mixer, early_sums = tie(grad_mixer, early_sums)
    if whole_dp:
        total_rows = product_right(grad_mixer, mixer_full[:, 256:]) + product_right(
            grad_attention, mixer_full[:, :256]
        )
        gain_rows = jnp.sum(total_rows * mixer_rows.astype(wide), axis=0, keepdims=True)
        own, *sends = [total_rows[at * block : (at + 1) * block] for at in range(parts)]
        sends = [item.astype(low) for item in sends]
    else:
        gain_rows, own, *sends = total_product(
            me_ref, grad_attention, grad_mixer, near_full, far_full, mixer_rows, parts
        )
    own, grad_mixer = tie(own, grad_mixer)
    late_terms = weight_sum(me_ref, [(mixer_rows, (grad_mixer,))])
    first_got = tensor_send(sends)
    in_gain = gain_rows[0] / norm_in_gain

    columns = late_terms.shape[-1]
    small = [
        in_gain,
        ffn_gain,
        grad_taps[:4, width:].reshape(-1),
        grad_taps[4, width:],
        grad_taps[:4, :width].reshape(-1),
        grad_taps[4, :width],
        grad_state_gain,
        grad_heads[0, :heads_state],
        grad_heads[1, :heads_state],
        grad_heads[2, :heads_state],
    ]
    sizes = [item.shape[0] for item in small]
    flat = jnp.concatenate(small)
    small_rows = -(-flat.shape[0] // (16 * columns)) * 16
    flat = jnp.pad(flat, (0, small_rows * columns - flat.shape[0])).reshape(small_rows, columns)
    late_sums, flat = chip_sum(late_terms, flat)
    feed_sums, feed_shard = tie(feed_sums, feed_shard)
    feed_sums = feed_sums.astype(wide)
    hidden_out = (middle + feed_shard.astype(wide)).astype(low)
    done = (
        hidden_out,
        early_sums[:, 128 + width : 128 + width + 128],
        early_sums[:, :128].T,
        early_sums[:, 128 : 128 + width].T,
        feed_sums[:, :units],
        feed_sums[:, units : 2 * units],
        feed_sums[:, 2 * units :].T,
    )
    late_sums, done = tie(late_sums, done)
    flat = flat.reshape(-1)

    common = sum(sizes[:4])
    common_rows = -(-common // (16 * 384)) * 16
    rows_here = mixer_local.shape[0]
    shared = jnp.concatenate(
        [
            jnp.concatenate([early_sums[:, 128 + width + 128 :], late_sums[:, :256]], axis=1),
            jnp.pad(flat[:common], (0, common_rows * 384 - common)).reshape(common_rows, 384),
        ]
    ).astype(low)
    near = shared.astype(wide) + swap(shared, "tensor", 1).astype(wide)
    near = near.astype(low)
    far = swap(near, "tensor", 2).astype(wide)
    near = near.astype(wide)
    both = near + far
    first_half = place < parts // 2
    head_low = jnp.where(first_half, near[:rows_here, :128], far[:rows_here, :128])
    head_high = jnp.where(first_half, far[:rows_here, :128], near[:rows_here, :128])
    common_sums = both[rows_here:].reshape(-1)
    shared = jnp.concatenate([head_low, head_high, both[:rows_here, 128:]], axis=1).astype(low)
    shared, first_got = tie(shared, first_got)
    grad_first = finish_scatter(own, first_got)
    shared = dp_gather(shared).astype(wide)
    gradient_key = jnp.concatenate([shared[:, :64], shared[:, 128:192]], axis=1)
    gradient_value = jnp.concatenate([shared[:, 64:128], shared[:, 192:256]], axis=1)

    weighted_first = grad_first * norm_in_gain
    inner_first = jnp.sum(weighted_first * rows_in, axis=-1, keepdims=True)
    gradient_hidden = (
        grad_middle
        + first_scale * weighted_first
        - rows_in * first_scale**3 * inner_first / rows_in.shape[-1]
    )

    cuts = []
    at = 0
    for index, size in enumerate(sizes):
        cuts.append((common_sums if index < 4 else flat)[at : at + size])
        at += size
    return (
        done[0],
        gradient_hidden,
        cuts[0],
        done[1],
        gradient_key,
        gradient_value,
        done[2],
        late_sums[:, 256 : 256 + width],
        late_sums[:, 256 + width : 256 + 2 * width],
        shared[:, 256:384],
        shared[:, 384:512],
        late_sums[:, 256 + 2 * width : 256 + 2 * width + heads_state],
        cuts[4].reshape(conv_weight.shape),
        cuts[5],
        cuts[2].reshape(pair_conv_weight.shape),
        cuts[3],
        cuts[7],
        cuts[8],
        cuts[9],
        cuts[6],
        done[3],
        cuts[1],
        done[4],
        done[5],
        done[6],
    )


def solution(mesh):
    placed = (
        P(("dp", "tensor"), None),
        P(),
        P("dp", "tensor"),
        P("dp", None),
        P("dp", None),
        P("tensor", "dp"),
        P("dp", "tensor"),
        P("dp", "tensor"),
        P("dp", None),
        P("dp", None),
        P("dp", "tensor"),
        P(None, "tensor"),
        P("tensor"),
        P(),
        P(),
        P("tensor"),
        P("tensor"),
        P("tensor"),
        P("tensor"),
        P("tensor", "dp"),
        P(),
        P("dp", "tensor"),
        P("dp", "tensor"),
        P("tensor", "dp"),
        P(("dp", "tensor"), None),
    )
    return jax.shard_map(
        body,
        mesh=mesh,
        in_specs=placed,
        out_specs=(
            P(("dp", "tensor"), None),
            P(("dp", "tensor"), None),
            P(),
            P("dp", "tensor"),
            P(),
            P(),
            P("tensor", "dp"),
            P("dp", "tensor"),
            P("dp", "tensor"),
            P(),
            P(),
            P("dp", "tensor"),
            P(None, "tensor"),
            P("tensor"),
            P(),
            P(),
            P("tensor"),
            P("tensor"),
            P("tensor"),
            P("tensor"),
            P("tensor", "dp"),
            P(),
            P("dp", "tensor"),
            P("dp", "tensor"),
            P("tensor", "dp"),
        ),
        check_vma=False,
    )
```

```python
import functools

import jax
import jax.numpy as jnp
import numpy as np
from jax import lax
from jax.experimental import pallas as pl
from jax.experimental.pallas import tpu as pltpu
from jax.sharding import PartitionSpec as P

QH = 8
KVH = 2
HD = 64
BLOCK = 128


EPS = 1e-05
THETA = 10000.0
HIGHEST = lax.Precision.HIGHEST


def product(left, right):
    return jnp.dot(left, right, preferred_element_type=jnp.float32)


def product_left(left, right):
    return lax.dot_general(
        left, right, (((0,), (0,)), ((), ())), preferred_element_type=jnp.float32
    )


def product_right(left, right):
    return lax.dot_general(
        left, right, (((1,), (1,)), ((), ())), preferred_element_type=jnp.float32
    )


def root_norm(rows, gain):
    scale = lax.rsqrt(jnp.mean(rows * rows, axis=-1, keepdims=True) + EPS)
    return (rows * scale * gain, scale)


def dot(left, right, dims=((1,), (0,)), precision=None):
    return lax.dot_general(
        left, right, (dims, ((), ())), precision=precision, preferred_element_type=jnp.float32
    )


NN = ((1,), (0,))
NT = ((1,), (1,))
TN = ((0,), (0,))


def sigmoid(values):
    return 1.0 / (1.0 + jnp.exp(-values))


def softplus(values):
    return jnp.maximum(values, 0.0) + jnp.log1p(jnp.exp(-jnp.abs(values)))


def lane_index(rows):
    return lax.broadcasted_iota(jnp.int32, (rows, 128), 1)


def spread_heads(values, width):
    first = lane_index(values.shape[0]) < HD
    return jnp.concatenate(
        [
            jnp.where(first, values[:, at : at + 1], values[:, at + 1 : at + 2])
            for at in range(0, width // HD, 2)
        ],
        axis=1,
    )


def slot_rows(place_ref, at):
    return pl.ds(pl.multiple_of((place_ref[0] ^ at) * BLOCK, BLOCK), BLOCK)


def lower_mask():
    rows = lax.broadcasted_iota(jnp.int32, (BLOCK, BLOCK), 0)
    columns = lax.broadcasted_iota(jnp.int32, (BLOCK, BLOCK), 1)
    return rows >= columns


def block_decay(raw_steps, step_bias, rate, lower):
    step = softplus(raw_steps + step_bias)
    running = dot(lower.astype(jnp.float32), step * rate, NN, HIGHEST)
    return step, running, running.T


def block_weights(running, running_t, lower, head):
    spread = running[:, head : head + 1] - running_t[head : head + 1, :]
    return jnp.exp(jnp.where(lower, spread, -1e30))


def fill_history(place_ref, raw_ref, history_ref, blocks, width):
    history_ref[0:8, :] = jnp.zeros((8, history_ref.shape[1]), jnp.float32)
    for at in range(blocks):
        rows = slot_rows(place_ref, at)
        here = slice(8 + at * BLOCK, 8 + (at + 1) * BLOCK)
        history_ref[here, 0:width] = raw_ref[rows, 512 + width : 512 + 2 * width]
        history_ref[here, width : width + 256] = raw_ref[rows, 256:512]


def state_forward_kernel(
    place_ref,
    raw_ref,
    taps_ref,
    heads_ref,
    skip_ref,
    gated_ref,
    power_ref,
    conv_ref,
    y_ref,
    states_ref,
    history_ref,
):
    low = jnp.bfloat16
    width = gated_ref.shape[1]
    blocks = gated_ref.shape[0] // BLOCK
    fill_history(place_ref, raw_ref, history_ref, blocks, width)
    lower = lower_mask()
    first = lane_index(BLOCK) < HD
    state = jnp.zeros((states_ref.shape[1], width), jnp.float32)
    for at in range(blocks):
        rows = slot_rows(place_ref, at)
        conv = taps_ref[4:5, :]
        for tap in range(4):
            conv = conv + taps_ref[tap : tap + 1, :] * history_ref[pl.ds(5 + tap + at * BLOCK, BLOCK), :]
        conv_ref[rows, :] = conv
        acted = conv * sigmoid(conv)
        inner = acted[:, :width]
        write = acted[:, width : width + 128].astype(low)
        read = acted[:, width + 128 :].astype(low)
        step, running, running_t = block_decay(
            raw_ref[rows, 512 + 2 * width :], heads_ref[0:1, :], heads_ref[1:2, :], lower
        )
        scaled = inner * spread_heads(step, width)
        scaled_low = scaled.astype(low)
        zero = jnp.zeros((BLOCK, 128), low)
        meet = dot(read, write, NT)
        inside = []
        for pair in range(width // 128):
            both = jnp.concatenate(
                [
                    (meet * block_weights(running, running_t, lower, 2 * pair)).astype(low),
                    (meet * block_weights(running, running_t, lower, 2 * pair + 1)).astype(low),
                ],
                axis=1,
            )
            piece = scaled_low[:, pair * 128 : (pair + 1) * 128]
            split = jnp.concatenate([jnp.where(first, piece, zero), jnp.where(first, zero, piece)])
            inside.append(dot(both, split))
        earlier = dot(read, state.astype(low))
        y = jnp.concatenate(inside, axis=1) + spread_heads(jnp.exp(running), width) * earlier
        y_ref[rows, :] = y
        states_ref[at] = state
        last = running[BLOCK - 1 : BLOCK, :]
        carried = (spread_heads(jnp.exp(last - running), width) * scaled).astype(low)
        state = spread_heads(jnp.exp(last), width) * state + dot(write, carried, TN)
        gate = raw_ref[rows, 512 : 512 + width]
        gated = (y + skip_ref[0:1, :] * inner) * gate * sigmoid(gate)
        gated_ref[rows, :] = gated
        power_ref[:, rows] = dot(jnp.ones((8, width), jnp.float32), gated * gated, NT, HIGHEST)


def state_backward_kernel(
    place_ref,
    raw_ref,
    conv_ref,
    y_ref,
    states_ref,
    up_ref,
    taps_ref,
    heads_ref,
    skip_ref,
    grad_ref,
    grad_taps_ref,
    grad_heads_ref,
    history_ref,
    later_ref,
):
    low = jnp.bfloat16
    width = up_ref.shape[1]
    blocks = up_ref.shape[0] // BLOCK
    length = up_ref.shape[0]
    every = width + 256
    fill_history(place_ref, raw_ref, history_ref, blocks, width)
    later_ref[length : length + 8, :] = jnp.zeros((8, every), jnp.float32)
    lower = lower_mask()
    first = lane_index(BLOCK) < HD
    zero = jnp.zeros((BLOCK, 128), low)
    picks = (
        lax.broadcasted_iota(jnp.int32, (width, 128), 0) // HD
        == lax.broadcasted_iota(jnp.int32, (width, 128), 1)
    ).astype(jnp.float32)
    skip = skip_ref[0:1, :]
    rate = heads_ref[1:2, :]
    grad_state = jnp.zeros((states_ref.shape[1], width), jnp.float32)
    grad_taps = [jnp.zeros((1, every), jnp.float32) for _ in range(5)]
    grad_bias = jnp.zeros((1, 128), jnp.float32)
    grad_decay = jnp.zeros((1, 128), jnp.float32)
    grad_skip = jnp.zeros((1, width), jnp.float32)
    for at in reversed(range(blocks)):
        rows = slot_rows(place_ref, at)
        gate = raw_ref[rows, 512 : 512 + width]
        gate_sigma = sigmoid(gate)
        conv = conv_ref[rows, :]
        conv_sigma = sigmoid(conv)
        acted = conv * conv_sigma
        inner = acted[:, :width]
        write = acted[:, width : width + 128].astype(low)
        read = acted[:, width + 128 :].astype(low)
        y = y_ref[rows, :]
        up = up_ref[rows, :]
        grad_gate = up * (y + skip * inner) * gate_sigma * (1.0 + gate * (1.0 - gate_sigma))
        grad_ref[rows, 256 : 256 + width] = grad_gate.astype(low)
        grad_y = up * gate * gate_sigma
        raw_steps = raw_ref[rows, 512 + 2 * width :]
        step, running, running_t = block_decay(raw_steps, heads_ref[0:1, :], rate, lower)
        step_wide = spread_heads(step, width)
        grow = spread_heads(jnp.exp(running), width)
        last = running[BLOCK - 1 : BLOCK, :]
        carry = spread_heads(jnp.exp(last - running), width)
        last_wide = spread_heads(jnp.exp(last), width)
        scaled = inner * step_wide
        scaled_low = scaled.astype(low)
        grad_low = grad_y.astype(low)
        grown_low = (grad_y * grow).astype(low)
        state = states_ref[at]
        state_low = state.astype(low)
        grad_state_low = grad_state.astype(low)
        meet = dot(read, write, NT)
        grad_meet = jnp.zeros((BLOCK, BLOCK), jnp.float32)
        inside = []
        for pair in range(width // 128):
            weights = [
                block_weights(running, running_t, lower, head) for head in (2 * pair, 2 * pair + 1)
            ]
            both = jnp.concatenate([(meet * item).astype(low) for item in weights], axis=0)
            piece = grad_low[:, pair * 128 : (pair + 1) * 128]
            split = jnp.concatenate([jnp.where(first, piece, zero), jnp.where(first, zero, piece)])
            grad_both = dot(split, scaled_low[:, pair * 128 : (pair + 1) * 128], NT)
            grad_meet = (
                grad_meet + grad_both[:BLOCK] * weights[0] + grad_both[BLOCK:] * weights[1]
            )
            inside.append(dot(both, split, TN))
        grad_inside = jnp.concatenate(inside, axis=1)
        from_state = carry * dot(write, grad_state_low)
        carried = carry * scaled
        grad_scaled = grad_inside + from_state
        moved = scaled * from_state
        turn = grad_low.astype(jnp.float32) * y - scaled_low.astype(jnp.float32) * grad_inside - moved
        direct = grad_y * inner
        ends = jnp.sum(moved, axis=0, keepdims=True) + last_wide * jnp.sum(
            state * grad_state, axis=0, keepdims=True
        )
        summed = dot(
            jnp.concatenate([turn, grad_scaled * inner, jnp.broadcast_to(ends, (8, width))]),
            picks,
            NN,
            HIGHEST,
        )
        grad_running = (
            dot(lower.astype(jnp.float32), summed[:BLOCK], TN, HIGHEST)
            + summed[2 * BLOCK : 2 * BLOCK + 1]
        )
        grad_step = grad_running * rate + summed[BLOCK : 2 * BLOCK]
        grad_decay = grad_decay + jnp.sum(grad_running * step * rate, axis=0, keepdims=True)
        grad_steps = grad_step * sigmoid(raw_steps + heads_ref[0:1, :])
        grad_bias = grad_bias + jnp.sum(grad_steps, axis=0, keepdims=True)
        grad_skip = grad_skip + jnp.sum(direct, axis=0, keepdims=True)
        grad_ref[rows, 256 + 2 * width :] = grad_steps.astype(low)
        grad_inner = grad_scaled * step_wide + skip * grad_y
        grad_meet_low = grad_meet.astype(low)
        grad_read = dot(grad_meet_low, write) + dot(grown_low, state_low, NT)
        grad_write = dot(grad_meet_low, read, TN) + dot(carried.astype(low), grad_state_low, NT)
        grad_state = last_wide * grad_state + dot(read, grown_low, TN)
        grad_conv = jnp.concatenate([grad_inner, grad_write, grad_read], axis=1) * (
            conv_sigma * (1.0 + conv * (1.0 - conv_sigma))
        )
        later_ref[at * BLOCK : (at + 1) * BLOCK, :] = grad_conv
        back = jnp.zeros((BLOCK, every), jnp.float32)
        for tap in range(4):
            back = back + taps_ref[tap : tap + 1, :] * later_ref[pl.ds(at * BLOCK + 3 - tap, BLOCK), :]
            seen = history_ref[pl.ds(5 + tap + at * BLOCK, BLOCK), :]
            grad_taps[tap] = grad_taps[tap] + jnp.sum(grad_conv * seen, axis=0, keepdims=True)
        grad_taps[4] = grad_taps[4] + jnp.sum(grad_conv, axis=0, keepdims=True)
        grad_ref[rows, 256 + width : 256 + 2 * width] = back[:, :width].astype(low)
        grad_ref[rows, 0:256] = back[:, width:].astype(low)
    for tap in range(5):
        grad_taps_ref[tap : tap + 1, :] = grad_taps[tap]
    grad_taps_ref[5:8, :] = jnp.zeros((3, every), jnp.float32)
    skip_heads = dot(jnp.broadcast_to(grad_skip, (8, width)), picks, NN, HIGHEST)
    grad_heads_ref[...] = jnp.zeros(grad_heads_ref.shape, jnp.float32)
    grad_heads_ref[0:1, :] = grad_bias
    grad_heads_ref[1:2, :] = grad_decay
    grad_heads_ref[2:3, :] = skip_heads[0:1]


def turned(values, cosine, sine):
    early = lane_index(values.shape[0]) % HD < HD // 2
    other = jnp.where(early, pltpu.roll(values, 128 - HD // 2, 1), pltpu.roll(values, HD // 2, 1))
    return values * cosine + other * sine


def both_heads(values, first):
    zero = jnp.zeros(values.shape, values.dtype)
    return jnp.concatenate([jnp.where(first, values, zero), jnp.where(first, zero, values)])


def attention_forward_kernel(
    place_ref, raw_ref, angle_ref, mixed_ref, kept_ref, probs_ref
):
    low = jnp.bfloat16
    blocks = mixed_ref.shape[0] // BLOCK
    first = lane_index(BLOCK) < HD
    for at in range(blocks):
        rows = slot_rows(place_ref, at)
        here = slice(at * BLOCK, (at + 1) * BLOCK)
        cosine = angle_ref[here, 0:128]
        sine = angle_ref[here, 128:256]
        pair = raw_ref[rows, 128:256]
        key = turned(pair, cosine, sine)
        kept_ref[here, 0:128] = turned(raw_ref[rows, 0:128], cosine, sine).astype(low)
        kept_ref[here, 128:256] = jnp.where(first, key, pltpu.roll(key, HD, 1)).astype(low)
        kept_ref[here, 256:384] = jnp.where(first, pltpu.roll(pair, HD, 1), pair).astype(low)
    for at in range(blocks):
        rows = slot_rows(place_ref, at)
        here = slice(at * BLOCK, (at + 1) * BLOCK)
        reach = (at + 1) * BLOCK
        query = both_heads(kept_ref[here, 0:128], first)
        scores = dot(query, kept_ref[0:reach, 128:256], NT) * (HD ** (-0.5))
        row = lax.broadcasted_iota(jnp.int32, (2 * BLOCK, reach), 0) % BLOCK + at * BLOCK
        column = lax.broadcasted_iota(jnp.int32, (2 * BLOCK, reach), 1)
        scores = jnp.where(row >= column, scores, -1e30)
        exponent = jnp.exp(scores - jnp.max(scores, axis=1, keepdims=True))
        probs = (exponent / jnp.sum(exponent, axis=1, keepdims=True)).astype(low)
        probs_ref[at, :, 0:reach] = probs
        out = dot(probs, kept_ref[0:reach, 256:384])
        mixed_ref[rows, :] = jnp.where(first, out[:BLOCK], out[BLOCK:]).astype(low)


def attention_backward_kernel(
    place_ref, up_ref, angle_ref, kept_ref, probs_ref, grad_ref, key_ref, value_ref
):
    low = jnp.bfloat16
    blocks = up_ref.shape[0] // BLOCK
    first = lane_index(BLOCK) < HD
    scale = HD ** (-0.5)
    key_ref[...] = jnp.zeros(key_ref.shape, jnp.float32)
    value_ref[...] = jnp.zeros(value_ref.shape, jnp.float32)
    for at in range(blocks):
        rows = slot_rows(place_ref, at)
        here = slice(at * BLOCK, (at + 1) * BLOCK)
        reach = (at + 1) * BLOCK
        query = both_heads(kept_ref[here, 0:128], first)
        up = both_heads(up_ref[rows, :], first)
        probs_low = probs_ref[at, :, 0:reach]
        probs = probs_low.astype(jnp.float32)
        grad_probs = dot(up, kept_ref[0:reach, 256:384], NT)
        inner = jnp.sum(probs * grad_probs, axis=1, keepdims=True)
        grad_scores = (probs * (grad_probs - inner)).astype(low)
        both = dot(grad_scores, kept_ref[0:reach, 128:256]) * scale
        grad_query = jnp.where(first, both[:BLOCK], both[BLOCK:])
        grad_ref[rows, 0:128] = turned(
            grad_query, angle_ref[here, 0:128], -angle_ref[here, 128:256]
        ).astype(low)
        key_ref[0:reach, :] += dot(grad_scores, query, TN)
        value_ref[0:reach, :] += dot(probs_low, up, TN)
    for at in range(blocks):
        rows = slot_rows(place_ref, at)
        here = slice(at * BLOCK, (at + 1) * BLOCK)
        key = key_ref[here, :]
        value = value_ref[here, :]
        key = (key + pltpu.roll(key, HD, 1)) * scale
        key = turned(key, angle_ref[here, 0:128], -angle_ref[here, 128:256])
        value = value + pltpu.roll(value, HD, 1)
        grad_ref[rows, 128:256] = jnp.where(first, key, value).astype(low)


def angle_table(length):
    half = HD // 2
    freq = THETA ** (-np.arange(half, dtype=np.float32) / half)
    angle = np.arange(length, dtype=np.float32)[:, None] * freq[None, :]
    cosine = np.tile(np.cos(angle), (1, 4))
    sine = np.tile(np.concatenate([-np.sin(angle), np.sin(angle)], axis=1), (1, 2))
    return np.concatenate([cosine, sine], axis=1).astype(np.float32)


def run_kernel(kernel, place, operands, outs, scratch, name, flops=2e8):
    whole = pl.BlockSpec(memory_space=pltpu.VMEM)
    return pl.pallas_call(
        kernel,
        out_shape=[jax.ShapeDtypeStruct(shape, dtype) for shape, dtype in outs],
        in_specs=[pl.BlockSpec(memory_space=pltpu.SMEM)] + [whole] * len(operands),
        out_specs=[whole] * len(outs),
        scratch_shapes=scratch,
        compiler_params=pltpu.CompilerParams(vmem_limit_bytes=60 * 2**20),
        cost_estimate=pl.CostEstimate(flops=int(flops), bytes_accessed=1 << 20, transcendentals=0),
        name=name,
    )(place, *operands)


def state_forward(place, raw, taps, heads, skip, states):
    length = raw.shape[0]
    width = skip.shape[1]
    wide = jnp.float32
    return run_kernel(
        state_forward_kernel,
        place,
        (raw, taps, heads, skip),
        [
            ((length, width), wide),
            ((8, length), wide),
            ((length, width + 256), wide),
            ((length, width), wide),
            ((length // BLOCK, states, width), wide),
        ],
        [pltpu.VMEM((length + 8, width + 256), wide)],
        "state_forward",
    )


def state_backward(place, raw, conv, y, states, up, taps, heads, skip):
    length = raw.shape[0]
    width = skip.shape[1]
    wide = jnp.float32
    return run_kernel(
        state_backward_kernel,
        place,
        (raw, conv, y, states, up, taps, heads, skip),
        [
            ((length, 256 + 2 * width + 128), jnp.bfloat16),
            ((8, width + 256), wide),
            ((8, 128), wide),
        ],
        [pltpu.VMEM((length + 8, width + 256), wide), pltpu.VMEM((length + 8, width + 256), wide)],
        "state_backward",
    )


def attention_forward(place, raw, angles):
    length = raw.shape[0]
    low = jnp.bfloat16
    return run_kernel(
        attention_forward_kernel,
        place,
        (raw, angles),
        [
            ((length, 128), low),
            ((length, 384), low),
            ((length // BLOCK, 2 * BLOCK, length), low),
        ],
        [],
        "attention_forward",
    )


def attention_backward(place, up, angles, kept, probs):
    length = up.shape[0]
    return run_kernel(
        attention_backward_kernel,
        place,
        (up, angles, kept, probs),
        [((length, 256), jnp.bfloat16)],
        [pltpu.VMEM((length, 128), jnp.float32), pltpu.VMEM((length, 128), jnp.float32)],
        "attention_backward",
    )[0]


def block_columns(me_ref, mask):
    return pl.ds(pl.multiple_of((me_ref[0] ^ mask) * 128, 128), 128)


def join_rows(slots, whole_ref):
    rows = slots[0].shape[0]
    for at, slot in enumerate(slots):
        whole_ref[at * rows : (at + 1) * rows, :] = slot[...]


def pack_kernel(
    head_ref,
    rows_ref,
    gain_ref,
    query_ref,
    key_ref,
    value_ref,
    write_ref,
    read_ref,
    gate_ref,
    inner_ref,
    step_ref,
    output_ref,
    state_ref,
    feed_gate_ref,
    feed_up_ref,
    feed_down_ref,
    normed_ref,
    mixer_ref,
    feed_ref,
):
    rows = rows_ref[...].astype(jnp.float32)
    scale = lax.rsqrt(jnp.mean(rows * rows, axis=1, keepdims=True) + EPS)
    normed_ref[...] = (rows * scale * gain_ref[0:1, :]).astype(normed_ref.dtype)

    def turned_over(ref):
        return ref[...].astype(jnp.float32).T.astype(mixer_ref.dtype)

    low_head = head_ref[0] == 0
    first = lane_index(rows.shape[0]) < HD
    key = key_ref[...].astype(jnp.float32)
    value = value_ref[...].astype(jnp.float32)
    key = jnp.where(low_head, key, pltpu.roll(key, HD, 1))
    value = jnp.where(low_head, pltpu.roll(value, HD, 1), value)
    mixer_ref[:, 0:128] = query_ref[...]
    mixer_ref[:, 128:256] = jnp.where(first, key, value).astype(mixer_ref.dtype)
    mixer_ref[:, 256:384] = write_ref[...]
    mixer_ref[:, 384:512] = read_ref[...]
    at = 512
    for ref in (gate_ref, inner_ref):
        mixer_ref[:, at : at + ref.shape[1]] = ref[...]
        at += ref.shape[1]
    mixer_ref[:, at : at + 128] = jnp.zeros((rows.shape[0], 128), mixer_ref.dtype)
    mixer_ref[:, at : at + step_ref.shape[1]] = step_ref[...]
    mixer_ref[:, at + 128 : at + 256] = turned_over(output_ref)
    mixer_ref[:, at + 256 :] = turned_over(state_ref)
    units = feed_gate_ref.shape[1]
    feed_ref[:, :units] = feed_gate_ref[...]
    feed_ref[:, units : 2 * units] = feed_up_ref[...]
    feed_ref[:, 2 * units :] = turned_over(feed_down_ref)


def gather_columns(me_ref, rows_ref, side, chips):
    return jnp.concatenate(
        [rows_ref[:, block_columns(me_ref, 2 * at + side)] for at in range(chips)], axis=1
    )


def project_kernel(me_ref, *refs):
    slots, (near_ref, far_ref, rows_ref, raw_ref) = refs[:-4], refs[-4:]
    join_rows(slots, rows_ref)
    chips = near_ref.shape[0] // 128
    columns = raw_ref.shape[1]
    raw_ref[...] = dot(
        gather_columns(me_ref, rows_ref, 0, chips), near_ref[:, :columns]
    ) + dot(gather_columns(me_ref, rows_ref, 1, chips), far_ref[:, :columns])


def write_spread(total, own_ref, sends):
    rows = own_ref.shape[0]
    own_ref[...] = total[:rows]
    for at, send in enumerate(sends):
        send[...] = total[(at + 1) * rows : (at + 2) * rows].astype(jnp.bfloat16)


def spread_kernel(start, me_ref, mixed_ref, state_ref, near_ref, far_ref, own_ref, *rest):
    sends, total_ref = rest[:-1], rest[-1]
    left = jnp.concatenate([mixed_ref[...], state_ref[...]], axis=1)
    spread_total(me_ref, left, near_ref, far_ref, slice(start, start + left.shape[1]), total_ref)
    write_spread(total_ref[...], own_ref, sends)


def spread_total(me_ref, left, near_ref, far_ref, columns, total_ref):
    chips = near_ref.shape[0] // 128
    for side, weight_ref in enumerate((near_ref, far_ref)):
        piece = dot(left, weight_ref[:, columns], NT)
        for at in range(chips):
            total_ref[:, block_columns(me_ref, 2 * at + side)] = piece[:, at * 128 : (at + 1) * 128]


def slot_kernel(start, place_ref, left_ref, weight_ref, own_ref, *sends):
    total = dot(left_ref[...], weight_ref[:, start : start + left_ref.shape[1]], NT)
    write_spread(total, own_ref, sends)


def early_grad_kernel(
    place_ref, cot_ref, mixed_ref, state_ref, rows_ref, attention_ref, out_ref
):
    both = jnp.concatenate([mixed_ref[...], state_ref[...]], axis=1)
    for at in range(0, rows_ref.shape[1], 256):
        here = slice(at, at + 256)
        out_ref[here, : both.shape[1]] = dot(cot_ref[:, here], both, TN).astype(out_ref.dtype)
        out_ref[here, both.shape[1] :] = dot(
            rows_ref[:, here], attention_ref[:, :128], TN
        ).astype(out_ref.dtype)


def total_kernel(
    me_ref, attention_ref, mixer_ref, near_ref, far_ref, rows_ref, gain_ref, own_ref, *rest
):
    sends, total_ref = rest[:-1], rest[-1]
    left = jnp.concatenate([attention_ref[...], mixer_ref[...]], axis=1)
    spread_total(me_ref, left, near_ref, far_ref, slice(0, left.shape[1]), total_ref)
    total = total_ref[...]
    gain_ref[...] = jnp.broadcast_to(
        jnp.sum(total * rows_ref[...].astype(jnp.float32), axis=0, keepdims=True), gain_ref.shape
    )
    write_spread(total, own_ref, sends)


def feed_kernel(place_ref, *refs):
    low = jnp.bfloat16
    slots, cots_ref = refs[:4], refs[4]
    feed_ref, pair_ref, active_ref, own_ref = refs[5:9]
    sends = refs[9:12]
    units = active_ref.shape[1]
    rows = slots[0].shape[0]
    for half in range(2):
        here = slice(2 * half * rows, 2 * (half + 1) * rows)
        left = jnp.concatenate([slots[2 * half][...], slots[2 * half + 1][...]])
        cot = jnp.concatenate([cots_ref[slot_rows(place_ref, 2 * half + at), :] for at in range(2)])
        gate_up = dot(left, feed_ref[:, : 2 * units])
        grad_active = dot(cot, feed_ref[:, 2 * units :])
        gate = gate_up[:, :units]
        up = gate_up[:, units:]
        sigma = sigmoid(gate)
        swish = gate * sigma
        active_ref[here, :] = (swish * up).astype(low)
        grad_gate = grad_active * up * sigma * (1.0 + gate * (1.0 - sigma))
        pair = jnp.concatenate([grad_gate, grad_active * swish], axis=1).astype(low)
        pair_ref[here, :] = pair
        total = dot(pair, feed_ref[:, : 2 * units], NT)
        if half == 0:
            own_ref[...] = total[:rows]
            sends[0][...] = total[rows:].astype(low)
        else:
            sends[1][...] = total[:rows].astype(low)
            sends[2][...] = total[rows:].astype(low)


def write_halves(piece, even, keep_ref, give_ref, chip):
    piece = piece.astype(keep_ref.dtype)
    keep_ref[chip] = jnp.where(even, piece[:128], piece[128:])
    give_ref[chip] = jnp.where(even, piece[128:], piece[:128])


def feed_grad_kernel(place_ref, *refs):
    slots, cots_ref = refs[:4], refs[4]
    pair_ref, active_ref, keep_ref, give_ref, rows_ref, cot_ref = refs[5:]
    join_rows(slots, rows_ref)
    for at in range(len(slots)):
        cot_ref[at * BLOCK : (at + 1) * BLOCK, :] = cots_ref[slot_rows(place_ref, at), :]
    even = place_ref[1] % 2 == 0
    for chip in range(keep_ref.shape[0]):
        here = slice(chip * 256, (chip + 1) * 256)
        piece = jnp.concatenate(
            [dot(rows_ref[:, here], pair_ref[...], TN), dot(cot_ref[:, here], active_ref[...], TN)],
            axis=1,
        )
        write_halves(piece, even, keep_ref, give_ref, chip)


def weight_grad_kernel(groups, me_ref, *refs):
    keep_ref, give_ref = refs[-2:]
    even = me_ref[0] % 2 == 0
    for chip in range(keep_ref.shape[0]):
        here = slice(chip * 256, (chip + 1) * 256)
        pieces = []
        at = 0
        for count in groups:
            left = refs[at][:, here]
            right = jnp.concatenate([item[...] for item in refs[at + 1 : at + 1 + count]], axis=1)
            pieces.append(dot(left, right, TN))
            at += 1 + count
        write_halves(jnp.concatenate(pieces, axis=1), even, keep_ref, give_ref, chip)


def mixer_back_kernel(start, me_ref, *refs):
    slots = refs[:4]
    near_ref, far_ref, gated_ref, gain_ref, cot_ref, mixed_ref, state_ref, inner_ref = refs[4:]
    join_rows(slots, cot_ref)
    chips = near_ref.shape[0] // 128
    both = dot(gather_columns(me_ref, cot_ref, 0, chips), near_ref[:, start:]) + dot(
        gather_columns(me_ref, cot_ref, 1, chips), far_ref[:, start:]
    )
    mixed_ref[...] = both[:, :128].astype(jnp.bfloat16)
    state = both[:, 128:]
    state_ref[...] = state
    product_rows = state * gain_ref[0:1, :] * gated_ref[...]
    inner_ref[...] = dot(
        jnp.ones((8, product_rows.shape[1]), jnp.float32), product_rows, NT, HIGHEST
    )


def pack(head, hidden, gain, *weights):
    rows, columns = hidden.shape
    low = jnp.bfloat16
    width = weights[5].shape[1]
    units = weights[-3].shape[1]
    return run_kernel(
        pack_kernel,
        head,
        (hidden, gain, *weights),
        [((rows, columns), low), ((rows, 768 + 3 * width), low), ((rows, 3 * units), low)],
        [],
        "pack",
    )


def project(me, slots, near, far, columns):
    length = len(slots) * slots[0].shape[0]
    return run_kernel(
        project_kernel,
        me,
        (*slots, near, far),
        [((length, slots[0].shape[1]), jnp.bfloat16), ((length, columns), jnp.float32)],
        [],
        "project",
    )


def spread_outs(rows, columns, parts):
    return [((rows, columns), jnp.float32)] + [((rows, columns), jnp.bfloat16)] * (parts - 1)


def spread_product(me, mixed, state, near, far, start, parts):
    length, columns = mixed.shape[0], 2 * near.shape[0]
    return run_kernel(
        functools.partial(spread_kernel, start),
        me,
        (mixed, state, near, far),
        spread_outs(length // parts, columns, parts),
        [pltpu.VMEM((length, columns), jnp.float32)],
        "spread_product",
    )


def slot_product(place, left, weight, start, parts):
    return run_kernel(
        functools.partial(slot_kernel, start),
        place,
        (left, weight),
        spread_outs(left.shape[0] // parts, weight.shape[0], parts),
        [],
        "slot_product",
    )


def early_grad(place, cot, mixed, state, rows, attention):
    columns = mixed.shape[1] + state.shape[1] + 128
    return run_kernel(
        early_grad_kernel,
        place,
        (cot, mixed, state, rows, attention),
        [((cot.shape[1], columns), jnp.bfloat16)],
        [],
        "early_grad",
    )[0]


def total_product(me, attention, mixer, near, far, rows, parts):
    length, columns = rows.shape
    return run_kernel(
        total_kernel,
        me,
        (attention, mixer, near, far, rows),
        [((8, columns), jnp.float32)] + spread_outs(length // parts, columns, parts),
        [pltpu.VMEM((length, columns), jnp.float32)],
        "total_product",
    )


def feed_forward(place, slots, cotangent, feed):
    rows, columns = slots[0].shape
    units = feed.shape[1] // 3
    parts = len(slots)
    return run_kernel(
        feed_kernel,
        place,
        (*slots, cotangent, feed),
        [((parts * rows, 2 * units), jnp.bfloat16), ((parts * rows, units), jnp.bfloat16)]
        + spread_outs(rows, columns, parts),
        [],
        "feed_forward",
    )


def feed_grad(place, slots, cotangent, pair, active):
    length, columns = pair.shape[0], slots[0].shape[1]
    scratch = pltpu.VMEM((length, columns), jnp.bfloat16)
    return run_kernel(
        feed_grad_kernel,
        place,
        (*slots, cotangent, pair, active),
        [((columns // 256, 128, pair.shape[1] + active.shape[1]), jnp.bfloat16)] * 2,
        [scratch, scratch],
        "feed_grad",
    )


def weight_grad(me, groups):
    counts = tuple(len(rights) for _, rights in groups)
    columns = sum(item.shape[1] for _, rights in groups for item in rights)
    operands = [item for left, rights in groups for item in (left, *rights)]
    blocks = groups[0][0].shape[1] // 256
    return run_kernel(
        functools.partial(weight_grad_kernel, counts),
        me,
        operands,
        [((blocks, 128, columns), jnp.bfloat16)] * 2,
        [],
        "weight_grad",
    )


def mixer_back(me, slots, near, far, start, gated, gain):
    rows, columns = slots[0].shape
    length = len(slots) * rows
    width = gated.shape[1]
    return run_kernel(
        functools.partial(mixer_back_kernel, start),
        me,
        (*slots, near, far, gated, gain),
        [
            ((length, columns), jnp.bfloat16),
            ((length, 128), jnp.bfloat16),
            ((length, width), jnp.float32),
            ((8, length), jnp.float32),
        ],
        [],
        "mixer_back",
    )


def swap(values, axis, mask):
    size = lax.axis_size(axis)
    return lax.ppermute(values, axis, [(index, index ^ mask) for index in range(size)])


def tensor_gather(block):
    masks = reversed(range(1, lax.axis_size("tensor")))
    return [block] + [swap(block, "tensor", mask) for mask in masks][::-1]


def paired_sum(terms):
    while len(terms) > 1:
        terms = [terms[at] + terms[at + 1] for at in range(0, len(terms), 2)]
    return terms[0]


def tensor_send(sends):
    return [swap(item, "tensor", at + 1) for at, item in enumerate(sends)]


def finish_scatter(own, got):
    return paired_sum([own] + [item.astype(jnp.float32) for item in got])


def cut(total, parts):
    blocks = jnp.split(total, parts)
    return blocks[:1] + [item.astype(jnp.bfloat16) for item in blocks[1:]]


def slot_sum(values):
    parts = lax.axis_size("tensor")
    shaped = values.reshape(parts, -1)
    terms = [shaped]
    for mask in range(1, parts):
        got = swap(shaped, "tensor", mask)
        terms.append(jnp.stack([got[at ^ mask] for at in range(parts)]))
    return paired_sum(terms).reshape(-1)


def tie(*values):
    return lax.optimization_barrier(values)


def dp_pieces(block):
    mine = jnp.stack([block] + [swap(block, "dp", 2 * chip) for chip in range(1, 4)])
    return mine.reshape(-1, block.shape[1])


def dp_gather(block):
    size = lax.axis_size("dp")
    if size != 8:
        return lax.all_gather(block, "dp", axis=0, tiled=True)
    me = lax.axis_index("dp")
    rows = block.shape[0]
    mine = dp_pieces(block)
    other = swap(mine, "dp", 1)
    whole = jnp.zeros((size * rows,) + block.shape[1:], block.dtype)
    for chip in range(size // 2):
        here = slice(chip * rows, (chip + 1) * rows)
        whole = lax.dynamic_update_slice_in_dim(whole, mine[here], (me ^ 2 * chip) * rows, 0)
        whole = lax.dynamic_update_slice_in_dim(whole, other[here], (me ^ 2 * chip ^ 1) * rows, 0)
    return whole


def core_sum(keep, give):
    give = swap(give, "dp", 1)
    return (keep.astype(jnp.float32) + give.astype(jnp.float32)).astype(jnp.bfloat16)


def weight_sum(me_ref, groups):
    if lax.axis_size("dp") != 8:
        return jnp.concatenate(
            [product_left(left, jnp.concatenate(rights, axis=1)) for left, rights in groups], axis=1
        ).astype(jnp.bfloat16)
    return core_sum(*weight_grad(me_ref, groups))


def chip_sum(both, small=None, after=None):
    size = lax.axis_size("dp")
    if size != 8:
        summed = lax.psum_scatter(both, "dp", scatter_dimension=0, tiled=True)
        return summed.astype(jnp.float32), None if small is None else lax.psum(small, "dp")
    chip = lax.axis_index("dp") // 2
    rows = both.shape[1]
    if small is not None:
        small = small.astype(jnp.bfloat16)
        near = swap(small, "dp", 1)
        small = (small.astype(jnp.float32) + near.astype(jnp.float32)).astype(jnp.bfloat16)
    terms = []
    for mask in range(size // 2):
        part = lax.dynamic_index_in_dim(both, chip ^ mask, 0, keepdims=False)
        if small is not None:
            part = jnp.concatenate([part, small])
        if after is not None and mask == size // 2 - 1:
            part, _ = tie(part, after)
        terms.append((swap(part, "dp", 2 * mask) if mask else part).astype(jnp.float32))
    summed = paired_sum(terms)
    return summed[:rows], None if small is None else summed[rows:]


def body(
    hidden_in,
    norm_in_gain,
    query_weight,
    key_weight,
    value_weight,
    output_weight,
    gate_weight,
    inner_weight,
    write_weight,
    read_weight,
    step_weight,
    conv_weight,
    conv_bias,
    pair_conv_weight,
    pair_conv_bias,
    step_bias,
    decay_log,
    skip_gain,
    state_gain,
    state_out_weight,
    norm_ffn_gain,
    feed_gate_weight,
    feed_up_weight,
    feed_down_weight,
    out_cotangent,
):
    low = jnp.bfloat16
    wide = jnp.float32
    parts = lax.axis_size("tensor")
    place = lax.axis_index("tensor")
    place_ref = place.astype(jnp.int32).reshape(1)
    heads_here = query_weight.shape[1] // HD
    key_head = place * heads_here // (QH // KVH)
    heads_state = step_weight.shape[1]
    width = gate_weight.shape[1]
    units = feed_gate_weight.shape[1]
    states = write_weight.shape[1]

    out_start = 640 + 2 * width
    whole_dp = lax.axis_size("dp") != 8
    rows_in = hidden_in.astype(wide)
    normed, first_scale = root_norm(rows_in, norm_in_gain)
    if whole_dp:
        normed_low = normed.astype(low)
        mixer_local = jnp.concatenate(
            [
                query_weight,
                lax.dynamic_slice_in_dim(key_weight, key_head * HD, HD, 1),
                lax.dynamic_slice_in_dim(value_weight, key_head * HD, HD, 1),
                write_weight,
                read_weight,
                gate_weight,
                inner_weight,
                jnp.pad(step_weight, ((0, 0), (0, 128 - heads_state))),
                output_weight.T,
                state_out_weight.T,
            ],
            axis=1,
        )
        feed_local = jnp.concatenate([feed_gate_weight, feed_up_weight, feed_down_weight.T], axis=1)
    else:
        normed_low, mixer_local, feed_local = pack(
            key_head.astype(jnp.int32).reshape(1),
            hidden_in,
            norm_in_gain[None],
            query_weight,
            key_weight,
            value_weight,
            write_weight,
            read_weight,
            gate_weight,
            inner_weight,
            step_weight,
            output_weight,
            state_out_weight,
            feed_gate_weight,
            feed_up_weight,
            feed_down_weight,
        )
    row_slots = tensor_gather(normed_low)
    me_ref = lax.axis_index("dp").astype(jnp.int32).reshape(1)
    if whole_dp:
        mixer_full = lax.all_gather(mixer_local, "dp", axis=0, tiled=True)
        mixer_rows = jnp.concatenate(row_slots)
        out_full = mixer_full[:, out_start:]
        mixer_full = mixer_full[:, :out_start]
        raw = product(mixer_rows, mixer_full)
    else:
        near_full = dp_pieces(mixer_local)
        near_full, row_slots = tie(near_full, row_slots)
        far_full = swap(near_full, "dp", 1)
    row_slots, feed_local, cot_block = tie(row_slots, feed_local, out_cotangent)
    cotangent = lax.all_gather(cot_block, "tensor", axis=0, tiled=True)
    feed_full = lax.all_gather(feed_local, "dp", axis=0, tiled=True)
    if not whole_dp:
        mixer_rows, raw = project(me_ref, row_slots, near_full, far_full, out_start)
    length = mixer_rows.shape[0]
    block = length // parts

    taps = jnp.concatenate(
        [
            jnp.concatenate([conv_weight, conv_bias[None]]),
            jnp.concatenate([pair_conv_weight, pair_conv_bias[None]]),
        ],
        axis=1,
    )
    taps = jnp.pad(taps, ((0, 3), (0, 0)))
    heads = jnp.pad(
        jnp.stack([step_bias, -jnp.exp(decay_log)]), ((0, 6), (0, 128 - heads_state))
    )
    skip = jnp.repeat(skip_gain, HD)[None]
    angles = jnp.asarray(angle_table(length))

    gated, power, conv, y, kept_states = state_forward(place_ref, raw, taps, heads, skip, states)
    mixed_low, kept, probs = attention_forward(place_ref, raw, angles)
    width_all = width * parts
    power = slot_sum(power[0])
    state_scale = lax.rsqrt(power / width_all + EPS)[:, None]
    state_low = (gated * state_scale * state_gain).astype(low)
    if whole_dp:
        total = product_right(jnp.concatenate([mixed_low, state_low], axis=1), out_full)
        own, *sends = cut(total, parts)
    else:
        own, *sends = spread_product(
            me_ref, mixed_low, state_low, near_full, far_full, out_start, parts
        )
    mixer_shard = finish_scatter(own, tensor_send(sends))
    middle = rows_in + mixer_shard
    second, second_scale = root_norm(middle, norm_ffn_gain)
    feed_slots = tensor_gather(second.astype(low))
    grad_pair, active, own, *sends = feed_forward(place_ref, feed_slots, cotangent, feed_full)
    grad_second = finish_scatter(own, tensor_send(sends))
    if whole_dp:
        cot_slots = jnp.split(cotangent, parts)
        cot_slots = jnp.concatenate(
            [lax.dynamic_index_in_dim(jnp.stack(cot_slots), place ^ at, 0, False) for at in range(parts)]
        )
        feed_both = jnp.concatenate(
            [product_left(jnp.concatenate(feed_slots), grad_pair), product_left(cot_slots, active)],
            axis=1,
        ).astype(low)
    else:
        spot_ref = jnp.concatenate([place_ref, me_ref])
        feed_both = core_sum(*feed_grad(spot_ref, feed_slots, cotangent, grad_pair, active))
    grad_second, feed_both = tie(grad_second, feed_both)

    weighted_second = grad_second * norm_ffn_gain
    inner_second = jnp.sum(weighted_second * middle, axis=-1, keepdims=True)
    grad_middle = (
        out_cotangent.astype(wide)
        + second_scale * weighted_second
        - middle * second_scale**3 * inner_second / middle.shape[-1]
    )
    ffn_gain = jnp.sum(grad_second * middle * second_scale, axis=0)
    cot_rows = tensor_gather(grad_middle.astype(low))
    feed_sums, _ = chip_sum(feed_both, after=cot_rows[1])
    cot_rows, feed_sums = tie(cot_rows, feed_sums)
    if whole_dp:
        mixer_cot = jnp.concatenate(cot_rows)
        grad_both = product(mixer_cot, out_full)
        grad_mixed, grad_state = grad_both[:, :128].astype(low), grad_both[:, 128:]
        inner_sum = jnp.sum(grad_state * state_gain * gated, axis=1)[None]
    else:
        mixer_cot, grad_mixed, grad_state, inner_sum = mixer_back(
            me_ref, cot_rows, near_full, far_full, out_start, gated, state_gain[None]
        )
    grad_mixed, active = tie(grad_mixed, active)
    weighted = grad_state * state_gain
    inner_sum = slot_sum(inner_sum[0])
    grad_attention = attention_backward(place_ref, grad_mixed, angles, kept, probs)
    early_terms = early_grad(
        place_ref, mixer_cot, mixed_low, state_low, mixer_rows, grad_attention
    )
    feed_own, *sends = slot_product(place_ref, active, feed_full, 2 * units, parts)
    feed_got = tensor_send(sends)
    early_terms, inner_sum, grad_attention = tie(early_terms, inner_sum, grad_attention)
    early_sums = lax.psum_scatter(early_terms, "dp", scatter_dimension=0, tiled=True)
    grad_gated = (
        state_scale * weighted - gated * state_scale**3 * (inner_sum / width_all)[:, None]
    )
    grad_state_gain = jnp.sum(grad_state * gated * state_scale, axis=0)
    grad_mixer, grad_taps, grad_heads = state_backward(
        place_ref, raw, conv, y, kept_states, grad_gated, taps, heads, skip
    )
    grad_pair = grad_attention[:, 128:]
    grad_mixer, feed_got = tie(grad_mixer, feed_got)
    hidden_out = (middle + finish_scatter(feed_own, feed_got)).astype(low)
    if whole_dp:
        total_rows = product_right(grad_mixer, mixer_full[:, 256:]) + product_right(
            grad_attention, mixer_full[:, :256]
        )
        gain_rows = jnp.sum(total_rows * mixer_rows.astype(wide), axis=0, keepdims=True)
        own, *sends = cut(total_rows, parts)
    else:
        gain_rows, own, *sends = total_product(
            me_ref, grad_attention, grad_mixer, near_full, far_full, mixer_rows, parts
        )
    own, grad_mixer = tie(own, grad_mixer)
    late_terms = weight_sum(me_ref, [(mixer_rows, (grad_pair, grad_mixer))])
    first_got = tensor_send(sends)
    in_gain = gain_rows[0] / norm_in_gain

    columns = late_terms.shape[-1]
    small = [
        in_gain,
        ffn_gain,
        grad_taps[:4, width:].reshape(-1),
        grad_taps[4, width:],
        grad_taps[:4, :width].reshape(-1),
        grad_taps[4, :width],
        grad_state_gain,
        grad_heads[0, :heads_state],
        grad_heads[1, :heads_state],
        grad_heads[2, :heads_state],
    ]
    sizes = [item.shape[0] for item in small]
    flat = jnp.concatenate(small)
    small_rows = -(-flat.shape[0] // (16 * columns)) * 16
    flat = jnp.pad(flat, (0, small_rows * columns - flat.shape[0])).reshape(small_rows, columns)
    late_sums, flat = chip_sum(late_terms, flat)
    early_sums = early_sums.astype(wide)
    done = (
        hidden_out,
        early_sums[:, 128 + width : 128 + width + 128],
        early_sums[:, :128].T,
        early_sums[:, 128 : 128 + width].T,
        feed_sums[:, :units],
        feed_sums[:, units : 2 * units],
        feed_sums[:, 2 * units :].T,
    )
    flat = flat.reshape(-1)

    common = sum(sizes[:4])
    common_rows = -(-common // (16 * 384)) * 16
    rows_here = mixer_local.shape[0]
    shared = jnp.concatenate(
        [
            late_sums[:, :384],
            jnp.pad(flat[:common], (0, common_rows * 384 - common)).reshape(common_rows, 384),
        ]
    ).astype(low)
    near = shared.astype(wide) + swap(shared, "tensor", 1).astype(wide)
    near = near.astype(low)
    far = swap(near, "tensor", 2).astype(wide)
    near = near.astype(wide)
    both = near + far
    first_half = place < parts // 2
    head_low = jnp.where(first_half, near[:rows_here, :128], far[:rows_here, :128])
    head_high = jnp.where(first_half, far[:rows_here, :128], near[:rows_here, :128])
    common_sums = both[rows_here:].reshape(-1)
    shared = jnp.concatenate([head_low, head_high, both[:rows_here, 128:]], axis=1).astype(low)
    shared, first_got, done = tie(shared, first_got, done)
    grad_first = finish_scatter(own, first_got)
    shared = dp_gather(shared).astype(wide)
    gradient_key = jnp.concatenate([shared[:, :64], shared[:, 128:192]], axis=1)
    gradient_value = jnp.concatenate([shared[:, 64:128], shared[:, 192:256]], axis=1)

    weighted_first = grad_first * norm_in_gain
    inner_first = jnp.sum(weighted_first * rows_in, axis=-1, keepdims=True)
    gradient_hidden = (
        grad_middle
        + first_scale * weighted_first
        - rows_in * first_scale**3 * inner_first / rows_in.shape[-1]
    )

    cuts = []
    at = 0
    for index, size in enumerate(sizes):
        cuts.append((common_sums if index < 4 else flat)[at : at + size])
        at += size
    return (
        done[0],
        gradient_hidden,
        cuts[0],
        done[1],
        gradient_key,
        gradient_value,
        done[2],
        late_sums[:, 384 : 384 + width],
        late_sums[:, 384 + width : 384 + 2 * width],
        shared[:, 256:384],
        shared[:, 384:512],
        late_sums[:, 384 + 2 * width : 384 + 2 * width + heads_state],
        cuts[4].reshape(conv_weight.shape),
        cuts[5],
        cuts[2].reshape(pair_conv_weight.shape),
        cuts[3],
        cuts[7],
        cuts[8],
        cuts[9],
        cuts[6],
        done[3],
        cuts[1],
        done[4],
        done[5],
        done[6],
    )


def solution(mesh):
    placed = (
        P(("dp", "tensor"), None),
        P(),
        P("dp", "tensor"),
        P("dp", None),
        P("dp", None),
        P("tensor", "dp"),
        P("dp", "tensor"),
        P("dp", "tensor"),
        P("dp", None),
        P("dp", None),
        P("dp", "tensor"),
        P(None, "tensor"),
        P("tensor"),
        P(),
        P(),
        P("tensor"),
        P("tensor"),
        P("tensor"),
        P("tensor"),
        P("tensor", "dp"),
        P(),
        P("dp", "tensor"),
        P("dp", "tensor"),
        P("tensor", "dp"),
        P(("dp", "tensor"), None),
    )
    return jax.shard_map(
        body,
        mesh=mesh,
        in_specs=placed,
        out_specs=(
            P(("dp", "tensor"), None),
            P(("dp", "tensor"), None),
            P(),
            P("dp", "tensor"),
            P(),
            P(),
            P("tensor", "dp"),
            P("dp", "tensor"),
            P("dp", "tensor"),
            P(),
            P(),
            P("dp", "tensor"),
            P(None, "tensor"),
            P("tensor"),
            P(),
            P(),
            P("tensor"),
            P("tensor"),
            P("tensor"),
            P("tensor"),
            P("tensor", "dp"),
            P(),
            P("dp", "tensor"),
            P("dp", "tensor"),
            P("tensor", "dp"),
        ),
        check_vma=False,
    )
```

```python
import functools
import math

import jax
import jax.numpy as jnp
import numpy as np
from jax import lax
from jax.experimental import pallas as pl
from jax.experimental.pallas import tpu as pltpu
from jax.sharding import PartitionSpec as P

QH = 8
KVH = 2
HD = 64
BLOCK = 128


EPS = 1e-05
THETA = 10000.0
HIGHEST = lax.Precision.HIGHEST


def product(left, right):
    return jnp.dot(left, right, preferred_element_type=jnp.float32)


def product_left(left, right):
    return lax.dot_general(
        left, right, (((0,), (0,)), ((), ())), preferred_element_type=jnp.float32
    )


def product_right(left, right):
    return lax.dot_general(
        left, right, (((1,), (1,)), ((), ())), preferred_element_type=jnp.float32
    )


def root_norm(rows, gain):
    scale = lax.rsqrt(jnp.mean(rows * rows, axis=-1, keepdims=True) + EPS)
    return (rows * scale * gain, scale)


def dot(left, right, dims=((1,), (0,)), precision=None):
    return lax.dot_general(
        left, right, (dims, ((), ())), precision=precision, preferred_element_type=jnp.float32
    )


NN = ((1,), (0,))
NT = ((1,), (1,))
TN = ((0,), (0,))


def sigmoid(values):
    return 1.0 / (1.0 + jnp.exp(-values))


def softplus(values):
    return jnp.maximum(values, 0.0) + jnp.log1p(jnp.exp(-jnp.abs(values)))


def lane_index(rows):
    return lax.broadcasted_iota(jnp.int32, (rows, 128), 1)


def spread_heads(values, width):
    first = lane_index(values.shape[0]) < HD
    return jnp.concatenate(
        [
            jnp.where(first, values[:, at : at + 1], values[:, at + 1 : at + 2])
            for at in range(0, width // HD, 2)
        ],
        axis=1,
    )


def slot_rows(place_ref, at):
    return pl.ds(pl.multiple_of((place_ref[0] ^ at) * BLOCK, BLOCK), BLOCK)


def lower_mask():
    rows = lax.broadcasted_iota(jnp.int32, (BLOCK, BLOCK), 0)
    columns = lax.broadcasted_iota(jnp.int32, (BLOCK, BLOCK), 1)
    return rows >= columns


def block_decay(raw_steps, step_bias, rate, lower):
    step = softplus(raw_steps + step_bias)
    running = dot(lower.astype(jnp.float32), step * rate, NN, HIGHEST)
    return step, running, running.T


def block_weights(running, running_t, lower, head):
    spread = running[:, head : head + 1] - running_t[head : head + 1, :]
    return jnp.exp(jnp.where(lower, spread, -1e30))


def fill_history(place_ref, raw_ref, history_ref, blocks, width):
    history_ref[0:8, :] = jnp.zeros((8, history_ref.shape[1]), jnp.float32)
    for at in range(blocks):
        rows = slot_rows(place_ref, at)
        here = slice(8 + at * BLOCK, 8 + (at + 1) * BLOCK)
        history_ref[here, 0:width] = raw_ref[rows, 512 + width : 512 + 2 * width]
        history_ref[here, width : width + 256] = raw_ref[rows, 256:512]


def state_forward_kernel(
    place_ref,
    raw_ref,
    taps_ref,
    heads_ref,
    skip_ref,
    gated_ref,
    power_ref,
    conv_ref,
    y_ref,
    states_ref,
    history_ref,
):
    low = jnp.bfloat16
    width = gated_ref.shape[1]
    blocks = gated_ref.shape[0] // BLOCK
    fill_history(place_ref, raw_ref, history_ref, blocks, width)
    lower = lower_mask()
    first = lane_index(BLOCK) < HD
    state = jnp.zeros((states_ref.shape[1], width), jnp.float32)
    for at in range(blocks):
        rows = slot_rows(place_ref, at)
        conv = taps_ref[4:5, :]
        for tap in range(4):
            conv = conv + taps_ref[tap : tap + 1, :] * history_ref[pl.ds(5 + tap + at * BLOCK, BLOCK), :]
        conv_ref[rows, :] = conv
        acted = conv * sigmoid(conv)
        inner = acted[:, :width]
        write = acted[:, width : width + 128].astype(low)
        read = acted[:, width + 128 :].astype(low)
        step, running, running_t = block_decay(
            raw_ref[rows, 512 + 2 * width :], heads_ref[0:1, :], heads_ref[1:2, :], lower
        )
        scaled = inner * spread_heads(step, width)
        scaled_low = scaled.astype(low)
        zero = jnp.zeros((BLOCK, 128), low)
        meet = dot(read, write, NT)
        inside = []
        for pair in range(width // 128):
            both = jnp.concatenate(
                [
                    (meet * block_weights(running, running_t, lower, 2 * pair)).astype(low),
                    (meet * block_weights(running, running_t, lower, 2 * pair + 1)).astype(low),
                ],
                axis=1,
            )
            piece = scaled_low[:, pair * 128 : (pair + 1) * 128]
            split = jnp.concatenate([jnp.where(first, piece, zero), jnp.where(first, zero, piece)])
            inside.append(dot(both, split))
        earlier = dot(read, state.astype(low))
        y = jnp.concatenate(inside, axis=1) + spread_heads(jnp.exp(running), width) * earlier
        y_ref[rows, :] = y
        states_ref[at] = state
        last = running[BLOCK - 1 : BLOCK, :]
        carried = (spread_heads(jnp.exp(last - running), width) * scaled).astype(low)
        state = spread_heads(jnp.exp(last), width) * state + dot(write, carried, TN)
        gate = raw_ref[rows, 512 : 512 + width]
        gated = (y + skip_ref[0:1, :] * inner) * gate * sigmoid(gate)
        gated_ref[rows, :] = gated
        power_ref[:, rows] = dot(jnp.ones((8, width), jnp.float32), gated * gated, NT, HIGHEST)


def state_backward_kernel(
    place_ref,
    raw_ref,
    conv_ref,
    y_ref,
    states_ref,
    up_ref,
    taps_ref,
    heads_ref,
    skip_ref,
    grad_ref,
    grad_taps_ref,
    grad_heads_ref,
    history_ref,
    later_ref,
):
    low = jnp.bfloat16
    width = up_ref.shape[1]
    blocks = up_ref.shape[0] // BLOCK
    length = up_ref.shape[0]
    every = width + 256
    fill_history(place_ref, raw_ref, history_ref, blocks, width)
    later_ref[length : length + 8, :] = jnp.zeros((8, every), jnp.float32)
    lower = lower_mask()
    first = lane_index(BLOCK) < HD
    zero = jnp.zeros((BLOCK, 128), low)
    picks = (
        lax.broadcasted_iota(jnp.int32, (width, 128), 0) // HD
        == lax.broadcasted_iota(jnp.int32, (width, 128), 1)
    ).astype(jnp.float32)
    skip = skip_ref[0:1, :]
    rate = heads_ref[1:2, :]
    grad_state = jnp.zeros((states_ref.shape[1], width), jnp.float32)
    grad_taps = [jnp.zeros((1, every), jnp.float32) for _ in range(5)]
    grad_bias = jnp.zeros((1, 128), jnp.float32)
    grad_decay = jnp.zeros((1, 128), jnp.float32)
    grad_skip = jnp.zeros((1, width), jnp.float32)
    for at in reversed(range(blocks)):
        rows = slot_rows(place_ref, at)
        gate = raw_ref[rows, 512 : 512 + width]
        gate_sigma = sigmoid(gate)
        conv = conv_ref[rows, :]
        conv_sigma = sigmoid(conv)
        acted = conv * conv_sigma
        inner = acted[:, :width]
        write = acted[:, width : width + 128].astype(low)
        read = acted[:, width + 128 :].astype(low)
        y = y_ref[rows, :]
        up = up_ref[rows, :]
        grad_gate = up * (y + skip * inner) * gate_sigma * (1.0 + gate * (1.0 - gate_sigma))
        grad_ref[rows, 256 : 256 + width] = grad_gate.astype(low)
        grad_y = up * gate * gate_sigma
        raw_steps = raw_ref[rows, 512 + 2 * width :]
        step, running, running_t = block_decay(raw_steps, heads_ref[0:1, :], rate, lower)
        step_wide = spread_heads(step, width)
        grow = spread_heads(jnp.exp(running), width)
        last = running[BLOCK - 1 : BLOCK, :]
        carry = spread_heads(jnp.exp(last - running), width)
        last_wide = spread_heads(jnp.exp(last), width)
        scaled = inner * step_wide
        scaled_low = scaled.astype(low)
        grad_low = grad_y.astype(low)
        grown_low = (grad_y * grow).astype(low)
        state = states_ref[at]
        state_low = state.astype(low)
        grad_state_low = grad_state.astype(low)
        meet = dot(read, write, NT)
        grad_meet = jnp.zeros((BLOCK, BLOCK), jnp.float32)
        inside = []
        for pair in range(width // 128):
            weights = [
                block_weights(running, running_t, lower, head) for head in (2 * pair, 2 * pair + 1)
            ]
            both = jnp.concatenate([(meet * item).astype(low) for item in weights], axis=0)
            piece = grad_low[:, pair * 128 : (pair + 1) * 128]
            split = jnp.concatenate([jnp.where(first, piece, zero), jnp.where(first, zero, piece)])
            grad_both = dot(split, scaled_low[:, pair * 128 : (pair + 1) * 128], NT)
            grad_meet = (
                grad_meet + grad_both[:BLOCK] * weights[0] + grad_both[BLOCK:] * weights[1]
            )
            inside.append(dot(both, split, TN))
        grad_inside = jnp.concatenate(inside, axis=1)
        from_state = carry * dot(write, grad_state_low)
        carried = carry * scaled
        grad_scaled = grad_inside + from_state
        moved = scaled * from_state
        turn = grad_low.astype(jnp.float32) * y - scaled_low.astype(jnp.float32) * grad_inside - moved
        direct = grad_y * inner
        ends = jnp.sum(moved, axis=0, keepdims=True) + last_wide * jnp.sum(
            state * grad_state, axis=0, keepdims=True
        )
        summed = dot(
            jnp.concatenate([turn, grad_scaled * inner, jnp.broadcast_to(ends, (8, width))]),
            picks,
            NN,
            HIGHEST,
        )
        grad_running = (
            dot(lower.astype(jnp.float32), summed[:BLOCK], TN, HIGHEST)
            + summed[2 * BLOCK : 2 * BLOCK + 1]
        )
        grad_step = grad_running * rate + summed[BLOCK : 2 * BLOCK]
        grad_decay = grad_decay + jnp.sum(grad_running * step * rate, axis=0, keepdims=True)
        grad_steps = grad_step * sigmoid(raw_steps + heads_ref[0:1, :])
        grad_bias = grad_bias + jnp.sum(grad_steps, axis=0, keepdims=True)
        grad_skip = grad_skip + jnp.sum(direct, axis=0, keepdims=True)
        grad_ref[rows, 256 + 2 * width :] = grad_steps.astype(low)
        grad_inner = grad_scaled * step_wide + skip * grad_y
        grad_meet_low = grad_meet.astype(low)
        grad_read = dot(grad_meet_low, write) + dot(grown_low, state_low, NT)
        grad_write = dot(grad_meet_low, read, TN) + dot(carried.astype(low), grad_state_low, NT)
        grad_state = last_wide * grad_state + dot(read, grown_low, TN)
        grad_conv = jnp.concatenate([grad_inner, grad_write, grad_read], axis=1) * (
            conv_sigma * (1.0 + conv * (1.0 - conv_sigma))
        )
        later_ref[at * BLOCK : (at + 1) * BLOCK, :] = grad_conv
        back = jnp.zeros((BLOCK, every), jnp.float32)
        for tap in range(4):
            back = back + taps_ref[tap : tap + 1, :] * later_ref[pl.ds(at * BLOCK + 3 - tap, BLOCK), :]
            seen = history_ref[pl.ds(5 + tap + at * BLOCK, BLOCK), :]
            grad_taps[tap] = grad_taps[tap] + jnp.sum(grad_conv * seen, axis=0, keepdims=True)
        grad_taps[4] = grad_taps[4] + jnp.sum(grad_conv, axis=0, keepdims=True)
        grad_ref[rows, 256 + width : 256 + 2 * width] = back[:, :width].astype(low)
        grad_ref[rows, 0:256] = back[:, width:].astype(low)
    for tap in range(5):
        grad_taps_ref[tap : tap + 1, :] = grad_taps[tap]
    grad_taps_ref[5:8, :] = jnp.zeros((3, every), jnp.float32)
    skip_heads = dot(jnp.broadcast_to(grad_skip, (8, width)), picks, NN, HIGHEST)
    grad_heads_ref[...] = jnp.zeros(grad_heads_ref.shape, jnp.float32)
    grad_heads_ref[0:1, :] = grad_bias
    grad_heads_ref[1:2, :] = grad_decay
    grad_heads_ref[2:3, :] = skip_heads[0:1]


def turned(values, cosine, sine):
    early = lane_index(values.shape[0]) % HD < HD // 2
    other = jnp.where(early, pltpu.roll(values, 128 - HD // 2, 1), pltpu.roll(values, HD // 2, 1))
    return values * cosine + other * sine


def both_heads(values, first):
    zero = jnp.zeros(values.shape, values.dtype)
    return jnp.concatenate([jnp.where(first, values, zero), jnp.where(first, zero, values)])


def attention_forward_kernel(
    place_ref, raw_ref, angle_ref, mixed_ref, kept_ref, probs_ref
):
    low = jnp.bfloat16
    blocks = mixed_ref.shape[0] // BLOCK
    first = lane_index(BLOCK) < HD
    for at in range(blocks):
        rows = slot_rows(place_ref, at)
        here = slice(at * BLOCK, (at + 1) * BLOCK)
        cosine = angle_ref[here, 0:128]
        sine = angle_ref[here, 128:256]
        pair = raw_ref[rows, 128:256]
        key = turned(pair, cosine, sine)
        kept_ref[here, 0:128] = turned(raw_ref[rows, 0:128], cosine, sine).astype(low)
        kept_ref[here, 128:256] = jnp.where(first, key, pltpu.roll(key, HD, 1)).astype(low)
        kept_ref[here, 256:384] = jnp.where(first, pltpu.roll(pair, HD, 1), pair).astype(low)
    for at in range(blocks):
        rows = slot_rows(place_ref, at)
        here = slice(at * BLOCK, (at + 1) * BLOCK)
        reach = (at + 1) * BLOCK
        query = both_heads(kept_ref[here, 0:128], first)
        scores = dot(query, kept_ref[0:reach, 128:256], NT) * (HD ** (-0.5))
        row = lax.broadcasted_iota(jnp.int32, (2 * BLOCK, reach), 0) % BLOCK + at * BLOCK
        column = lax.broadcasted_iota(jnp.int32, (2 * BLOCK, reach), 1)
        scores = jnp.where(row >= column, scores, -1e30)
        exponent = jnp.exp(scores - jnp.max(scores, axis=1, keepdims=True))
        probs = (exponent / jnp.sum(exponent, axis=1, keepdims=True)).astype(low)
        probs_ref[at, :, 0:reach] = probs
        out = dot(probs, kept_ref[0:reach, 256:384])
        mixed_ref[rows, :] = jnp.where(first, out[:BLOCK], out[BLOCK:]).astype(low)


def attention_backward_kernel(
    place_ref, up_ref, angle_ref, kept_ref, probs_ref, grad_ref, key_ref, value_ref
):
    low = jnp.bfloat16
    blocks = up_ref.shape[0] // BLOCK
    first = lane_index(BLOCK) < HD
    scale = HD ** (-0.5)
    key_ref[...] = jnp.zeros(key_ref.shape, jnp.float32)
    value_ref[...] = jnp.zeros(value_ref.shape, jnp.float32)
    for at in range(blocks):
        rows = slot_rows(place_ref, at)
        here = slice(at * BLOCK, (at + 1) * BLOCK)
        reach = (at + 1) * BLOCK
        query = both_heads(kept_ref[here, 0:128], first)
        up = both_heads(up_ref[rows, :], first)
        probs_low = probs_ref[at, :, 0:reach]
        probs = probs_low.astype(jnp.float32)
        grad_probs = dot(up, kept_ref[0:reach, 256:384], NT)
        inner = jnp.sum(probs * grad_probs, axis=1, keepdims=True)
        grad_scores = (probs * (grad_probs - inner)).astype(low)
        both = dot(grad_scores, kept_ref[0:reach, 128:256]) * scale
        grad_query = jnp.where(first, both[:BLOCK], both[BLOCK:])
        grad_ref[rows, 0:128] = turned(
            grad_query, angle_ref[here, 0:128], -angle_ref[here, 128:256]
        ).astype(low)
        key_ref[0:reach, :] += dot(grad_scores, query, TN)
        value_ref[0:reach, :] += dot(probs_low, up, TN)
    for at in range(blocks):
        rows = slot_rows(place_ref, at)
        here = slice(at * BLOCK, (at + 1) * BLOCK)
        key = key_ref[here, :]
        value = value_ref[here, :]
        key = (key + pltpu.roll(key, HD, 1)) * scale
        key = turned(key, angle_ref[here, 0:128], -angle_ref[here, 128:256])
        value = value + pltpu.roll(value, HD, 1)
        grad_ref[rows, 128:256] = jnp.where(first, key, value).astype(low)


def angle_table(length):
    half = HD // 2
    freq = THETA ** (-np.arange(half, dtype=np.float32) / half)
    angle = np.arange(length, dtype=np.float32)[:, None] * freq[None, :]
    cosine = np.tile(np.cos(angle), (1, 4))
    sine = np.tile(np.concatenate([-np.sin(angle), np.sin(angle)], axis=1), (1, 2))
    return np.concatenate([cosine, sine], axis=1).astype(np.float32)


def run_kernel(kernel, place, operands, outs, scratch, name, flops=2e8):
    whole = pl.BlockSpec(memory_space=pltpu.VMEM)
    held = sum(item.size * item.dtype.itemsize for item in operands)
    held += sum(math.prod(shape) * jnp.dtype(dtype).itemsize for shape, dtype in outs)
    held += sum(math.prod(item.shape) * jnp.dtype(item.dtype).itemsize for item in scratch)
    return pl.pallas_call(
        kernel,
        out_shape=[jax.ShapeDtypeStruct(shape, dtype) for shape, dtype in outs],
        in_specs=[pl.BlockSpec(memory_space=pltpu.SMEM)] + [whole] * len(operands),
        out_specs=[whole] * len(outs),
        scratch_shapes=scratch,
        compiler_params=pltpu.CompilerParams(vmem_limit_bytes=held + 8 * 2**20),
        cost_estimate=pl.CostEstimate(flops=int(flops), bytes_accessed=1 << 20, transcendentals=0),
        name=name,
    )(place, *operands)


def state_forward(place, raw, taps, heads, skip, states):
    length = raw.shape[0]
    width = skip.shape[1]
    wide = jnp.float32
    return run_kernel(
        state_forward_kernel,
        place,
        (raw, taps, heads, skip),
        [
            ((length, width), wide),
            ((8, length), wide),
            ((length, width + 256), wide),
            ((length, width), wide),
            ((length // BLOCK, states, width), wide),
        ],
        [pltpu.VMEM((length + 8, width + 256), wide)],
        "state_forward",
    )


def state_backward(place, raw, conv, y, states, up, taps, heads, skip):
    length = raw.shape[0]
    width = skip.shape[1]
    wide = jnp.float32
    return run_kernel(
        state_backward_kernel,
        place,
        (raw, conv, y, states, up, taps, heads, skip),
        [
            ((length, 256 + 2 * width + 128), jnp.bfloat16),
            ((8, width + 256), wide),
            ((8, 128), wide),
        ],
        [pltpu.VMEM((length + 8, width + 256), wide), pltpu.VMEM((length + 8, width + 256), wide)],
        "state_backward",
    )


def attention_forward(place, raw, angles):
    length = raw.shape[0]
    low = jnp.bfloat16
    return run_kernel(
        attention_forward_kernel,
        place,
        (raw, angles),
        [
            ((length, 128), low),
            ((length, 384), low),
            ((length // BLOCK, 2 * BLOCK, length), low),
        ],
        [],
        "attention_forward",
    )


def attention_backward(place, up, angles, kept, probs):
    length = up.shape[0]
    return run_kernel(
        attention_backward_kernel,
        place,
        (up, angles, kept, probs),
        [((length, 256), jnp.bfloat16)],
        [pltpu.VMEM((length, 128), jnp.float32), pltpu.VMEM((length, 128), jnp.float32)],
        "attention_backward",
    )[0]


def block_columns(me_ref, mask):
    return pl.ds(pl.multiple_of((me_ref[0] ^ mask) * 128, 128), 128)


def join_rows(slots, whole_ref):
    rows = slots[0].shape[0]
    for at, slot in enumerate(slots):
        whole_ref[at * rows : (at + 1) * rows, :] = slot[...]


def pack_kernel(
    head_ref,
    rows_ref,
    gain_ref,
    query_ref,
    key_ref,
    value_ref,
    write_ref,
    read_ref,
    gate_ref,
    inner_ref,
    step_ref,
    output_ref,
    state_ref,
    feed_gate_ref,
    feed_up_ref,
    feed_down_ref,
    normed_ref,
    mixer_ref,
    feed_ref,
):
    rows = rows_ref[...].astype(jnp.float32)
    scale = lax.rsqrt(jnp.mean(rows * rows, axis=1, keepdims=True) + EPS)
    normed_ref[...] = (rows * scale * gain_ref[0:1, :]).astype(normed_ref.dtype)

    def turned_over(ref):
        return ref[...].astype(jnp.float32).T.astype(mixer_ref.dtype)

    low_head = head_ref[0] == 0
    first = lane_index(rows.shape[0]) < HD
    key = key_ref[...].astype(jnp.float32)
    value = value_ref[...].astype(jnp.float32)
    key = jnp.where(low_head, key, pltpu.roll(key, HD, 1))
    value = jnp.where(low_head, pltpu.roll(value, HD, 1), value)
    mixer_ref[:, 0:128] = query_ref[...]
    mixer_ref[:, 128:256] = jnp.where(first, key, value).astype(mixer_ref.dtype)
    mixer_ref[:, 256:384] = write_ref[...]
    mixer_ref[:, 384:512] = read_ref[...]
    at = 512
    for ref in (gate_ref, inner_ref):
        mixer_ref[:, at : at + ref.shape[1]] = ref[...]
        at += ref.shape[1]
    mixer_ref[:, at : at + 128] = jnp.zeros((rows.shape[0], 128), mixer_ref.dtype)
    mixer_ref[:, at : at + step_ref.shape[1]] = step_ref[...]
    mixer_ref[:, at + 128 : at + 256] = turned_over(output_ref)
    mixer_ref[:, at + 256 :] = turned_over(state_ref)
    units = feed_gate_ref.shape[1]
    feed_ref[:, :units] = feed_gate_ref[...]
    feed_ref[:, units : 2 * units] = feed_up_ref[...]
    feed_ref[:, 2 * units :] = turned_over(feed_down_ref)


def gather_columns(me_ref, rows_ref, side, chips):
    return jnp.concatenate(
        [rows_ref[:, block_columns(me_ref, 2 * at + side)] for at in range(chips)], axis=1
    )


def project_kernel(me_ref, *refs):
    slots, (near_ref, far_ref, rows_ref, raw_ref) = refs[:-4], refs[-4:]
    join_rows(slots, rows_ref)
    chips = near_ref.shape[0] // 128
    columns = raw_ref.shape[1]
    raw_ref[...] = dot(
        gather_columns(me_ref, rows_ref, 0, chips), near_ref[:, :columns]
    ) + dot(gather_columns(me_ref, rows_ref, 1, chips), far_ref[:, :columns])


def write_spread(total, own_ref, sends):
    rows = own_ref.shape[0]
    own_ref[...] = total[:rows]
    for at, send in enumerate(sends):
        send[...] = total[(at + 1) * rows : (at + 2) * rows].astype(jnp.bfloat16)


def spread_kernel(start, me_ref, mixed_ref, state_ref, near_ref, far_ref, own_ref, *rest):
    sends, total_ref = rest[:-1], rest[-1]
    left = jnp.concatenate([mixed_ref[...], state_ref[...]], axis=1)
    spread_total(me_ref, left, near_ref, far_ref, slice(start, start + left.shape[1]), total_ref)
    write_spread(total_ref[...], own_ref, sends)


def spread_total(me_ref, left, near_ref, far_ref, columns, total_ref):
    chips = near_ref.shape[0] // 128
    for side, weight_ref in enumerate((near_ref, far_ref)):
        piece = dot(left, weight_ref[:, columns], NT)
        for at in range(chips):
            total_ref[:, block_columns(me_ref, 2 * at + side)] = piece[:, at * 128 : (at + 1) * 128]


def ordered_kernel(start, place_ref, left_ref, weight_ref, out_ref):
    total = dot(left_ref[...], weight_ref[:, start : start + left_ref.shape[1]], NT)
    for at in range(total.shape[0] // BLOCK):
        out_ref[slot_rows(place_ref, at), :] = total[at * BLOCK : (at + 1) * BLOCK].astype(
            out_ref.dtype
        )


def total_kernel(
    spot_ref, attention_ref, mixer_ref, near_ref, far_ref, rows_ref, gain_ref, out_ref, total_ref
):
    left = jnp.concatenate([attention_ref[...], mixer_ref[...]], axis=1)
    spread_total(spot_ref.at[1:2], left, near_ref, far_ref, slice(0, left.shape[1]), total_ref)
    total = total_ref[...]
    gain_ref[...] = jnp.broadcast_to(
        jnp.sum(total * rows_ref[...].astype(jnp.float32), axis=0, keepdims=True), gain_ref.shape
    )
    for at in range(total.shape[0] // BLOCK):
        out_ref[slot_rows(spot_ref, at), :] = total[at * BLOCK : (at + 1) * BLOCK].astype(
            out_ref.dtype
        )


def feed_kernel(place_ref, *refs):
    low = jnp.bfloat16
    slots, cots_ref = refs[:4], refs[4]
    feed_ref, pair_ref, active_ref, own_ref = refs[5:9]
    sends = refs[9:12]
    units = active_ref.shape[1]
    rows = slots[0].shape[0]
    for half in range(2):
        here = slice(2 * half * rows, 2 * (half + 1) * rows)
        left = jnp.concatenate([slots[2 * half][...], slots[2 * half + 1][...]])
        cot = jnp.concatenate([cots_ref[slot_rows(place_ref, 2 * half + at), :] for at in range(2)])
        gate_up = dot(left, feed_ref[:, : 2 * units])
        grad_active = dot(cot, feed_ref[:, 2 * units :])
        gate = gate_up[:, :units]
        up = gate_up[:, units:]
        sigma = sigmoid(gate)
        swish = gate * sigma
        active_ref[here, :] = (swish * up).astype(low)
        grad_gate = grad_active * up * sigma * (1.0 + gate * (1.0 - sigma))
        pair = jnp.concatenate([grad_gate, grad_active * swish], axis=1).astype(low)
        pair_ref[here, :] = pair
        total = dot(pair, feed_ref[:, : 2 * units], NT)
        if half == 0:
            own_ref[...] = total[:rows]
            sends[0][...] = total[rows:].astype(low)
        else:
            sends[1][...] = total[:rows].astype(low)
            sends[2][...] = total[rows:].astype(low)


def write_halves(piece, even, keep_ref, give_ref, chip):
    piece = piece.astype(keep_ref.dtype)
    keep_ref[chip] = jnp.where(even, piece[:128], piece[128:])
    give_ref[chip] = jnp.where(even, piece[128:], piece[:128])


def feed_grad_kernel(place_ref, *refs):
    slots, cots_ref = refs[:4], refs[4]
    pair_ref, active_ref, out_ref, rows_ref, cot_ref = refs[5:]
    join_rows(slots, rows_ref)
    for at in range(len(slots)):
        cot_ref[at * BLOCK : (at + 1) * BLOCK, :] = cots_ref[slot_rows(place_ref, at), :]
    both = pair_ref.shape[1]
    for at in range(0, rows_ref.shape[1], 256):
        here = slice(at, at + 256)
        out_ref[here, :both] = dot(rows_ref[:, here], pair_ref[...], TN).astype(out_ref.dtype)
        out_ref[here, both:] = dot(cot_ref[:, here], active_ref[...], TN).astype(out_ref.dtype)


def core_add_kernel(me_ref, *refs):
    outs = refs[-4:]
    chip = me_ref[0] // 2
    keep_ref, got_ref = refs[:2]
    rows = keep_ref.shape[1]
    for mask, out in enumerate(outs):
        at = chip ^ mask
        total = keep_ref[at].astype(jnp.float32) + got_ref[at].astype(jnp.float32)
        out[0:rows, :] = total.astype(out.dtype)
        if len(refs) > 6:
            total = refs[2][...].astype(jnp.float32) + refs[3][...].astype(jnp.float32)
            out[rows:, :] = total.astype(out.dtype)


def finish_kernel(layout, place_ref, *refs):
    terms, outs = refs[: len(refs) - len(layout)], refs[len(refs) - len(layout) :]
    total = paired_sum([item[...].astype(jnp.float32) for item in terms])
    for (start, stop, over), out in zip(layout, outs):
        piece = total[:, start:stop]
        out[...] = piece.T if over else piece


def assemble_kernel(me_ref, near_ref, far_ref, key_ref, value_ref, write_ref, read_ref):
    wide = jnp.float32
    rows = 128
    first = lane_index(rows) < HD
    for side, ref in enumerate((near_ref, far_ref)):
        for chip in range(near_ref.shape[0] // rows):
            here = slice(chip * rows, (chip + 1) * rows)
            there = pl.ds(pl.multiple_of((me_ref[0] ^ (2 * chip + side)) * rows, rows), rows)
            low_head = ref[here, 0:128].astype(wide)
            high_head = ref[here, 128:256].astype(wide)
            key_ref[there, :] = jnp.where(first, low_head, pltpu.roll(high_head, HD, 1))
            value_ref[there, :] = jnp.where(first, pltpu.roll(low_head, HD, 1), high_head)
            write_ref[there, :] = ref[here, 256:384].astype(wide)
            read_ref[there, :] = ref[here, 384:512].astype(wide)


def weight_grad_kernel(groups, me_ref, *refs):
    keep_ref, give_ref = refs[-2:]
    even = me_ref[0] % 2 == 0
    for chip in range(keep_ref.shape[0]):
        here = slice(chip * 256, (chip + 1) * 256)
        pieces = []
        at = 0
        for count in groups:
            left = refs[at][:, here]
            right = jnp.concatenate([item[...] for item in refs[at + 1 : at + 1 + count]], axis=1)
            pieces.append(dot(left, right, TN))
            at += 1 + count
        write_halves(jnp.concatenate(pieces, axis=1), even, keep_ref, give_ref, chip)


def mixer_back_kernel(start, me_ref, *refs):
    slots = refs[:4]
    near_ref, far_ref, gated_ref, gain_ref, cot_ref, mixed_ref, state_ref, inner_ref = refs[4:]
    join_rows(slots, cot_ref)
    chips = near_ref.shape[0] // 128
    both = dot(gather_columns(me_ref, cot_ref, 0, chips), near_ref[:, start:]) + dot(
        gather_columns(me_ref, cot_ref, 1, chips), far_ref[:, start:]
    )
    mixed_ref[...] = both[:, :128].astype(jnp.bfloat16)
    state = both[:, 128:]
    state_ref[...] = state
    product_rows = state * gain_ref[0:1, :] * gated_ref[...]
    inner_ref[...] = dot(
        jnp.ones((8, product_rows.shape[1]), jnp.float32), product_rows, NT, HIGHEST
    )


def pack(head, hidden, gain, *weights):
    rows, columns = hidden.shape
    low = jnp.bfloat16
    width = weights[5].shape[1]
    units = weights[-3].shape[1]
    return run_kernel(
        pack_kernel,
        head,
        (hidden, gain, *weights),
        [((rows, columns), low), ((rows, 768 + 3 * width), low), ((rows, 3 * units), low)],
        [],
        "pack",
    )


def project(me, slots, near, far, columns):
    length = len(slots) * slots[0].shape[0]
    return run_kernel(
        project_kernel,
        me,
        (*slots, near, far),
        [((length, slots[0].shape[1]), jnp.bfloat16), ((length, columns), jnp.float32)],
        [],
        "project",
    )


def spread_outs(rows, columns, parts):
    return [((rows, columns), jnp.float32)] + [((rows, columns), jnp.bfloat16)] * (parts - 1)


def spread_product(me, mixed, state, near, far, start, parts):
    length, columns = mixed.shape[0], 2 * near.shape[0]
    return run_kernel(
        functools.partial(spread_kernel, start),
        me,
        (mixed, state, near, far),
        spread_outs(length // parts, columns, parts),
        [pltpu.VMEM((length, columns), jnp.float32)],
        "spread_product",
    )


def ordered_product(place, left, weight, start):
    return run_kernel(
        functools.partial(ordered_kernel, start),
        place,
        (left, weight),
        [((left.shape[0], weight.shape[0]), jnp.bfloat16)],
        [],
        "ordered_product",
    )[0]


def total_product(spot, attention, mixer, near, far, rows):
    length, columns = rows.shape
    return run_kernel(
        total_kernel,
        spot,
        (attention, mixer, near, far, rows),
        [((8, columns), jnp.float32), ((length, columns), jnp.bfloat16)],
        [pltpu.VMEM((length, columns), jnp.float32)],
        "total_product",
    )


def feed_forward(place, slots, cotangent, feed):
    rows, columns = slots[0].shape
    units = feed.shape[1] // 3
    parts = len(slots)
    return run_kernel(
        feed_kernel,
        place,
        (*slots, cotangent, feed),
        [((parts * rows, 2 * units), jnp.bfloat16), ((parts * rows, units), jnp.bfloat16)]
        + spread_outs(rows, columns, parts),
        [],
        "feed_forward",
    )


def feed_grad(place, slots, cotangent, pair, active):
    length, columns = pair.shape[0], slots[0].shape[1]
    scratch = pltpu.VMEM((length, columns), jnp.bfloat16)
    return run_kernel(
        feed_grad_kernel,
        place,
        (*slots, cotangent, pair, active),
        [((columns, pair.shape[1] + active.shape[1]), jnp.bfloat16)],
        [scratch, scratch],
        "feed_grad",
    )[0]


def weight_grad(me, groups):
    counts = tuple(len(rights) for _, rights in groups)
    columns = sum(item.shape[1] for _, rights in groups for item in rights)
    operands = [item for left, rights in groups for item in (left, *rights)]
    blocks = groups[0][0].shape[1] // 256
    return run_kernel(
        functools.partial(weight_grad_kernel, counts),
        me,
        operands,
        [((blocks, 128, columns), jnp.bfloat16)] * 2,
        [],
        "weight_grad",
    )


def core_add(me, operands):
    keep = operands[0]
    rows = keep.shape[1] + (operands[2].shape[0] if len(operands) > 2 else 0)
    return run_kernel(
        core_add_kernel,
        me,
        operands,
        [((rows, keep.shape[2]), jnp.bfloat16)] * 4,
        [],
        "core_add",
    )


def finish(place, terms, layout):
    rows = terms[0].shape[0]
    if rows != 128:
        total = terms[0].astype(jnp.float32)
        pieces = [total[:, start:stop] for start, stop, _ in layout]
        return [item.T if over else item for item, (_, _, over) in zip(pieces, layout)]
    shapes = [
        ((stop - start, rows) if over else (rows, stop - start), jnp.float32)
        for start, stop, over in layout
    ]
    return run_kernel(
        functools.partial(finish_kernel, layout), place, terms, shapes, [], "finish"
    )


def assemble(me, near, far):
    rows = 2 * near.shape[0]
    return run_kernel(
        assemble_kernel, me, (near, far), [((rows, 128), jnp.float32)] * 4, [], "assemble"
    )


def mixer_back(me, slots, near, far, start, gated, gain):
    rows, columns = slots[0].shape
    length = len(slots) * rows
    width = gated.shape[1]
    return run_kernel(
        functools.partial(mixer_back_kernel, start),
        me,
        (*slots, near, far, gated, gain),
        [
            ((length, columns), jnp.bfloat16),
            ((length, 128), jnp.bfloat16),
            ((length, width), jnp.float32),
            ((8, length), jnp.float32),
        ],
        [],
        "mixer_back",
    )


def swap(values, axis, mask):
    size = lax.axis_size(axis)
    return lax.ppermute(values, axis, [(index, index ^ mask) for index in range(size)])


def tensor_gather(block):
    masks = reversed(range(1, lax.axis_size("tensor")))
    return [block] + [swap(block, "tensor", mask) for mask in masks][::-1]


def paired_sum(terms):
    while len(terms) > 1:
        terms = [terms[at] + terms[at + 1] for at in range(0, len(terms), 2)]
    return terms[0]


def tensor_send(sends):
    return [swap(item, "tensor", at + 1) for at, item in enumerate(sends)]


def finish_scatter(own, got):
    return paired_sum([own] + [item.astype(jnp.float32) for item in got])


def cut(total, parts):
    blocks = jnp.split(total, parts)
    return blocks[:1] + [item.astype(jnp.bfloat16) for item in blocks[1:]]


def slot_sum(values):
    parts = lax.axis_size("tensor")
    shaped = values.reshape(parts, -1)
    terms = [shaped]
    for mask in range(1, parts):
        got = swap(shaped, "tensor", mask)
        terms.append(jnp.stack([got[at ^ mask] for at in range(parts)]))
    return paired_sum(terms).reshape(-1)


def tie(*values):
    return lax.optimization_barrier(values)


def dp_pieces(block):
    mine = jnp.stack([block] + [swap(block, "dp", 2 * chip) for chip in range(1, 4)])
    return mine.reshape(-1, block.shape[1])


def core_terms(me_ref, groups):
    if lax.axis_size("dp") != 8:
        return jnp.concatenate(
            [product_left(left, jnp.concatenate(rights, axis=1)) for left, rights in groups], axis=1
        ).astype(jnp.bfloat16)
    keep, give = weight_grad(me_ref, groups)
    return keep, swap(give, "dp", 1)


def chip_terms(me_ref, both, small=None, after=None):
    if lax.axis_size("dp") != 8:
        summed = lax.psum_scatter(both, "dp", scatter_dimension=0, tiled=True).astype(jnp.float32)
        if small is not None:
            summed = jnp.concatenate([summed, lax.psum(small, "dp")])
        return [summed]
    operands = both
    if small is not None:
        small = small.astype(jnp.bfloat16)
        operands = (*both, small, swap(small, "dp", 1))
    own, *sends = core_add(me_ref, operands)
    if after is not None:
        sends, _ = tie(sends, after)
    return [own] + [swap(item, "dp", 2 * (at + 1)) for at, item in enumerate(sends)]


def body(
    hidden_in,
    norm_in_gain,
    query_weight,
    key_weight,
    value_weight,
    output_weight,
    gate_weight,
    inner_weight,
    write_weight,
    read_weight,
    step_weight,
    conv_weight,
    conv_bias,
    pair_conv_weight,
    pair_conv_bias,
    step_bias,
    decay_log,
    skip_gain,
    state_gain,
    state_out_weight,
    norm_ffn_gain,
    feed_gate_weight,
    feed_up_weight,
    feed_down_weight,
    out_cotangent,
):
    low = jnp.bfloat16
    wide = jnp.float32
    parts = lax.axis_size("tensor")
    place = lax.axis_index("tensor")
    place_ref = place.astype(jnp.int32).reshape(1)
    heads_here = query_weight.shape[1] // HD
    key_head = place * heads_here // (QH // KVH)
    heads_state = step_weight.shape[1]
    width = gate_weight.shape[1]
    units = feed_gate_weight.shape[1]
    states = write_weight.shape[1]

    out_start = 640 + 2 * width
    whole_dp = lax.axis_size("dp") != 8
    rows_in = hidden_in.astype(wide)
    normed, first_scale = root_norm(rows_in, norm_in_gain)
    if whole_dp:
        normed_low = normed.astype(low)
        mixer_local = jnp.concatenate(
            [
                query_weight,
                lax.dynamic_slice_in_dim(key_weight, key_head * HD, HD, 1),
                lax.dynamic_slice_in_dim(value_weight, key_head * HD, HD, 1),
                write_weight,
                read_weight,
                gate_weight,
                inner_weight,
                jnp.pad(step_weight, ((0, 0), (0, 128 - heads_state))),
                output_weight.T,
                state_out_weight.T,
            ],
            axis=1,
        )
        feed_local = jnp.concatenate([feed_gate_weight, feed_up_weight, feed_down_weight.T], axis=1)
    else:
        normed_low, mixer_local, feed_local = pack(
            key_head.astype(jnp.int32).reshape(1),
            hidden_in,
            norm_in_gain[None],
            query_weight,
            key_weight,
            value_weight,
            write_weight,
            read_weight,
            gate_weight,
            inner_weight,
            step_weight,
            output_weight,
            state_out_weight,
            feed_gate_weight,
            feed_up_weight,
            feed_down_weight,
        )
    row_slots = tensor_gather(normed_low)
    me_ref = lax.axis_index("dp").astype(jnp.int32).reshape(1)
    spot_ref = jnp.concatenate([place_ref, me_ref])
    if whole_dp:
        mixer_full = lax.all_gather(mixer_local, "dp", axis=0, tiled=True)
        mixer_rows = jnp.concatenate(row_slots)
        out_full = mixer_full[:, out_start:]
        mixer_full = mixer_full[:, :out_start]
        raw = product(mixer_rows, mixer_full)
    else:
        near_full = dp_pieces(mixer_local)
        near_full, row_slots = tie(near_full, row_slots)
        far_full = swap(near_full, "dp", 1)
    row_slots, feed_local, cot_block = tie(row_slots, feed_local, out_cotangent)
    cotangent = lax.all_gather(cot_block, "tensor", axis=0, tiled=True)
    feed_full = lax.all_gather(feed_local, "dp", axis=0, tiled=True)
    if not whole_dp:
        mixer_rows, raw = project(me_ref, row_slots, near_full, far_full, out_start)
    length = mixer_rows.shape[0]
    block = length // parts

    taps = jnp.concatenate(
        [
            jnp.concatenate([conv_weight, conv_bias[None]]),
            jnp.concatenate([pair_conv_weight, pair_conv_bias[None]]),
        ],
        axis=1,
    )
    taps = jnp.pad(taps, ((0, 3), (0, 0)))
    heads = jnp.pad(
        jnp.stack([step_bias, -jnp.exp(decay_log)]), ((0, 6), (0, 128 - heads_state))
    )
    skip = jnp.repeat(skip_gain, HD)[None]
    angles = jnp.asarray(angle_table(length))

    gated, power, conv, y, kept_states = state_forward(place_ref, raw, taps, heads, skip, states)
    mixed_low, kept, probs = attention_forward(place_ref, raw, angles)
    width_all = width * parts
    power = slot_sum(power[0])
    state_scale = lax.rsqrt(power / width_all + EPS)[:, None]
    state_low = (gated * state_scale * state_gain).astype(low)
    if whole_dp:
        total = product_right(jnp.concatenate([mixed_low, state_low], axis=1), out_full)
        own, *sends = cut(total, parts)
    else:
        own, *sends = spread_product(
            me_ref, mixed_low, state_low, near_full, far_full, out_start, parts
        )
    mixer_shard = finish_scatter(own, tensor_send(sends))
    middle = rows_in + mixer_shard
    second, second_scale = root_norm(middle, norm_ffn_gain)
    feed_slots = tensor_gather(second.astype(low))
    grad_pair, active, own, *sends = feed_forward(place_ref, feed_slots, cotangent, feed_full)
    second_got = tensor_send(sends)
    if whole_dp:
        cot_slots = jnp.split(cotangent, parts)
        cot_slots = jnp.concatenate(
            [lax.dynamic_index_in_dim(jnp.stack(cot_slots), place ^ at, 0, False) for at in range(parts)]
        )
        feed_both = jnp.concatenate(
            [product_left(jnp.concatenate(feed_slots), grad_pair), product_left(cot_slots, active)],
            axis=1,
        ).astype(low)
    else:
        feed_both = feed_grad(place_ref, feed_slots, cotangent, grad_pair, active)
    second_got, feed_both = tie(second_got, feed_both)
    grad_second = finish_scatter(own, second_got)
    feed_sums = lax.psum_scatter(feed_both, "dp", scatter_dimension=0, tiled=True)

    weighted_second = grad_second * norm_ffn_gain
    inner_second = jnp.sum(weighted_second * middle, axis=-1, keepdims=True)
    grad_middle = (
        out_cotangent.astype(wide)
        + second_scale * weighted_second
        - middle * second_scale**3 * inner_second / middle.shape[-1]
    )
    ffn_gain = jnp.sum(grad_second * middle * second_scale, axis=0)
    cot_rows = tensor_gather(grad_middle.astype(low))
    if whole_dp:
        mixer_cot = jnp.concatenate(cot_rows)
        grad_both = product(mixer_cot, out_full)
        grad_mixed, grad_state = grad_both[:, :128].astype(low), grad_both[:, 128:]
        inner_sum = jnp.sum(grad_state * state_gain * gated, axis=1)[None]
    else:
        mixer_cot, grad_mixed, grad_state, inner_sum = mixer_back(
            me_ref, cot_rows, near_full, far_full, out_start, gated, state_gain[None]
        )
    grad_mixed, active = tie(grad_mixed, active)
    weighted = grad_state * state_gain
    inner_sum = slot_sum(inner_sum[0])
    grad_attention = attention_backward(place_ref, grad_mixed, angles, kept, probs)
    early_both = core_terms(
        me_ref, [(mixer_cot, (mixed_low, state_low)), (mixer_rows, (grad_attention,))]
    )
    active, feed_sums = tie(active, feed_sums)
    feed_terms = ordered_product(place_ref, active, feed_full, 2 * units)
    early_both, inner_sum = tie(early_both, inner_sum)
    early_parts = chip_terms(me_ref, early_both)
    grad_gated = (
        state_scale * weighted - gated * state_scale**3 * (inner_sum / width_all)[:, None]
    )
    grad_gated, feed_terms = tie(grad_gated, feed_terms)
    feed_shard = lax.psum_scatter(feed_terms, "tensor", scatter_dimension=0, tiled=True)
    grad_state_gain = jnp.sum(grad_state * gated * state_scale, axis=0)
    grad_mixer, grad_taps, grad_heads = state_backward(
        place_ref, raw, conv, y, kept_states, grad_gated, taps, heads, skip
    )
    grad_mixer, early_parts = tie(grad_mixer, early_parts)
    pair_both = core_terms(me_ref, [(mixer_rows, (grad_mixer[:, :256],))])
    if whole_dp:
        total_rows = product_right(grad_mixer, mixer_full[:, 256:]) + product_right(
            grad_attention, mixer_full[:, :256]
        )
        gain_rows = jnp.sum(total_rows * mixer_rows.astype(wide), axis=0, keepdims=True)
        total_rows = total_rows.astype(low).reshape(parts, block, -1)
        total_rows = jnp.concatenate(
            [lax.dynamic_index_in_dim(total_rows, place ^ at, 0, False) for at in range(parts)]
        )
    else:
        gain_rows, total_rows = total_product(
            spot_ref, grad_attention, grad_mixer, near_full, far_full, mixer_rows
        )
    grad_first = lax.psum_scatter(total_rows, "tensor", scatter_dimension=0, tiled=True)
    gain_rows, grad_mixer = tie(gain_rows, grad_mixer)
    late_both = core_terms(me_ref, [(mixer_rows, (grad_mixer[:, 256:],))])
    late_parts = chip_terms(me_ref, late_both)
    in_gain = gain_rows[0] / norm_in_gain

    columns = 256
    small = [
        in_gain,
        ffn_gain,
        grad_taps[:4, width:].reshape(-1),
        grad_taps[4, width:],
        grad_taps[:4, :width].reshape(-1),
        grad_taps[4, :width],
        grad_state_gain,
        grad_heads[0, :heads_state],
        grad_heads[1, :heads_state],
        grad_heads[2, :heads_state],
    ]
    sizes = [item.shape[0] for item in small]
    flat = jnp.concatenate(small)
    small_rows = -(-flat.shape[0] // (16 * columns)) * 16
    flat = jnp.pad(flat, (0, small_rows * columns - flat.shape[0])).reshape(small_rows, columns)
    pair_sums = paired_sum([item.astype(wide) for item in chip_terms(me_ref, pair_both, flat)])
    rows_here = query_weight.shape[0]
    flat = pair_sums[rows_here:].reshape(-1)
    early_done = finish(
        place_ref,
        early_parts,
        (
            (0, 128, True),
            (128, 128 + width, True),
            (128 + width, 256 + width, False),
            (256 + width, 384 + width, False),
        ),
    )

    common = sum(sizes[:4])
    common_rows = -(-common // (16 * 384)) * 16
    shared = jnp.concatenate(
        [
            jnp.concatenate([early_done[3], pair_sums[:rows_here]], axis=1),
            jnp.pad(flat[:common], (0, common_rows * 384 - common)).reshape(common_rows, 384),
        ]
    ).astype(low)
    near = shared.astype(wide) + swap(shared, "tensor", 1).astype(wide)
    near = near.astype(low)
    far = swap(near, "tensor", 2).astype(wide)
    near = near.astype(wide)
    both = near + far
    first_half = place < parts // 2
    head_low = jnp.where(first_half, near[:rows_here, :128], far[:rows_here, :128])
    head_high = jnp.where(first_half, far[:rows_here, :128], near[:rows_here, :128])
    common_sums = both[rows_here:].reshape(-1)
    shared = jnp.concatenate([head_low, head_high, both[:rows_here, 128:]], axis=1).astype(low)
    late_done = finish(
        place_ref,
        late_parts,
        ((0, width, False), (width, 2 * width, False), (2 * width, 2 * width + heads_state, False)),
    )
    hidden_out = (middle + feed_shard.astype(wide)).astype(low)
    feed_done = finish(
        place_ref,
        [feed_sums],
        ((0, units, False), (units, 2 * units, False), (2 * units, 3 * units, True)),
    )
    shared, early_done, late_done, hidden_out, feed_done = tie(
        shared, early_done, late_done, hidden_out, feed_done
    )
    if whole_dp:
        shared = lax.all_gather(shared, "dp", axis=0, tiled=True).astype(wide)
        gradient_key = jnp.concatenate([shared[:, :64], shared[:, 128:192]], axis=1)
        gradient_value = jnp.concatenate([shared[:, 64:128], shared[:, 192:256]], axis=1)
        gradient_write, gradient_read = shared[:, 256:384], shared[:, 384:512]
    else:
        near = dp_pieces(shared)
        gradient_key, gradient_value, gradient_write, gradient_read = assemble(
            me_ref, near, swap(near, "dp", 1)
        )

    grad_first = grad_first.astype(wide)
    weighted_first = grad_first * norm_in_gain
    inner_first = jnp.sum(weighted_first * rows_in, axis=-1, keepdims=True)
    gradient_hidden = (
        grad_middle
        + first_scale * weighted_first
        - rows_in * first_scale**3 * inner_first / rows_in.shape[-1]
    )

    cuts = []
    at = 0
    for index, size in enumerate(sizes):
        cuts.append((common_sums if index < 4 else flat)[at : at + size])
        at += size
    return (
        hidden_out,
        gradient_hidden,
        cuts[0],
        early_done[2],
        gradient_key,
        gradient_value,
        early_done[0],
        late_done[0],
        late_done[1],
        gradient_write,
        gradient_read,
        late_done[2],
        cuts[4].reshape(conv_weight.shape),
        cuts[5],
        cuts[2].reshape(pair_conv_weight.shape),
        cuts[3],
        cuts[7],
        cuts[8],
        cuts[9],
        cuts[6],
        early_done[1],
        cuts[1],
        feed_done[0],
        feed_done[1],
        feed_done[2],
    )


def solution(mesh):
    placed = (
        P(("dp", "tensor"), None),
        P(),
        P("dp", "tensor"),
        P("dp", None),
        P("dp", None),
        P("tensor", "dp"),
        P("dp", "tensor"),
        P("dp", "tensor"),
        P("dp", None),
        P("dp", None),
        P("dp", "tensor"),
        P(None, "tensor"),
        P("tensor"),
        P(),
        P(),
        P("tensor"),
        P("tensor"),
        P("tensor"),
        P("tensor"),
        P("tensor", "dp"),
        P(),
        P("dp", "tensor"),
        P("dp", "tensor"),
        P("tensor", "dp"),
        P(("dp", "tensor"), None),
    )
    return jax.shard_map(
        body,
        mesh=mesh,
        in_specs=placed,
        out_specs=(
            P(("dp", "tensor"), None),
            P(("dp", "tensor"), None),
            P(),
            P("dp", "tensor"),
            P(),
            P(),
            P("tensor", "dp"),
            P("dp", "tensor"),
            P("dp", "tensor"),
            P(),
            P(),
            P("dp", "tensor"),
            P(None, "tensor"),
            P("tensor"),
            P(),
            P(),
            P("tensor"),
            P("tensor"),
            P("tensor"),
            P("tensor"),
            P("tensor", "dp"),
            P(),
            P("dp", "tensor"),
            P("dp", "tensor"),
            P("tensor", "dp"),
        ),
        check_vma=False,
    )
```

```python
import functools
import math

import jax
import jax.numpy as jnp
import numpy as np
from jax import lax
from jax.experimental import pallas as pl
from jax.experimental.pallas import tpu as pltpu
from jax.sharding import PartitionSpec as P

QH = 8
KVH = 2
HD = 64
BLOCK = 128


EPS = 1e-05
THETA = 10000.0
HIGHEST = lax.Precision.HIGHEST


def product(left, right):
    return jnp.dot(left, right, preferred_element_type=jnp.float32)


def product_left(left, right):
    return lax.dot_general(
        left, right, (((0,), (0,)), ((), ())), preferred_element_type=jnp.float32
    )


def product_right(left, right):
    return lax.dot_general(
        left, right, (((1,), (1,)), ((), ())), preferred_element_type=jnp.float32
    )


def root_norm(rows, gain):
    scale = lax.rsqrt(jnp.mean(rows * rows, axis=-1, keepdims=True) + EPS)
    return (rows * scale * gain, scale)


def dot(left, right, dims=((1,), (0,)), precision=None):
    return lax.dot_general(
        left, right, (dims, ((), ())), precision=precision, preferred_element_type=jnp.float32
    )


NN = ((1,), (0,))
NT = ((1,), (1,))
TN = ((0,), (0,))


def sigmoid(values):
    return 1.0 / (1.0 + jnp.exp(-values))


def softplus(values):
    return jnp.maximum(values, 0.0) + jnp.log1p(jnp.exp(-jnp.abs(values)))


def lane_index(rows):
    return lax.broadcasted_iota(jnp.int32, (rows, 128), 1)


def spread_heads(values, width):
    first = lane_index(values.shape[0]) < HD
    return jnp.concatenate(
        [
            jnp.where(first, values[:, at : at + 1], values[:, at + 1 : at + 2])
            for at in range(0, width // HD, 2)
        ],
        axis=1,
    )


def slot_rows(place_ref, at):
    return pl.ds(pl.multiple_of((place_ref[0] ^ at) * BLOCK, BLOCK), BLOCK)


def lower_mask():
    rows = lax.broadcasted_iota(jnp.int32, (BLOCK, BLOCK), 0)
    columns = lax.broadcasted_iota(jnp.int32, (BLOCK, BLOCK), 1)
    return rows >= columns


def block_decay(raw_steps, step_bias, rate, lower):
    step = softplus(raw_steps + step_bias)
    running = dot(lower.astype(jnp.float32), step * rate, NN, HIGHEST)
    return step, running, running.T


def block_weights(running, running_t, lower, head):
    spread = running[:, head : head + 1] - running_t[head : head + 1, :]
    return jnp.exp(jnp.where(lower, spread, -1e30))


def fill_history(place_ref, raw_ref, history_ref, blocks, width):
    history_ref[0:8, :] = jnp.zeros((8, history_ref.shape[1]), jnp.float32)
    for at in range(blocks):
        rows = slot_rows(place_ref, at)
        here = slice(8 + at * BLOCK, 8 + (at + 1) * BLOCK)
        history_ref[here, 0:width] = raw_ref[rows, 512 + width : 512 + 2 * width]
        history_ref[here, width : width + 256] = raw_ref[rows, 256:512]


def state_forward_kernel(
    place_ref,
    raw_ref,
    taps_ref,
    heads_ref,
    skip_ref,
    gated_ref,
    power_ref,
    conv_ref,
    y_ref,
    states_ref,
    history_ref,
):
    low = jnp.bfloat16
    width = gated_ref.shape[1]
    blocks = gated_ref.shape[0] // BLOCK
    fill_history(place_ref, raw_ref, history_ref, blocks, width)
    lower = lower_mask()
    first = lane_index(BLOCK) < HD
    state = jnp.zeros((states_ref.shape[1], width), jnp.float32)
    for at in range(blocks):
        rows = slot_rows(place_ref, at)
        conv = taps_ref[4:5, :]
        for tap in range(4):
            conv = conv + taps_ref[tap : tap + 1, :] * history_ref[pl.ds(5 + tap + at * BLOCK, BLOCK), :]
        conv_ref[rows, :] = conv
        acted = conv * sigmoid(conv)
        inner = acted[:, :width]
        write = acted[:, width : width + 128].astype(low)
        read = acted[:, width + 128 :].astype(low)
        step, running, running_t = block_decay(
            raw_ref[rows, 512 + 2 * width :], heads_ref[0:1, :], heads_ref[1:2, :], lower
        )
        scaled = inner * spread_heads(step, width)
        scaled_low = scaled.astype(low)
        zero = jnp.zeros((BLOCK, 128), low)
        meet = dot(read, write, NT)
        inside = []
        for pair in range(width // 128):
            both = jnp.concatenate(
                [
                    (meet * block_weights(running, running_t, lower, 2 * pair)).astype(low),
                    (meet * block_weights(running, running_t, lower, 2 * pair + 1)).astype(low),
                ],
                axis=1,
            )
            piece = scaled_low[:, pair * 128 : (pair + 1) * 128]
            split = jnp.concatenate([jnp.where(first, piece, zero), jnp.where(first, zero, piece)])
            inside.append(dot(both, split))
        earlier = dot(read, state.astype(low))
        y = jnp.concatenate(inside, axis=1) + spread_heads(jnp.exp(running), width) * earlier
        y_ref[rows, :] = y
        states_ref[at] = state
        last = running[BLOCK - 1 : BLOCK, :]
        carried = (spread_heads(jnp.exp(last - running), width) * scaled).astype(low)
        state = spread_heads(jnp.exp(last), width) * state + dot(write, carried, TN)
        gate = raw_ref[rows, 512 : 512 + width]
        gated = (y + skip_ref[0:1, :] * inner) * gate * sigmoid(gate)
        gated_ref[rows, :] = gated
        power_ref[:, rows] = dot(jnp.ones((8, width), jnp.float32), gated * gated, NT, HIGHEST)


def state_backward_kernel(
    place_ref,
    raw_ref,
    conv_ref,
    y_ref,
    states_ref,
    up_ref,
    taps_ref,
    heads_ref,
    skip_ref,
    grad_ref,
    grad_taps_ref,
    grad_heads_ref,
    history_ref,
    later_ref,
):
    low = jnp.bfloat16
    width = up_ref.shape[1]
    blocks = up_ref.shape[0] // BLOCK
    length = up_ref.shape[0]
    every = width + 256
    fill_history(place_ref, raw_ref, history_ref, blocks, width)
    later_ref[length : length + 8, :] = jnp.zeros((8, every), jnp.float32)
    lower = lower_mask()
    first = lane_index(BLOCK) < HD
    zero = jnp.zeros((BLOCK, 128), low)
    picks = (
        lax.broadcasted_iota(jnp.int32, (width, 128), 0) // HD
        == lax.broadcasted_iota(jnp.int32, (width, 128), 1)
    ).astype(jnp.float32)
    skip = skip_ref[0:1, :]
    rate = heads_ref[1:2, :]
    grad_state = jnp.zeros((states_ref.shape[1], width), jnp.float32)
    grad_taps = [jnp.zeros((1, every), jnp.float32) for _ in range(5)]
    grad_bias = jnp.zeros((1, 128), jnp.float32)
    grad_decay = jnp.zeros((1, 128), jnp.float32)
    grad_skip = jnp.zeros((1, width), jnp.float32)
    for at in reversed(range(blocks)):
        rows = slot_rows(place_ref, at)
        gate = raw_ref[rows, 512 : 512 + width]
        gate_sigma = sigmoid(gate)
        conv = conv_ref[rows, :]
        conv_sigma = sigmoid(conv)
        acted = conv * conv_sigma
        inner = acted[:, :width]
        write = acted[:, width : width + 128].astype(low)
        read = acted[:, width + 128 :].astype(low)
        y = y_ref[rows, :]
        up = up_ref[rows, :]
        grad_gate = up * (y + skip * inner) * gate_sigma * (1.0 + gate * (1.0 - gate_sigma))
        grad_ref[rows, 256 : 256 + width] = grad_gate.astype(low)
        grad_y = up * gate * gate_sigma
        raw_steps = raw_ref[rows, 512 + 2 * width :]
        step, running, running_t = block_decay(raw_steps, heads_ref[0:1, :], rate, lower)
        step_wide = spread_heads(step, width)
        grow = spread_heads(jnp.exp(running), width)
        last = running[BLOCK - 1 : BLOCK, :]
        carry = spread_heads(jnp.exp(last - running), width)
        last_wide = spread_heads(jnp.exp(last), width)
        scaled = inner * step_wide
        scaled_low = scaled.astype(low)
        grad_low = grad_y.astype(low)
        grown_low = (grad_y * grow).astype(low)
        state = states_ref[at]
        state_low = state.astype(low)
        grad_state_low = grad_state.astype(low)
        meet = dot(read, write, NT)
        grad_meet = jnp.zeros((BLOCK, BLOCK), jnp.float32)
        inside = []
        for pair in range(width // 128):
            weights = [
                block_weights(running, running_t, lower, head) for head in (2 * pair, 2 * pair + 1)
            ]
            both = jnp.concatenate([(meet * item).astype(low) for item in weights], axis=0)
            piece = grad_low[:, pair * 128 : (pair + 1) * 128]
            split = jnp.concatenate([jnp.where(first, piece, zero), jnp.where(first, zero, piece)])
            grad_both = dot(split, scaled_low[:, pair * 128 : (pair + 1) * 128], NT)
            grad_meet = (
                grad_meet + grad_both[:BLOCK] * weights[0] + grad_both[BLOCK:] * weights[1]
            )
            inside.append(dot(both, split, TN))
        grad_inside = jnp.concatenate(inside, axis=1)
        from_state = carry * dot(write, grad_state_low)
        carried = carry * scaled
        grad_scaled = grad_inside + from_state
        moved = scaled * from_state
        turn = grad_low.astype(jnp.float32) * y - scaled_low.astype(jnp.float32) * grad_inside - moved
        direct = grad_y * inner
        ends = jnp.sum(moved, axis=0, keepdims=True) + last_wide * jnp.sum(
            state * grad_state, axis=0, keepdims=True
        )
        summed = dot(
            jnp.concatenate([turn, grad_scaled * inner, jnp.broadcast_to(ends, (8, width))]),
            picks,
            NN,
            HIGHEST,
        )
        grad_running = (
            dot(lower.astype(jnp.float32), summed[:BLOCK], TN, HIGHEST)
            + summed[2 * BLOCK : 2 * BLOCK + 1]
        )
        grad_step = grad_running * rate + summed[BLOCK : 2 * BLOCK]
        grad_decay = grad_decay + jnp.sum(grad_running * step * rate, axis=0, keepdims=True)
        grad_steps = grad_step * sigmoid(raw_steps + heads_ref[0:1, :])
        grad_bias = grad_bias + jnp.sum(grad_steps, axis=0, keepdims=True)
        grad_skip = grad_skip + jnp.sum(direct, axis=0, keepdims=True)
        grad_ref[rows, 256 + 2 * width :] = grad_steps.astype(low)
        grad_inner = grad_scaled * step_wide + skip * grad_y
        grad_meet_low = grad_meet.astype(low)
        grad_read = dot(grad_meet_low, write) + dot(grown_low, state_low, NT)
        grad_write = dot(grad_meet_low, read, TN) + dot(carried.astype(low), grad_state_low, NT)
        grad_state = last_wide * grad_state + dot(read, grown_low, TN)
        grad_conv = jnp.concatenate([grad_inner, grad_write, grad_read], axis=1) * (
            conv_sigma * (1.0 + conv * (1.0 - conv_sigma))
        )
        later_ref[at * BLOCK : (at + 1) * BLOCK, :] = grad_conv
        back = jnp.zeros((BLOCK, every), jnp.float32)
        for tap in range(4):
            back = back + taps_ref[tap : tap + 1, :] * later_ref[pl.ds(at * BLOCK + 3 - tap, BLOCK), :]
            seen = history_ref[pl.ds(5 + tap + at * BLOCK, BLOCK), :]
            grad_taps[tap] = grad_taps[tap] + jnp.sum(grad_conv * seen, axis=0, keepdims=True)
        grad_taps[4] = grad_taps[4] + jnp.sum(grad_conv, axis=0, keepdims=True)
        grad_ref[rows, 256 + width : 256 + 2 * width] = back[:, :width].astype(low)
        grad_ref[rows, 0:256] = back[:, width:].astype(low)
    for tap in range(5):
        grad_taps_ref[tap : tap + 1, :] = grad_taps[tap]
    grad_taps_ref[5:8, :] = jnp.zeros((3, every), jnp.float32)
    skip_heads = dot(jnp.broadcast_to(grad_skip, (8, width)), picks, NN, HIGHEST)
    grad_heads_ref[...] = jnp.zeros(grad_heads_ref.shape, jnp.float32)
    grad_heads_ref[0:1, :] = grad_bias
    grad_heads_ref[1:2, :] = grad_decay
    grad_heads_ref[2:3, :] = skip_heads[0:1]


def turned(values, cosine, sine):
    early = lane_index(values.shape[0]) % HD < HD // 2
    other = jnp.where(early, pltpu.roll(values, 128 - HD // 2, 1), pltpu.roll(values, HD // 2, 1))
    return values * cosine + other * sine


def both_heads(values, first):
    zero = jnp.zeros(values.shape, values.dtype)
    return jnp.concatenate([jnp.where(first, values, zero), jnp.where(first, zero, values)])


def attention_forward_kernel(
    place_ref, raw_ref, angle_ref, mixed_ref, kept_ref, probs_ref
):
    low = jnp.bfloat16
    blocks = mixed_ref.shape[0] // BLOCK
    first = lane_index(BLOCK) < HD
    for at in range(blocks):
        rows = slot_rows(place_ref, at)
        here = slice(at * BLOCK, (at + 1) * BLOCK)
        cosine = angle_ref[here, 0:128]
        sine = angle_ref[here, 128:256]
        pair = raw_ref[rows, 128:256]
        key = turned(pair, cosine, sine)
        kept_ref[here, 0:128] = turned(raw_ref[rows, 0:128], cosine, sine).astype(low)
        kept_ref[here, 128:256] = jnp.where(first, key, pltpu.roll(key, HD, 1)).astype(low)
        kept_ref[here, 256:384] = jnp.where(first, pltpu.roll(pair, HD, 1), pair).astype(low)
    for at in range(blocks):
        rows = slot_rows(place_ref, at)
        here = slice(at * BLOCK, (at + 1) * BLOCK)
        reach = (at + 1) * BLOCK
        query = both_heads(kept_ref[here, 0:128], first)
        scores = dot(query, kept_ref[0:reach, 128:256], NT) * (HD ** (-0.5))
        row = lax.broadcasted_iota(jnp.int32, (2 * BLOCK, reach), 0) % BLOCK + at * BLOCK
        column = lax.broadcasted_iota(jnp.int32, (2 * BLOCK, reach), 1)
        scores = jnp.where(row >= column, scores, -1e30)
        exponent = jnp.exp(scores - jnp.max(scores, axis=1, keepdims=True))
        probs = (exponent / jnp.sum(exponent, axis=1, keepdims=True)).astype(low)
        probs_ref[at, :, 0:reach] = probs
        out = dot(probs, kept_ref[0:reach, 256:384])
        mixed_ref[rows, :] = jnp.where(first, out[:BLOCK], out[BLOCK:]).astype(low)


def attention_backward_kernel(
    place_ref, up_ref, angle_ref, kept_ref, probs_ref, grad_ref, key_ref, value_ref
):
    low = jnp.bfloat16
    blocks = up_ref.shape[0] // BLOCK
    first = lane_index(BLOCK) < HD
    scale = HD ** (-0.5)
    key_ref[...] = jnp.zeros(key_ref.shape, jnp.float32)
    value_ref[...] = jnp.zeros(value_ref.shape, jnp.float32)
    for at in range(blocks):
        rows = slot_rows(place_ref, at)
        here = slice(at * BLOCK, (at + 1) * BLOCK)
        reach = (at + 1) * BLOCK
        query = both_heads(kept_ref[here, 0:128], first)
        up = both_heads(up_ref[rows, :], first)
        probs_low = probs_ref[at, :, 0:reach]
        probs = probs_low.astype(jnp.float32)
        grad_probs = dot(up, kept_ref[0:reach, 256:384], NT)
        inner = jnp.sum(probs * grad_probs, axis=1, keepdims=True)
        grad_scores = (probs * (grad_probs - inner)).astype(low)
        both = dot(grad_scores, kept_ref[0:reach, 128:256]) * scale
        grad_query = jnp.where(first, both[:BLOCK], both[BLOCK:])
        grad_ref[rows, 0:128] = turned(
            grad_query, angle_ref[here, 0:128], -angle_ref[here, 128:256]
        ).astype(low)
        key_ref[0:reach, :] += dot(grad_scores, query, TN)
        value_ref[0:reach, :] += dot(probs_low, up, TN)
    for at in range(blocks):
        rows = slot_rows(place_ref, at)
        here = slice(at * BLOCK, (at + 1) * BLOCK)
        key = key_ref[here, :]
        value = value_ref[here, :]
        key = (key + pltpu.roll(key, HD, 1)) * scale
        key = turned(key, angle_ref[here, 0:128], -angle_ref[here, 128:256])
        value = value + pltpu.roll(value, HD, 1)
        grad_ref[rows, 128:256] = jnp.where(first, key, value).astype(low)


def angle_table(length):
    half = HD // 2
    freq = THETA ** (-np.arange(half, dtype=np.float32) / half)
    angle = np.arange(length, dtype=np.float32)[:, None] * freq[None, :]
    cosine = np.tile(np.cos(angle), (1, 4))
    sine = np.tile(np.concatenate([-np.sin(angle), np.sin(angle)], axis=1), (1, 2))
    return np.concatenate([cosine, sine], axis=1).astype(np.float32)


def run_kernel(kernel, place, operands, outs, scratch, name, flops=2e8, limit=None):
    whole = pl.BlockSpec(memory_space=pltpu.VMEM)
    held = sum(item.size * item.dtype.itemsize for item in operands)
    held += sum(math.prod(shape) * jnp.dtype(dtype).itemsize for shape, dtype in outs)
    held += sum(math.prod(item.shape) * jnp.dtype(item.dtype).itemsize for item in scratch)
    return pl.pallas_call(
        kernel,
        out_shape=[jax.ShapeDtypeStruct(shape, dtype) for shape, dtype in outs],
        in_specs=[pl.BlockSpec(memory_space=pltpu.SMEM)] + [whole] * len(operands),
        out_specs=[whole] * len(outs),
        scratch_shapes=scratch,
        compiler_params=pltpu.CompilerParams(vmem_limit_bytes=limit or held + 8 * 2**20),
        cost_estimate=pl.CostEstimate(flops=int(flops), bytes_accessed=1 << 20, transcendentals=0),
        name=name,
    )(place, *operands)


def state_forward(place, raw, taps, heads, skip, states):
    length = raw.shape[0]
    width = skip.shape[1]
    wide = jnp.float32
    return run_kernel(
        state_forward_kernel,
        place,
        (raw, taps, heads, skip),
        [
            ((length, width), wide),
            ((8, length), wide),
            ((length, width + 256), wide),
            ((length, width), wide),
            ((length // BLOCK, states, width), wide),
        ],
        [pltpu.VMEM((length + 8, width + 256), wide)],
        "state_forward",
    )


def state_backward(place, raw, conv, y, states, up, taps, heads, skip):
    length = raw.shape[0]
    width = skip.shape[1]
    wide = jnp.float32
    return run_kernel(
        state_backward_kernel,
        place,
        (raw, conv, y, states, up, taps, heads, skip),
        [
            ((length, 256 + 2 * width + 128), jnp.bfloat16),
            ((8, width + 256), wide),
            ((8, 128), wide),
        ],
        [pltpu.VMEM((length + 8, width + 256), wide), pltpu.VMEM((length + 8, width + 256), wide)],
        "state_backward",
    )


def attention_forward(place, raw, angles):
    length = raw.shape[0]
    low = jnp.bfloat16
    return run_kernel(
        attention_forward_kernel,
        place,
        (raw, angles),
        [
            ((length, 128), low),
            ((length, 384), low),
            ((length // BLOCK, 2 * BLOCK, length), low),
        ],
        [],
        "attention_forward",
    )


def attention_backward(place, up, angles, kept, probs):
    length = up.shape[0]
    return run_kernel(
        attention_backward_kernel,
        place,
        (up, angles, kept, probs),
        [((length, 256), jnp.bfloat16)],
        [pltpu.VMEM((length, 128), jnp.float32), pltpu.VMEM((length, 128), jnp.float32)],
        "attention_backward",
    )[0]


def block_columns(me_ref, mask):
    return pl.ds(pl.multiple_of((me_ref[0] ^ mask) * 128, 128), 128)


def join_rows(slots, whole_ref):
    rows = slots[0].shape[0]
    for at, slot in enumerate(slots):
        whole_ref[at * rows : (at + 1) * rows, :] = slot[...]


def pack_kernel(
    head_ref,
    rows_ref,
    gain_ref,
    query_ref,
    key_ref,
    value_ref,
    write_ref,
    read_ref,
    gate_ref,
    inner_ref,
    step_ref,
    output_ref,
    state_ref,
    feed_gate_ref,
    feed_up_ref,
    feed_down_ref,
    normed_ref,
    mixer_ref,
    feed_ref,
):
    rows = rows_ref[...].astype(jnp.float32)
    scale = lax.rsqrt(jnp.mean(rows * rows, axis=1, keepdims=True) + EPS)
    normed_ref[...] = (rows * scale * gain_ref[0:1, :]).astype(normed_ref.dtype)

    def turned_over(ref):
        return ref[...].astype(jnp.float32).T.astype(mixer_ref.dtype)

    low_head = head_ref[0] == 0
    first = lane_index(rows.shape[0]) < HD
    key = key_ref[...].astype(jnp.float32)
    value = value_ref[...].astype(jnp.float32)
    key = jnp.where(low_head, key, pltpu.roll(key, HD, 1))
    value = jnp.where(low_head, pltpu.roll(value, HD, 1), value)
    mixer_ref[:, 0:128] = query_ref[...]
    mixer_ref[:, 128:256] = jnp.where(first, key, value).astype(mixer_ref.dtype)
    mixer_ref[:, 256:384] = write_ref[...]
    mixer_ref[:, 384:512] = read_ref[...]
    at = 512
    for ref in (gate_ref, inner_ref):
        mixer_ref[:, at : at + ref.shape[1]] = ref[...]
        at += ref.shape[1]
    mixer_ref[:, at : at + 128] = jnp.zeros((rows.shape[0], 128), mixer_ref.dtype)
    mixer_ref[:, at : at + step_ref.shape[1]] = step_ref[...]
    mixer_ref[:, at + 128 : at + 256] = turned_over(output_ref)
    mixer_ref[:, at + 256 :] = turned_over(state_ref)
    units = feed_gate_ref.shape[1]
    feed_ref[:, :units] = feed_gate_ref[...]
    feed_ref[:, units : 2 * units] = feed_up_ref[...]
    feed_ref[:, 2 * units :] = turned_over(feed_down_ref)


def gather_columns(me_ref, rows_ref, side, chips):
    return jnp.concatenate(
        [rows_ref[:, block_columns(me_ref, 2 * at + side)] for at in range(chips)], axis=1
    )


def project_kernel(me_ref, *refs):
    slots, (near_ref, far_ref, rows_ref, raw_ref) = refs[:-4], refs[-4:]
    join_rows(slots, rows_ref)
    chips = near_ref.shape[0] // 128
    columns = raw_ref.shape[1]
    raw_ref[...] = dot(
        gather_columns(me_ref, rows_ref, 0, chips), near_ref[:, :columns]
    ) + dot(gather_columns(me_ref, rows_ref, 1, chips), far_ref[:, :columns])


def write_spread(total, own_ref, sends):
    rows = own_ref.shape[0]
    own_ref[...] = total[:rows]
    for at, send in enumerate(sends):
        send[...] = total[(at + 1) * rows : (at + 2) * rows].astype(jnp.bfloat16)


def spread_kernel(start, me_ref, mixed_ref, state_ref, near_ref, far_ref, own_ref, *rest):
    sends, total_ref = rest[:-1], rest[-1]
    left = jnp.concatenate([mixed_ref[...], state_ref[...]], axis=1)
    spread_total(me_ref, left, near_ref, far_ref, slice(start, start + left.shape[1]), total_ref)
    write_spread(total_ref[...], own_ref, sends)


def spread_total(me_ref, left, near_ref, far_ref, columns, total_ref):
    chips = near_ref.shape[0] // 128
    for side, weight_ref in enumerate((near_ref, far_ref)):
        piece = dot(left, weight_ref[:, columns], NT)
        for at in range(chips):
            total_ref[:, block_columns(me_ref, 2 * at + side)] = piece[:, at * 128 : (at + 1) * 128]


def ordered_kernel(start, place_ref, left_ref, weight_ref, out_ref):
    total = dot(left_ref[...], weight_ref[:, start : start + left_ref.shape[1]], NT)
    for at in range(total.shape[0] // BLOCK):
        out_ref[slot_rows(place_ref, at), :] = total[at * BLOCK : (at + 1) * BLOCK].astype(
            out_ref.dtype
        )


def total_kernel(
    spot_ref, attention_ref, mixer_ref, near_ref, far_ref, rows_ref, gain_ref, out_ref, total_ref
):
    left = jnp.concatenate([attention_ref[...], mixer_ref[...]], axis=1)
    spread_total(spot_ref.at[1:2], left, near_ref, far_ref, slice(0, left.shape[1]), total_ref)
    total = total_ref[...]
    gain_ref[...] = jnp.broadcast_to(
        jnp.sum(total * rows_ref[...].astype(jnp.float32), axis=0, keepdims=True), gain_ref.shape
    )
    for at in range(total.shape[0] // BLOCK):
        out_ref[slot_rows(spot_ref, at), :] = total[at * BLOCK : (at + 1) * BLOCK].astype(
            out_ref.dtype
        )


def feed_kernel(place_ref, *refs):
    low = jnp.bfloat16
    slots, cots_ref = refs[:4], refs[4]
    feed_ref, pair_ref, active_ref, own_ref = refs[5:9]
    sends = refs[9:12]
    units = active_ref.shape[1]
    rows = slots[0].shape[0]
    for half in range(2):
        here = slice(2 * half * rows, 2 * (half + 1) * rows)
        left = jnp.concatenate([slots[2 * half][...], slots[2 * half + 1][...]])
        cot = jnp.concatenate([cots_ref[slot_rows(place_ref, 2 * half + at), :] for at in range(2)])
        gate_up = dot(left, feed_ref[:, : 2 * units])
        grad_active = dot(cot, feed_ref[:, 2 * units :])
        gate = gate_up[:, :units]
        up = gate_up[:, units:]
        sigma = sigmoid(gate)
        swish = gate * sigma
        active_ref[here, :] = (swish * up).astype(low)
        grad_gate = grad_active * up * sigma * (1.0 + gate * (1.0 - sigma))
        pair = jnp.concatenate([grad_gate, grad_active * swish], axis=1).astype(low)
        pair_ref[here, :] = pair
        total = dot(pair, feed_ref[:, : 2 * units], NT)
        if half == 0:
            own_ref[...] = total[:rows]
            sends[0][...] = total[rows:].astype(low)
        else:
            sends[1][...] = total[:rows].astype(low)
            sends[2][...] = total[rows:].astype(low)


def write_halves(piece, even, keep_ref, give_ref, chip):
    piece = piece.astype(keep_ref.dtype)
    keep_ref[chip] = jnp.where(even, piece[:128], piece[128:])
    give_ref[chip] = jnp.where(even, piece[128:], piece[:128])


def feed_grad_kernel(place_ref, *refs):
    slots, cots_ref = refs[:4], refs[4]
    pair_ref, active_ref, out_ref, rows_ref, cot_ref = refs[5:]
    join_rows(slots, rows_ref)
    for at in range(len(slots)):
        cot_ref[at * BLOCK : (at + 1) * BLOCK, :] = cots_ref[slot_rows(place_ref, at), :]
    both = pair_ref.shape[1]
    for at in range(0, rows_ref.shape[1], 256):
        here = slice(at, at + 256)
        out_ref[here, :both] = dot(rows_ref[:, here], pair_ref[...], TN).astype(out_ref.dtype)
        out_ref[here, both:] = dot(cot_ref[:, here], active_ref[...], TN).astype(out_ref.dtype)


def core_add_kernel(me_ref, *refs):
    outs = refs[-4:]
    chip = me_ref[0] // 2
    keep_ref, got_ref = refs[:2]
    rows = keep_ref.shape[1]
    for mask, out in enumerate(outs):
        at = chip ^ mask
        total = keep_ref[at].astype(jnp.float32) + got_ref[at].astype(jnp.float32)
        out[0:rows, :] = total.astype(out.dtype)
        if len(refs) > 6:
            total = refs[2][...].astype(jnp.float32) + refs[3][...].astype(jnp.float32)
            out[rows:, :] = total.astype(out.dtype)


def finish_kernel(layout, place_ref, *refs):
    terms, outs = refs[: len(refs) - len(layout)], refs[len(refs) - len(layout) :]
    total = paired_sum([item[...].astype(jnp.float32) for item in terms])
    for (start, stop, over), out in zip(layout, outs):
        piece = total[:, start:stop]
        out[...] = piece.T if over else piece


def assemble_kernel(me_ref, near_ref, far_ref, key_ref, value_ref, write_ref, read_ref):
    wide = jnp.float32
    rows = 128
    first = lane_index(rows) < HD
    for side, ref in enumerate((near_ref, far_ref)):
        for chip in range(near_ref.shape[0] // rows):
            here = slice(chip * rows, (chip + 1) * rows)
            there = pl.ds(pl.multiple_of((me_ref[0] ^ (2 * chip + side)) * rows, rows), rows)
            low_head = ref[here, 0:128].astype(wide)
            high_head = ref[here, 128:256].astype(wide)
            key_ref[there, :] = jnp.where(first, low_head, pltpu.roll(high_head, HD, 1))
            value_ref[there, :] = jnp.where(first, pltpu.roll(low_head, HD, 1), high_head)
            write_ref[there, :] = ref[here, 256:384].astype(wide)
            read_ref[there, :] = ref[here, 384:512].astype(wide)


def weight_grad_kernel(groups, me_ref, *refs):
    keep_ref, give_ref = refs[-2:]
    even = me_ref[0] % 2 == 0
    for chip in range(keep_ref.shape[0]):
        here = slice(chip * 256, (chip + 1) * 256)
        pieces = []
        at = 0
        for count in groups:
            left = refs[at][:, here]
            right = jnp.concatenate([item[...] for item in refs[at + 1 : at + 1 + count]], axis=1)
            pieces.append(dot(left, right, TN))
            at += 1 + count
        write_halves(jnp.concatenate(pieces, axis=1), even, keep_ref, give_ref, chip)


def mixer_back_kernel(start, me_ref, *refs):
    slots = refs[:4]
    near_ref, far_ref, gated_ref, gain_ref, normed_ref = refs[4:9]
    cot_ref, mixed_ref, state_ref, inner_ref, gain_out_ref = refs[9:]
    join_rows(slots, cot_ref)
    chips = near_ref.shape[0] // 128
    both = dot(gather_columns(me_ref, cot_ref, 0, chips), near_ref[:, start:]) + dot(
        gather_columns(me_ref, cot_ref, 1, chips), far_ref[:, start:]
    )
    mixed_ref[...] = both[:, :128].astype(jnp.bfloat16)
    state = both[:, 128:]
    state_ref[...] = state
    gain_sum = jnp.sum(state * normed_ref[...].astype(jnp.float32), axis=0, keepdims=True)
    gain_out_ref[...] = jnp.broadcast_to(gain_sum / gain_ref[0:1, :], gain_out_ref.shape)
    product_rows = state * gain_ref[0:1, :] * gated_ref[...]
    inner_ref[...] = dot(
        jnp.ones((8, product_rows.shape[1]), jnp.float32), product_rows, NT, HIGHEST
    )


def pack(head, hidden, gain, *weights):
    rows, columns = hidden.shape
    low = jnp.bfloat16
    width = weights[5].shape[1]
    units = weights[-3].shape[1]
    return run_kernel(
        pack_kernel,
        head,
        (hidden, gain, *weights),
        [((rows, columns), low), ((rows, 768 + 3 * width), low), ((rows, 3 * units), low)],
        [],
        "pack",
        limit=60 * 2**20,
    )


def middle_kernel(
    spot_ref,
    up_ref,
    angle_ref,
    kept_ref,
    probs_ref,
    cot_ref,
    mixed_ref,
    state_ref,
    rows_ref,
    active_ref,
    feed_ref,
    grad_ref,
    keep_ref,
    give_ref,
    terms_ref,
    key_ref,
    value_ref,
):
    attention_backward_kernel(
        spot_ref, up_ref, angle_ref, kept_ref, probs_ref, grad_ref, key_ref, value_ref
    )
    weight_grad_kernel(
        (2, 1),
        spot_ref.at[1:2],
        cot_ref,
        mixed_ref,
        state_ref,
        rows_ref,
        grad_ref,
        keep_ref,
        give_ref,
    )
    units = active_ref.shape[1]
    ordered_kernel(2 * units, spot_ref, active_ref, feed_ref, terms_ref)


def small_pieces(in_gain, ffn_gain, grad_taps, state_gain, grad_heads):
    width = state_gain.shape[1]
    wide = jnp.float32

    def fill(row):
        missing = -row.shape[1] % 256
        if missing:
            row = jnp.concatenate([row, jnp.zeros((1, missing), wide)], axis=1)
        return [row[:, at : at + 256] for at in range(0, row.shape[1], 256)]

    pieces = fill(in_gain) + fill(ffn_gain)
    for tap in range(5):
        pieces += fill(grad_taps[tap : tap + 1, width:])
    for tap in range(5):
        pieces += fill(grad_taps[tap : tap + 1, :width])
    pieces += fill(state_gain)
    for row in range(3):
        pieces += fill(grad_heads[row : row + 1, :])
    return pieces + [jnp.zeros((1, 256), wide)] * (32 - len(pieces))


def last_kernel(
    spot_ref,
    raw_ref,
    conv_ref,
    y_ref,
    states_ref,
    up_ref,
    taps_ref,
    heads_ref,
    skip_ref,
    attention_ref,
    near_ref,
    far_ref,
    rows_ref,
    in_gain_ref,
    second_ref,
    normed_ref,
    ffn_gain_ref,
    state_gain_ref,
    pair_keep_ref,
    pair_give_ref,
    late_keep_ref,
    late_give_ref,
    total_low_ref,
    small_ref,
    grad_ref,
    grad_taps_ref,
    grad_heads_ref,
    history_ref,
    later_ref,
    gain_ref,
    total_ref,
    rows_small_ref,
):
    state_backward_kernel(
        spot_ref,
        raw_ref,
        conv_ref,
        y_ref,
        states_ref,
        up_ref,
        taps_ref,
        heads_ref,
        skip_ref,
        grad_ref,
        grad_taps_ref,
        grad_heads_ref,
        history_ref,
        later_ref,
    )
    me_ref = spot_ref.at[1:2]
    weight_grad_kernel(
        (1,), me_ref, rows_ref, grad_ref.at[:, 0:256], pair_keep_ref, pair_give_ref
    )
    total_kernel(
        spot_ref,
        attention_ref,
        grad_ref,
        near_ref,
        far_ref,
        rows_ref,
        gain_ref,
        total_low_ref,
        total_ref,
    )
    weight_grad_kernel(
        (1,),
        me_ref,
        rows_ref,
        grad_ref.at[:, 256 : grad_ref.shape[1]],
        late_keep_ref,
        late_give_ref,
    )
    ffn_gain = jnp.sum(
        second_ref[...] * normed_ref[...].astype(jnp.float32), axis=0, keepdims=True
    )
    pieces = small_pieces(
        gain_ref[0:1, :] / in_gain_ref[0:1, :],
        ffn_gain / ffn_gain_ref[0:1, :],
        grad_taps_ref[...],
        state_gain_ref[0:1, :],
        grad_heads_ref[...],
    )
    for at, piece in enumerate(pieces):
        rows_small_ref[at : at + 1, :] = piece
    small_ref[...] = rows_small_ref[...].astype(small_ref.dtype)


def middle(spot, up, angles, kept, probs, cot, mixed, state, rows, active, feed):
    length = up.shape[0]
    low = jnp.bfloat16
    columns = mixed.shape[1] + state.shape[1] + 256
    scratch = pltpu.VMEM((length, 128), jnp.float32)
    return run_kernel(
        middle_kernel,
        spot,
        (up, angles, kept, probs, cot, mixed, state, rows, active, feed),
        [
            ((length, 256), low),
            ((4, 128, columns), low),
            ((4, 128, columns), low),
            ((length, rows.shape[1]), low),
        ],
        [scratch, scratch],
        "middle",
    )


def last(spot, *operands):
    raw, skip, rows = operands[0], operands[7], operands[11]
    length, width = raw.shape[0], skip.shape[1]
    low, wide = jnp.bfloat16, jnp.float32
    rest = 2 * width + 128
    every = width + 256
    return run_kernel(
        last_kernel,
        spot,
        operands,
        [
            ((4, 128, 256), low),
            ((4, 128, 256), low),
            ((4, 128, rest), low),
            ((4, 128, rest), low),
            (rows.shape, low),
            ((32, 256), low),
        ],
        [
            pltpu.VMEM((length, 256 + rest), low),
            pltpu.VMEM((8, every), wide),
            pltpu.VMEM((8, 128), wide),
            pltpu.VMEM((length + 8, every), wide),
            pltpu.VMEM((length + 8, every), wide),
            pltpu.VMEM((8, rows.shape[1]), wide),
            pltpu.VMEM(rows.shape, wide),
            pltpu.VMEM((32, 256), wide),
        ],
        "last",
        flops=2e10,
    )


def project(me, slots, near, far, columns):
    length = len(slots) * slots[0].shape[0]
    return run_kernel(
        project_kernel,
        me,
        (*slots, near, far),
        [((length, slots[0].shape[1]), jnp.bfloat16), ((length, columns), jnp.float32)],
        [],
        "project",
    )


def spread_outs(rows, columns, parts):
    return [((rows, columns), jnp.float32)] + [((rows, columns), jnp.bfloat16)] * (parts - 1)


def spread_product(me, mixed, state, near, far, start, parts):
    length, columns = mixed.shape[0], 2 * near.shape[0]
    return run_kernel(
        functools.partial(spread_kernel, start),
        me,
        (mixed, state, near, far),
        spread_outs(length // parts, columns, parts),
        [pltpu.VMEM((length, columns), jnp.float32)],
        "spread_product",
    )


def ordered_product(place, left, weight, start):
    return run_kernel(
        functools.partial(ordered_kernel, start),
        place,
        (left, weight),
        [((left.shape[0], weight.shape[0]), jnp.bfloat16)],
        [],
        "ordered_product",
    )[0]


def total_product(spot, attention, mixer, near, far, rows):
    length, columns = rows.shape
    return run_kernel(
        total_kernel,
        spot,
        (attention, mixer, near, far, rows),
        [((8, columns), jnp.float32), ((length, columns), jnp.bfloat16)],
        [pltpu.VMEM((length, columns), jnp.float32)],
        "total_product",
    )


def feed_forward(place, slots, cotangent, feed):
    rows, columns = slots[0].shape
    units = feed.shape[1] // 3
    parts = len(slots)
    return run_kernel(
        feed_kernel,
        place,
        (*slots, cotangent, feed),
        [((parts * rows, 2 * units), jnp.bfloat16), ((parts * rows, units), jnp.bfloat16)]
        + spread_outs(rows, columns, parts),
        [],
        "feed_forward",
    )


def feed_grad(place, slots, cotangent, pair, active):
    length, columns = pair.shape[0], slots[0].shape[1]
    scratch = pltpu.VMEM((length, columns), jnp.bfloat16)
    return run_kernel(
        feed_grad_kernel,
        place,
        (*slots, cotangent, pair, active),
        [((columns, pair.shape[1] + active.shape[1]), jnp.bfloat16)],
        [scratch, scratch],
        "feed_grad",
    )[0]


def weight_grad(me, groups):
    counts = tuple(len(rights) for _, rights in groups)
    columns = sum(item.shape[1] for _, rights in groups for item in rights)
    operands = [item for left, rights in groups for item in (left, *rights)]
    blocks = groups[0][0].shape[1] // 256
    return run_kernel(
        functools.partial(weight_grad_kernel, counts),
        me,
        operands,
        [((blocks, 128, columns), jnp.bfloat16)] * 2,
        [],
        "weight_grad",
    )


def core_add(me, operands):
    keep = operands[0]
    rows = keep.shape[1] + (operands[2].shape[0] if len(operands) > 2 else 0)
    return run_kernel(
        core_add_kernel,
        me,
        operands,
        [((rows, keep.shape[2]), jnp.bfloat16)] * 4,
        [],
        "core_add",
    )


def finish(place, terms, layout):
    rows = terms[0].shape[0]
    if rows != 128:
        total = terms[0].astype(jnp.float32)
        pieces = [total[:, start:stop] for start, stop, _ in layout]
        return [item.T if over else item for item, (_, _, over) in zip(pieces, layout)]
    shapes = [
        ((stop - start, rows) if over else (rows, stop - start), jnp.float32)
        for start, stop, over in layout
    ]
    return run_kernel(
        functools.partial(finish_kernel, layout), place, terms, shapes, [], "finish"
    )


def assemble(me, near, far):
    rows = 2 * near.shape[0]
    return run_kernel(
        assemble_kernel, me, (near, far), [((rows, 128), jnp.float32)] * 4, [], "assemble"
    )


def mixer_back(me, slots, near, far, start, gated, gain, normed):
    rows, columns = slots[0].shape
    length = len(slots) * rows
    width = gated.shape[1]
    return run_kernel(
        functools.partial(mixer_back_kernel, start),
        me,
        (*slots, near, far, gated, gain, normed),
        [
            ((length, columns), jnp.bfloat16),
            ((length, 128), jnp.bfloat16),
            ((length, width), jnp.float32),
            ((8, length), jnp.float32),
            ((8, width), jnp.float32),
        ],
        [],
        "mixer_back",
    )


def swap(values, axis, mask):
    size = lax.axis_size(axis)
    return lax.ppermute(values, axis, [(index, index ^ mask) for index in range(size)])


def tensor_gather(block):
    masks = reversed(range(1, lax.axis_size("tensor")))
    return [block] + [swap(block, "tensor", mask) for mask in masks][::-1]


def paired_sum(terms):
    while len(terms) > 1:
        terms = [terms[at] + terms[at + 1] for at in range(0, len(terms), 2)]
    return terms[0]


def tensor_send(sends):
    return [swap(item, "tensor", at + 1) for at, item in enumerate(sends)]


def finish_scatter(own, got):
    return paired_sum([own] + [item.astype(jnp.float32) for item in got])


def cut(total, parts):
    blocks = jnp.split(total, parts)
    return blocks[:1] + [item.astype(jnp.bfloat16) for item in blocks[1:]]


def slot_sum(values):
    parts = lax.axis_size("tensor")
    shaped = values.reshape(parts, -1)
    terms = [shaped]
    for mask in range(1, parts):
        got = swap(shaped, "tensor", mask)
        terms.append(jnp.stack([got[at ^ mask] for at in range(parts)]))
    return paired_sum(terms).reshape(-1)


def tie(*values):
    return lax.optimization_barrier(values)


def dp_pieces(block):
    mine = jnp.stack([block] + [swap(block, "dp", 2 * chip) for chip in range(1, 4)])
    return mine.reshape(-1, block.shape[1])


def core_terms(me_ref, groups):
    if lax.axis_size("dp") != 8:
        return jnp.concatenate(
            [product_left(left, jnp.concatenate(rights, axis=1)) for left, rights in groups], axis=1
        ).astype(jnp.bfloat16)
    keep, give = weight_grad(me_ref, groups)
    return keep, swap(give, "dp", 1)


def chip_terms(me_ref, both, small=None, after=None):
    if lax.axis_size("dp") != 8:
        summed = lax.psum_scatter(both, "dp", scatter_dimension=0, tiled=True).astype(jnp.float32)
        if small is not None:
            summed = jnp.concatenate([summed, lax.psum(small, "dp")])
        return [summed]
    operands = both
    if small is not None:
        small = small.astype(jnp.bfloat16)
        operands = (*both, small, swap(small, "dp", 1))
    own, *sends = core_add(me_ref, operands)
    if after is not None:
        sends, _ = tie(sends, after)
    return [own] + [swap(item, "dp", 2 * (at + 1)) for at, item in enumerate(sends)]


def body(
    hidden_in,
    norm_in_gain,
    query_weight,
    key_weight,
    value_weight,
    output_weight,
    gate_weight,
    inner_weight,
    write_weight,
    read_weight,
    step_weight,
    conv_weight,
    conv_bias,
    pair_conv_weight,
    pair_conv_bias,
    step_bias,
    decay_log,
    skip_gain,
    state_gain,
    state_out_weight,
    norm_ffn_gain,
    feed_gate_weight,
    feed_up_weight,
    feed_down_weight,
    out_cotangent,
):
    low = jnp.bfloat16
    wide = jnp.float32
    parts = lax.axis_size("tensor")
    place = lax.axis_index("tensor")
    place_ref = place.astype(jnp.int32).reshape(1)
    heads_here = query_weight.shape[1] // HD
    key_head = place * heads_here // (QH // KVH)
    heads_state = step_weight.shape[1]
    width = gate_weight.shape[1]
    units = feed_gate_weight.shape[1]
    states = write_weight.shape[1]

    out_start = 640 + 2 * width
    whole_dp = lax.axis_size("dp") != 8
    rows_in = hidden_in.astype(wide)
    normed, first_scale = root_norm(rows_in, norm_in_gain)
    if whole_dp:
        normed_low = normed.astype(low)
        mixer_local = jnp.concatenate(
            [
                query_weight,
                lax.dynamic_slice_in_dim(key_weight, key_head * HD, HD, 1),
                lax.dynamic_slice_in_dim(value_weight, key_head * HD, HD, 1),
                write_weight,
                read_weight,
                gate_weight,
                inner_weight,
                jnp.pad(step_weight, ((0, 0), (0, 128 - heads_state))),
                output_weight.T,
                state_out_weight.T,
            ],
            axis=1,
        )
        feed_local = jnp.concatenate([feed_gate_weight, feed_up_weight, feed_down_weight.T], axis=1)
    else:
        normed_low, mixer_local, feed_local = pack(
            key_head.astype(jnp.int32).reshape(1),
            hidden_in,
            norm_in_gain[None],
            query_weight,
            key_weight,
            value_weight,
            write_weight,
            read_weight,
            gate_weight,
            inner_weight,
            step_weight,
            output_weight,
            state_out_weight,
            feed_gate_weight,
            feed_up_weight,
            feed_down_weight,
        )
    row_slots = tensor_gather(normed_low)
    me_ref = lax.axis_index("dp").astype(jnp.int32).reshape(1)
    spot_ref = jnp.concatenate([place_ref, me_ref])
    if whole_dp:
        mixer_full = lax.all_gather(mixer_local, "dp", axis=0, tiled=True)
        mixer_rows = jnp.concatenate(row_slots)
        out_full = mixer_full[:, out_start:]
        mixer_full = mixer_full[:, :out_start]
        raw = product(mixer_rows, mixer_full)
    else:
        near_full = dp_pieces(mixer_local)
        near_full, row_slots = tie(near_full, row_slots)
        far_full = swap(near_full, "dp", 1)
    row_slots, feed_local, cot_block = tie(row_slots, feed_local, out_cotangent)
    cotangent = lax.all_gather(cot_block, "tensor", axis=0, tiled=True)
    feed_full = lax.all_gather(feed_local, "dp", axis=0, tiled=True)
    if not whole_dp:
        mixer_rows, raw = project(me_ref, row_slots, near_full, far_full, out_start)
    length = mixer_rows.shape[0]
    block = length // parts

    taps = jnp.concatenate(
        [
            jnp.concatenate([conv_weight, conv_bias[None]]),
            jnp.concatenate([pair_conv_weight, pair_conv_bias[None]]),
        ],
        axis=1,
    )
    taps = jnp.pad(taps, ((0, 3), (0, 0)))
    heads = jnp.pad(
        jnp.stack([step_bias, -jnp.exp(decay_log)]), ((0, 6), (0, 128 - heads_state))
    )
    skip = jnp.repeat(skip_gain, HD)[None]
    angles = jnp.asarray(angle_table(length))

    gated, power, conv, y, kept_states = state_forward(place_ref, raw, taps, heads, skip, states)
    mixed_low, kept, probs = attention_forward(place_ref, raw, angles)
    width_all = width * parts
    power = slot_sum(power[0])
    state_scale = lax.rsqrt(power / width_all + EPS)[:, None]
    state_low = (gated * state_scale * state_gain).astype(low)
    if whole_dp:
        total = product_right(jnp.concatenate([mixed_low, state_low], axis=1), out_full)
        own, *sends = cut(total, parts)
    else:
        own, *sends = spread_product(
            me_ref, mixed_low, state_low, near_full, far_full, out_start, parts
        )
    mixer_shard = finish_scatter(own, tensor_send(sends))
    middle_rows = rows_in + mixer_shard
    second, second_scale = root_norm(middle_rows, norm_ffn_gain)
    second_low = second.astype(low)
    feed_slots = tensor_gather(second_low)
    grad_pair, active, own, *sends = feed_forward(place_ref, feed_slots, cotangent, feed_full)
    second_got = tensor_send(sends)
    if whole_dp:
        cot_slots = jnp.split(cotangent, parts)
        cot_slots = jnp.concatenate(
            [lax.dynamic_index_in_dim(jnp.stack(cot_slots), place ^ at, 0, False) for at in range(parts)]
        )
        feed_both = jnp.concatenate(
            [product_left(jnp.concatenate(feed_slots), grad_pair), product_left(cot_slots, active)],
            axis=1,
        ).astype(low)
    else:
        feed_both = feed_grad(place_ref, feed_slots, cotangent, grad_pair, active)
    second_got, feed_both = tie(second_got, feed_both)
    grad_second = finish_scatter(own, second_got)
    feed_sums = lax.psum_scatter(feed_both, "dp", scatter_dimension=0, tiled=True)

    weighted_second = grad_second * norm_ffn_gain
    inner_second = jnp.sum(weighted_second * middle_rows, axis=-1, keepdims=True)
    grad_middle = (
        out_cotangent.astype(wide)
        + second_scale * weighted_second
        - middle_rows * second_scale**3 * inner_second / middle_rows.shape[-1]
    )
    cot_rows = tensor_gather(grad_middle.astype(low))
    if whole_dp:
        mixer_cot = jnp.concatenate(cot_rows)
        grad_both = product(mixer_cot, out_full)
        grad_mixed, grad_state = grad_both[:, :128].astype(low), grad_both[:, 128:]
        inner_sum = jnp.sum(grad_state * state_gain * gated, axis=1)[None]
        grad_state_gain = jnp.sum(grad_state * gated * state_scale, axis=0, keepdims=True)
    else:
        mixer_cot, grad_mixed, grad_state, inner_sum, grad_state_gain = mixer_back(
            me_ref, cot_rows, near_full, far_full, out_start, gated, state_gain[None], state_low
        )
    grad_mixed, active = tie(grad_mixed, active)
    weighted = grad_state * state_gain
    inner_sum = slot_sum(inner_sum[0])
    if whole_dp:
        grad_attention = attention_backward(place_ref, grad_mixed, angles, kept, probs)
        early_both = core_terms(
            me_ref, [(mixer_cot, (mixed_low, state_low)), (mixer_rows, (grad_attention,))]
        )
        feed_terms = ordered_product(place_ref, active, feed_full, 2 * units)
    else:
        grad_attention, keep, give, feed_terms = middle(
            spot_ref,
            grad_mixed,
            angles,
            kept,
            probs,
            mixer_cot,
            mixed_low,
            state_low,
            mixer_rows,
            active,
            feed_full,
        )
        early_both = (keep, swap(give, "dp", 1))
    early_both, inner_sum = tie(early_both, inner_sum)
    early_parts = chip_terms(me_ref, early_both)
    grad_gated = (
        state_scale * weighted - gated * state_scale**3 * (inner_sum / width_all)[:, None]
    )
    grad_gated, feed_terms, feed_sums = tie(grad_gated, feed_terms, feed_sums)
    feed_shard = lax.psum_scatter(feed_terms, "tensor", scatter_dimension=0, tiled=True)
    if whole_dp:
        grad_mixer, grad_taps, grad_heads = state_backward(
            place_ref, raw, conv, y, kept_states, grad_gated, taps, heads, skip
        )
        pair_both = core_terms(me_ref, [(mixer_rows, (grad_mixer[:, :256],))])
        total_rows = product_right(grad_mixer, mixer_full[:, 256:]) + product_right(
            grad_attention, mixer_full[:, :256]
        )
        gain_rows = jnp.sum(total_rows * mixer_rows.astype(wide), axis=0, keepdims=True)
        total_rows = total_rows.astype(low).reshape(parts, block, -1)
        total_rows = jnp.concatenate(
            [lax.dynamic_index_in_dim(total_rows, place ^ at, 0, False) for at in range(parts)]
        )
        late_both = core_terms(me_ref, [(mixer_rows, (grad_mixer[:, 256:],))])
        ffn_gain = jnp.sum(grad_second * second_low.astype(wide), axis=0)
        small = jnp.concatenate(
            small_pieces(
                gain_rows / norm_in_gain,
                (ffn_gain / norm_ffn_gain)[None],
                grad_taps,
                grad_state_gain,
                grad_heads,
            )
        )
    else:
        pair_keep, pair_give, late_keep, late_give, total_rows, small = last(
            spot_ref,
            raw,
            conv,
            y,
            kept_states,
            grad_gated,
            taps,
            heads,
            skip,
            grad_attention,
            near_full,
            far_full,
            mixer_rows,
            norm_in_gain[None],
            grad_second,
            second_low,
            norm_ffn_gain[None],
            grad_state_gain,
        )
        small, early_parts = tie(small, early_parts)
        pair_both = (pair_keep, swap(pair_give, "dp", 1))
        late_both = (late_keep, swap(late_give, "dp", 1))
    grad_first = lax.psum_scatter(total_rows, "tensor", scatter_dimension=0, tiled=True)
    late_parts = chip_terms(me_ref, late_both)
    pair_sums = paired_sum([item.astype(wide) for item in chip_terms(me_ref, pair_both, small)])
    rows_here = query_weight.shape[0]
    flat = pair_sums[rows_here:]
    early_done = finish(
        place_ref,
        early_parts,
        (
            (0, 128, True),
            (128, 128 + width, True),
            (128 + width, 256 + width, False),
            (256 + width, 384 + width, False),
        ),
    )

    shared = jnp.concatenate(
        [
            jnp.concatenate([early_done[3], pair_sums[:rows_here]], axis=1),
            jnp.pad(flat[:16], ((0, 0), (0, 128))),
        ]
    ).astype(low)
    near = shared.astype(wide) + swap(shared, "tensor", 1).astype(wide)
    near = near.astype(low)
    near, grad_first = tie(near, grad_first)
    far = swap(near, "tensor", 2).astype(wide)
    near = near.astype(wide)
    both = near + far
    first_half = place < parts // 2
    head_low = jnp.where(first_half, near[:rows_here, :128], far[:rows_here, :128])
    head_high = jnp.where(first_half, far[:rows_here, :128], near[:rows_here, :128])
    common_sums = both[rows_here:, :256]
    shared = jnp.concatenate([head_low, head_high, both[:rows_here, 128:]], axis=1).astype(low)
    late_done = finish(
        place_ref,
        late_parts,
        ((0, width, False), (width, 2 * width, False), (2 * width, 2 * width + heads_state, False)),
    )
    hidden_out = (middle_rows + feed_shard.astype(wide)).astype(low)
    feed_done = finish(
        place_ref,
        [feed_sums],
        ((0, units, False), (units, 2 * units, False), (2 * units, 3 * units, True)),
    )
    shared, early_done, late_done, hidden_out, feed_done = tie(
        shared, early_done, late_done, hidden_out, feed_done
    )
    if whole_dp:
        shared = lax.all_gather(shared, "dp", axis=0, tiled=True).astype(wide)
        gradient_key = jnp.concatenate([shared[:, :64], shared[:, 128:192]], axis=1)
        gradient_value = jnp.concatenate([shared[:, 64:128], shared[:, 192:256]], axis=1)
        gradient_write, gradient_read = shared[:, 256:384], shared[:, 384:512]
    else:
        near = dp_pieces(shared)
        gradient_key, gradient_value, gradient_write, gradient_read = assemble(
            me_ref, near, swap(near, "dp", 1)
        )

    grad_first = grad_first.astype(wide)
    weighted_first = grad_first * norm_in_gain
    inner_first = jnp.sum(weighted_first * rows_in, axis=-1, keepdims=True)
    gradient_hidden = (
        grad_middle
        + first_scale * weighted_first
        - rows_in * first_scale**3 * inner_first / rows_in.shape[-1]
    )

    conv_sums = flat[13:23].reshape(5, 512)[:, :width]
    return (
        hidden_out,
        gradient_hidden,
        common_sums[:4].reshape(-1),
        early_done[2],
        gradient_key,
        gradient_value,
        early_done[0],
        late_done[0],
        late_done[1],
        gradient_write,
        gradient_read,
        late_done[2],
        conv_sums[:4],
        conv_sums[4],
        common_sums[8:12],
        common_sums[12],
        flat[25, :heads_state],
        flat[26, :heads_state],
        flat[27, :heads_state],
        flat[23:25].reshape(-1)[:width],
        early_done[1],
        common_sums[4:8].reshape(-1),
        feed_done[0],
        feed_done[1],
        feed_done[2],
    )


def solution(mesh):
    placed = (
        P(("dp", "tensor"), None),
        P(),
        P("dp", "tensor"),
        P("dp", None),
        P("dp", None),
        P("tensor", "dp"),
        P("dp", "tensor"),
        P("dp", "tensor"),
        P("dp", None),
        P("dp", None),
        P("dp", "tensor"),
        P(None, "tensor"),
        P("tensor"),
        P(),
        P(),
        P("tensor"),
        P("tensor"),
        P("tensor"),
        P("tensor"),
        P("tensor", "dp"),
        P(),
        P("dp", "tensor"),
        P("dp", "tensor"),
        P("tensor", "dp"),
        P(("dp", "tensor"), None),
    )
    return jax.shard_map(
        body,
        mesh=mesh,
        in_specs=placed,
        out_specs=(
            P(("dp", "tensor"), None),
            P(("dp", "tensor"), None),
            P(),
            P("dp", "tensor"),
            P(),
            P(),
            P("tensor", "dp"),
            P("dp", "tensor"),
            P("dp", "tensor"),
            P(),
            P(),
            P("dp", "tensor"),
            P(None, "tensor"),
            P("tensor"),
            P(),
            P(),
            P("tensor"),
            P("tensor"),
            P("tensor"),
            P("tensor"),
            P("tensor", "dp"),
            P(),
            P("dp", "tensor"),
            P("dp", "tensor"),
            P("tensor", "dp"),
        ),
        check_vma=False,
    )
```

```python
import functools
import math

import jax
import jax.numpy as jnp
import numpy as np
from jax import lax
from jax.experimental import pallas as pl
from jax.experimental.pallas import tpu as pltpu
from jax.sharding import PartitionSpec as P

QH = 8
KVH = 2
HD = 64
BLOCK = 128


EPS = 1e-05
THETA = 10000.0
HIGHEST = lax.Precision.HIGHEST


def product(left, right):
    return jnp.dot(left, right, preferred_element_type=jnp.float32)


def product_left(left, right):
    return lax.dot_general(
        left, right, (((0,), (0,)), ((), ())), preferred_element_type=jnp.float32
    )


def product_right(left, right):
    return lax.dot_general(
        left, right, (((1,), (1,)), ((), ())), preferred_element_type=jnp.float32
    )


def root_norm(rows, gain):
    scale = lax.rsqrt(jnp.mean(rows * rows, axis=-1, keepdims=True) + EPS)
    return (rows * scale * gain, scale)


def dot(left, right, dims=((1,), (0,)), precision=None):
    return lax.dot_general(
        left, right, (dims, ((), ())), precision=precision, preferred_element_type=jnp.float32
    )


NN = ((1,), (0,))
NT = ((1,), (1,))
TN = ((0,), (0,))


def sigmoid(values):
    return 1.0 / (1.0 + jnp.exp(-values))


def softplus(values):
    return jnp.maximum(values, 0.0) + jnp.log1p(jnp.exp(-jnp.abs(values)))


def lane_index(rows):
    return lax.broadcasted_iota(jnp.int32, (rows, 128), 1)


def spread_heads(values, width):
    first = lane_index(values.shape[0]) < HD
    return jnp.concatenate(
        [
            jnp.where(first, values[:, at : at + 1], values[:, at + 1 : at + 2])
            for at in range(0, width // HD, 2)
        ],
        axis=1,
    )


def slot_rows(place_ref, at):
    return pl.ds(pl.multiple_of((place_ref[0] ^ at) * BLOCK, BLOCK), BLOCK)


def lower_mask():
    rows = lax.broadcasted_iota(jnp.int32, (BLOCK, BLOCK), 0)
    columns = lax.broadcasted_iota(jnp.int32, (BLOCK, BLOCK), 1)
    return rows >= columns


def block_decay(raw_steps, step_bias, rate, lower):
    step = softplus(raw_steps + step_bias)
    running = dot(lower.astype(jnp.float32), step * rate, NN, HIGHEST)
    return step, running, running.T


def block_weights(running, running_t, lower, head):
    spread = running[:, head : head + 1] - running_t[head : head + 1, :]
    return jnp.exp(jnp.where(lower, spread, -1e30))


def fill_history(place_ref, raw_ref, history_ref, blocks, width):
    history_ref[0:8, :] = jnp.zeros((8, history_ref.shape[1]), jnp.float32)
    for at in range(blocks):
        rows = slot_rows(place_ref, at)
        here = slice(8 + at * BLOCK, 8 + (at + 1) * BLOCK)
        history_ref[here, 0:width] = raw_ref[rows, 512 + width : 512 + 2 * width]
        history_ref[here, width : width + 256] = raw_ref[rows, 256:512]


def state_forward_kernel(
    place_ref,
    raw_ref,
    taps_ref,
    heads_ref,
    skip_ref,
    gated_ref,
    power_ref,
    conv_ref,
    y_ref,
    states_ref,
    history_ref,
):
    low = jnp.bfloat16
    width = gated_ref.shape[1]
    blocks = gated_ref.shape[0] // BLOCK
    fill_history(place_ref, raw_ref, history_ref, blocks, width)
    lower = lower_mask()
    first = lane_index(BLOCK) < HD
    state = jnp.zeros((states_ref.shape[1], width), jnp.float32)
    for at in range(blocks):
        rows = slot_rows(place_ref, at)
        conv = taps_ref[4:5, :]
        for tap in range(4):
            conv = conv + taps_ref[tap : tap + 1, :] * history_ref[pl.ds(5 + tap + at * BLOCK, BLOCK), :]
        conv_ref[rows, :] = conv
        acted = conv * sigmoid(conv)
        inner = acted[:, :width]
        write = acted[:, width : width + 128].astype(low)
        read = acted[:, width + 128 :].astype(low)
        step, running, running_t = block_decay(
            raw_ref[rows, 512 + 2 * width :], heads_ref[0:1, :], heads_ref[1:2, :], lower
        )
        scaled = inner * spread_heads(step, width)
        scaled_low = scaled.astype(low)
        zero = jnp.zeros((BLOCK, 128), low)
        meet = dot(read, write, NT)
        inside = []
        for pair in range(width // 128):
            both = jnp.concatenate(
                [
                    (meet * block_weights(running, running_t, lower, 2 * pair)).astype(low),
                    (meet * block_weights(running, running_t, lower, 2 * pair + 1)).astype(low),
                ],
                axis=1,
            )
            piece = scaled_low[:, pair * 128 : (pair + 1) * 128]
            split = jnp.concatenate([jnp.where(first, piece, zero), jnp.where(first, zero, piece)])
            inside.append(dot(both, split))
        earlier = dot(read, state.astype(low))
        y = jnp.concatenate(inside, axis=1) + spread_heads(jnp.exp(running), width) * earlier
        y_ref[rows, :] = y
        states_ref[at] = state
        last = running[BLOCK - 1 : BLOCK, :]
        carried = (spread_heads(jnp.exp(last - running), width) * scaled).astype(low)
        state = spread_heads(jnp.exp(last), width) * state + dot(write, carried, TN)
        gate = raw_ref[rows, 512 : 512 + width]
        gated = (y + skip_ref[0:1, :] * inner) * gate * sigmoid(gate)
        gated_ref[rows, :] = gated
        power_ref[:, rows] = dot(jnp.ones((8, width), jnp.float32), gated * gated, NT, HIGHEST)


def state_backward_kernel(
    place_ref,
    raw_ref,
    conv_ref,
    y_ref,
    states_ref,
    up_ref,
    taps_ref,
    heads_ref,
    skip_ref,
    grad_ref,
    grad_taps_ref,
    grad_heads_ref,
    history_ref,
    later_ref,
):
    low = jnp.bfloat16
    width = up_ref.shape[1]
    blocks = up_ref.shape[0] // BLOCK
    length = up_ref.shape[0]
    every = width + 256
    fill_history(place_ref, raw_ref, history_ref, blocks, width)
    later_ref[length : length + 8, :] = jnp.zeros((8, every), jnp.float32)
    lower = lower_mask()
    first = lane_index(BLOCK) < HD
    zero = jnp.zeros((BLOCK, 128), low)
    picks = (
        lax.broadcasted_iota(jnp.int32, (width, 128), 0) // HD
        == lax.broadcasted_iota(jnp.int32, (width, 128), 1)
    ).astype(jnp.float32)
    skip = skip_ref[0:1, :]
    rate = heads_ref[1:2, :]
    grad_state = jnp.zeros((states_ref.shape[1], width), jnp.float32)
    grad_taps = [jnp.zeros((1, every), jnp.float32) for _ in range(5)]
    grad_bias = jnp.zeros((1, 128), jnp.float32)
    grad_decay = jnp.zeros((1, 128), jnp.float32)
    grad_skip = jnp.zeros((1, width), jnp.float32)
    for at in reversed(range(blocks)):
        rows = slot_rows(place_ref, at)
        gate = raw_ref[rows, 512 : 512 + width]
        gate_sigma = sigmoid(gate)
        conv = conv_ref[rows, :]
        conv_sigma = sigmoid(conv)
        acted = conv * conv_sigma
        inner = acted[:, :width]
        write = acted[:, width : width + 128].astype(low)
        read = acted[:, width + 128 :].astype(low)
        y = y_ref[rows, :]
        up = up_ref[rows, :]
        grad_gate = up * (y + skip * inner) * gate_sigma * (1.0 + gate * (1.0 - gate_sigma))
        grad_ref[rows, 256 : 256 + width] = grad_gate.astype(low)
        grad_y = up * gate * gate_sigma
        raw_steps = raw_ref[rows, 512 + 2 * width :]
        step, running, running_t = block_decay(raw_steps, heads_ref[0:1, :], rate, lower)
        step_wide = spread_heads(step, width)
        grow = spread_heads(jnp.exp(running), width)
        last = running[BLOCK - 1 : BLOCK, :]
        carry = spread_heads(jnp.exp(last - running), width)
        last_wide = spread_heads(jnp.exp(last), width)
        scaled = inner * step_wide
        scaled_low = scaled.astype(low)
        grad_low = grad_y.astype(low)
        grown_low = (grad_y * grow).astype(low)
        state = states_ref[at]
        state_low = state.astype(low)
        grad_state_low = grad_state.astype(low)
        meet = dot(read, write, NT)
        grad_meet = jnp.zeros((BLOCK, BLOCK), jnp.float32)
        inside = []
        for pair in range(width // 128):
            weights = [
                block_weights(running, running_t, lower, head) for head in (2 * pair, 2 * pair + 1)
            ]
            both = jnp.concatenate([(meet * item).astype(low) for item in weights], axis=0)
            piece = grad_low[:, pair * 128 : (pair + 1) * 128]
            split = jnp.concatenate([jnp.where(first, piece, zero), jnp.where(first, zero, piece)])
            grad_both = dot(split, scaled_low[:, pair * 128 : (pair + 1) * 128], NT)
            grad_meet = (
                grad_meet + grad_both[:BLOCK] * weights[0] + grad_both[BLOCK:] * weights[1]
            )
            inside.append(dot(both, split, TN))
        grad_inside = jnp.concatenate(inside, axis=1)
        from_state = carry * dot(write, grad_state_low)
        carried = carry * scaled
        grad_scaled = grad_inside + from_state
        moved = scaled * from_state
        turn = grad_low.astype(jnp.float32) * y - scaled_low.astype(jnp.float32) * grad_inside - moved
        direct = grad_y * inner
        ends = jnp.sum(moved, axis=0, keepdims=True) + last_wide * jnp.sum(
            state * grad_state, axis=0, keepdims=True
        )
        summed = dot(
            jnp.concatenate([turn, grad_scaled * inner, jnp.broadcast_to(ends, (8, width))]),
            picks,
            NN,
            HIGHEST,
        )
        grad_running = (
            dot(lower.astype(jnp.float32), summed[:BLOCK], TN, HIGHEST)
            + summed[2 * BLOCK : 2 * BLOCK + 1]
        )
        grad_step = grad_running * rate + summed[BLOCK : 2 * BLOCK]
        grad_decay = grad_decay + jnp.sum(grad_running * step * rate, axis=0, keepdims=True)
        grad_steps = grad_step * sigmoid(raw_steps + heads_ref[0:1, :])
        grad_bias = grad_bias + jnp.sum(grad_steps, axis=0, keepdims=True)
        grad_skip = grad_skip + jnp.sum(direct, axis=0, keepdims=True)
        grad_ref[rows, 256 + 2 * width :] = grad_steps.astype(low)
        grad_inner = grad_scaled * step_wide + skip * grad_y
        grad_meet_low = grad_meet.astype(low)
        grad_read = dot(grad_meet_low, write) + dot(grown_low, state_low, NT)
        grad_write = dot(grad_meet_low, read, TN) + dot(carried.astype(low), grad_state_low, NT)
        grad_state = last_wide * grad_state + dot(read, grown_low, TN)
        grad_conv = jnp.concatenate([grad_inner, grad_write, grad_read], axis=1) * (
            conv_sigma * (1.0 + conv * (1.0 - conv_sigma))
        )
        later_ref[at * BLOCK : (at + 1) * BLOCK, :] = grad_conv
        back = jnp.zeros((BLOCK, every), jnp.float32)
        for tap in range(4):
            back = back + taps_ref[tap : tap + 1, :] * later_ref[pl.ds(at * BLOCK + 3 - tap, BLOCK), :]
            seen = history_ref[pl.ds(5 + tap + at * BLOCK, BLOCK), :]
            grad_taps[tap] = grad_taps[tap] + jnp.sum(grad_conv * seen, axis=0, keepdims=True)
        grad_taps[4] = grad_taps[4] + jnp.sum(grad_conv, axis=0, keepdims=True)
        grad_ref[rows, 256 + width : 256 + 2 * width] = back[:, :width].astype(low)
        grad_ref[rows, 0:256] = back[:, width:].astype(low)
    for tap in range(5):
        grad_taps_ref[tap : tap + 1, :] = grad_taps[tap]
    grad_taps_ref[5:8, :] = jnp.zeros((3, every), jnp.float32)
    skip_heads = dot(jnp.broadcast_to(grad_skip, (8, width)), picks, NN, HIGHEST)
    grad_heads_ref[...] = jnp.zeros(grad_heads_ref.shape, jnp.float32)
    grad_heads_ref[0:1, :] = grad_bias
    grad_heads_ref[1:2, :] = grad_decay
    grad_heads_ref[2:3, :] = skip_heads[0:1]


def turned(values, cosine, sine):
    early = lane_index(values.shape[0]) % HD < HD // 2
    other = jnp.where(early, pltpu.roll(values, 128 - HD // 2, 1), pltpu.roll(values, HD // 2, 1))
    return values * cosine + other * sine


def both_heads(values, first):
    zero = jnp.zeros(values.shape, values.dtype)
    return jnp.concatenate([jnp.where(first, values, zero), jnp.where(first, zero, values)])


def attention_forward_kernel(
    place_ref, raw_ref, angle_ref, mixed_ref, kept_ref, probs_ref
):
    low = jnp.bfloat16
    blocks = mixed_ref.shape[0] // BLOCK
    first = lane_index(BLOCK) < HD
    for at in range(blocks):
        rows = slot_rows(place_ref, at)
        here = slice(at * BLOCK, (at + 1) * BLOCK)
        cosine = angle_ref[here, 0:128]
        sine = angle_ref[here, 128:256]
        pair = raw_ref[rows, 128:256]
        key = turned(pair, cosine, sine)
        kept_ref[here, 0:128] = turned(raw_ref[rows, 0:128], cosine, sine).astype(low)
        kept_ref[here, 128:256] = jnp.where(first, key, pltpu.roll(key, HD, 1)).astype(low)
        kept_ref[here, 256:384] = jnp.where(first, pltpu.roll(pair, HD, 1), pair).astype(low)
    for at in range(blocks):
        rows = slot_rows(place_ref, at)
        here = slice(at * BLOCK, (at + 1) * BLOCK)
        reach = (at + 1) * BLOCK
        query = both_heads(kept_ref[here, 0:128], first)
        scores = dot(query, kept_ref[0:reach, 128:256], NT) * (HD ** (-0.5))
        row = lax.broadcasted_iota(jnp.int32, (2 * BLOCK, reach), 0) % BLOCK + at * BLOCK
        column = lax.broadcasted_iota(jnp.int32, (2 * BLOCK, reach), 1)
        scores = jnp.where(row >= column, scores, -1e30)
        exponent = jnp.exp(scores - jnp.max(scores, axis=1, keepdims=True))
        probs = (exponent / jnp.sum(exponent, axis=1, keepdims=True)).astype(low)
        probs_ref[at, :, 0:reach] = probs
        out = dot(probs, kept_ref[0:reach, 256:384])
        mixed_ref[rows, :] = jnp.where(first, out[:BLOCK], out[BLOCK:]).astype(low)


def attention_backward_kernel(
    place_ref, up_ref, angle_ref, kept_ref, probs_ref, grad_ref, key_ref, value_ref
):
    low = jnp.bfloat16
    blocks = up_ref.shape[0] // BLOCK
    first = lane_index(BLOCK) < HD
    scale = HD ** (-0.5)
    key_ref[...] = jnp.zeros(key_ref.shape, jnp.float32)
    value_ref[...] = jnp.zeros(value_ref.shape, jnp.float32)
    for at in range(blocks):
        rows = slot_rows(place_ref, at)
        here = slice(at * BLOCK, (at + 1) * BLOCK)
        reach = (at + 1) * BLOCK
        query = both_heads(kept_ref[here, 0:128], first)
        up = both_heads(up_ref[rows, :], first)
        probs_low = probs_ref[at, :, 0:reach]
        probs = probs_low.astype(jnp.float32)
        grad_probs = dot(up, kept_ref[0:reach, 256:384], NT)
        inner = jnp.sum(probs * grad_probs, axis=1, keepdims=True)
        grad_scores = (probs * (grad_probs - inner)).astype(low)
        both = dot(grad_scores, kept_ref[0:reach, 128:256]) * scale
        grad_query = jnp.where(first, both[:BLOCK], both[BLOCK:])
        grad_ref[rows, 0:128] = turned(
            grad_query, angle_ref[here, 0:128], -angle_ref[here, 128:256]
        ).astype(low)
        key_ref[0:reach, :] += dot(grad_scores, query, TN)
        value_ref[0:reach, :] += dot(probs_low, up, TN)
    for at in range(blocks):
        rows = slot_rows(place_ref, at)
        here = slice(at * BLOCK, (at + 1) * BLOCK)
        key = key_ref[here, :]
        value = value_ref[here, :]
        key = (key + pltpu.roll(key, HD, 1)) * scale
        key = turned(key, angle_ref[here, 0:128], -angle_ref[here, 128:256])
        value = value + pltpu.roll(value, HD, 1)
        grad_ref[rows, 128:256] = jnp.where(first, key, value).astype(low)


def angle_table(length):
    half = HD // 2
    freq = THETA ** (-np.arange(half, dtype=np.float32) / half)
    angle = np.arange(length, dtype=np.float32)[:, None] * freq[None, :]
    cosine = np.tile(np.cos(angle), (1, 4))
    sine = np.tile(np.concatenate([-np.sin(angle), np.sin(angle)], axis=1), (1, 2))
    return np.concatenate([cosine, sine], axis=1).astype(np.float32)


def run_kernel(kernel, place, operands, outs, scratch, name, flops=2e8, limit=None):
    whole = pl.BlockSpec(memory_space=pltpu.VMEM)
    held = sum(item.size * item.dtype.itemsize for item in operands)
    held += sum(math.prod(shape) * jnp.dtype(dtype).itemsize for shape, dtype in outs)
    held += sum(math.prod(item.shape) * jnp.dtype(item.dtype).itemsize for item in scratch)
    return pl.pallas_call(
        kernel,
        out_shape=[jax.ShapeDtypeStruct(shape, dtype) for shape, dtype in outs],
        in_specs=[pl.BlockSpec(memory_space=pltpu.SMEM)] + [whole] * len(operands),
        out_specs=[whole] * len(outs),
        scratch_shapes=scratch,
        compiler_params=pltpu.CompilerParams(vmem_limit_bytes=limit or held + 8 * 2**20),
        cost_estimate=pl.CostEstimate(flops=int(flops), bytes_accessed=1 << 20, transcendentals=0),
        name=name,
    )(place, *operands)


def state_forward(place, raw, taps, heads, skip, states):
    length = raw.shape[0]
    width = skip.shape[1]
    wide = jnp.float32
    return run_kernel(
        state_forward_kernel,
        place,
        (raw, taps, heads, skip),
        [
            ((length, width), wide),
            ((8, length), wide),
            ((length, width + 256), wide),
            ((length, width), wide),
            ((length // BLOCK, states, width), wide),
        ],
        [pltpu.VMEM((length + 8, width + 256), wide)],
        "state_forward",
    )


def state_backward(place, raw, conv, y, states, up, taps, heads, skip):
    length = raw.shape[0]
    width = skip.shape[1]
    wide = jnp.float32
    return run_kernel(
        state_backward_kernel,
        place,
        (raw, conv, y, states, up, taps, heads, skip),
        [
            ((length, 256 + 2 * width + 128), jnp.bfloat16),
            ((8, width + 256), wide),
            ((8, 128), wide),
        ],
        [pltpu.VMEM((length + 8, width + 256), wide), pltpu.VMEM((length + 8, width + 256), wide)],
        "state_backward",
    )


def attention_forward(place, raw, angles):
    length = raw.shape[0]
    low = jnp.bfloat16
    return run_kernel(
        attention_forward_kernel,
        place,
        (raw, angles),
        [
            ((length, 128), low),
            ((length, 384), low),
            ((length // BLOCK, 2 * BLOCK, length), low),
        ],
        [],
        "attention_forward",
    )


def attention_backward(place, up, angles, kept, probs):
    length = up.shape[0]
    return run_kernel(
        attention_backward_kernel,
        place,
        (up, angles, kept, probs),
        [((length, 256), jnp.bfloat16)],
        [pltpu.VMEM((length, 128), jnp.float32), pltpu.VMEM((length, 128), jnp.float32)],
        "attention_backward",
    )[0]


def block_columns(me_ref, mask):
    return pl.ds(pl.multiple_of((me_ref[0] ^ mask) * 128, 128), 128)


def join_rows(slots, whole_ref):
    rows = slots[0].shape[0]
    for at, slot in enumerate(slots):
        whole_ref[at * rows : (at + 1) * rows, :] = slot[...]


def pack_kernel(
    head_ref,
    rows_ref,
    gain_ref,
    query_ref,
    key_ref,
    value_ref,
    write_ref,
    read_ref,
    gate_ref,
    inner_ref,
    step_ref,
    output_ref,
    state_ref,
    feed_gate_ref,
    feed_up_ref,
    feed_down_ref,
    normed_ref,
    mixer_ref,
    feed_ref,
):
    rows = rows_ref[...].astype(jnp.float32)
    scale = lax.rsqrt(jnp.mean(rows * rows, axis=1, keepdims=True) + EPS)
    normed_ref[...] = (rows * scale * gain_ref[0:1, :]).astype(normed_ref.dtype)

    def turned_over(ref):
        return ref[...].astype(jnp.float32).T.astype(mixer_ref.dtype)

    low_head = head_ref[0] == 0
    first = lane_index(rows.shape[0]) < HD
    key = key_ref[...].astype(jnp.float32)
    value = value_ref[...].astype(jnp.float32)
    key = jnp.where(low_head, key, pltpu.roll(key, HD, 1))
    value = jnp.where(low_head, pltpu.roll(value, HD, 1), value)
    mixer_ref[:, 0:128] = query_ref[...]
    mixer_ref[:, 128:256] = jnp.where(first, key, value).astype(mixer_ref.dtype)
    mixer_ref[:, 256:384] = write_ref[...]
    mixer_ref[:, 384:512] = read_ref[...]
    at = 512
    for ref in (gate_ref, inner_ref):
        mixer_ref[:, at : at + ref.shape[1]] = ref[...]
        at += ref.shape[1]
    mixer_ref[:, at : at + 128] = jnp.zeros((rows.shape[0], 128), mixer_ref.dtype)
    mixer_ref[:, at : at + step_ref.shape[1]] = step_ref[...]
    mixer_ref[:, at + 128 : at + 256] = turned_over(output_ref)
    mixer_ref[:, at + 256 :] = turned_over(state_ref)
    units = feed_gate_ref.shape[1]
    feed_ref[:, :units] = feed_gate_ref[...]
    feed_ref[:, units : 2 * units] = feed_up_ref[...]
    feed_ref[:, 2 * units :] = turned_over(feed_down_ref)


def gather_columns(me_ref, rows_ref, side, chips):
    return jnp.concatenate(
        [rows_ref[:, block_columns(me_ref, 2 * at + side)] for at in range(chips)], axis=1
    )


def project_kernel(me_ref, *refs):
    slots, (near_ref, far_ref, rows_ref, raw_ref) = refs[:-4], refs[-4:]
    join_rows(slots, rows_ref)
    chips = near_ref.shape[0] // 128
    columns = raw_ref.shape[1]
    raw_ref[...] = dot(
        gather_columns(me_ref, rows_ref, 0, chips), near_ref[:, :columns]
    ) + dot(gather_columns(me_ref, rows_ref, 1, chips), far_ref[:, :columns])


def write_spread(total, own_ref, sends):
    rows = own_ref.shape[0]
    own_ref[...] = total[:rows]
    for at, send in enumerate(sends):
        send[...] = total[(at + 1) * rows : (at + 2) * rows].astype(jnp.bfloat16)


def spread_kernel(start, me_ref, mixed_ref, state_ref, near_ref, far_ref, own_ref, *rest):
    sends, total_ref = rest[:-1], rest[-1]
    left = jnp.concatenate([mixed_ref[...], state_ref[...]], axis=1)
    spread_total(me_ref, left, near_ref, far_ref, slice(start, start + left.shape[1]), total_ref)
    write_spread(total_ref[...], own_ref, sends)


def spread_total(me_ref, left, near_ref, far_ref, columns, total_ref):
    chips = near_ref.shape[0] // 128
    for side, weight_ref in enumerate((near_ref, far_ref)):
        piece = dot(left, weight_ref[:, columns], NT)
        for at in range(chips):
            total_ref[:, block_columns(me_ref, 2 * at + side)] = piece[:, at * 128 : (at + 1) * 128]


def ordered_kernel(start, place_ref, left_ref, weight_ref, out_ref):
    total = dot(left_ref[...], weight_ref[:, start : start + left_ref.shape[1]], NT)
    for at in range(total.shape[0] // BLOCK):
        out_ref[slot_rows(place_ref, at), :] = total[at * BLOCK : (at + 1) * BLOCK].astype(
            out_ref.dtype
        )


def total_kernel(
    spot_ref, attention_ref, mixer_ref, near_ref, far_ref, rows_ref, gain_ref, out_ref, total_ref
):
    left = jnp.concatenate([attention_ref[...], mixer_ref[...]], axis=1)
    spread_total(spot_ref.at[1:2], left, near_ref, far_ref, slice(0, left.shape[1]), total_ref)
    total = total_ref[...]
    gain_ref[...] = jnp.broadcast_to(
        jnp.sum(total * rows_ref[...].astype(jnp.float32), axis=0, keepdims=True), gain_ref.shape
    )
    for at in range(total.shape[0] // BLOCK):
        out_ref[slot_rows(spot_ref, at), :] = total[at * BLOCK : (at + 1) * BLOCK].astype(
            out_ref.dtype
        )


def feed_kernel(place_ref, *refs):
    low = jnp.bfloat16
    slots, cots_ref = refs[:4], refs[4]
    feed_ref, pair_ref, active_ref, own_ref = refs[5:9]
    sends = refs[9:12]
    units = active_ref.shape[1]
    rows = slots[0].shape[0]
    for half in range(2):
        here = slice(2 * half * rows, 2 * (half + 1) * rows)
        left = jnp.concatenate([slots[2 * half][...], slots[2 * half + 1][...]])
        cot = jnp.concatenate([cots_ref[slot_rows(place_ref, 2 * half + at), :] for at in range(2)])
        gate_up = dot(left, feed_ref[:, : 2 * units])
        grad_active = dot(cot, feed_ref[:, 2 * units :])
        gate = gate_up[:, :units]
        up = gate_up[:, units:]
        sigma = sigmoid(gate)
        swish = gate * sigma
        active_ref[here, :] = (swish * up).astype(low)
        grad_gate = grad_active * up * sigma * (1.0 + gate * (1.0 - sigma))
        pair = jnp.concatenate([grad_gate, grad_active * swish], axis=1).astype(low)
        pair_ref[here, :] = pair
        total = dot(pair, feed_ref[:, : 2 * units], NT)
        if half == 0:
            own_ref[...] = total[:rows]
            sends[0][...] = total[rows:].astype(low)
        else:
            sends[1][...] = total[:rows].astype(low)
            sends[2][...] = total[rows:].astype(low)


def write_halves(piece, even, keep_ref, give_ref, chip):
    piece = piece.astype(keep_ref.dtype)
    keep_ref[chip] = jnp.where(even, piece[:128], piece[128:])
    give_ref[chip] = jnp.where(even, piece[128:], piece[:128])


def feed_grad_kernel(place_ref, *refs):
    slots, cots_ref = refs[:4], refs[4]
    pair_ref, active_ref, out_ref, rows_ref, cot_ref = refs[5:]
    join_rows(slots, rows_ref)
    for at in range(len(slots)):
        cot_ref[at * BLOCK : (at + 1) * BLOCK, :] = cots_ref[slot_rows(place_ref, at), :]
    both = pair_ref.shape[1]
    for at in range(0, rows_ref.shape[1], 256):
        here = slice(at, at + 256)
        out_ref[here, :both] = dot(rows_ref[:, here], pair_ref[...], TN).astype(out_ref.dtype)
        out_ref[here, both:] = dot(cot_ref[:, here], active_ref[...], TN).astype(out_ref.dtype)


def core_add_kernel(me_ref, *refs):
    outs = refs[-4:]
    chip = me_ref[0] // 2
    keep_ref, got_ref = refs[:2]
    rows = keep_ref.shape[1]
    for mask, out in enumerate(outs):
        at = chip ^ mask
        total = keep_ref[at].astype(jnp.float32) + got_ref[at].astype(jnp.float32)
        out[0:rows, :] = total.astype(out.dtype)
        if len(refs) > 6:
            total = refs[2][...].astype(jnp.float32) + refs[3][...].astype(jnp.float32)
            out[rows:, :] = total.astype(out.dtype)


def finish_kernel(layout, place_ref, *refs):
    terms, outs = refs[: len(refs) - len(layout)], refs[len(refs) - len(layout) :]
    total = paired_sum([item[...].astype(jnp.float32) for item in terms])
    for (start, stop, over), out in zip(layout, outs):
        piece = total[:, start:stop]
        out[...] = piece.T if over else piece


def assemble_kernel(me_ref, near_ref, far_ref, key_ref, value_ref, write_ref, read_ref):
    wide = jnp.float32
    rows = 128
    first = lane_index(rows) < HD
    for side, ref in enumerate((near_ref, far_ref)):
        for chip in range(near_ref.shape[0] // rows):
            here = slice(chip * rows, (chip + 1) * rows)
            there = pl.ds(pl.multiple_of((me_ref[0] ^ (2 * chip + side)) * rows, rows), rows)
            low_head = ref[here, 0:128].astype(wide)
            high_head = ref[here, 128:256].astype(wide)
            key_ref[there, :] = jnp.where(first, low_head, pltpu.roll(high_head, HD, 1))
            value_ref[there, :] = jnp.where(first, pltpu.roll(low_head, HD, 1), high_head)
            write_ref[there, :] = ref[here, 256:384].astype(wide)
            read_ref[there, :] = ref[here, 384:512].astype(wide)


def weight_grad_kernel(groups, me_ref, *refs):
    keep_ref, give_ref = refs[-2:]
    even = me_ref[0] % 2 == 0
    for chip in range(keep_ref.shape[0]):
        here = slice(chip * 256, (chip + 1) * 256)
        pieces = []
        at = 0
        for count in groups:
            left = refs[at][:, here]
            right = jnp.concatenate([item[...] for item in refs[at + 1 : at + 1 + count]], axis=1)
            pieces.append(dot(left, right, TN))
            at += 1 + count
        write_halves(jnp.concatenate(pieces, axis=1), even, keep_ref, give_ref, chip)


def mixer_back_kernel(start, me_ref, *refs):
    slots = refs[:4]
    near_ref, far_ref, gated_ref, gain_ref, normed_ref = refs[4:9]
    cot_ref, mixed_ref, state_ref, inner_ref, gain_out_ref = refs[9:]
    join_rows(slots, cot_ref)
    chips = near_ref.shape[0] // 128
    both = dot(gather_columns(me_ref, cot_ref, 0, chips), near_ref[:, start:]) + dot(
        gather_columns(me_ref, cot_ref, 1, chips), far_ref[:, start:]
    )
    mixed_ref[...] = both[:, :128].astype(jnp.bfloat16)
    state = both[:, 128:]
    state_ref[...] = state
    gain_sum = jnp.sum(state * normed_ref[...].astype(jnp.float32), axis=0, keepdims=True)
    gain_out_ref[...] = jnp.broadcast_to(gain_sum / gain_ref[0:1, :], gain_out_ref.shape)
    product_rows = state * gain_ref[0:1, :] * gated_ref[...]
    inner_ref[...] = dot(
        jnp.ones((8, product_rows.shape[1]), jnp.float32), product_rows, NT, HIGHEST
    )


def pack(head, hidden, gain, *weights):
    rows, columns = hidden.shape
    low = jnp.bfloat16
    width = weights[5].shape[1]
    units = weights[-3].shape[1]
    return run_kernel(
        pack_kernel,
        head,
        (hidden, gain, *weights),
        [((rows, columns), low), ((rows, 768 + 3 * width), low), ((rows, 3 * units), low)],
        [],
        "pack",
        limit=60 * 2**20,
    )


def middle_kernel(
    spot_ref,
    up_ref,
    angle_ref,
    kept_ref,
    probs_ref,
    cot_ref,
    mixed_ref,
    state_ref,
    rows_ref,
    active_ref,
    feed_ref,
    grad_ref,
    keep_ref,
    give_ref,
    terms_ref,
    key_ref,
    value_ref,
):
    attention_backward_kernel(
        spot_ref, up_ref, angle_ref, kept_ref, probs_ref, grad_ref, key_ref, value_ref
    )
    weight_grad_kernel(
        (2, 1),
        spot_ref.at[1:2],
        cot_ref,
        mixed_ref,
        state_ref,
        rows_ref,
        grad_ref,
        keep_ref,
        give_ref,
    )
    units = active_ref.shape[1]
    ordered_kernel(2 * units, spot_ref, active_ref, feed_ref, terms_ref)


def small_pieces(in_gain, ffn_gain, grad_taps, state_gain, grad_heads):
    width = state_gain.shape[1]
    wide = jnp.float32

    def fill(row):
        missing = -row.shape[1] % 256
        if missing:
            row = jnp.concatenate([row, jnp.zeros((1, missing), wide)], axis=1)
        return [row[:, at : at + 256] for at in range(0, row.shape[1], 256)]

    pieces = fill(in_gain) + fill(ffn_gain)
    for tap in range(5):
        pieces += fill(grad_taps[tap : tap + 1, width:])
    for tap in range(5):
        pieces += fill(grad_taps[tap : tap + 1, :width])
    pieces += fill(state_gain)
    for row in range(3):
        pieces += fill(grad_heads[row : row + 1, :])
    return pieces + [jnp.zeros((1, 256), wide)] * (32 - len(pieces))


def last_kernel(
    spot_ref,
    raw_ref,
    conv_ref,
    y_ref,
    states_ref,
    up_ref,
    taps_ref,
    heads_ref,
    skip_ref,
    attention_ref,
    near_ref,
    far_ref,
    rows_ref,
    in_gain_ref,
    second_ref,
    normed_ref,
    ffn_gain_ref,
    state_gain_ref,
    pair_keep_ref,
    pair_give_ref,
    late_keep_ref,
    late_give_ref,
    total_low_ref,
    small_ref,
    grad_ref,
    grad_taps_ref,
    grad_heads_ref,
    history_ref,
    later_ref,
    gain_ref,
    total_ref,
    rows_small_ref,
):
    state_backward_kernel(
        spot_ref,
        raw_ref,
        conv_ref,
        y_ref,
        states_ref,
        up_ref,
        taps_ref,
        heads_ref,
        skip_ref,
        grad_ref,
        grad_taps_ref,
        grad_heads_ref,
        history_ref,
        later_ref,
    )
    me_ref = spot_ref.at[1:2]
    weight_grad_kernel(
        (1,), me_ref, rows_ref, grad_ref.at[:, 0:256], pair_keep_ref, pair_give_ref
    )
    total_kernel(
        spot_ref,
        attention_ref,
        grad_ref,
        near_ref,
        far_ref,
        rows_ref,
        gain_ref,
        total_low_ref,
        total_ref,
    )
    weight_grad_kernel(
        (1,),
        me_ref,
        rows_ref,
        grad_ref.at[:, 256 : grad_ref.shape[1]],
        late_keep_ref,
        late_give_ref,
    )
    ffn_gain = jnp.sum(
        second_ref[...] * normed_ref[...].astype(jnp.float32), axis=0, keepdims=True
    )
    pieces = small_pieces(
        gain_ref[0:1, :] / in_gain_ref[0:1, :],
        ffn_gain / ffn_gain_ref[0:1, :],
        grad_taps_ref[...],
        state_gain_ref[0:1, :],
        grad_heads_ref[...],
    )
    for at, piece in enumerate(pieces):
        rows_small_ref[at : at + 1, :] = piece
    small_ref[...] = rows_small_ref[...].astype(small_ref.dtype)


def middle(spot, up, angles, kept, probs, cot, mixed, state, rows, active, feed):
    length = up.shape[0]
    low = jnp.bfloat16
    columns = mixed.shape[1] + state.shape[1] + 256
    scratch = pltpu.VMEM((length, 128), jnp.float32)
    return run_kernel(
        middle_kernel,
        spot,
        (up, angles, kept, probs, cot, mixed, state, rows, active, feed),
        [
            ((length, 256), low),
            ((4, 128, columns), low),
            ((4, 128, columns), low),
            ((length, rows.shape[1]), low),
        ],
        [scratch, scratch],
        "middle",
    )


def last(spot, *operands):
    raw, skip, rows = operands[0], operands[7], operands[11]
    length, width = raw.shape[0], skip.shape[1]
    low, wide = jnp.bfloat16, jnp.float32
    rest = 2 * width + 128
    every = width + 256
    return run_kernel(
        last_kernel,
        spot,
        operands,
        [
            ((4, 128, 256), low),
            ((4, 128, 256), low),
            ((4, 128, rest), low),
            ((4, 128, rest), low),
            (rows.shape, low),
            ((32, 256), low),
        ],
        [
            pltpu.VMEM((length, 256 + rest), low),
            pltpu.VMEM((8, every), wide),
            pltpu.VMEM((8, 128), wide),
            pltpu.VMEM((length + 8, every), wide),
            pltpu.VMEM((length + 8, every), wide),
            pltpu.VMEM((8, rows.shape[1]), wide),
            pltpu.VMEM(rows.shape, wide),
            pltpu.VMEM((32, 256), wide),
        ],
        "last",
    )


def project(me, slots, near, far, columns):
    length = len(slots) * slots[0].shape[0]
    return run_kernel(
        project_kernel,
        me,
        (*slots, near, far),
        [((length, slots[0].shape[1]), jnp.bfloat16), ((length, columns), jnp.float32)],
        [],
        "project",
    )


def spread_outs(rows, columns, parts):
    return [((rows, columns), jnp.float32)] + [((rows, columns), jnp.bfloat16)] * (parts - 1)


def spread_product(me, mixed, state, near, far, start, parts):
    length, columns = mixed.shape[0], 2 * near.shape[0]
    return run_kernel(
        functools.partial(spread_kernel, start),
        me,
        (mixed, state, near, far),
        spread_outs(length // parts, columns, parts),
        [pltpu.VMEM((length, columns), jnp.float32)],
        "spread_product",
    )


def ordered_product(place, left, weight, start):
    return run_kernel(
        functools.partial(ordered_kernel, start),
        place,
        (left, weight),
        [((left.shape[0], weight.shape[0]), jnp.bfloat16)],
        [],
        "ordered_product",
    )[0]


def total_product(spot, attention, mixer, near, far, rows):
    length, columns = rows.shape
    return run_kernel(
        total_kernel,
        spot,
        (attention, mixer, near, far, rows),
        [((8, columns), jnp.float32), ((length, columns), jnp.bfloat16)],
        [pltpu.VMEM((length, columns), jnp.float32)],
        "total_product",
    )


def feed_forward(place, slots, cotangent, feed):
    rows, columns = slots[0].shape
    units = feed.shape[1] // 3
    parts = len(slots)
    return run_kernel(
        feed_kernel,
        place,
        (*slots, cotangent, feed),
        [((parts * rows, 2 * units), jnp.bfloat16), ((parts * rows, units), jnp.bfloat16)]
        + spread_outs(rows, columns, parts),
        [],
        "feed_forward",
    )


def feed_grad(place, slots, cotangent, pair, active):
    length, columns = pair.shape[0], slots[0].shape[1]
    scratch = pltpu.VMEM((length, columns), jnp.bfloat16)
    return run_kernel(
        feed_grad_kernel,
        place,
        (*slots, cotangent, pair, active),
        [((columns, pair.shape[1] + active.shape[1]), jnp.bfloat16)],
        [scratch, scratch],
        "feed_grad",
    )[0]


def weight_grad(me, groups):
    counts = tuple(len(rights) for _, rights in groups)
    columns = sum(item.shape[1] for _, rights in groups for item in rights)
    operands = [item for left, rights in groups for item in (left, *rights)]
    blocks = groups[0][0].shape[1] // 256
    return run_kernel(
        functools.partial(weight_grad_kernel, counts),
        me,
        operands,
        [((blocks, 128, columns), jnp.bfloat16)] * 2,
        [],
        "weight_grad",
    )


def core_add(me, operands):
    keep = operands[0]
    rows = keep.shape[1] + (operands[2].shape[0] if len(operands) > 2 else 0)
    return run_kernel(
        core_add_kernel,
        me,
        operands,
        [((rows, keep.shape[2]), jnp.bfloat16)] * 4,
        [],
        "core_add",
    )


def finish(place, terms, layout):
    rows = terms[0].shape[0]
    if rows != 128:
        total = terms[0].astype(jnp.float32)
        pieces = [total[:, start:stop] for start, stop, _ in layout]
        return [item.T if over else item for item, (_, _, over) in zip(pieces, layout)]
    shapes = [
        ((stop - start, rows) if over else (rows, stop - start), jnp.float32)
        for start, stop, over in layout
    ]
    return run_kernel(
        functools.partial(finish_kernel, layout), place, terms, shapes, [], "finish"
    )


def assemble(me, near, far):
    rows = 2 * near.shape[0]
    return run_kernel(
        assemble_kernel, me, (near, far), [((rows, 128), jnp.float32)] * 4, [], "assemble"
    )


def mixer_back(me, slots, near, far, start, gated, gain, normed):
    rows, columns = slots[0].shape
    length = len(slots) * rows
    width = gated.shape[1]
    return run_kernel(
        functools.partial(mixer_back_kernel, start),
        me,
        (*slots, near, far, gated, gain, normed),
        [
            ((length, columns), jnp.bfloat16),
            ((length, 128), jnp.bfloat16),
            ((length, width), jnp.float32),
            ((8, length), jnp.float32),
            ((8, width), jnp.float32),
        ],
        [],
        "mixer_back",
    )


def swap(values, axis, mask):
    size = lax.axis_size(axis)
    return lax.ppermute(values, axis, [(index, index ^ mask) for index in range(size)])


def tensor_gather(block):
    masks = reversed(range(1, lax.axis_size("tensor")))
    return [block] + [swap(block, "tensor", mask) for mask in masks][::-1]


def paired_sum(terms):
    while len(terms) > 1:
        terms = [terms[at] + terms[at + 1] for at in range(0, len(terms), 2)]
    return terms[0]


def tensor_send(sends):
    return [swap(item, "tensor", at + 1) for at, item in enumerate(sends)]


def finish_scatter(own, got):
    return paired_sum([own] + [item.astype(jnp.float32) for item in got])


def cut(total, parts):
    blocks = jnp.split(total, parts)
    return blocks[:1] + [item.astype(jnp.bfloat16) for item in blocks[1:]]


def slot_sum(values):
    parts = lax.axis_size("tensor")
    shaped = values.reshape(parts, -1)
    terms = [shaped]
    for mask in range(1, parts):
        got = swap(shaped, "tensor", mask)
        terms.append(jnp.stack([got[at ^ mask] for at in range(parts)]))
    return paired_sum(terms).reshape(-1)


def tie(*values):
    return lax.optimization_barrier(values)


def dp_pieces(block):
    mine = jnp.stack([block] + [swap(block, "dp", 2 * chip) for chip in range(1, 4)])
    return mine.reshape(-1, block.shape[1])


def core_terms(me_ref, groups):
    if lax.axis_size("dp") != 8:
        return jnp.concatenate(
            [product_left(left, jnp.concatenate(rights, axis=1)) for left, rights in groups], axis=1
        ).astype(jnp.bfloat16)
    keep, give = weight_grad(me_ref, groups)
    return keep, swap(give, "dp", 1)


def chip_terms(me_ref, both, small=None, after=None):
    if lax.axis_size("dp") != 8:
        summed = lax.psum_scatter(both, "dp", scatter_dimension=0, tiled=True).astype(jnp.float32)
        if small is not None:
            summed = jnp.concatenate([summed, lax.psum(small, "dp")])
        return [summed]
    operands = both
    if small is not None:
        small = small.astype(jnp.bfloat16)
        operands = (*both, small, swap(small, "dp", 1))
    own, *sends = core_add(me_ref, operands)
    if after is not None:
        sends, _ = tie(sends, after)
    return [own] + [swap(item, "dp", 2 * (at + 1)) for at, item in enumerate(sends)]


def body(
    hidden_in,
    norm_in_gain,
    query_weight,
    key_weight,
    value_weight,
    output_weight,
    gate_weight,
    inner_weight,
    write_weight,
    read_weight,
    step_weight,
    conv_weight,
    conv_bias,
    pair_conv_weight,
    pair_conv_bias,
    step_bias,
    decay_log,
    skip_gain,
    state_gain,
    state_out_weight,
    norm_ffn_gain,
    feed_gate_weight,
    feed_up_weight,
    feed_down_weight,
    out_cotangent,
):
    low = jnp.bfloat16
    wide = jnp.float32
    parts = lax.axis_size("tensor")
    place = lax.axis_index("tensor")
    place_ref = place.astype(jnp.int32).reshape(1)
    heads_here = query_weight.shape[1] // HD
    key_head = place * heads_here // (QH // KVH)
    heads_state = step_weight.shape[1]
    width = gate_weight.shape[1]
    units = feed_gate_weight.shape[1]
    states = write_weight.shape[1]

    out_start = 640 + 2 * width
    whole_dp = lax.axis_size("dp") != 8
    rows_in = hidden_in.astype(wide)
    normed, first_scale = root_norm(rows_in, norm_in_gain)
    if whole_dp:
        normed_low = normed.astype(low)
        mixer_local = jnp.concatenate(
            [
                query_weight,
                lax.dynamic_slice_in_dim(key_weight, key_head * HD, HD, 1),
                lax.dynamic_slice_in_dim(value_weight, key_head * HD, HD, 1),
                write_weight,
                read_weight,
                gate_weight,
                inner_weight,
                jnp.pad(step_weight, ((0, 0), (0, 128 - heads_state))),
                output_weight.T,
                state_out_weight.T,
            ],
            axis=1,
        )
        feed_local = jnp.concatenate([feed_gate_weight, feed_up_weight, feed_down_weight.T], axis=1)
    else:
        normed_low, mixer_local, feed_local = pack(
            key_head.astype(jnp.int32).reshape(1),
            hidden_in,
            norm_in_gain[None],
            query_weight,
            key_weight,
            value_weight,
            write_weight,
            read_weight,
            gate_weight,
            inner_weight,
            step_weight,
            output_weight,
            state_out_weight,
            feed_gate_weight,
            feed_up_weight,
            feed_down_weight,
        )
    row_slots = tensor_gather(normed_low)
    me_ref = lax.axis_index("dp").astype(jnp.int32).reshape(1)
    spot_ref = jnp.concatenate([place_ref, me_ref])
    if whole_dp:
        mixer_full = lax.all_gather(mixer_local, "dp", axis=0, tiled=True)
        mixer_rows = jnp.concatenate(row_slots)
        out_full = mixer_full[:, out_start:]
        mixer_full = mixer_full[:, :out_start]
        raw = product(mixer_rows, mixer_full)
    else:
        near_full = dp_pieces(mixer_local)
        near_full, row_slots = tie(near_full, row_slots)
        far_full = swap(near_full, "dp", 1)
    row_slots, feed_local, cot_block = tie(row_slots, feed_local, out_cotangent)
    cotangent = lax.all_gather(cot_block, "tensor", axis=0, tiled=True)
    feed_full = lax.all_gather(feed_local, "dp", axis=0, tiled=True)
    if not whole_dp:
        mixer_rows, raw = project(me_ref, row_slots, near_full, far_full, out_start)
    length = mixer_rows.shape[0]
    block = length // parts

    taps = jnp.concatenate(
        [
            jnp.concatenate([conv_weight, conv_bias[None]]),
            jnp.concatenate([pair_conv_weight, pair_conv_bias[None]]),
        ],
        axis=1,
    )
    taps = jnp.pad(taps, ((0, 3), (0, 0)))
    heads = jnp.pad(
        jnp.stack([step_bias, -jnp.exp(decay_log)]), ((0, 6), (0, 128 - heads_state))
    )
    skip = jnp.repeat(skip_gain, HD)[None]
    angles = jnp.asarray(angle_table(length))

    gated, power, conv, y, kept_states = state_forward(place_ref, raw, taps, heads, skip, states)
    mixed_low, kept, probs = attention_forward(place_ref, raw, angles)
    width_all = width * parts
    power = slot_sum(power[0])
    state_scale = lax.rsqrt(power / width_all + EPS)[:, None]
    state_low = (gated * state_scale * state_gain).astype(low)
    if whole_dp:
        total = product_right(jnp.concatenate([mixed_low, state_low], axis=1), out_full)
        own, *sends = cut(total, parts)
    else:
        own, *sends = spread_product(
            me_ref, mixed_low, state_low, near_full, far_full, out_start, parts
        )
    mixer_shard = finish_scatter(own, tensor_send(sends))
    middle_rows = rows_in + mixer_shard
    second, second_scale = root_norm(middle_rows, norm_ffn_gain)
    second_low = second.astype(low)
    feed_slots = tensor_gather(second_low)
    grad_pair, active, own, *sends = feed_forward(place_ref, feed_slots, cotangent, feed_full)
    second_got = tensor_send(sends)
    if whole_dp:
        cot_slots = jnp.split(cotangent, parts)
        cot_slots = jnp.concatenate(
            [lax.dynamic_index_in_dim(jnp.stack(cot_slots), place ^ at, 0, False) for at in range(parts)]
        )
        feed_both = jnp.concatenate(
            [product_left(jnp.concatenate(feed_slots), grad_pair), product_left(cot_slots, active)],
            axis=1,
        ).astype(low)
    else:
        feed_both = feed_grad(place_ref, feed_slots, cotangent, grad_pair, active)
    second_got, feed_both = tie(second_got, feed_both)
    grad_second = finish_scatter(own, second_got)
    feed_sums = lax.psum_scatter(feed_both, "dp", scatter_dimension=0, tiled=True)

    weighted_second = grad_second * norm_ffn_gain
    inner_second = jnp.sum(weighted_second * middle_rows, axis=-1, keepdims=True)
    grad_middle = (
        out_cotangent.astype(wide)
        + second_scale * weighted_second
        - middle_rows * second_scale**3 * inner_second / middle_rows.shape[-1]
    )
    cot_rows = tensor_gather(grad_middle.astype(low))
    if whole_dp:
        mixer_cot = jnp.concatenate(cot_rows)
        grad_both = product(mixer_cot, out_full)
        grad_mixed, grad_state = grad_both[:, :128].astype(low), grad_both[:, 128:]
        inner_sum = jnp.sum(grad_state * state_gain * gated, axis=1)[None]
        grad_state_gain = jnp.sum(grad_state * gated * state_scale, axis=0, keepdims=True)
    else:
        mixer_cot, grad_mixed, grad_state, inner_sum, grad_state_gain = mixer_back(
            me_ref, cot_rows, near_full, far_full, out_start, gated, state_gain[None], state_low
        )
    grad_mixed, active = tie(grad_mixed, active)
    weighted = grad_state * state_gain
    inner_sum = slot_sum(inner_sum[0])
    if whole_dp:
        grad_attention = attention_backward(place_ref, grad_mixed, angles, kept, probs)
        early_both = core_terms(
            me_ref, [(mixer_cot, (mixed_low, state_low)), (mixer_rows, (grad_attention,))]
        )
        feed_terms = ordered_product(place_ref, active, feed_full, 2 * units)
    else:
        grad_attention, keep, give, feed_terms = middle(
            spot_ref,
            grad_mixed,
            angles,
            kept,
            probs,
            mixer_cot,
            mixed_low,
            state_low,
            mixer_rows,
            active,
            feed_full,
        )
        early_both = (keep, swap(give, "dp", 1))
    early_both, inner_sum = tie(early_both, inner_sum)
    early_parts = chip_terms(me_ref, early_both)
    grad_gated = (
        state_scale * weighted - gated * state_scale**3 * (inner_sum / width_all)[:, None]
    )
    grad_gated, feed_terms, feed_sums = tie(grad_gated, feed_terms, feed_sums)
    feed_shard = lax.psum_scatter(feed_terms, "tensor", scatter_dimension=0, tiled=True)
    if whole_dp:
        grad_mixer, grad_taps, grad_heads = state_backward(
            place_ref, raw, conv, y, kept_states, grad_gated, taps, heads, skip
        )
        pair_both = core_terms(me_ref, [(mixer_rows, (grad_mixer[:, :256],))])
        total_rows = product_right(grad_mixer, mixer_full[:, 256:]) + product_right(
            grad_attention, mixer_full[:, :256]
        )
        gain_rows = jnp.sum(total_rows * mixer_rows.astype(wide), axis=0, keepdims=True)
        total_rows = total_rows.astype(low).reshape(parts, block, -1)
        total_rows = jnp.concatenate(
            [lax.dynamic_index_in_dim(total_rows, place ^ at, 0, False) for at in range(parts)]
        )
        late_both = core_terms(me_ref, [(mixer_rows, (grad_mixer[:, 256:],))])
        ffn_gain = jnp.sum(grad_second * second_low.astype(wide), axis=0)
        small = jnp.concatenate(
            small_pieces(
                gain_rows / norm_in_gain,
                (ffn_gain / norm_ffn_gain)[None],
                grad_taps,
                grad_state_gain,
                grad_heads,
            )
        )
    else:
        pair_keep, pair_give, late_keep, late_give, total_rows, small = last(
            spot_ref,
            raw,
            conv,
            y,
            kept_states,
            grad_gated,
            taps,
            heads,
            skip,
            grad_attention,
            near_full,
            far_full,
            mixer_rows,
            norm_in_gain[None],
            grad_second,
            second_low,
            norm_ffn_gain[None],
            grad_state_gain,
        )
        pair_keep, pair_give, late_keep, late_give, total_rows, small, *beside = tie(
            pair_keep,
            pair_give,
            late_keep,
            late_give,
            total_rows,
            small,
            early_parts,
            feed_shard,
        )
        early_parts, feed_shard = beside
        pair_both = (pair_keep, swap(pair_give, "dp", 1))
        late_both = (late_keep, swap(late_give, "dp", 1))
    grad_first = lax.psum_scatter(total_rows, "tensor", scatter_dimension=0, tiled=True)
    late_parts = chip_terms(me_ref, late_both)
    pair_sums = paired_sum([item.astype(wide) for item in chip_terms(me_ref, pair_both, small)])
    rows_here = query_weight.shape[0]
    flat = pair_sums[rows_here:]
    early_done = finish(
        place_ref,
        early_parts,
        (
            (0, 128, True),
            (128, 128 + width, True),
            (128 + width, 256 + width, False),
            (256 + width, 384 + width, False),
        ),
    )

    shared = jnp.concatenate(
        [
            jnp.concatenate([early_done[3], pair_sums[:rows_here]], axis=1),
            jnp.pad(flat[:16], ((0, 0), (0, 128))),
        ]
    ).astype(low)
    near = shared.astype(wide) + swap(shared, "tensor", 1).astype(wide)
    near = near.astype(low)
    near, grad_first = tie(near, grad_first)
    far = swap(near, "tensor", 2).astype(wide)
    near = near.astype(wide)
    both = near + far
    first_half = place < parts // 2
    head_low = jnp.where(first_half, near[:rows_here, :128], far[:rows_here, :128])
    head_high = jnp.where(first_half, far[:rows_here, :128], near[:rows_here, :128])
    common_sums = both[rows_here:, :256]
    shared = jnp.concatenate([head_low, head_high, both[:rows_here, 128:]], axis=1).astype(low)
    late_done = finish(
        place_ref,
        late_parts,
        ((0, width, False), (width, 2 * width, False), (2 * width, 2 * width + heads_state, False)),
    )
    hidden_out = (middle_rows + feed_shard.astype(wide)).astype(low)
    feed_done = finish(
        place_ref,
        [feed_sums],
        ((0, units, False), (units, 2 * units, False), (2 * units, 3 * units, True)),
    )
    shared, early_done, hidden_out, feed_done = tie(shared, early_done, hidden_out, feed_done)
    if whole_dp:
        shared = lax.all_gather(shared, "dp", axis=0, tiled=True).astype(wide)
        gradient_key = jnp.concatenate([shared[:, :64], shared[:, 128:192]], axis=1)
        gradient_value = jnp.concatenate([shared[:, 64:128], shared[:, 192:256]], axis=1)
        gradient_write, gradient_read = shared[:, 256:384], shared[:, 384:512]
    else:
        near = dp_pieces(shared)
        gradient_key, gradient_value, gradient_write, gradient_read = assemble(
            me_ref, near, swap(near, "dp", 1)
        )

    grad_first = grad_first.astype(wide)
    weighted_first = grad_first * norm_in_gain
    inner_first = jnp.sum(weighted_first * rows_in, axis=-1, keepdims=True)
    gradient_hidden = (
        grad_middle
        + first_scale * weighted_first
        - rows_in * first_scale**3 * inner_first / rows_in.shape[-1]
    )

    conv_sums = flat[13:23].reshape(5, 512)[:, :width]
    return (
        hidden_out,
        gradient_hidden,
        common_sums[:4].reshape(-1),
        early_done[2],
        gradient_key,
        gradient_value,
        early_done[0],
        late_done[0],
        late_done[1],
        gradient_write,
        gradient_read,
        late_done[2],
        conv_sums[:4],
        conv_sums[4],
        common_sums[8:12],
        common_sums[12],
        flat[25, :heads_state],
        flat[26, :heads_state],
        flat[27, :heads_state],
        flat[23:25].reshape(-1)[:width],
        early_done[1],
        common_sums[4:8].reshape(-1),
        feed_done[0],
        feed_done[1],
        feed_done[2],
    )


def solution(mesh):
    placed = (
        P(("dp", "tensor"), None),
        P(),
        P("dp", "tensor"),
        P("dp", None),
        P("dp", None),
        P("tensor", "dp"),
        P("dp", "tensor"),
        P("dp", "tensor"),
        P("dp", None),
        P("dp", None),
        P("dp", "tensor"),
        P(None, "tensor"),
        P("tensor"),
        P(),
        P(),
        P("tensor"),
        P("tensor"),
        P("tensor"),
        P("tensor"),
        P("tensor", "dp"),
        P(),
        P("dp", "tensor"),
        P("dp", "tensor"),
        P("tensor", "dp"),
        P(("dp", "tensor"), None),
    )
    return jax.shard_map(
        body,
        mesh=mesh,
        in_specs=placed,
        out_specs=(
            P(("dp", "tensor"), None),
            P(("dp", "tensor"), None),
            P(),
            P("dp", "tensor"),
            P(),
            P(),
            P("tensor", "dp"),
            P("dp", "tensor"),
            P("dp", "tensor"),
            P(),
            P(),
            P("dp", "tensor"),
            P(None, "tensor"),
            P("tensor"),
            P(),
            P(),
            P("tensor"),
            P("tensor"),
            P("tensor"),
            P("tensor"),
            P("tensor", "dp"),
            P(),
            P("dp", "tensor"),
            P("dp", "tensor"),
            P("tensor", "dp"),
        ),
        check_vma=False,
    )
```

```python
import functools
import math

import jax
import jax.numpy as jnp
import numpy as np
from jax import lax
from jax.experimental import pallas as pl
from jax.experimental.pallas import tpu as pltpu
from jax.sharding import PartitionSpec as P

QH = 8
KVH = 2
HD = 64
BLOCK = 128


EPS = 1e-05
THETA = 10000.0
HIGHEST = lax.Precision.HIGHEST


def product(left, right):
    return jnp.dot(left, right, preferred_element_type=jnp.float32)


def product_left(left, right):
    return lax.dot_general(
        left, right, (((0,), (0,)), ((), ())), preferred_element_type=jnp.float32
    )


def product_right(left, right):
    return lax.dot_general(
        left, right, (((1,), (1,)), ((), ())), preferred_element_type=jnp.float32
    )


def root_norm(rows, gain):
    scale = lax.rsqrt(jnp.mean(rows * rows, axis=-1, keepdims=True) + EPS)
    return (rows * scale * gain, scale)


def dot(left, right, dims=((1,), (0,)), precision=None):
    return lax.dot_general(
        left, right, (dims, ((), ())), precision=precision, preferred_element_type=jnp.float32
    )


NN = ((1,), (0,))
NT = ((1,), (1,))
TN = ((0,), (0,))


def sigmoid(values):
    return 1.0 / (1.0 + jnp.exp(-values))


def softplus(values):
    return jnp.maximum(values, 0.0) + jnp.log1p(jnp.exp(-jnp.abs(values)))


def lane_index(rows):
    return lax.broadcasted_iota(jnp.int32, (rows, 128), 1)


def spread_heads(values, width):
    first = lane_index(values.shape[0]) < HD
    return jnp.concatenate(
        [
            jnp.where(first, values[:, at : at + 1], values[:, at + 1 : at + 2])
            for at in range(0, width // HD, 2)
        ],
        axis=1,
    )


def slot_rows(place_ref, at):
    return pl.ds(pl.multiple_of((place_ref[0] ^ at) * BLOCK, BLOCK), BLOCK)


def lower_mask():
    rows = lax.broadcasted_iota(jnp.int32, (BLOCK, BLOCK), 0)
    columns = lax.broadcasted_iota(jnp.int32, (BLOCK, BLOCK), 1)
    return rows >= columns


def block_decay(raw_steps, step_bias, rate, lower):
    step = softplus(raw_steps + step_bias)
    running = dot(lower.astype(jnp.float32), step * rate, NN, HIGHEST)
    return step, running, running.T


def block_weights(running, running_t, lower, head):
    spread = running[:, head : head + 1] - running_t[head : head + 1, :]
    return jnp.exp(jnp.where(lower, spread, -1e30))


def fill_history(place_ref, raw_ref, history_ref, blocks, width):
    history_ref[0:8, :] = jnp.zeros((8, history_ref.shape[1]), jnp.float32)
    for at in range(blocks):
        rows = slot_rows(place_ref, at)
        here = slice(8 + at * BLOCK, 8 + (at + 1) * BLOCK)
        history_ref[here, 0:width] = raw_ref[rows, 512 + width : 512 + 2 * width]
        history_ref[here, width : width + 256] = raw_ref[rows, 256:512]


def state_forward_kernel(
    place_ref,
    raw_ref,
    taps_ref,
    heads_ref,
    skip_ref,
    gated_ref,
    power_ref,
    conv_ref,
    y_ref,
    states_ref,
    history_ref,
):
    low = jnp.bfloat16
    width = gated_ref.shape[1]
    blocks = gated_ref.shape[0] // BLOCK
    fill_history(place_ref, raw_ref, history_ref, blocks, width)
    lower = lower_mask()
    first = lane_index(BLOCK) < HD
    state = jnp.zeros((states_ref.shape[1], width), jnp.float32)
    for at in range(blocks):
        rows = slot_rows(place_ref, at)
        conv = taps_ref[4:5, :]
        for tap in range(4):
            conv = conv + taps_ref[tap : tap + 1, :] * history_ref[pl.ds(5 + tap + at * BLOCK, BLOCK), :]
        conv_ref[rows, :] = conv
        acted = conv * sigmoid(conv)
        inner = acted[:, :width]
        write = acted[:, width : width + 128].astype(low)
        read = acted[:, width + 128 :].astype(low)
        step, running, running_t = block_decay(
            raw_ref[rows, 512 + 2 * width :], heads_ref[0:1, :], heads_ref[1:2, :], lower
        )
        scaled = inner * spread_heads(step, width)
        scaled_low = scaled.astype(low)
        zero = jnp.zeros((BLOCK, 128), low)
        meet = dot(read, write, NT)
        inside = []
        for pair in range(width // 128):
            both = jnp.concatenate(
                [
                    (meet * block_weights(running, running_t, lower, 2 * pair)).astype(low),
                    (meet * block_weights(running, running_t, lower, 2 * pair + 1)).astype(low),
                ],
                axis=1,
            )
            piece = scaled_low[:, pair * 128 : (pair + 1) * 128]
            split = jnp.concatenate([jnp.where(first, piece, zero), jnp.where(first, zero, piece)])
            inside.append(dot(both, split))
        earlier = dot(read, state.astype(low))
        y = jnp.concatenate(inside, axis=1) + spread_heads(jnp.exp(running), width) * earlier
        y_ref[rows, :] = y
        states_ref[at] = state
        last = running[BLOCK - 1 : BLOCK, :]
        carried = (spread_heads(jnp.exp(last - running), width) * scaled).astype(low)
        state = spread_heads(jnp.exp(last), width) * state + dot(write, carried, TN)
        gate = raw_ref[rows, 512 : 512 + width]
        gated = (y + skip_ref[0:1, :] * inner) * gate * sigmoid(gate)
        gated_ref[rows, :] = gated
        power_ref[:, rows] = dot(jnp.ones((8, width), jnp.float32), gated * gated, NT, HIGHEST)


def state_backward_kernel(
    place_ref,
    raw_ref,
    conv_ref,
    y_ref,
    states_ref,
    up_ref,
    taps_ref,
    heads_ref,
    skip_ref,
    grad_ref,
    grad_taps_ref,
    grad_heads_ref,
    history_ref,
    later_ref,
):
    low = jnp.bfloat16
    width = up_ref.shape[1]
    blocks = up_ref.shape[0] // BLOCK
    length = up_ref.shape[0]
    every = width + 256
    fill_history(place_ref, raw_ref, history_ref, blocks, width)
    later_ref[length : length + 8, :] = jnp.zeros((8, every), jnp.float32)
    lower = lower_mask()
    first = lane_index(BLOCK) < HD
    zero = jnp.zeros((BLOCK, 128), low)
    picks = (
        lax.broadcasted_iota(jnp.int32, (width, 128), 0) // HD
        == lax.broadcasted_iota(jnp.int32, (width, 128), 1)
    ).astype(jnp.float32)
    skip = skip_ref[0:1, :]
    rate = heads_ref[1:2, :]
    grad_state = jnp.zeros((states_ref.shape[1], width), jnp.float32)
    grad_taps = [jnp.zeros((1, every), jnp.float32) for _ in range(5)]
    grad_bias = jnp.zeros((1, 128), jnp.float32)
    grad_decay = jnp.zeros((1, 128), jnp.float32)
    grad_skip = jnp.zeros((1, width), jnp.float32)
    for at in reversed(range(blocks)):
        rows = slot_rows(place_ref, at)
        gate = raw_ref[rows, 512 : 512 + width]
        gate_sigma = sigmoid(gate)
        conv = conv_ref[rows, :]
        conv_sigma = sigmoid(conv)
        acted = conv * conv_sigma
        inner = acted[:, :width]
        write = acted[:, width : width + 128].astype(low)
        read = acted[:, width + 128 :].astype(low)
        y = y_ref[rows, :]
        up = up_ref[rows, :]
        grad_gate = up * (y + skip * inner) * gate_sigma * (1.0 + gate * (1.0 - gate_sigma))
        grad_ref[rows, 256 : 256 + width] = grad_gate.astype(low)
        grad_y = up * gate * gate_sigma
        raw_steps = raw_ref[rows, 512 + 2 * width :]
        step, running, running_t = block_decay(raw_steps, heads_ref[0:1, :], rate, lower)
        step_wide = spread_heads(step, width)
        grow = spread_heads(jnp.exp(running), width)
        last = running[BLOCK - 1 : BLOCK, :]
        carry = spread_heads(jnp.exp(last - running), width)
        last_wide = spread_heads(jnp.exp(last), width)
        scaled = inner * step_wide
        scaled_low = scaled.astype(low)
        grad_low = grad_y.astype(low)
        grown_low = (grad_y * grow).astype(low)
        state = states_ref[at]
        state_low = state.astype(low)
        grad_state_low = grad_state.astype(low)
        meet = dot(read, write, NT)
        grad_meet = jnp.zeros((BLOCK, BLOCK), jnp.float32)
        inside = []
        for pair in range(width // 128):
            weights = [
                block_weights(running, running_t, lower, head) for head in (2 * pair, 2 * pair + 1)
            ]
            both = jnp.concatenate([(meet * item).astype(low) for item in weights], axis=0)
            piece = grad_low[:, pair * 128 : (pair + 1) * 128]
            split = jnp.concatenate([jnp.where(first, piece, zero), jnp.where(first, zero, piece)])
            grad_both = dot(split, scaled_low[:, pair * 128 : (pair + 1) * 128], NT)
            grad_meet = (
                grad_meet + grad_both[:BLOCK] * weights[0] + grad_both[BLOCK:] * weights[1]
            )
            inside.append(dot(both, split, TN))
        grad_inside = jnp.concatenate(inside, axis=1)
        from_state = carry * dot(write, grad_state_low)
        carried = carry * scaled
        grad_scaled = grad_inside + from_state
        moved = scaled * from_state
        turn = grad_low.astype(jnp.float32) * y - scaled_low.astype(jnp.float32) * grad_inside - moved
        direct = grad_y * inner
        ends = jnp.sum(moved, axis=0, keepdims=True) + last_wide * jnp.sum(
            state * grad_state, axis=0, keepdims=True
        )
        summed = dot(
            jnp.concatenate([turn, grad_scaled * inner, jnp.broadcast_to(ends, (8, width))]),
            picks,
            NN,
            HIGHEST,
        )
        grad_running = (
            dot(lower.astype(jnp.float32), summed[:BLOCK], TN, HIGHEST)
            + summed[2 * BLOCK : 2 * BLOCK + 1]
        )
        grad_step = grad_running * rate + summed[BLOCK : 2 * BLOCK]
        grad_decay = grad_decay + jnp.sum(grad_running * step * rate, axis=0, keepdims=True)
        grad_steps = grad_step * sigmoid(raw_steps + heads_ref[0:1, :])
        grad_bias = grad_bias + jnp.sum(grad_steps, axis=0, keepdims=True)
        grad_skip = grad_skip + jnp.sum(direct, axis=0, keepdims=True)
        grad_ref[rows, 256 + 2 * width :] = grad_steps.astype(low)
        grad_inner = grad_scaled * step_wide + skip * grad_y
        grad_meet_low = grad_meet.astype(low)
        grad_read = dot(grad_meet_low, write) + dot(grown_low, state_low, NT)
        grad_write = dot(grad_meet_low, read, TN) + dot(carried.astype(low), grad_state_low, NT)
        grad_state = last_wide * grad_state + dot(read, grown_low, TN)
        grad_conv = jnp.concatenate([grad_inner, grad_write, grad_read], axis=1) * (
            conv_sigma * (1.0 + conv * (1.0 - conv_sigma))
        )
        later_ref[at * BLOCK : (at + 1) * BLOCK, :] = grad_conv
        back = jnp.zeros((BLOCK, every), jnp.float32)
        for tap in range(4):
            back = back + taps_ref[tap : tap + 1, :] * later_ref[pl.ds(at * BLOCK + 3 - tap, BLOCK), :]
            seen = history_ref[pl.ds(5 + tap + at * BLOCK, BLOCK), :]
            grad_taps[tap] = grad_taps[tap] + jnp.sum(grad_conv * seen, axis=0, keepdims=True)
        grad_taps[4] = grad_taps[4] + jnp.sum(grad_conv, axis=0, keepdims=True)
        grad_ref[rows, 256 + width : 256 + 2 * width] = back[:, :width].astype(low)
        grad_ref[rows, 0:256] = back[:, width:].astype(low)
    for tap in range(5):
        grad_taps_ref[tap : tap + 1, :] = grad_taps[tap]
    grad_taps_ref[5:8, :] = jnp.zeros((3, every), jnp.float32)
    skip_heads = dot(jnp.broadcast_to(grad_skip, (8, width)), picks, NN, HIGHEST)
    grad_heads_ref[...] = jnp.zeros(grad_heads_ref.shape, jnp.float32)
    grad_heads_ref[0:1, :] = grad_bias
    grad_heads_ref[1:2, :] = grad_decay
    grad_heads_ref[2:3, :] = skip_heads[0:1]


def turned(values, cosine, sine):
    early = lane_index(values.shape[0]) % HD < HD // 2
    other = jnp.where(early, pltpu.roll(values, 128 - HD // 2, 1), pltpu.roll(values, HD // 2, 1))
    return values * cosine + other * sine


def both_heads(values, first):
    zero = jnp.zeros(values.shape, values.dtype)
    return jnp.concatenate([jnp.where(first, values, zero), jnp.where(first, zero, values)])


def attention_forward_kernel(
    place_ref, raw_ref, angle_ref, mixed_ref, kept_ref, probs_ref
):
    low = jnp.bfloat16
    blocks = mixed_ref.shape[0] // BLOCK
    first = lane_index(BLOCK) < HD
    for at in range(blocks):
        rows = slot_rows(place_ref, at)
        here = slice(at * BLOCK, (at + 1) * BLOCK)
        cosine = angle_ref[here, 0:128]
        sine = angle_ref[here, 128:256]
        pair = raw_ref[rows, 128:256]
        key = turned(pair, cosine, sine)
        kept_ref[here, 0:128] = turned(raw_ref[rows, 0:128], cosine, sine).astype(low)
        kept_ref[here, 128:256] = jnp.where(first, key, pltpu.roll(key, HD, 1)).astype(low)
        kept_ref[here, 256:384] = jnp.where(first, pltpu.roll(pair, HD, 1), pair).astype(low)
    for at in range(blocks):
        rows = slot_rows(place_ref, at)
        here = slice(at * BLOCK, (at + 1) * BLOCK)
        reach = (at + 1) * BLOCK
        query = both_heads(kept_ref[here, 0:128], first)
        scores = dot(query, kept_ref[0:reach, 128:256], NT) * (HD ** (-0.5))
        row = lax.broadcasted_iota(jnp.int32, (2 * BLOCK, reach), 0) % BLOCK + at * BLOCK
        column = lax.broadcasted_iota(jnp.int32, (2 * BLOCK, reach), 1)
        scores = jnp.where(row >= column, scores, -1e30)
        exponent = jnp.exp(scores - jnp.max(scores, axis=1, keepdims=True))
        probs = (exponent / jnp.sum(exponent, axis=1, keepdims=True)).astype(low)
        probs_ref[at, :, 0:reach] = probs
        out = dot(probs, kept_ref[0:reach, 256:384])
        mixed_ref[rows, :] = jnp.where(first, out[:BLOCK], out[BLOCK:]).astype(low)


def attention_backward_kernel(
    place_ref, up_ref, angle_ref, kept_ref, probs_ref, grad_ref, key_ref, value_ref
):
    low = jnp.bfloat16
    blocks = up_ref.shape[0] // BLOCK
    first = lane_index(BLOCK) < HD
    scale = HD ** (-0.5)
    key_ref[...] = jnp.zeros(key_ref.shape, jnp.float32)
    value_ref[...] = jnp.zeros(value_ref.shape, jnp.float32)
    for at in range(blocks):
        rows = slot_rows(place_ref, at)
        here = slice(at * BLOCK, (at + 1) * BLOCK)
        reach = (at + 1) * BLOCK
        query = both_heads(kept_ref[here, 0:128], first)
        up = both_heads(up_ref[rows, :], first)
        probs_low = probs_ref[at, :, 0:reach]
        probs = probs_low.astype(jnp.float32)
        grad_probs = dot(up, kept_ref[0:reach, 256:384], NT)
        inner = jnp.sum(probs * grad_probs, axis=1, keepdims=True)
        grad_scores = (probs * (grad_probs - inner)).astype(low)
        both = dot(grad_scores, kept_ref[0:reach, 128:256]) * scale
        grad_query = jnp.where(first, both[:BLOCK], both[BLOCK:])
        grad_ref[rows, 0:128] = turned(
            grad_query, angle_ref[here, 0:128], -angle_ref[here, 128:256]
        ).astype(low)
        key_ref[0:reach, :] += dot(grad_scores, query, TN)
        value_ref[0:reach, :] += dot(probs_low, up, TN)
    for at in range(blocks):
        rows = slot_rows(place_ref, at)
        here = slice(at * BLOCK, (at + 1) * BLOCK)
        key = key_ref[here, :]
        value = value_ref[here, :]
        key = (key + pltpu.roll(key, HD, 1)) * scale
        key = turned(key, angle_ref[here, 0:128], -angle_ref[here, 128:256])
        value = value + pltpu.roll(value, HD, 1)
        grad_ref[rows, 128:256] = jnp.where(first, key, value).astype(low)


def angle_table(length):
    half = HD // 2
    freq = THETA ** (-np.arange(half, dtype=np.float32) / half)
    angle = np.arange(length, dtype=np.float32)[:, None] * freq[None, :]
    cosine = np.tile(np.cos(angle), (1, 4))
    sine = np.tile(np.concatenate([-np.sin(angle), np.sin(angle)], axis=1), (1, 2))
    return np.concatenate([cosine, sine], axis=1).astype(np.float32)


def run_kernel(kernel, place, operands, outs, scratch, name, flops=2e8, limit=None, fetched=()):
    whole = pl.BlockSpec(memory_space=pltpu.VMEM)
    held = sum(item.size * item.dtype.itemsize for item in operands)
    held += sum(math.prod(shape) * jnp.dtype(dtype).itemsize for shape, dtype in outs)
    held += sum(
        math.prod(item.shape) * jnp.dtype(item.dtype).itemsize
        for item in (scratch[:-1] if fetched else scratch)
    )
    held -= sum(operands[at].size * operands[at].dtype.itemsize for at in fetched)
    return pl.pallas_call(
        kernel,
        out_shape=[jax.ShapeDtypeStruct(shape, dtype) for shape, dtype in outs],
        in_specs=[pl.BlockSpec(memory_space=pltpu.SMEM)]
        + [
            pl.BlockSpec(memory_space=pl.ANY) if at in fetched else whole
            for at in range(len(operands))
        ],
        out_specs=[whole] * len(outs),
        scratch_shapes=scratch,
        compiler_params=pltpu.CompilerParams(vmem_limit_bytes=limit or held + 8 * 2**20),
        cost_estimate=pl.CostEstimate(flops=int(flops), bytes_accessed=1 << 20, transcendentals=0),
        name=name,
    )(place, *operands)


def state_forward(place, raw, taps, heads, skip, states):
    length = raw.shape[0]
    width = skip.shape[1]
    wide = jnp.float32
    return run_kernel(
        state_forward_kernel,
        place,
        (raw, taps, heads, skip),
        [
            ((length, width), wide),
            ((8, length), wide),
            ((length, width + 256), wide),
            ((length, width), wide),
            ((length // BLOCK, states, width), wide),
        ],
        [pltpu.VMEM((length + 8, width + 256), wide)],
        "state_forward",
    )


def state_backward(place, raw, conv, y, states, up, taps, heads, skip):
    length = raw.shape[0]
    width = skip.shape[1]
    wide = jnp.float32
    return run_kernel(
        state_backward_kernel,
        place,
        (raw, conv, y, states, up, taps, heads, skip),
        [
            ((length, 256 + 2 * width + 128), jnp.bfloat16),
            ((8, width + 256), wide),
            ((8, 128), wide),
        ],
        [pltpu.VMEM((length + 8, width + 256), wide), pltpu.VMEM((length + 8, width + 256), wide)],
        "state_backward",
    )


def attention_forward(place, raw, angles):
    length = raw.shape[0]
    low = jnp.bfloat16
    return run_kernel(
        attention_forward_kernel,
        place,
        (raw, angles),
        [
            ((length, 128), low),
            ((length, 384), low),
            ((length // BLOCK, 2 * BLOCK, length), low),
        ],
        [],
        "attention_forward",
    )


def attention_backward(place, up, angles, kept, probs):
    length = up.shape[0]
    return run_kernel(
        attention_backward_kernel,
        place,
        (up, angles, kept, probs),
        [((length, 256), jnp.bfloat16)],
        [pltpu.VMEM((length, 128), jnp.float32), pltpu.VMEM((length, 128), jnp.float32)],
        "attention_backward",
    )[0]


def block_columns(me_ref, mask):
    return pl.ds(pl.multiple_of((me_ref[0] ^ mask) * 128, 128), 128)


def join_rows(slots, whole_ref):
    rows = slots[0].shape[0]
    for at, slot in enumerate(slots):
        whole_ref[at * rows : (at + 1) * rows, :] = slot[...]


def pack_kernel(
    head_ref,
    rows_ref,
    gain_ref,
    query_ref,
    key_ref,
    value_ref,
    write_ref,
    read_ref,
    gate_ref,
    inner_ref,
    step_ref,
    output_ref,
    state_ref,
    feed_gate_ref,
    feed_up_ref,
    feed_down_ref,
    normed_ref,
    mixer_ref,
    feed_ref,
):
    rows = rows_ref[...].astype(jnp.float32)
    scale = lax.rsqrt(jnp.mean(rows * rows, axis=1, keepdims=True) + EPS)
    normed_ref[...] = (rows * scale * gain_ref[0:1, :]).astype(normed_ref.dtype)

    def turned_over(ref):
        return ref[...].astype(jnp.float32).T.astype(mixer_ref.dtype)

    low_head = head_ref[0] == 0
    first = lane_index(rows.shape[0]) < HD
    key = key_ref[...].astype(jnp.float32)
    value = value_ref[...].astype(jnp.float32)
    key = jnp.where(low_head, key, pltpu.roll(key, HD, 1))
    value = jnp.where(low_head, pltpu.roll(value, HD, 1), value)
    mixer_ref[:, 0:128] = query_ref[...]
    mixer_ref[:, 128:256] = jnp.where(first, key, value).astype(mixer_ref.dtype)
    mixer_ref[:, 256:384] = write_ref[...]
    mixer_ref[:, 384:512] = read_ref[...]
    at = 512
    for ref in (gate_ref, inner_ref):
        mixer_ref[:, at : at + ref.shape[1]] = ref[...]
        at += ref.shape[1]
    mixer_ref[:, at : at + 128] = jnp.zeros((rows.shape[0], 128), mixer_ref.dtype)
    mixer_ref[:, at : at + step_ref.shape[1]] = step_ref[...]
    mixer_ref[:, at + 128 : at + 256] = turned_over(output_ref)
    mixer_ref[:, at + 256 :] = turned_over(state_ref)
    units = feed_gate_ref.shape[1]
    feed_ref[:, :units] = feed_gate_ref[...]
    feed_ref[:, units : 2 * units] = feed_up_ref[...]
    feed_ref[:, 2 * units :] = turned_over(feed_down_ref)


def gather_columns(me_ref, rows_ref, side, chips):
    return jnp.concatenate(
        [rows_ref[:, block_columns(me_ref, 2 * at + side)] for at in range(chips)], axis=1
    )


def project_kernel(me_ref, *refs):
    slots, (near_ref, far_ref, rows_ref, raw_ref) = refs[:-4], refs[-4:]
    join_rows(slots, rows_ref)
    chips = near_ref.shape[0] // 128
    columns = raw_ref.shape[1]
    raw_ref[...] = dot(
        gather_columns(me_ref, rows_ref, 0, chips), near_ref[:, :columns]
    ) + dot(gather_columns(me_ref, rows_ref, 1, chips), far_ref[:, :columns])


def write_spread(total, own_ref, sends):
    rows = own_ref.shape[0]
    own_ref[...] = total[:rows]
    for at, send in enumerate(sends):
        send[...] = total[(at + 1) * rows : (at + 2) * rows].astype(jnp.bfloat16)


def spread_kernel(start, me_ref, mixed_ref, state_ref, near_ref, far_ref, own_ref, *rest):
    sends, total_ref = rest[:-1], rest[-1]
    left = jnp.concatenate([mixed_ref[...], state_ref[...]], axis=1)
    spread_total(me_ref, left, near_ref, far_ref, slice(start, start + left.shape[1]), total_ref)
    write_spread(total_ref[...], own_ref, sends)


def spread_total(me_ref, left, near_ref, far_ref, columns, total_ref):
    chips = near_ref.shape[0] // 128
    for side, weight_ref in enumerate((near_ref, far_ref)):
        piece = dot(left, weight_ref[:, columns], NT)
        for at in range(chips):
            total_ref[:, block_columns(me_ref, 2 * at + side)] = piece[:, at * 128 : (at + 1) * 128]


def ordered_kernel(start, place_ref, left_ref, weight_ref, out_ref):
    total = dot(left_ref[...], weight_ref[:, start : start + left_ref.shape[1]], NT)
    for at in range(total.shape[0] // BLOCK):
        out_ref[slot_rows(place_ref, at), :] = total[at * BLOCK : (at + 1) * BLOCK].astype(
            out_ref.dtype
        )


def total_kernel(
    spot_ref, attention_ref, mixer_ref, near_ref, far_ref, rows_ref, gain_ref, out_ref, total_ref
):
    left = jnp.concatenate([attention_ref[...], mixer_ref[...]], axis=1)
    spread_total(spot_ref.at[1:2], left, near_ref, far_ref, slice(0, left.shape[1]), total_ref)
    total = total_ref[...]
    gain_ref[...] = jnp.broadcast_to(
        jnp.sum(total * rows_ref[...].astype(jnp.float32), axis=0, keepdims=True), gain_ref.shape
    )
    for at in range(total.shape[0] // BLOCK):
        out_ref[slot_rows(spot_ref, at), :] = total[at * BLOCK : (at + 1) * BLOCK].astype(
            out_ref.dtype
        )


def feed_kernel(place_ref, *refs):
    low = jnp.bfloat16
    slots, cots_ref = refs[:4], refs[4]
    feed_ref, pair_ref, active_ref, own_ref = refs[5:9]
    sends = refs[9:12]
    units = active_ref.shape[1]
    rows = slots[0].shape[0]
    for half in range(2):
        here = slice(2 * half * rows, 2 * (half + 1) * rows)
        left = jnp.concatenate([slots[2 * half][...], slots[2 * half + 1][...]])
        cot = jnp.concatenate([cots_ref[slot_rows(place_ref, 2 * half + at), :] for at in range(2)])
        gate_up = dot(left, feed_ref[:, : 2 * units])
        grad_active = dot(cot, feed_ref[:, 2 * units :])
        gate = gate_up[:, :units]
        up = gate_up[:, units:]
        sigma = sigmoid(gate)
        swish = gate * sigma
        active_ref[here, :] = (swish * up).astype(low)
        grad_gate = grad_active * up * sigma * (1.0 + gate * (1.0 - sigma))
        pair = jnp.concatenate([grad_gate, grad_active * swish], axis=1).astype(low)
        pair_ref[here, :] = pair
        total = dot(pair, feed_ref[:, : 2 * units], NT)
        if half == 0:
            own_ref[...] = total[:rows]
            sends[0][...] = total[rows:].astype(low)
        else:
            sends[1][...] = total[:rows].astype(low)
            sends[2][...] = total[rows:].astype(low)


def write_halves(piece, even, keep_ref, give_ref, chip):
    piece = piece.astype(keep_ref.dtype)
    keep_ref[chip] = jnp.where(even, piece[:128], piece[128:])
    give_ref[chip] = jnp.where(even, piece[128:], piece[:128])


def feed_grad_kernel(place_ref, *refs):
    slots, cots_ref = refs[:4], refs[4]
    pair_ref, active_ref, out_ref, rows_ref, cot_ref = refs[5:]
    join_rows(slots, rows_ref)
    for at in range(len(slots)):
        cot_ref[at * BLOCK : (at + 1) * BLOCK, :] = cots_ref[slot_rows(place_ref, at), :]
    both = pair_ref.shape[1]
    for at in range(0, rows_ref.shape[1], 256):
        here = slice(at, at + 256)
        out_ref[here, :both] = dot(rows_ref[:, here], pair_ref[...], TN).astype(out_ref.dtype)
        out_ref[here, both:] = dot(cot_ref[:, here], active_ref[...], TN).astype(out_ref.dtype)


def core_add_kernel(me_ref, *refs):
    outs = refs[-4:]
    chip = me_ref[0] // 2
    keep_ref, got_ref = refs[:2]
    rows = keep_ref.shape[1]
    for mask, out in enumerate(outs):
        at = chip ^ mask
        total = keep_ref[at].astype(jnp.float32) + got_ref[at].astype(jnp.float32)
        out[0:rows, :] = total.astype(out.dtype)
        if len(refs) > 6:
            total = refs[2][...].astype(jnp.float32) + refs[3][...].astype(jnp.float32)
            out[rows:, :] = total.astype(out.dtype)


def finish_kernel(layout, place_ref, *refs):
    terms, outs = refs[: len(refs) - len(layout)], refs[len(refs) - len(layout) :]
    total = paired_sum([item[...].astype(jnp.float32) for item in terms])
    for (start, stop, over), out in zip(layout, outs):
        piece = total[:, start:stop]
        out[...] = piece.T if over else piece


def assemble_kernel(me_ref, near_ref, far_ref, key_ref, value_ref, write_ref, read_ref):
    wide = jnp.float32
    rows = 128
    first = lane_index(rows) < HD
    for side, ref in enumerate((near_ref, far_ref)):
        for chip in range(near_ref.shape[0] // rows):
            here = slice(chip * rows, (chip + 1) * rows)
            there = pl.ds(pl.multiple_of((me_ref[0] ^ (2 * chip + side)) * rows, rows), rows)
            low_head = ref[here, 0:128].astype(wide)
            high_head = ref[here, 128:256].astype(wide)
            key_ref[there, :] = jnp.where(first, low_head, pltpu.roll(high_head, HD, 1))
            value_ref[there, :] = jnp.where(first, pltpu.roll(low_head, HD, 1), high_head)
            write_ref[there, :] = ref[here, 256:384].astype(wide)
            read_ref[there, :] = ref[here, 384:512].astype(wide)


def weight_grad_kernel(groups, me_ref, *refs):
    keep_ref, give_ref = refs[-2:]
    even = me_ref[0] % 2 == 0
    for chip in range(keep_ref.shape[0]):
        here = slice(chip * 256, (chip + 1) * 256)
        pieces = []
        at = 0
        for count in groups:
            left = refs[at][:, here]
            right = jnp.concatenate([item[...] for item in refs[at + 1 : at + 1 + count]], axis=1)
            pieces.append(dot(left, right, TN))
            at += 1 + count
        write_halves(jnp.concatenate(pieces, axis=1), even, keep_ref, give_ref, chip)


def mixer_back_kernel(start, me_ref, *refs):
    slots = refs[:4]
    near_ref, far_ref, gated_ref, gain_ref, normed_ref = refs[4:9]
    cot_ref, mixed_ref, state_ref, inner_ref, gain_out_ref = refs[9:]
    join_rows(slots, cot_ref)
    chips = near_ref.shape[0] // 128
    both = dot(gather_columns(me_ref, cot_ref, 0, chips), near_ref[:, start:]) + dot(
        gather_columns(me_ref, cot_ref, 1, chips), far_ref[:, start:]
    )
    mixed_ref[...] = both[:, :128].astype(jnp.bfloat16)
    state = both[:, 128:]
    state_ref[...] = state
    gain_sum = jnp.sum(state * normed_ref[...].astype(jnp.float32), axis=0, keepdims=True)
    gain_out_ref[...] = jnp.broadcast_to(gain_sum / gain_ref[0:1, :], gain_out_ref.shape)
    product_rows = state * gain_ref[0:1, :] * gated_ref[...]
    inner_ref[...] = dot(
        jnp.ones((8, product_rows.shape[1]), jnp.float32), product_rows, NT, HIGHEST
    )


def pack(head, hidden, gain, *weights):
    rows, columns = hidden.shape
    low = jnp.bfloat16
    width = weights[5].shape[1]
    units = weights[-3].shape[1]
    return run_kernel(
        pack_kernel,
        head,
        (hidden, gain, *weights),
        [((rows, columns), low), ((rows, 768 + 3 * width), low), ((rows, 3 * units), low)],
        [],
        "pack",
        limit=60 * 2**20,
    )


def middle_kernel(
    spot_ref,
    up_ref,
    angle_ref,
    kept_ref,
    probs_ref,
    cot_ref,
    mixed_ref,
    state_ref,
    rows_ref,
    active_ref,
    feed_ref,
    grad_ref,
    keep_ref,
    give_ref,
    terms_ref,
    key_ref,
    value_ref,
):
    attention_backward_kernel(
        spot_ref, up_ref, angle_ref, kept_ref, probs_ref, grad_ref, key_ref, value_ref
    )
    weight_grad_kernel(
        (2, 1),
        spot_ref.at[1:2],
        cot_ref,
        mixed_ref,
        state_ref,
        rows_ref,
        grad_ref,
        keep_ref,
        give_ref,
    )
    units = active_ref.shape[1]
    ordered_kernel(2 * units, spot_ref, active_ref, feed_ref, terms_ref)


def small_pieces(in_gain, ffn_gain, grad_taps, state_gain, grad_heads):
    width = state_gain.shape[1]
    wide = jnp.float32

    def fill(row):
        missing = -row.shape[1] % 256
        if missing:
            row = jnp.concatenate([row, jnp.zeros((1, missing), wide)], axis=1)
        return [row[:, at : at + 256] for at in range(0, row.shape[1], 256)]

    pieces = fill(in_gain) + fill(ffn_gain)
    for tap in range(5):
        pieces += fill(grad_taps[tap : tap + 1, width:])
    for tap in range(5):
        pieces += fill(grad_taps[tap : tap + 1, :width])
    pieces += fill(state_gain)
    for row in range(3):
        pieces += fill(grad_heads[row : row + 1, :])
    return pieces + [jnp.zeros((1, 256), wide)] * (32 - len(pieces))


def last_kernel(
    ready,
    spot_ref,
    raw_ref,
    conv_ref,
    y_ref,
    states_ref,
    up_ref,
    taps_ref,
    heads_ref,
    skip_ref,
    attention_ref,
    near_ref,
    far_ref,
    rows_ref,
    in_gain_ref,
    second_ref,
    normed_ref,
    ffn_gain_ref,
    state_gain_ref,
    pair_keep_ref,
    pair_give_ref,
    late_keep_ref,
    late_give_ref,
    total_low_ref,
    small_ref,
    grad_ref,
    grad_taps_ref,
    grad_heads_ref,
    history_ref,
    later_ref,
    gain_ref,
    total_ref,
    rows_small_ref,
):
    state_backward_kernel(
        spot_ref,
        raw_ref,
        conv_ref,
        y_ref,
        states_ref,
        up_ref,
        taps_ref,
        heads_ref,
        skip_ref,
        grad_ref,
        grad_taps_ref,
        grad_heads_ref,
        history_ref,
        later_ref,
    )
    ready()
    me_ref = spot_ref.at[1:2]
    weight_grad_kernel(
        (1,), me_ref, rows_ref, grad_ref.at[:, 0:256], pair_keep_ref, pair_give_ref
    )
    total_kernel(
        spot_ref,
        attention_ref,
        grad_ref,
        near_ref,
        far_ref,
        rows_ref,
        gain_ref,
        total_low_ref,
        total_ref,
    )
    weight_grad_kernel(
        (1,),
        me_ref,
        rows_ref,
        grad_ref.at[:, 256 : grad_ref.shape[1]],
        late_keep_ref,
        late_give_ref,
    )
    ffn_gain = jnp.sum(
        second_ref[...] * normed_ref[...].astype(jnp.float32), axis=0, keepdims=True
    )
    pieces = small_pieces(
        gain_ref[0:1, :] / in_gain_ref[0:1, :],
        ffn_gain / ffn_gain_ref[0:1, :],
        grad_taps_ref[...],
        state_gain_ref[0:1, :],
        grad_heads_ref[...],
    )
    for at, piece in enumerate(pieces):
        rows_small_ref[at : at + 1, :] = piece
    small_ref[...] = rows_small_ref[...].astype(small_ref.dtype)


FETCHED = (0, 1, 2, 3, 4, 8, 9, 10, 11, 13, 14)


def last_fetch_kernel(spot_ref, *refs):
    ins, rest = list(refs[:17]), refs[17:]
    count = len(FETCHED)
    buffers, sems = rest[-1 - count : -1], rest[-1]
    copies = []
    for slot, (at, buffer) in enumerate(zip(FETCHED, buffers)):
        copies.append(pltpu.make_async_copy(ins[at], buffer, sems.at[slot]))
        copies[-1].start()
        ins[at] = buffer
    for copy in copies[:5]:
        copy.wait()

    def ready():
        for copy in copies[5:]:
            copy.wait()

    last_kernel(ready, spot_ref, *ins, *rest[: -1 - count])


def middle(spot, up, angles, kept, probs, cot, mixed, state, rows, active, feed):
    length = up.shape[0]
    low = jnp.bfloat16
    columns = mixed.shape[1] + state.shape[1] + 256
    scratch = pltpu.VMEM((length, 128), jnp.float32)
    return run_kernel(
        middle_kernel,
        spot,
        (up, angles, kept, probs, cot, mixed, state, rows, active, feed),
        [
            ((length, 256), low),
            ((4, 128, columns), low),
            ((4, 128, columns), low),
            ((length, rows.shape[1]), low),
        ],
        [scratch, scratch],
        "middle",
    )


def last(spot, *operands):
    raw, skip, rows = operands[0], operands[7], operands[11]
    length, width = raw.shape[0], skip.shape[1]
    low, wide = jnp.bfloat16, jnp.float32
    rest = 2 * width + 128
    every = width + 256
    buffers = [pltpu.VMEM(operands[at].shape, operands[at].dtype) for at in FETCHED]
    return run_kernel(
        last_fetch_kernel,
        spot,
        operands,
        [
            ((4, 128, 256), low),
            ((4, 128, 256), low),
            ((4, 128, rest), low),
            ((4, 128, rest), low),
            (rows.shape, low),
            ((32, 256), low),
        ],
        [
            pltpu.VMEM((length, 256 + rest), low),
            pltpu.VMEM((8, every), wide),
            pltpu.VMEM((8, 128), wide),
            pltpu.VMEM((length + 8, every), wide),
            pltpu.VMEM((length + 8, every), wide),
            pltpu.VMEM((8, rows.shape[1]), wide),
            pltpu.VMEM(rows.shape, wide),
            pltpu.VMEM((32, 256), wide),
            *buffers,
            pltpu.SemaphoreType.DMA((len(FETCHED),)),
        ],
        "last",
        fetched=FETCHED,
    )


def project(me, slots, near, far, columns):
    length = len(slots) * slots[0].shape[0]
    return run_kernel(
        project_kernel,
        me,
        (*slots, near, far),
        [((length, slots[0].shape[1]), jnp.bfloat16), ((length, columns), jnp.float32)],
        [],
        "project",
    )


def spread_outs(rows, columns, parts):
    return [((rows, columns), jnp.float32)] + [((rows, columns), jnp.bfloat16)] * (parts - 1)


def spread_product(me, mixed, state, near, far, start, parts):
    length, columns = mixed.shape[0], 2 * near.shape[0]
    return run_kernel(
        functools.partial(spread_kernel, start),
        me,
        (mixed, state, near, far),
        spread_outs(length // parts, columns, parts),
        [pltpu.VMEM((length, columns), jnp.float32)],
        "spread_product",
    )


def ordered_product(place, left, weight, start):
    return run_kernel(
        functools.partial(ordered_kernel, start),
        place,
        (left, weight),
        [((left.shape[0], weight.shape[0]), jnp.bfloat16)],
        [],
        "ordered_product",
    )[0]


def total_product(spot, attention, mixer, near, far, rows):
    length, columns = rows.shape
    return run_kernel(
        total_kernel,
        spot,
        (attention, mixer, near, far, rows),
        [((8, columns), jnp.float32), ((length, columns), jnp.bfloat16)],
        [pltpu.VMEM((length, columns), jnp.float32)],
        "total_product",
    )


def feed_forward(place, slots, cotangent, feed):
    rows, columns = slots[0].shape
    units = feed.shape[1] // 3
    parts = len(slots)
    return run_kernel(
        feed_kernel,
        place,
        (*slots, cotangent, feed),
        [((parts * rows, 2 * units), jnp.bfloat16), ((parts * rows, units), jnp.bfloat16)]
        + spread_outs(rows, columns, parts),
        [],
        "feed_forward",
    )


def feed_grad(place, slots, cotangent, pair, active):
    length, columns = pair.shape[0], slots[0].shape[1]
    scratch = pltpu.VMEM((length, columns), jnp.bfloat16)
    return run_kernel(
        feed_grad_kernel,
        place,
        (*slots, cotangent, pair, active),
        [((columns, pair.shape[1] + active.shape[1]), jnp.bfloat16)],
        [scratch, scratch],
        "feed_grad",
    )[0]


def weight_grad(me, groups):
    counts = tuple(len(rights) for _, rights in groups)
    columns = sum(item.shape[1] for _, rights in groups for item in rights)
    operands = [item for left, rights in groups for item in (left, *rights)]
    blocks = groups[0][0].shape[1] // 256
    return run_kernel(
        functools.partial(weight_grad_kernel, counts),
        me,
        operands,
        [((blocks, 128, columns), jnp.bfloat16)] * 2,
        [],
        "weight_grad",
    )


def core_add(me, operands):
    keep = operands[0]
    rows = keep.shape[1] + (operands[2].shape[0] if len(operands) > 2 else 0)
    return run_kernel(
        core_add_kernel,
        me,
        operands,
        [((rows, keep.shape[2]), jnp.bfloat16)] * 4,
        [],
        "core_add",
    )


def finish(place, terms, layout):
    rows = terms[0].shape[0]
    if rows != 128:
        total = terms[0].astype(jnp.float32)
        pieces = [total[:, start:stop] for start, stop, _ in layout]
        return [item.T if over else item for item, (_, _, over) in zip(pieces, layout)]
    shapes = [
        ((stop - start, rows) if over else (rows, stop - start), jnp.float32)
        for start, stop, over in layout
    ]
    return run_kernel(
        functools.partial(finish_kernel, layout), place, terms, shapes, [], "finish"
    )


def assemble(me, near, far):
    rows = 2 * near.shape[0]
    return run_kernel(
        assemble_kernel, me, (near, far), [((rows, 128), jnp.float32)] * 4, [], "assemble"
    )


def mixer_back(me, slots, near, far, start, gated, gain, normed):
    rows, columns = slots[0].shape
    length = len(slots) * rows
    width = gated.shape[1]
    return run_kernel(
        functools.partial(mixer_back_kernel, start),
        me,
        (*slots, near, far, gated, gain, normed),
        [
            ((length, columns), jnp.bfloat16),
            ((length, 128), jnp.bfloat16),
            ((length, width), jnp.float32),
            ((8, length), jnp.float32),
            ((8, width), jnp.float32),
        ],
        [],
        "mixer_back",
    )


def swap(values, axis, mask):
    size = lax.axis_size(axis)
    return lax.ppermute(values, axis, [(index, index ^ mask) for index in range(size)])


def tensor_gather(block):
    masks = reversed(range(1, lax.axis_size("tensor")))
    return [block] + [swap(block, "tensor", mask) for mask in masks][::-1]


def paired_sum(terms):
    while len(terms) > 1:
        terms = [terms[at] + terms[at + 1] for at in range(0, len(terms), 2)]
    return terms[0]


def tensor_send(sends):
    return [swap(item, "tensor", at + 1) for at, item in enumerate(sends)]


def finish_scatter(own, got):
    return paired_sum([own] + [item.astype(jnp.float32) for item in got])


def cut(total, parts):
    blocks = jnp.split(total, parts)
    return blocks[:1] + [item.astype(jnp.bfloat16) for item in blocks[1:]]


def slot_sum(values):
    parts = lax.axis_size("tensor")
    shaped = values.reshape(parts, -1)
    terms = [shaped]
    for mask in range(1, parts):
        got = swap(shaped, "tensor", mask)
        terms.append(jnp.stack([got[at ^ mask] for at in range(parts)]))
    return paired_sum(terms).reshape(-1)


def tie(*values):
    return lax.optimization_barrier(values)


def dp_pieces(block):
    mine = jnp.stack([block] + [swap(block, "dp", 2 * chip) for chip in range(1, 4)])
    return mine.reshape(-1, block.shape[1])


def core_terms(me_ref, groups):
    if lax.axis_size("dp") != 8:
        return jnp.concatenate(
            [product_left(left, jnp.concatenate(rights, axis=1)) for left, rights in groups], axis=1
        ).astype(jnp.bfloat16)
    keep, give = weight_grad(me_ref, groups)
    return keep, swap(give, "dp", 1)


def chip_terms(me_ref, both, small=None, after=None):
    if lax.axis_size("dp") != 8:
        summed = lax.psum_scatter(both, "dp", scatter_dimension=0, tiled=True).astype(jnp.float32)
        if small is not None:
            summed = jnp.concatenate([summed, lax.psum(small, "dp")])
        return [summed]
    operands = both
    if small is not None:
        small = small.astype(jnp.bfloat16)
        operands = (*both, small, swap(small, "dp", 1))
    own, *sends = core_add(me_ref, operands)
    if after is not None:
        sends, _ = tie(sends, after)
    return [own] + [swap(item, "dp", 2 * (at + 1)) for at, item in enumerate(sends)]


def body(
    hidden_in,
    norm_in_gain,
    query_weight,
    key_weight,
    value_weight,
    output_weight,
    gate_weight,
    inner_weight,
    write_weight,
    read_weight,
    step_weight,
    conv_weight,
    conv_bias,
    pair_conv_weight,
    pair_conv_bias,
    step_bias,
    decay_log,
    skip_gain,
    state_gain,
    state_out_weight,
    norm_ffn_gain,
    feed_gate_weight,
    feed_up_weight,
    feed_down_weight,
    out_cotangent,
):
    low = jnp.bfloat16
    wide = jnp.float32
    parts = lax.axis_size("tensor")
    place = lax.axis_index("tensor")
    place_ref = place.astype(jnp.int32).reshape(1)
    heads_here = query_weight.shape[1] // HD
    key_head = place * heads_here // (QH // KVH)
    heads_state = step_weight.shape[1]
    width = gate_weight.shape[1]
    units = feed_gate_weight.shape[1]
    states = write_weight.shape[1]

    out_start = 640 + 2 * width
    whole_dp = lax.axis_size("dp") != 8
    rows_in = hidden_in.astype(wide)
    normed, first_scale = root_norm(rows_in, norm_in_gain)
    if whole_dp:
        normed_low = normed.astype(low)
        mixer_local = jnp.concatenate(
            [
                query_weight,
                lax.dynamic_slice_in_dim(key_weight, key_head * HD, HD, 1),
                lax.dynamic_slice_in_dim(value_weight, key_head * HD, HD, 1),
                write_weight,
                read_weight,
                gate_weight,
                inner_weight,
                jnp.pad(step_weight, ((0, 0), (0, 128 - heads_state))),
                output_weight.T,
                state_out_weight.T,
            ],
            axis=1,
        )
        feed_local = jnp.concatenate([feed_gate_weight, feed_up_weight, feed_down_weight.T], axis=1)
    else:
        normed_low, mixer_local, feed_local = pack(
            key_head.astype(jnp.int32).reshape(1),
            hidden_in,
            norm_in_gain[None],
            query_weight,
            key_weight,
            value_weight,
            write_weight,
            read_weight,
            gate_weight,
            inner_weight,
            step_weight,
            output_weight,
            state_out_weight,
            feed_gate_weight,
            feed_up_weight,
            feed_down_weight,
        )
    row_slots = tensor_gather(normed_low)
    me_ref = lax.axis_index("dp").astype(jnp.int32).reshape(1)
    spot_ref = jnp.concatenate([place_ref, me_ref])
    if whole_dp:
        mixer_full = lax.all_gather(mixer_local, "dp", axis=0, tiled=True)
        mixer_rows = jnp.concatenate(row_slots)
        out_full = mixer_full[:, out_start:]
        mixer_full = mixer_full[:, :out_start]
        raw = product(mixer_rows, mixer_full)
    else:
        near_full = dp_pieces(mixer_local)
        near_full, row_slots = tie(near_full, row_slots)
        far_full = swap(near_full, "dp", 1)
    row_slots, feed_local, cot_block = tie(row_slots, feed_local, out_cotangent)
    cotangent = lax.all_gather(cot_block, "tensor", axis=0, tiled=True)
    feed_full = lax.all_gather(feed_local, "dp", axis=0, tiled=True)
    if not whole_dp:
        mixer_rows, raw = project(me_ref, row_slots, near_full, far_full, out_start)
    length = mixer_rows.shape[0]
    block = length // parts

    taps = jnp.concatenate(
        [
            jnp.concatenate([conv_weight, conv_bias[None]]),
            jnp.concatenate([pair_conv_weight, pair_conv_bias[None]]),
        ],
        axis=1,
    )
    taps = jnp.pad(taps, ((0, 3), (0, 0)))
    heads = jnp.pad(
        jnp.stack([step_bias, -jnp.exp(decay_log)]), ((0, 6), (0, 128 - heads_state))
    )
    skip = jnp.repeat(skip_gain, HD)[None]
    angles = jnp.asarray(angle_table(length))

    gated, power, conv, y, kept_states = state_forward(place_ref, raw, taps, heads, skip, states)
    mixed_low, kept, probs = attention_forward(place_ref, raw, angles)
    width_all = width * parts
    power = slot_sum(power[0])
    state_scale = lax.rsqrt(power / width_all + EPS)[:, None]
    state_low = (gated * state_scale * state_gain).astype(low)
    if whole_dp:
        total = product_right(jnp.concatenate([mixed_low, state_low], axis=1), out_full)
        own, *sends = cut(total, parts)
    else:
        own, *sends = spread_product(
            me_ref, mixed_low, state_low, near_full, far_full, out_start, parts
        )
    mixer_shard = finish_scatter(own, tensor_send(sends))
    middle_rows = rows_in + mixer_shard
    second, second_scale = root_norm(middle_rows, norm_ffn_gain)
    second_low = second.astype(low)
    feed_slots = tensor_gather(second_low)
    grad_pair, active, own, *sends = feed_forward(place_ref, feed_slots, cotangent, feed_full)
    second_got = tensor_send(sends)
    if whole_dp:
        cot_slots = jnp.split(cotangent, parts)
        cot_slots = jnp.concatenate(
            [lax.dynamic_index_in_dim(jnp.stack(cot_slots), place ^ at, 0, False) for at in range(parts)]
        )
        feed_both = jnp.concatenate(
            [product_left(jnp.concatenate(feed_slots), grad_pair), product_left(cot_slots, active)],
            axis=1,
        ).astype(low)
    else:
        feed_both = feed_grad(place_ref, feed_slots, cotangent, grad_pair, active)
    second_got, feed_both = tie(second_got, feed_both)
    grad_second = finish_scatter(own, second_got)
    feed_sums = lax.psum_scatter(feed_both, "dp", scatter_dimension=0, tiled=True)

    weighted_second = grad_second * norm_ffn_gain
    inner_second = jnp.sum(weighted_second * middle_rows, axis=-1, keepdims=True)
    grad_middle = (
        out_cotangent.astype(wide)
        + second_scale * weighted_second
        - middle_rows * second_scale**3 * inner_second / middle_rows.shape[-1]
    )
    cot_rows = tensor_gather(grad_middle.astype(low))
    if whole_dp:
        mixer_cot = jnp.concatenate(cot_rows)
        grad_both = product(mixer_cot, out_full)
        grad_mixed, grad_state = grad_both[:, :128].astype(low), grad_both[:, 128:]
        inner_sum = jnp.sum(grad_state * state_gain * gated, axis=1)[None]
        grad_state_gain = jnp.sum(grad_state * gated * state_scale, axis=0, keepdims=True)
    else:
        mixer_cot, grad_mixed, grad_state, inner_sum, grad_state_gain = mixer_back(
            me_ref, cot_rows, near_full, far_full, out_start, gated, state_gain[None], state_low
        )
    grad_mixed, active = tie(grad_mixed, active)
    weighted = grad_state * state_gain
    inner_sum = slot_sum(inner_sum[0])
    if whole_dp:
        grad_attention = attention_backward(place_ref, grad_mixed, angles, kept, probs)
        early_both = core_terms(
            me_ref, [(mixer_cot, (mixed_low, state_low)), (mixer_rows, (grad_attention,))]
        )
        feed_terms = ordered_product(place_ref, active, feed_full, 2 * units)
    else:
        grad_attention, keep, give, feed_terms = middle(
            spot_ref,
            grad_mixed,
            angles,
            kept,
            probs,
            mixer_cot,
            mixed_low,
            state_low,
            mixer_rows,
            active,
            feed_full,
        )
        early_both = (keep, swap(give, "dp", 1))
    early_both, inner_sum = tie(early_both, inner_sum)
    early_parts = chip_terms(me_ref, early_both)
    grad_gated = (
        state_scale * weighted - gated * state_scale**3 * (inner_sum / width_all)[:, None]
    )
    grad_gated, feed_terms, feed_sums = tie(grad_gated, feed_terms, feed_sums)
    feed_shard = lax.psum_scatter(feed_terms, "tensor", scatter_dimension=0, tiled=True)
    if whole_dp:
        grad_mixer, grad_taps, grad_heads = state_backward(
            place_ref, raw, conv, y, kept_states, grad_gated, taps, heads, skip
        )
        pair_both = core_terms(me_ref, [(mixer_rows, (grad_mixer[:, :256],))])
        total_rows = product_right(grad_mixer, mixer_full[:, 256:]) + product_right(
            grad_attention, mixer_full[:, :256]
        )
        gain_rows = jnp.sum(total_rows * mixer_rows.astype(wide), axis=0, keepdims=True)
        total_rows = total_rows.astype(low).reshape(parts, block, -1)
        total_rows = jnp.concatenate(
            [lax.dynamic_index_in_dim(total_rows, place ^ at, 0, False) for at in range(parts)]
        )
        late_both = core_terms(me_ref, [(mixer_rows, (grad_mixer[:, 256:],))])
        ffn_gain = jnp.sum(grad_second * second_low.astype(wide), axis=0)
        small = jnp.concatenate(
            small_pieces(
                gain_rows / norm_in_gain,
                (ffn_gain / norm_ffn_gain)[None],
                grad_taps,
                grad_state_gain,
                grad_heads,
            )
        )
    else:
        pair_keep, pair_give, late_keep, late_give, total_rows, small = last(
            spot_ref,
            raw,
            conv,
            y,
            kept_states,
            grad_gated,
            taps,
            heads,
            skip,
            grad_attention,
            near_full,
            far_full,
            mixer_rows,
            norm_in_gain[None],
            grad_second,
            second_low,
            norm_ffn_gain[None],
            grad_state_gain,
        )
        pair_keep, pair_give, late_keep, late_give, total_rows, small, *beside = tie(
            pair_keep,
            pair_give,
            late_keep,
            late_give,
            total_rows,
            small,
            early_parts,
            feed_shard,
        )
        early_parts, feed_shard = beside
        pair_both = (pair_keep, swap(pair_give, "dp", 1))
        late_both = (late_keep, swap(late_give, "dp", 1))
    grad_first = lax.psum_scatter(total_rows, "tensor", scatter_dimension=0, tiled=True)
    late_parts = chip_terms(me_ref, late_both)
    pair_sums = paired_sum([item.astype(wide) for item in chip_terms(me_ref, pair_both, small)])
    rows_here = query_weight.shape[0]
    flat = pair_sums[rows_here:]
    early_done = finish(
        place_ref,
        early_parts,
        (
            (0, 128, True),
            (128, 128 + width, True),
            (128 + width, 256 + width, False),
            (256 + width, 384 + width, False),
        ),
    )

    shared = jnp.concatenate(
        [
            jnp.concatenate([early_done[3], pair_sums[:rows_here]], axis=1),
            jnp.pad(flat[:16], ((0, 0), (0, 128))),
        ]
    ).astype(low)
    terms = [item.astype(wide) for item in tensor_gather(shared)]
    near = paired_sum(terms[: parts // 2])
    far = paired_sum(terms[parts // 2 :])
    both = near + far
    first_half = place < parts // 2
    head_low = jnp.where(first_half, near[:rows_here, :128], far[:rows_here, :128])
    head_high = jnp.where(first_half, far[:rows_here, :128], near[:rows_here, :128])
    common_sums = both[rows_here:, :256]
    shared = jnp.concatenate([head_low, head_high, both[:rows_here, 128:]], axis=1).astype(low)
    late_done = finish(
        place_ref,
        late_parts,
        ((0, width, False), (width, 2 * width, False), (2 * width, 2 * width + heads_state, False)),
    )
    hidden_out = (middle_rows + feed_shard.astype(wide)).astype(low)
    feed_done = finish(
        place_ref,
        [feed_sums],
        ((0, units, False), (units, 2 * units, False), (2 * units, 3 * units, True)),
    )
    shared, early_done, hidden_out, feed_done, grad_first = tie(
        shared, early_done, hidden_out, feed_done, grad_first
    )
    if whole_dp:
        shared = lax.all_gather(shared, "dp", axis=0, tiled=True).astype(wide)
        gradient_key = jnp.concatenate([shared[:, :64], shared[:, 128:192]], axis=1)
        gradient_value = jnp.concatenate([shared[:, 64:128], shared[:, 192:256]], axis=1)
        gradient_write, gradient_read = shared[:, 256:384], shared[:, 384:512]
    else:
        near = dp_pieces(shared)
        gradient_key, gradient_value, gradient_write, gradient_read = assemble(
            me_ref, near, swap(near, "dp", 1)
        )

    grad_first = grad_first.astype(wide)
    weighted_first = grad_first * norm_in_gain
    inner_first = jnp.sum(weighted_first * rows_in, axis=-1, keepdims=True)
    gradient_hidden = (
        grad_middle
        + first_scale * weighted_first
        - rows_in * first_scale**3 * inner_first / rows_in.shape[-1]
    )

    conv_sums = flat[13:23].reshape(5, 512)[:, :width]
    return (
        hidden_out,
        gradient_hidden,
        common_sums[:4].reshape(-1),
        early_done[2],
        gradient_key,
        gradient_value,
        early_done[0],
        late_done[0],
        late_done[1],
        gradient_write,
        gradient_read,
        late_done[2],
        conv_sums[:4],
        conv_sums[4],
        common_sums[8:12],
        common_sums[12],
        flat[25, :heads_state],
        flat[26, :heads_state],
        flat[27, :heads_state],
        flat[23:25].reshape(-1)[:width],
        early_done[1],
        common_sums[4:8].reshape(-1),
        feed_done[0],
        feed_done[1],
        feed_done[2],
    )


def solution(mesh):
    placed = (
        P(("dp", "tensor"), None),
        P(),
        P("dp", "tensor"),
        P("dp", None),
        P("dp", None),
        P("tensor", "dp"),
        P("dp", "tensor"),
        P("dp", "tensor"),
        P("dp", None),
        P("dp", None),
        P("dp", "tensor"),
        P(None, "tensor"),
        P("tensor"),
        P(),
        P(),
        P("tensor"),
        P("tensor"),
        P("tensor"),
        P("tensor"),
        P("tensor", "dp"),
        P(),
        P("dp", "tensor"),
        P("dp", "tensor"),
        P("tensor", "dp"),
        P(("dp", "tensor"), None),
    )
    return jax.shard_map(
        body,
        mesh=mesh,
        in_specs=placed,
        out_specs=(
            P(("dp", "tensor"), None),
            P(("dp", "tensor"), None),
            P(),
            P("dp", "tensor"),
            P(),
            P(),
            P("tensor", "dp"),
            P("dp", "tensor"),
            P("dp", "tensor"),
            P(),
            P(),
            P("dp", "tensor"),
            P(None, "tensor"),
            P("tensor"),
            P(),
            P(),
            P("tensor"),
            P("tensor"),
            P("tensor"),
            P("tensor"),
            P("tensor", "dp"),
            P(),
            P("dp", "tensor"),
            P("dp", "tensor"),
            P("tensor", "dp"),
        ),
        check_vma=False,
    )
```

```python
import functools
import math

import jax
import jax.numpy as jnp
import numpy as np
from jax import lax
from jax.experimental import pallas as pl
from jax.experimental.pallas import tpu as pltpu
from jax.sharding import PartitionSpec as P

QH = 8
KVH = 2
HD = 64
BLOCK = 128


EPS = 1e-05
THETA = 10000.0
HIGHEST = lax.Precision.HIGHEST


def product(left, right):
    return jnp.dot(left, right, preferred_element_type=jnp.float32)


def product_left(left, right):
    return lax.dot_general(
        left, right, (((0,), (0,)), ((), ())), preferred_element_type=jnp.float32
    )


def product_right(left, right):
    return lax.dot_general(
        left, right, (((1,), (1,)), ((), ())), preferred_element_type=jnp.float32
    )


def root_norm(rows, gain):
    scale = lax.rsqrt(jnp.mean(rows * rows, axis=-1, keepdims=True) + EPS)
    return (rows * scale * gain, scale)


def dot(left, right, dims=((1,), (0,)), precision=None):
    return lax.dot_general(
        left, right, (dims, ((), ())), precision=precision, preferred_element_type=jnp.float32
    )


NN = ((1,), (0,))
NT = ((1,), (1,))
TN = ((0,), (0,))


def sigmoid(values):
    return 1.0 / (1.0 + jnp.exp(-values))


def softplus(values):
    return jnp.maximum(values, 0.0) + jnp.log1p(jnp.exp(-jnp.abs(values)))


def lane_index(rows):
    return lax.broadcasted_iota(jnp.int32, (rows, 128), 1)


def spread_heads(values, width):
    first = lane_index(values.shape[0]) < HD
    return jnp.concatenate(
        [
            jnp.where(first, values[:, at : at + 1], values[:, at + 1 : at + 2])
            for at in range(0, width // HD, 2)
        ],
        axis=1,
    )


def slot_rows(place_ref, at):
    return pl.ds(pl.multiple_of((place_ref[0] ^ at) * BLOCK, BLOCK), BLOCK)


def lower_mask():
    rows = lax.broadcasted_iota(jnp.int32, (BLOCK, BLOCK), 0)
    columns = lax.broadcasted_iota(jnp.int32, (BLOCK, BLOCK), 1)
    return rows >= columns


def block_decay(raw_steps, step_bias, rate, lower):
    step = softplus(raw_steps + step_bias)
    running = dot(lower.astype(jnp.float32), step * rate, NN, HIGHEST)
    return step, running, running.T


def block_weights(running, running_t, lower, head):
    spread = running[:, head : head + 1] - running_t[head : head + 1, :]
    return jnp.exp(jnp.where(lower, spread, -1e30))


def fill_history(place_ref, raw_ref, history_ref, blocks, width):
    history_ref[0:8, :] = jnp.zeros((8, history_ref.shape[1]), jnp.float32)
    for at in range(blocks):
        rows = slot_rows(place_ref, at)
        here = slice(8 + at * BLOCK, 8 + (at + 1) * BLOCK)
        history_ref[here, 0:width] = raw_ref[rows, 512 + width : 512 + 2 * width]
        history_ref[here, width : width + 256] = raw_ref[rows, 256:512]


def state_forward_kernel(
    place_ref,
    raw_ref,
    taps_ref,
    heads_ref,
    skip_ref,
    gated_ref,
    power_ref,
    conv_ref,
    y_ref,
    states_ref,
    history_ref,
):
    low = jnp.bfloat16
    width = gated_ref.shape[1]
    blocks = gated_ref.shape[0] // BLOCK
    fill_history(place_ref, raw_ref, history_ref, blocks, width)
    lower = lower_mask()
    first = lane_index(BLOCK) < HD
    state = jnp.zeros((states_ref.shape[1], width), jnp.float32)
    for at in range(blocks):
        rows = slot_rows(place_ref, at)
        conv = taps_ref[4:5, :]
        for tap in range(4):
            conv = conv + taps_ref[tap : tap + 1, :] * history_ref[pl.ds(5 + tap + at * BLOCK, BLOCK), :]
        conv_ref[rows, :] = conv
        acted = conv * sigmoid(conv)
        inner = acted[:, :width]
        write = acted[:, width : width + 128].astype(low)
        read = acted[:, width + 128 :].astype(low)
        step, running, running_t = block_decay(
            raw_ref[rows, 512 + 2 * width :], heads_ref[0:1, :], heads_ref[1:2, :], lower
        )
        scaled = inner * spread_heads(step, width)
        scaled_low = scaled.astype(low)
        zero = jnp.zeros((BLOCK, 128), low)
        meet = dot(read, write, NT)
        inside = []
        for pair in range(width // 128):
            both = jnp.concatenate(
                [
                    (meet * block_weights(running, running_t, lower, 2 * pair)).astype(low),
                    (meet * block_weights(running, running_t, lower, 2 * pair + 1)).astype(low),
                ],
                axis=1,
            )
            piece = scaled_low[:, pair * 128 : (pair + 1) * 128]
            split = jnp.concatenate([jnp.where(first, piece, zero), jnp.where(first, zero, piece)])
            inside.append(dot(both, split))
        earlier = dot(read, state.astype(low))
        y = jnp.concatenate(inside, axis=1) + spread_heads(jnp.exp(running), width) * earlier
        y_ref[rows, :] = y
        states_ref[at] = state
        last = running[BLOCK - 1 : BLOCK, :]
        carried = (spread_heads(jnp.exp(last - running), width) * scaled).astype(low)
        state = spread_heads(jnp.exp(last), width) * state + dot(write, carried, TN)
        gate = raw_ref[rows, 512 : 512 + width]
        gated = (y + skip_ref[0:1, :] * inner) * gate * sigmoid(gate)
        gated_ref[rows, :] = gated
        power_ref[:, rows] = dot(jnp.ones((8, width), jnp.float32), gated * gated, NT, HIGHEST)


def state_backward_kernel(
    place_ref,
    raw_ref,
    conv_ref,
    y_ref,
    states_ref,
    up_ref,
    taps_ref,
    heads_ref,
    skip_ref,
    grad_ref,
    grad_taps_ref,
    grad_heads_ref,
    history_ref,
    later_ref,
):
    low = jnp.bfloat16
    width = up_ref.shape[1]
    blocks = up_ref.shape[0] // BLOCK
    length = up_ref.shape[0]
    every = width + 256
    fill_history(place_ref, raw_ref, history_ref, blocks, width)
    later_ref[length : length + 8, :] = jnp.zeros((8, every), jnp.float32)
    lower = lower_mask()
    first = lane_index(BLOCK) < HD
    zero = jnp.zeros((BLOCK, 128), low)
    picks = (
        lax.broadcasted_iota(jnp.int32, (width, 128), 0) // HD
        == lax.broadcasted_iota(jnp.int32, (width, 128), 1)
    ).astype(jnp.float32)
    skip = skip_ref[0:1, :]
    rate = heads_ref[1:2, :]
    grad_state = jnp.zeros((states_ref.shape[1], width), jnp.float32)
    grad_taps = [jnp.zeros((1, every), jnp.float32) for _ in range(5)]
    grad_bias = jnp.zeros((1, 128), jnp.float32)
    grad_decay = jnp.zeros((1, 128), jnp.float32)
    grad_skip = jnp.zeros((1, width), jnp.float32)
    for at in reversed(range(blocks)):
        rows = slot_rows(place_ref, at)
        gate = raw_ref[rows, 512 : 512 + width]
        gate_sigma = sigmoid(gate)
        conv = conv_ref[rows, :]
        conv_sigma = sigmoid(conv)
        acted = conv * conv_sigma
        inner = acted[:, :width]
        write = acted[:, width : width + 128].astype(low)
        read = acted[:, width + 128 :].astype(low)
        y = y_ref[rows, :]
        up = up_ref[rows, :]
        grad_gate = up * (y + skip * inner) * gate_sigma * (1.0 + gate * (1.0 - gate_sigma))
        grad_ref[rows, 256 : 256 + width] = grad_gate.astype(low)
        grad_y = up * gate * gate_sigma
        raw_steps = raw_ref[rows, 512 + 2 * width :]
        step, running, running_t = block_decay(raw_steps, heads_ref[0:1, :], rate, lower)
        step_wide = spread_heads(step, width)
        grow = spread_heads(jnp.exp(running), width)
        last = running[BLOCK - 1 : BLOCK, :]
        carry = spread_heads(jnp.exp(last - running), width)
        last_wide = spread_heads(jnp.exp(last), width)
        scaled = inner * step_wide
        scaled_low = scaled.astype(low)
        grad_low = grad_y.astype(low)
        grown_low = (grad_y * grow).astype(low)
        state = states_ref[at]
        state_low = state.astype(low)
        grad_state_low = grad_state.astype(low)
        meet = dot(read, write, NT)
        grad_meet = jnp.zeros((BLOCK, BLOCK), jnp.float32)
        inside = []
        for pair in range(width // 128):
            weights = [
                block_weights(running, running_t, lower, head) for head in (2 * pair, 2 * pair + 1)
            ]
            both = jnp.concatenate([(meet * item).astype(low) for item in weights], axis=0)
            piece = grad_low[:, pair * 128 : (pair + 1) * 128]
            split = jnp.concatenate([jnp.where(first, piece, zero), jnp.where(first, zero, piece)])
            grad_both = dot(split, scaled_low[:, pair * 128 : (pair + 1) * 128], NT)
            grad_meet = (
                grad_meet + grad_both[:BLOCK] * weights[0] + grad_both[BLOCK:] * weights[1]
            )
            inside.append(dot(both, split, TN))
        grad_inside = jnp.concatenate(inside, axis=1)
        from_state = carry * dot(write, grad_state_low)
        carried = carry * scaled
        grad_scaled = grad_inside + from_state
        moved = scaled * from_state
        turn = grad_low.astype(jnp.float32) * y - scaled_low.astype(jnp.float32) * grad_inside - moved
        direct = grad_y * inner
        ends = jnp.sum(moved, axis=0, keepdims=True) + last_wide * jnp.sum(
            state * grad_state, axis=0, keepdims=True
        )
        summed = dot(
            jnp.concatenate([turn, grad_scaled * inner, jnp.broadcast_to(ends, (8, width))]),
            picks,
            NN,
            HIGHEST,
        )
        grad_running = (
            dot(lower.astype(jnp.float32), summed[:BLOCK], TN, HIGHEST)
            + summed[2 * BLOCK : 2 * BLOCK + 1]
        )
        grad_step = grad_running * rate + summed[BLOCK : 2 * BLOCK]
        grad_decay = grad_decay + jnp.sum(grad_running * step * rate, axis=0, keepdims=True)
        grad_steps = grad_step * sigmoid(raw_steps + heads_ref[0:1, :])
        grad_bias = grad_bias + jnp.sum(grad_steps, axis=0, keepdims=True)
        grad_skip = grad_skip + jnp.sum(direct, axis=0, keepdims=True)
        grad_ref[rows, 256 + 2 * width :] = grad_steps.astype(low)
        grad_inner = grad_scaled * step_wide + skip * grad_y
        grad_meet_low = grad_meet.astype(low)
        grad_read = dot(grad_meet_low, write) + dot(grown_low, state_low, NT)
        grad_write = dot(grad_meet_low, read, TN) + dot(carried.astype(low), grad_state_low, NT)
        grad_state = last_wide * grad_state + dot(read, grown_low, TN)
        grad_conv = jnp.concatenate([grad_inner, grad_write, grad_read], axis=1) * (
            conv_sigma * (1.0 + conv * (1.0 - conv_sigma))
        )
        later_ref[at * BLOCK : (at + 1) * BLOCK, :] = grad_conv
        back = jnp.zeros((BLOCK, every), jnp.float32)
        for tap in range(4):
            back = back + taps_ref[tap : tap + 1, :] * later_ref[pl.ds(at * BLOCK + 3 - tap, BLOCK), :]
            seen = history_ref[pl.ds(5 + tap + at * BLOCK, BLOCK), :]
            grad_taps[tap] = grad_taps[tap] + jnp.sum(grad_conv * seen, axis=0, keepdims=True)
        grad_taps[4] = grad_taps[4] + jnp.sum(grad_conv, axis=0, keepdims=True)
        grad_ref[rows, 256 + width : 256 + 2 * width] = back[:, :width].astype(low)
        grad_ref[rows, 0:256] = back[:, width:].astype(low)
    for tap in range(5):
        grad_taps_ref[tap : tap + 1, :] = grad_taps[tap]
    grad_taps_ref[5:8, :] = jnp.zeros((3, every), jnp.float32)
    skip_heads = dot(jnp.broadcast_to(grad_skip, (8, width)), picks, NN, HIGHEST)
    grad_heads_ref[...] = jnp.zeros(grad_heads_ref.shape, jnp.float32)
    grad_heads_ref[0:1, :] = grad_bias
    grad_heads_ref[1:2, :] = grad_decay
    grad_heads_ref[2:3, :] = skip_heads[0:1]


def turned(values, cosine, sine):
    early = lane_index(values.shape[0]) % HD < HD // 2
    other = jnp.where(early, pltpu.roll(values, 128 - HD // 2, 1), pltpu.roll(values, HD // 2, 1))
    return values * cosine + other * sine


def both_heads(values, first):
    zero = jnp.zeros(values.shape, values.dtype)
    return jnp.concatenate([jnp.where(first, values, zero), jnp.where(first, zero, values)])


def attention_forward_kernel(
    place_ref, raw_ref, angle_ref, mixed_ref, kept_ref, probs_ref
):
    low = jnp.bfloat16
    blocks = mixed_ref.shape[0] // BLOCK
    first = lane_index(BLOCK) < HD
    for at in range(blocks):
        rows = slot_rows(place_ref, at)
        here = slice(at * BLOCK, (at + 1) * BLOCK)
        cosine = angle_ref[here, 0:128]
        sine = angle_ref[here, 128:256]
        pair = raw_ref[rows, 128:256]
        key = turned(pair, cosine, sine)
        kept_ref[here, 0:128] = turned(raw_ref[rows, 0:128], cosine, sine).astype(low)
        kept_ref[here, 128:256] = jnp.where(first, key, pltpu.roll(key, HD, 1)).astype(low)
        kept_ref[here, 256:384] = jnp.where(first, pltpu.roll(pair, HD, 1), pair).astype(low)
    for at in range(blocks):
        rows = slot_rows(place_ref, at)
        here = slice(at * BLOCK, (at + 1) * BLOCK)
        reach = (at + 1) * BLOCK
        query = both_heads(kept_ref[here, 0:128], first)
        scores = dot(query, kept_ref[0:reach, 128:256], NT) * (HD ** (-0.5))
        row = lax.broadcasted_iota(jnp.int32, (2 * BLOCK, reach), 0) % BLOCK + at * BLOCK
        column = lax.broadcasted_iota(jnp.int32, (2 * BLOCK, reach), 1)
        scores = jnp.where(row >= column, scores, -1e30)
        exponent = jnp.exp(scores - jnp.max(scores, axis=1, keepdims=True))
        probs = (exponent / jnp.sum(exponent, axis=1, keepdims=True)).astype(low)
        probs_ref[at, :, 0:reach] = probs
        out = dot(probs, kept_ref[0:reach, 256:384])
        mixed_ref[rows, :] = jnp.where(first, out[:BLOCK], out[BLOCK:]).astype(low)


def attention_backward_kernel(
    place_ref, up_ref, angle_ref, kept_ref, probs_ref, grad_ref, key_ref, value_ref
):
    low = jnp.bfloat16
    blocks = up_ref.shape[0] // BLOCK
    first = lane_index(BLOCK) < HD
    scale = HD ** (-0.5)
    key_ref[...] = jnp.zeros(key_ref.shape, jnp.float32)
    value_ref[...] = jnp.zeros(value_ref.shape, jnp.float32)
    for at in range(blocks):
        rows = slot_rows(place_ref, at)
        here = slice(at * BLOCK, (at + 1) * BLOCK)
        reach = (at + 1) * BLOCK
        query = both_heads(kept_ref[here, 0:128], first)
        up = both_heads(up_ref[rows, :], first)
        probs_low = probs_ref[at, :, 0:reach]
        probs = probs_low.astype(jnp.float32)
        grad_probs = dot(up, kept_ref[0:reach, 256:384], NT)
        inner = jnp.sum(probs * grad_probs, axis=1, keepdims=True)
        grad_scores = (probs * (grad_probs - inner)).astype(low)
        both = dot(grad_scores, kept_ref[0:reach, 128:256]) * scale
        grad_query = jnp.where(first, both[:BLOCK], both[BLOCK:])
        grad_ref[rows, 0:128] = turned(
            grad_query, angle_ref[here, 0:128], -angle_ref[here, 128:256]
        ).astype(low)
        key_ref[0:reach, :] += dot(grad_scores, query, TN)
        value_ref[0:reach, :] += dot(probs_low, up, TN)
    for at in range(blocks):
        rows = slot_rows(place_ref, at)
        here = slice(at * BLOCK, (at + 1) * BLOCK)
        key = key_ref[here, :]
        value = value_ref[here, :]
        key = (key + pltpu.roll(key, HD, 1)) * scale
        key = turned(key, angle_ref[here, 0:128], -angle_ref[here, 128:256])
        value = value + pltpu.roll(value, HD, 1)
        grad_ref[rows, 128:256] = jnp.where(first, key, value).astype(low)


def angle_table(length):
    half = HD // 2
    freq = THETA ** (-np.arange(half, dtype=np.float32) / half)
    angle = np.arange(length, dtype=np.float32)[:, None] * freq[None, :]
    cosine = np.tile(np.cos(angle), (1, 4))
    sine = np.tile(np.concatenate([-np.sin(angle), np.sin(angle)], axis=1), (1, 2))
    return np.concatenate([cosine, sine], axis=1).astype(np.float32)


def run_kernel(kernel, place, operands, outs, scratch, name, flops=2e8, limit=None):
    whole = pl.BlockSpec(memory_space=pltpu.VMEM)
    held = sum(item.size * item.dtype.itemsize for item in operands)
    held += sum(math.prod(shape) * jnp.dtype(dtype).itemsize for shape, dtype in outs)
    held += sum(math.prod(item.shape) * jnp.dtype(item.dtype).itemsize for item in scratch)
    return pl.pallas_call(
        kernel,
        out_shape=[jax.ShapeDtypeStruct(shape, dtype) for shape, dtype in outs],
        in_specs=[pl.BlockSpec(memory_space=pltpu.SMEM)] + [whole] * len(operands),
        out_specs=[whole] * len(outs),
        scratch_shapes=scratch,
        compiler_params=pltpu.CompilerParams(vmem_limit_bytes=limit or held + 8 * 2**20),
        cost_estimate=pl.CostEstimate(flops=int(flops), bytes_accessed=1 << 20, transcendentals=0),
        name=name,
    )(place, *operands)


def state_forward(place, raw, taps, heads, skip, states):
    length = raw.shape[0]
    width = skip.shape[1]
    wide = jnp.float32
    return run_kernel(
        state_forward_kernel,
        place,
        (raw, taps, heads, skip),
        [
            ((length, width), wide),
            ((8, length), wide),
            ((length, width + 256), wide),
            ((length, width), wide),
            ((length // BLOCK, states, width), wide),
        ],
        [pltpu.VMEM((length + 8, width + 256), wide)],
        "state_forward",
    )


def state_backward(place, raw, conv, y, states, up, taps, heads, skip):
    length = raw.shape[0]
    width = skip.shape[1]
    wide = jnp.float32
    return run_kernel(
        state_backward_kernel,
        place,
        (raw, conv, y, states, up, taps, heads, skip),
        [
            ((length, 256 + 2 * width + 128), jnp.bfloat16),
            ((8, width + 256), wide),
            ((8, 128), wide),
        ],
        [pltpu.VMEM((length + 8, width + 256), wide), pltpu.VMEM((length + 8, width + 256), wide)],
        "state_backward",
    )


def attention_forward(place, raw, angles):
    length = raw.shape[0]
    low = jnp.bfloat16
    return run_kernel(
        attention_forward_kernel,
        place,
        (raw, angles),
        [
            ((length, 128), low),
            ((length, 384), low),
            ((length // BLOCK, 2 * BLOCK, length), low),
        ],
        [],
        "attention_forward",
    )


def attention_backward(place, up, angles, kept, probs):
    length = up.shape[0]
    return run_kernel(
        attention_backward_kernel,
        place,
        (up, angles, kept, probs),
        [((length, 256), jnp.bfloat16)],
        [pltpu.VMEM((length, 128), jnp.float32), pltpu.VMEM((length, 128), jnp.float32)],
        "attention_backward",
    )[0]


def block_columns(me_ref, mask):
    return pl.ds(pl.multiple_of((me_ref[0] ^ mask) * 128, 128), 128)


def join_rows(slots, whole_ref):
    rows = slots[0].shape[0]
    for at, slot in enumerate(slots):
        whole_ref[at * rows : (at + 1) * rows, :] = slot[...]


def pack_kernel(
    head_ref,
    rows_ref,
    gain_ref,
    query_ref,
    key_ref,
    value_ref,
    write_ref,
    read_ref,
    gate_ref,
    inner_ref,
    step_ref,
    output_ref,
    state_ref,
    feed_gate_ref,
    feed_up_ref,
    feed_down_ref,
    normed_ref,
    mixer_ref,
    feed_ref,
):
    rows = rows_ref[...].astype(jnp.float32)
    scale = lax.rsqrt(jnp.mean(rows * rows, axis=1, keepdims=True) + EPS)
    normed_ref[...] = (rows * scale * gain_ref[0:1, :]).astype(normed_ref.dtype)

    def turned_over(ref):
        return ref[...].astype(jnp.float32).T.astype(mixer_ref.dtype)

    low_head = head_ref[0] == 0
    first = lane_index(rows.shape[0]) < HD
    key = key_ref[...].astype(jnp.float32)
    value = value_ref[...].astype(jnp.float32)
    key = jnp.where(low_head, key, pltpu.roll(key, HD, 1))
    value = jnp.where(low_head, pltpu.roll(value, HD, 1), value)
    mixer_ref[:, 0:128] = query_ref[...]
    mixer_ref[:, 128:256] = jnp.where(first, key, value).astype(mixer_ref.dtype)
    mixer_ref[:, 256:384] = write_ref[...]
    mixer_ref[:, 384:512] = read_ref[...]
    at = 512
    for ref in (gate_ref, inner_ref):
        mixer_ref[:, at : at + ref.shape[1]] = ref[...]
        at += ref.shape[1]
    mixer_ref[:, at : at + 128] = jnp.zeros((rows.shape[0], 128), mixer_ref.dtype)
    mixer_ref[:, at : at + step_ref.shape[1]] = step_ref[...]
    mixer_ref[:, at + 128 : at + 256] = turned_over(output_ref)
    mixer_ref[:, at + 256 :] = turned_over(state_ref)
    units = feed_gate_ref.shape[1]
    feed_ref[:, :units] = feed_gate_ref[...]
    feed_ref[:, units : 2 * units] = feed_up_ref[...]
    feed_ref[:, 2 * units :] = turned_over(feed_down_ref)


def gather_columns(me_ref, rows_ref, side, chips):
    return jnp.concatenate(
        [rows_ref[:, block_columns(me_ref, 2 * at + side)] for at in range(chips)], axis=1
    )


def project_kernel(me_ref, *refs):
    slots, (near_ref, far_ref, rows_ref, raw_ref) = refs[:-4], refs[-4:]
    join_rows(slots, rows_ref)
    chips = near_ref.shape[0] // 128
    columns = raw_ref.shape[1]
    raw_ref[...] = dot(
        gather_columns(me_ref, rows_ref, 0, chips), near_ref[:, :columns]
    ) + dot(gather_columns(me_ref, rows_ref, 1, chips), far_ref[:, :columns])


def write_spread(total, own_ref, sends):
    rows = own_ref.shape[0]
    own_ref[...] = total[:rows]
    for at, send in enumerate(sends):
        send[...] = total[(at + 1) * rows : (at + 2) * rows].astype(jnp.bfloat16)


def spread_kernel(start, me_ref, mixed_ref, state_ref, near_ref, far_ref, own_ref, *rest):
    sends, total_ref = rest[:-1], rest[-1]
    left = jnp.concatenate([mixed_ref[...], state_ref[...]], axis=1)
    spread_total(me_ref, left, near_ref, far_ref, slice(start, start + left.shape[1]), total_ref)
    write_spread(total_ref[...], own_ref, sends)


def spread_total(me_ref, left, near_ref, far_ref, columns, total_ref):
    chips = near_ref.shape[0] // 128
    for side, weight_ref in enumerate((near_ref, far_ref)):
        piece = dot(left, weight_ref[:, columns], NT)
        for at in range(chips):
            total_ref[:, block_columns(me_ref, 2 * at + side)] = piece[:, at * 128 : (at + 1) * 128]


def ordered_kernel(start, place_ref, left_ref, weight_ref, out_ref):
    total = dot(left_ref[...], weight_ref[:, start : start + left_ref.shape[1]], NT)
    for at in range(total.shape[0] // BLOCK):
        out_ref[slot_rows(place_ref, at), :] = total[at * BLOCK : (at + 1) * BLOCK].astype(
            out_ref.dtype
        )


def total_kernel(
    spot_ref, attention_ref, mixer_ref, near_ref, far_ref, rows_ref, gain_ref, out_ref, total_ref
):
    left = jnp.concatenate([attention_ref[...], mixer_ref[...]], axis=1)
    spread_total(spot_ref.at[1:2], left, near_ref, far_ref, slice(0, left.shape[1]), total_ref)
    total = total_ref[...]
    gain_ref[...] = jnp.broadcast_to(
        jnp.sum(total * rows_ref[...].astype(jnp.float32), axis=0, keepdims=True), gain_ref.shape
    )
    for at in range(total.shape[0] // BLOCK):
        out_ref[slot_rows(spot_ref, at), :] = total[at * BLOCK : (at + 1) * BLOCK].astype(
            out_ref.dtype
        )


def feed_kernel(place_ref, *refs):
    low = jnp.bfloat16
    slots, cots_ref = refs[:4], refs[4]
    feed_ref, pair_ref, active_ref, own_ref = refs[5:9]
    sends = refs[9:12]
    units = active_ref.shape[1]
    rows = slots[0].shape[0]
    for half in range(2):
        here = slice(2 * half * rows, 2 * (half + 1) * rows)
        left = jnp.concatenate([slots[2 * half][...], slots[2 * half + 1][...]])
        cot = jnp.concatenate([cots_ref[slot_rows(place_ref, 2 * half + at), :] for at in range(2)])
        gate_up = dot(left, feed_ref[:, : 2 * units])
        grad_active = dot(cot, feed_ref[:, 2 * units :])
        gate = gate_up[:, :units]
        up = gate_up[:, units:]
        sigma = sigmoid(gate)
        swish = gate * sigma
        active_ref[here, :] = (swish * up).astype(low)
        grad_gate = grad_active * up * sigma * (1.0 + gate * (1.0 - sigma))
        pair = jnp.concatenate([grad_gate, grad_active * swish], axis=1).astype(low)
        pair_ref[here, :] = pair
        total = dot(pair, feed_ref[:, : 2 * units], NT)
        if half == 0:
            own_ref[...] = total[:rows]
            sends[0][...] = total[rows:].astype(low)
        else:
            sends[1][...] = total[:rows].astype(low)
            sends[2][...] = total[rows:].astype(low)


def write_halves(piece, even, keep_ref, give_ref, chip):
    piece = piece.astype(keep_ref.dtype)
    keep_ref[chip] = jnp.where(even, piece[:128], piece[128:])
    give_ref[chip] = jnp.where(even, piece[128:], piece[:128])


def feed_grad_kernel(place_ref, *refs):
    slots, cots_ref = refs[:4], refs[4]
    pair_ref, active_ref, out_ref, rows_ref, cot_ref = refs[5:]
    join_rows(slots, rows_ref)
    for at in range(len(slots)):
        cot_ref[at * BLOCK : (at + 1) * BLOCK, :] = cots_ref[slot_rows(place_ref, at), :]
    both = pair_ref.shape[1]
    for at in range(0, rows_ref.shape[1], 256):
        here = slice(at, at + 256)
        out_ref[here, :both] = dot(rows_ref[:, here], pair_ref[...], TN).astype(out_ref.dtype)
        out_ref[here, both:] = dot(cot_ref[:, here], active_ref[...], TN).astype(out_ref.dtype)


def core_add_kernel(me_ref, *refs):
    outs = refs[-4:]
    chip = me_ref[0] // 2
    keep_ref, got_ref = refs[:2]
    rows = keep_ref.shape[1]
    for mask, out in enumerate(outs):
        at = chip ^ mask
        total = keep_ref[at].astype(jnp.float32) + got_ref[at].astype(jnp.float32)
        out[0:rows, :] = total.astype(out.dtype)
        if len(refs) > 6:
            total = refs[2][...].astype(jnp.float32) + refs[3][...].astype(jnp.float32)
            out[rows:, :] = total.astype(out.dtype)


def finish_kernel(layout, place_ref, *refs):
    terms, outs = refs[: len(refs) - len(layout)], refs[len(refs) - len(layout) :]
    total = paired_sum([item[...].astype(jnp.float32) for item in terms])
    for (start, stop, over), out in zip(layout, outs):
        piece = total[:, start:stop]
        out[...] = piece.T if over else piece


def assemble_kernel(me_ref, near_ref, far_ref, key_ref, value_ref, write_ref, read_ref):
    wide = jnp.float32
    rows = 128
    first = lane_index(rows) < HD
    for side, ref in enumerate((near_ref, far_ref)):
        for chip in range(near_ref.shape[0] // rows):
            here = slice(chip * rows, (chip + 1) * rows)
            there = pl.ds(pl.multiple_of((me_ref[0] ^ (2 * chip + side)) * rows, rows), rows)
            low_head = ref[here, 0:128].astype(wide)
            high_head = ref[here, 128:256].astype(wide)
            key_ref[there, :] = jnp.where(first, low_head, pltpu.roll(high_head, HD, 1))
            value_ref[there, :] = jnp.where(first, pltpu.roll(low_head, HD, 1), high_head)
            write_ref[there, :] = ref[here, 256:384].astype(wide)
            read_ref[there, :] = ref[here, 384:512].astype(wide)


def weight_grad_kernel(groups, me_ref, *refs):
    keep_ref, give_ref = refs[-2:]
    even = me_ref[0] % 2 == 0
    for chip in range(keep_ref.shape[0]):
        here = slice(chip * 256, (chip + 1) * 256)
        pieces = []
        at = 0
        for count in groups:
            left = refs[at][:, here]
            right = jnp.concatenate([item[...] for item in refs[at + 1 : at + 1 + count]], axis=1)
            pieces.append(dot(left, right, TN))
            at += 1 + count
        write_halves(jnp.concatenate(pieces, axis=1), even, keep_ref, give_ref, chip)


def mixer_back_kernel(start, me_ref, *refs):
    slots = refs[:4]
    near_ref, far_ref, gated_ref, gain_ref, normed_ref = refs[4:9]
    cot_ref, mixed_ref, state_ref, inner_ref, gain_out_ref = refs[9:]
    join_rows(slots, cot_ref)
    chips = near_ref.shape[0] // 128
    both = dot(gather_columns(me_ref, cot_ref, 0, chips), near_ref[:, start:]) + dot(
        gather_columns(me_ref, cot_ref, 1, chips), far_ref[:, start:]
    )
    mixed_ref[...] = both[:, :128].astype(jnp.bfloat16)
    state = both[:, 128:]
    state_ref[...] = state
    gain_sum = jnp.sum(state * normed_ref[...].astype(jnp.float32), axis=0, keepdims=True)
    gain_out_ref[...] = jnp.broadcast_to(gain_sum / gain_ref[0:1, :], gain_out_ref.shape)
    product_rows = state * gain_ref[0:1, :] * gated_ref[...]
    inner_ref[...] = dot(
        jnp.ones((8, product_rows.shape[1]), jnp.float32), product_rows, NT, HIGHEST
    )


def pack(head, hidden, gain, *weights):
    rows, columns = hidden.shape
    low = jnp.bfloat16
    width = weights[5].shape[1]
    units = weights[-3].shape[1]
    return run_kernel(
        pack_kernel,
        head,
        (hidden, gain, *weights),
        [((rows, columns), low), ((rows, 768 + 3 * width), low), ((rows, 3 * units), low)],
        [],
        "pack",
        limit=60 * 2**20,
    )


def middle_kernel(
    spot_ref,
    up_ref,
    angle_ref,
    kept_ref,
    probs_ref,
    cot_ref,
    mixed_ref,
    state_ref,
    rows_ref,
    active_ref,
    feed_ref,
    grad_ref,
    keep_ref,
    give_ref,
    terms_ref,
    key_ref,
    value_ref,
):
    attention_backward_kernel(
        spot_ref, up_ref, angle_ref, kept_ref, probs_ref, grad_ref, key_ref, value_ref
    )
    weight_grad_kernel(
        (2, 1),
        spot_ref.at[1:2],
        cot_ref,
        mixed_ref,
        state_ref,
        rows_ref,
        grad_ref,
        keep_ref,
        give_ref,
    )
    units = active_ref.shape[1]
    ordered_kernel(2 * units, spot_ref, active_ref, feed_ref, terms_ref)


def small_pieces(in_gain, ffn_gain, grad_taps, state_gain, grad_heads):
    width = state_gain.shape[1]
    wide = jnp.float32

    def fill(row):
        missing = -row.shape[1] % 256
        if missing:
            row = jnp.concatenate([row, jnp.zeros((1, missing), wide)], axis=1)
        return [row[:, at : at + 256] for at in range(0, row.shape[1], 256)]

    pieces = fill(in_gain) + fill(ffn_gain)
    for tap in range(5):
        pieces += fill(grad_taps[tap : tap + 1, width:])
    for tap in range(5):
        pieces += fill(grad_taps[tap : tap + 1, :width])
    pieces += fill(state_gain)
    for row in range(3):
        pieces += fill(grad_heads[row : row + 1, :])
    return pieces + [jnp.zeros((1, 256), wide)] * (32 - len(pieces))


def last_kernel(
    spot_ref,
    raw_ref,
    conv_ref,
    y_ref,
    states_ref,
    up_ref,
    taps_ref,
    heads_ref,
    skip_ref,
    attention_ref,
    near_ref,
    far_ref,
    rows_ref,
    in_gain_ref,
    second_ref,
    normed_ref,
    ffn_gain_ref,
    state_gain_ref,
    pair_keep_ref,
    pair_give_ref,
    late_keep_ref,
    late_give_ref,
    total_low_ref,
    small_ref,
    grad_ref,
    grad_taps_ref,
    grad_heads_ref,
    history_ref,
    later_ref,
    gain_ref,
    total_ref,
    rows_small_ref,
):
    state_backward_kernel(
        spot_ref,
        raw_ref,
        conv_ref,
        y_ref,
        states_ref,
        up_ref,
        taps_ref,
        heads_ref,
        skip_ref,
        grad_ref,
        grad_taps_ref,
        grad_heads_ref,
        history_ref,
        later_ref,
    )
    me_ref = spot_ref.at[1:2]
    weight_grad_kernel(
        (1,), me_ref, rows_ref, grad_ref.at[:, 0:256], pair_keep_ref, pair_give_ref
    )
    total_kernel(
        spot_ref,
        attention_ref,
        grad_ref,
        near_ref,
        far_ref,
        rows_ref,
        gain_ref,
        total_low_ref,
        total_ref,
    )
    weight_grad_kernel(
        (1,),
        me_ref,
        rows_ref,
        grad_ref.at[:, 256 : grad_ref.shape[1]],
        late_keep_ref,
        late_give_ref,
    )
    ffn_gain = jnp.sum(
        second_ref[...] * normed_ref[...].astype(jnp.float32), axis=0, keepdims=True
    )
    pieces = small_pieces(
        gain_ref[0:1, :] / in_gain_ref[0:1, :],
        ffn_gain / ffn_gain_ref[0:1, :],
        grad_taps_ref[...],
        state_gain_ref[0:1, :],
        grad_heads_ref[...],
    )
    for at, piece in enumerate(pieces):
        rows_small_ref[at : at + 1, :] = piece
    small_ref[...] = rows_small_ref[...].astype(small_ref.dtype)


def middle(spot, up, angles, kept, probs, cot, mixed, state, rows, active, feed):
    length = up.shape[0]
    low = jnp.bfloat16
    columns = mixed.shape[1] + state.shape[1] + 256
    scratch = pltpu.VMEM((length, 128), jnp.float32)
    return run_kernel(
        middle_kernel,
        spot,
        (up, angles, kept, probs, cot, mixed, state, rows, active, feed),
        [
            ((length, 256), low),
            ((4, 128, columns), low),
            ((4, 128, columns), low),
            ((length, rows.shape[1]), low),
        ],
        [scratch, scratch],
        "middle",
    )


def last(spot, *operands):
    raw, skip, rows = operands[0], operands[7], operands[11]
    length, width = raw.shape[0], skip.shape[1]
    low, wide = jnp.bfloat16, jnp.float32
    rest = 2 * width + 128
    every = width + 256
    return run_kernel(
        last_kernel,
        spot,
        operands,
        [
            ((4, 128, 256), low),
            ((4, 128, 256), low),
            ((4, 128, rest), low),
            ((4, 128, rest), low),
            (rows.shape, low),
            ((32, 256), low),
        ],
        [
            pltpu.VMEM((length, 256 + rest), low),
            pltpu.VMEM((8, every), wide),
            pltpu.VMEM((8, 128), wide),
            pltpu.VMEM((length + 8, every), wide),
            pltpu.VMEM((length + 8, every), wide),
            pltpu.VMEM((8, rows.shape[1]), wide),
            pltpu.VMEM(rows.shape, wide),
            pltpu.VMEM((32, 256), wide),
        ],
        "last",
        limit=60 * 2**20,
    )


def project(me, slots, near, far, columns):
    length = len(slots) * slots[0].shape[0]
    return run_kernel(
        project_kernel,
        me,
        (*slots, near, far),
        [((length, slots[0].shape[1]), jnp.bfloat16), ((length, columns), jnp.float32)],
        [],
        "project",
    )


def spread_outs(rows, columns, parts):
    return [((rows, columns), jnp.float32)] + [((rows, columns), jnp.bfloat16)] * (parts - 1)


def spread_product(me, mixed, state, near, far, start, parts):
    length, columns = mixed.shape[0], 2 * near.shape[0]
    return run_kernel(
        functools.partial(spread_kernel, start),
        me,
        (mixed, state, near, far),
        spread_outs(length // parts, columns, parts),
        [pltpu.VMEM((length, columns), jnp.float32)],
        "spread_product",
    )


def ordered_product(place, left, weight, start):
    return run_kernel(
        functools.partial(ordered_kernel, start),
        place,
        (left, weight),
        [((left.shape[0], weight.shape[0]), jnp.bfloat16)],
        [],
        "ordered_product",
    )[0]


def total_product(spot, attention, mixer, near, far, rows):
    length, columns = rows.shape
    return run_kernel(
        total_kernel,
        spot,
        (attention, mixer, near, far, rows),
        [((8, columns), jnp.float32), ((length, columns), jnp.bfloat16)],
        [pltpu.VMEM((length, columns), jnp.float32)],
        "total_product",
    )


def feed_forward(place, slots, cotangent, feed):
    rows, columns = slots[0].shape
    units = feed.shape[1] // 3
    parts = len(slots)
    return run_kernel(
        feed_kernel,
        place,
        (*slots, cotangent, feed),
        [((parts * rows, 2 * units), jnp.bfloat16), ((parts * rows, units), jnp.bfloat16)]
        + spread_outs(rows, columns, parts),
        [],
        "feed_forward",
    )


def feed_grad(place, slots, cotangent, pair, active):
    length, columns = pair.shape[0], slots[0].shape[1]
    scratch = pltpu.VMEM((length, columns), jnp.bfloat16)
    return run_kernel(
        feed_grad_kernel,
        place,
        (*slots, cotangent, pair, active),
        [((columns, pair.shape[1] + active.shape[1]), jnp.bfloat16)],
        [scratch, scratch],
        "feed_grad",
    )[0]


def weight_grad(me, groups):
    counts = tuple(len(rights) for _, rights in groups)
    columns = sum(item.shape[1] for _, rights in groups for item in rights)
    operands = [item for left, rights in groups for item in (left, *rights)]
    blocks = groups[0][0].shape[1] // 256
    return run_kernel(
        functools.partial(weight_grad_kernel, counts),
        me,
        operands,
        [((blocks, 128, columns), jnp.bfloat16)] * 2,
        [],
        "weight_grad",
    )


def core_add(me, operands):
    keep = operands[0]
    rows = keep.shape[1] + (operands[2].shape[0] if len(operands) > 2 else 0)
    return run_kernel(
        core_add_kernel,
        me,
        operands,
        [((rows, keep.shape[2]), jnp.bfloat16)] * 4,
        [],
        "core_add",
    )


def finish(place, terms, layout):
    rows = terms[0].shape[0]
    if rows != 128:
        total = terms[0].astype(jnp.float32)
        pieces = [total[:, start:stop] for start, stop, _ in layout]
        return [item.T if over else item for item, (_, _, over) in zip(pieces, layout)]
    shapes = [
        ((stop - start, rows) if over else (rows, stop - start), jnp.float32)
        for start, stop, over in layout
    ]
    return run_kernel(
        functools.partial(finish_kernel, layout), place, terms, shapes, [], "finish"
    )


def assemble(me, near, far):
    rows = 2 * near.shape[0]
    return run_kernel(
        assemble_kernel, me, (near, far), [((rows, 128), jnp.float32)] * 4, [], "assemble"
    )


def mixer_back(me, slots, near, far, start, gated, gain, normed):
    rows, columns = slots[0].shape
    length = len(slots) * rows
    width = gated.shape[1]
    return run_kernel(
        functools.partial(mixer_back_kernel, start),
        me,
        (*slots, near, far, gated, gain, normed),
        [
            ((length, columns), jnp.bfloat16),
            ((length, 128), jnp.bfloat16),
            ((length, width), jnp.float32),
            ((8, length), jnp.float32),
            ((8, width), jnp.float32),
        ],
        [],
        "mixer_back",
    )


def swap(values, axis, mask):
    size = lax.axis_size(axis)
    return lax.ppermute(values, axis, [(index, index ^ mask) for index in range(size)])


def tensor_gather(block):
    masks = reversed(range(1, lax.axis_size("tensor")))
    return [block] + [swap(block, "tensor", mask) for mask in masks][::-1]


def paired_sum(terms):
    while len(terms) > 1:
        terms = [terms[at] + terms[at + 1] for at in range(0, len(terms), 2)]
    return terms[0]


def tensor_send(sends):
    return [swap(item, "tensor", at + 1) for at, item in enumerate(sends)]


def finish_scatter(own, got):
    return paired_sum([own] + [item.astype(jnp.float32) for item in got])


def cut(total, parts):
    blocks = jnp.split(total, parts)
    return blocks[:1] + [item.astype(jnp.bfloat16) for item in blocks[1:]]


def slot_sum(values):
    parts = lax.axis_size("tensor")
    shaped = values.reshape(parts, -1)
    terms = [shaped]
    for mask in range(1, parts):
        got = swap(shaped, "tensor", mask)
        terms.append(jnp.stack([got[at ^ mask] for at in range(parts)]))
    return paired_sum(terms).reshape(-1)


def tie(*values):
    return lax.optimization_barrier(values)


def dp_pieces(block):
    mine = jnp.stack([block] + [swap(block, "dp", 2 * chip) for chip in range(1, 4)])
    return mine.reshape(-1, block.shape[1])


def core_terms(me_ref, groups):
    if lax.axis_size("dp") != 8:
        return jnp.concatenate(
            [product_left(left, jnp.concatenate(rights, axis=1)) for left, rights in groups], axis=1
        ).astype(jnp.bfloat16)
    keep, give = weight_grad(me_ref, groups)
    return keep, swap(give, "dp", 1)


def chip_terms(me_ref, both, small=None, after=None):
    if lax.axis_size("dp") != 8:
        summed = lax.psum_scatter(both, "dp", scatter_dimension=0, tiled=True).astype(jnp.float32)
        if small is not None:
            summed = jnp.concatenate([summed, lax.psum(small, "dp")])
        return [summed]
    operands = both
    if small is not None:
        small = small.astype(jnp.bfloat16)
        operands = (*both, small, swap(small, "dp", 1))
    own, *sends = core_add(me_ref, operands)
    if after is not None:
        sends, _ = tie(sends, after)
    return [own] + [swap(item, "dp", 2 * (at + 1)) for at, item in enumerate(sends)]


def body(
    hidden_in,
    norm_in_gain,
    query_weight,
    key_weight,
    value_weight,
    output_weight,
    gate_weight,
    inner_weight,
    write_weight,
    read_weight,
    step_weight,
    conv_weight,
    conv_bias,
    pair_conv_weight,
    pair_conv_bias,
    step_bias,
    decay_log,
    skip_gain,
    state_gain,
    state_out_weight,
    norm_ffn_gain,
    feed_gate_weight,
    feed_up_weight,
    feed_down_weight,
    out_cotangent,
):
    low = jnp.bfloat16
    wide = jnp.float32
    parts = lax.axis_size("tensor")
    place = lax.axis_index("tensor")
    place_ref = place.astype(jnp.int32).reshape(1)
    heads_here = query_weight.shape[1] // HD
    key_head = place * heads_here // (QH // KVH)
    heads_state = step_weight.shape[1]
    width = gate_weight.shape[1]
    units = feed_gate_weight.shape[1]
    states = write_weight.shape[1]

    out_start = 640 + 2 * width
    whole_dp = lax.axis_size("dp") != 8
    rows_in = hidden_in.astype(wide)
    normed, first_scale = root_norm(rows_in, norm_in_gain)
    if whole_dp:
        normed_low = normed.astype(low)
        mixer_local = jnp.concatenate(
            [
                query_weight,
                lax.dynamic_slice_in_dim(key_weight, key_head * HD, HD, 1),
                lax.dynamic_slice_in_dim(value_weight, key_head * HD, HD, 1),
                write_weight,
                read_weight,
                gate_weight,
                inner_weight,
                jnp.pad(step_weight, ((0, 0), (0, 128 - heads_state))),
                output_weight.T,
                state_out_weight.T,
            ],
            axis=1,
        )
        feed_local = jnp.concatenate([feed_gate_weight, feed_up_weight, feed_down_weight.T], axis=1)
    else:
        normed_low, mixer_local, feed_local = pack(
            key_head.astype(jnp.int32).reshape(1),
            hidden_in,
            norm_in_gain[None],
            query_weight,
            key_weight,
            value_weight,
            write_weight,
            read_weight,
            gate_weight,
            inner_weight,
            step_weight,
            output_weight,
            state_out_weight,
            feed_gate_weight,
            feed_up_weight,
            feed_down_weight,
        )
    row_slots = tensor_gather(normed_low)
    me_ref = lax.axis_index("dp").astype(jnp.int32).reshape(1)
    spot_ref = jnp.concatenate([place_ref, me_ref])
    if whole_dp:
        mixer_full = lax.all_gather(mixer_local, "dp", axis=0, tiled=True)
        mixer_rows = jnp.concatenate(row_slots)
        out_full = mixer_full[:, out_start:]
        mixer_full = mixer_full[:, :out_start]
        raw = product(mixer_rows, mixer_full)
    else:
        near_full = dp_pieces(mixer_local)
        near_full, row_slots = tie(near_full, row_slots)
        far_full = swap(near_full, "dp", 1)
    row_slots, feed_local, cot_block = tie(row_slots, feed_local, out_cotangent)
    cotangent = lax.all_gather(cot_block, "tensor", axis=0, tiled=True)
    feed_full = lax.all_gather(feed_local, "dp", axis=0, tiled=True)
    if not whole_dp:
        mixer_rows, raw = project(me_ref, row_slots, near_full, far_full, out_start)
    length = mixer_rows.shape[0]
    block = length // parts

    taps = jnp.concatenate(
        [
            jnp.concatenate([conv_weight, conv_bias[None]]),
            jnp.concatenate([pair_conv_weight, pair_conv_bias[None]]),
        ],
        axis=1,
    )
    taps = jnp.pad(taps, ((0, 3), (0, 0)))
    heads = jnp.pad(
        jnp.stack([step_bias, -jnp.exp(decay_log)]), ((0, 6), (0, 128 - heads_state))
    )
    skip = jnp.repeat(skip_gain, HD)[None]
    angles = jnp.asarray(angle_table(length))

    gated, power, conv, y, kept_states = state_forward(place_ref, raw, taps, heads, skip, states)
    mixed_low, kept, probs = attention_forward(place_ref, raw, angles)
    width_all = width * parts
    power = slot_sum(power[0])
    state_scale = lax.rsqrt(power / width_all + EPS)[:, None]
    state_low = (gated * state_scale * state_gain).astype(low)
    if whole_dp:
        total = product_right(jnp.concatenate([mixed_low, state_low], axis=1), out_full)
        own, *sends = cut(total, parts)
    else:
        own, *sends = spread_product(
            me_ref, mixed_low, state_low, near_full, far_full, out_start, parts
        )
    mixer_shard = finish_scatter(own, tensor_send(sends))
    middle_rows = rows_in + mixer_shard
    second, second_scale = root_norm(middle_rows, norm_ffn_gain)
    second_low = second.astype(low)
    feed_slots = tensor_gather(second_low)
    grad_pair, active, own, *sends = feed_forward(place_ref, feed_slots, cotangent, feed_full)
    second_got = tensor_send(sends)
    if whole_dp:
        cot_slots = jnp.split(cotangent, parts)
        cot_slots = jnp.concatenate(
            [lax.dynamic_index_in_dim(jnp.stack(cot_slots), place ^ at, 0, False) for at in range(parts)]
        )
        feed_both = jnp.concatenate(
            [product_left(jnp.concatenate(feed_slots), grad_pair), product_left(cot_slots, active)],
            axis=1,
        ).astype(low)
    else:
        feed_both = feed_grad(place_ref, feed_slots, cotangent, grad_pair, active)
    second_got, feed_both = tie(second_got, feed_both)
    grad_second = finish_scatter(own, second_got)
    feed_sums = lax.psum_scatter(feed_both, "dp", scatter_dimension=0, tiled=True)

    weighted_second = grad_second * norm_ffn_gain
    inner_second = jnp.sum(weighted_second * middle_rows, axis=-1, keepdims=True)
    grad_middle = (
        out_cotangent.astype(wide)
        + second_scale * weighted_second
        - middle_rows * second_scale**3 * inner_second / middle_rows.shape[-1]
    )
    cot_rows = tensor_gather(grad_middle.astype(low))
    if whole_dp:
        mixer_cot = jnp.concatenate(cot_rows)
        grad_both = product(mixer_cot, out_full)
        grad_mixed, grad_state = grad_both[:, :128].astype(low), grad_both[:, 128:]
        inner_sum = jnp.sum(grad_state * state_gain * gated, axis=1)[None]
        grad_state_gain = jnp.sum(grad_state * gated * state_scale, axis=0, keepdims=True)
    else:
        mixer_cot, grad_mixed, grad_state, inner_sum, grad_state_gain = mixer_back(
            me_ref, cot_rows, near_full, far_full, out_start, gated, state_gain[None], state_low
        )
    grad_mixed, active = tie(grad_mixed, active)
    weighted = grad_state * state_gain
    inner_sum = slot_sum(inner_sum[0])
    if whole_dp:
        grad_attention = attention_backward(place_ref, grad_mixed, angles, kept, probs)
        early_both = core_terms(
            me_ref, [(mixer_cot, (mixed_low, state_low)), (mixer_rows, (grad_attention,))]
        )
        feed_terms = ordered_product(place_ref, active, feed_full, 2 * units)
    else:
        grad_attention, keep, give, feed_terms = middle(
            spot_ref,
            grad_mixed,
            angles,
            kept,
            probs,
            mixer_cot,
            mixed_low,
            state_low,
            mixer_rows,
            active,
            feed_full,
        )
        early_both = (keep, swap(give, "dp", 1))
    early_both, inner_sum = tie(early_both, inner_sum)
    early_parts = chip_terms(me_ref, early_both)
    grad_gated = (
        state_scale * weighted - gated * state_scale**3 * (inner_sum / width_all)[:, None]
    )
    grad_gated, feed_terms, feed_sums = tie(grad_gated, feed_terms, feed_sums)
    feed_shard = lax.psum_scatter(feed_terms, "tensor", scatter_dimension=0, tiled=True)
    if whole_dp:
        grad_mixer, grad_taps, grad_heads = state_backward(
            place_ref, raw, conv, y, kept_states, grad_gated, taps, heads, skip
        )
        pair_both = core_terms(me_ref, [(mixer_rows, (grad_mixer[:, :256],))])
        total_rows = product_right(grad_mixer, mixer_full[:, 256:]) + product_right(
            grad_attention, mixer_full[:, :256]
        )
        gain_rows = jnp.sum(total_rows * mixer_rows.astype(wide), axis=0, keepdims=True)
        total_rows = total_rows.astype(low).reshape(parts, block, -1)
        total_rows = jnp.concatenate(
            [lax.dynamic_index_in_dim(total_rows, place ^ at, 0, False) for at in range(parts)]
        )
        late_both = core_terms(me_ref, [(mixer_rows, (grad_mixer[:, 256:],))])
        ffn_gain = jnp.sum(grad_second * second_low.astype(wide), axis=0)
        small = jnp.concatenate(
            small_pieces(
                gain_rows / norm_in_gain,
                (ffn_gain / norm_ffn_gain)[None],
                grad_taps,
                grad_state_gain,
                grad_heads,
            )
        )
    else:
        pair_keep, pair_give, late_keep, late_give, total_rows, small = last(
            spot_ref,
            raw,
            conv,
            y,
            kept_states,
            grad_gated,
            taps,
            heads,
            skip,
            grad_attention,
            near_full,
            far_full,
            mixer_rows,
            norm_in_gain[None],
            grad_second,
            second_low,
            norm_ffn_gain[None],
            grad_state_gain,
        )
        pair_keep, pair_give, late_keep, late_give, total_rows, small, *beside = tie(
            pair_keep,
            pair_give,
            late_keep,
            late_give,
            total_rows,
            small,
            early_parts,
            feed_shard,
        )
        early_parts, feed_shard = beside
        pair_both = (pair_keep, swap(pair_give, "dp", 1))
        late_both = (late_keep, swap(late_give, "dp", 1))
    grad_first = lax.psum_scatter(total_rows, "tensor", scatter_dimension=0, tiled=True)
    late_parts = chip_terms(me_ref, late_both)
    pair_sums = paired_sum([item.astype(wide) for item in chip_terms(me_ref, pair_both, small)])
    rows_here = query_weight.shape[0]
    flat = pair_sums[rows_here:]
    early_done = finish(
        place_ref,
        early_parts,
        (
            (0, 128, True),
            (128, 128 + width, True),
            (128 + width, 256 + width, False),
            (256 + width, 384 + width, False),
        ),
    )

    shared = jnp.concatenate(
        [
            jnp.concatenate([early_done[3], pair_sums[:rows_here]], axis=1),
            jnp.pad(flat[:16], ((0, 0), (0, 128))),
        ]
    ).astype(low)
    near = shared.astype(wide) + swap(shared, "tensor", 1).astype(wide)
    near = near.astype(low)
    far = swap(near, "tensor", 2).astype(wide)
    near = near.astype(wide)
    both = near + far
    first_half = place < parts // 2
    head_low = jnp.where(first_half, near[:rows_here, :128], far[:rows_here, :128])
    head_high = jnp.where(first_half, far[:rows_here, :128], near[:rows_here, :128])
    common_sums = both[rows_here:, :256]
    shared = jnp.concatenate([head_low, head_high, both[:rows_here, 128:]], axis=1).astype(low)
    late_done = finish(
        place_ref,
        late_parts,
        ((0, width, False), (width, 2 * width, False), (2 * width, 2 * width + heads_state, False)),
    )
    hidden_out = (middle_rows + feed_shard.astype(wide)).astype(low)
    feed_done = finish(
        place_ref,
        [feed_sums],
        ((0, units, False), (units, 2 * units, False), (2 * units, 3 * units, True)),
    )
    shared, early_done, hidden_out, feed_done, grad_first = tie(
        shared, early_done, hidden_out, feed_done, grad_first
    )
    if whole_dp:
        shared = lax.all_gather(shared, "dp", axis=0, tiled=True).astype(wide)
        gradient_key = jnp.concatenate([shared[:, :64], shared[:, 128:192]], axis=1)
        gradient_value = jnp.concatenate([shared[:, 64:128], shared[:, 192:256]], axis=1)
        gradient_write, gradient_read = shared[:, 256:384], shared[:, 384:512]
    else:
        near = dp_pieces(shared)
        gradient_key, gradient_value, gradient_write, gradient_read = assemble(
            me_ref, near, swap(near, "dp", 1)
        )

    grad_first = grad_first.astype(wide)
    weighted_first = grad_first * norm_in_gain
    inner_first = jnp.sum(weighted_first * rows_in, axis=-1, keepdims=True)
    gradient_hidden = (
        grad_middle
        + first_scale * weighted_first
        - rows_in * first_scale**3 * inner_first / rows_in.shape[-1]
    )

    conv_sums = flat[13:23].reshape(5, 512)[:, :width]
    return (
        hidden_out,
        gradient_hidden,
        common_sums[:4].reshape(-1),
        early_done[2],
        gradient_key,
        gradient_value,
        early_done[0],
        late_done[0],
        late_done[1],
        gradient_write,
        gradient_read,
        late_done[2],
        conv_sums[:4],
        conv_sums[4],
        common_sums[8:12],
        common_sums[12],
        flat[25, :heads_state],
        flat[26, :heads_state],
        flat[27, :heads_state],
        flat[23:25].reshape(-1)[:width],
        early_done[1],
        common_sums[4:8].reshape(-1),
        feed_done[0],
        feed_done[1],
        feed_done[2],
    )


def solution(mesh):
    placed = (
        P(("dp", "tensor"), None),
        P(),
        P("dp", "tensor"),
        P("dp", None),
        P("dp", None),
        P("tensor", "dp"),
        P("dp", "tensor"),
        P("dp", "tensor"),
        P("dp", None),
        P("dp", None),
        P("dp", "tensor"),
        P(None, "tensor"),
        P("tensor"),
        P(),
        P(),
        P("tensor"),
        P("tensor"),
        P("tensor"),
        P("tensor"),
        P("tensor", "dp"),
        P(),
        P("dp", "tensor"),
        P("dp", "tensor"),
        P("tensor", "dp"),
        P(("dp", "tensor"), None),
    )
    return jax.shard_map(
        body,
        mesh=mesh,
        in_specs=placed,
        out_specs=(
            P(("dp", "tensor"), None),
            P(("dp", "tensor"), None),
            P(),
            P("dp", "tensor"),
            P(),
            P(),
            P("tensor", "dp"),
            P("dp", "tensor"),
            P("dp", "tensor"),
            P(),
            P(),
            P("dp", "tensor"),
            P(None, "tensor"),
            P("tensor"),
            P(),
            P(),
            P("tensor"),
            P("tensor"),
            P("tensor"),
            P("tensor"),
            P("tensor", "dp"),
            P(),
            P("dp", "tensor"),
            P("dp", "tensor"),
            P("tensor", "dp"),
        ),
        check_vma=False,
    )
```
